32 devices in a mesh: fsdp: 8 (over z, x), tp: 4 (over y, core).
Axes of the slice: x: 2, y: 2, z: 4, core: 2. Of those that a mesh axis runs over, the one named last changes fastest.
Arguments:
- tokens: bfloat16 [2, 1024, 2048], P(None, 'fsdp'), may hold values from -6 to 6
- cotangent: bfloat16 [2, 1024, 2048], P(None, 'fsdp'), may hold values from -6 to 6
- expert_ids: int32 [2, 1024, 8], P(None, 'fsdp'), may hold values from 0 to 31, all different within a row; in each aligned block of 128 rows (0 to 127, 128 to 255, ..., all dimensions but the last counted through in order) at most 40 rows name the same one
- attention_gain: float32 [2048], replicated, may hold values from 0.5 to 1.5
- query_gain: float32 [128], replicated, may hold values from 0.5 to 1.5
- key_gain: float32 [128], replicated, may hold values from 0.5 to 1.5
- query_weight: bfloat16 [2048, 4096], P('fsdp', 'tp'), may hold values from -0.125 to 0.125
- key_weight: bfloat16 [2048, 512], P('fsdp', 'tp'), may hold values from -0.125 to 0.125
- value_weight: bfloat16 [2048, 512], P('fsdp', 'tp'), may hold values from -0.125 to 0.125
- output_weight: bfloat16 [2048, 4096], P('fsdp', 'tp'), may hold values from -0.75 to 0.75
- expert_gain: float32 [2048], replicated, may hold values from 0.5 to 1.5
- router_weight: bfloat16 [2048, 32], P('fsdp'), may hold values from -0.0625 to 0.0625
- gate_weight: bfloat16 [32, 768, 2048], P('fsdp', 'tp'), may hold values from -0.125 to 0.125
- up_weight: bfloat16 [32, 768, 2048], P('fsdp', 'tp'), may hold values from -0.125 to 0.125
- down_weight: bfloat16 [32, 768, 2048], P('fsdp', 'tp'), may hold values from -0.875 to 0.875
Outputs:
- layer_output: bfloat16 [2, 1024, 2048], P(None, 'fsdp')
- tokens_gradient: bfloat16 [2, 1024, 2048], P(None, 'fsdp')
- attention_gain_gradient: float32 [2048], P('fsdp')
- query_gain_gradient: float32 [128], P('fsdp')
- key_gain_gradient: float32 [128], P('fsdp')
- query_weight_gradient: float32 [2048, 4096], P('fsdp', 'tp')
- key_weight_gradient: float32 [2048, 512], P('fsdp', 'tp')
- value_weight_gradient: float32 [2048, 512], P('fsdp', 'tp')
- output_weight_gradient: float32 [2048, 4096], P('fsdp', 'tp')
- expert_gain_gradient: float32 [2048], P('fsdp')
- router_weight_gradient: float32 [2048, 32], P('fsdp')
- gate_weight_gradient: float32 [32, 768, 2048], P('fsdp', 'tp')
- up_weight_gradient: float32 [32, 768, 2048], P('fsdp', 'tp')
- down_weight_gradient: float32 [32, 768, 2048], P('fsdp', 'tp')
The draws below stay inside these ranges and needn't reach their ends.
Inputs may be any that keep to these rules, and one draw needn't show every extreme that they name: `expert_ids`: each row names 8 different experts. Among the 128 tokens of one micro-batch on one index of fsdp (aligned blocks of 128 rows), no expert is named more than 40 times, and in some such block some expert is named exactly 40 times.
All inputs are finite; a program needn't handle non-finite values.
Results may differ from the reference program's by a relative error of at most 0.029.
Values may be sent and summed in bfloat16 or wider, within the bound.
A program may use at most 256 MiB of HBM per device.

```python
import math
import jax
import jax.numpy as jnp
import numpy as np
from jax import lax

D = 2048
HEADS = 32
KV_HEADS = 4
HEAD_DIM = 128
FF = 768
TOP = 8
TOK_DEV = 128
MB = 2
EXPERTS = 32
SEQ = 1024
CAP = 40
N_FSDP = 8


def strengthened(values, rng, source, target, blocks, factor):
    def block_of(dim):
        return (jnp.arange(values.shape[dim]) // (values.shape[dim] // blocks)).reshape((-1,) + (1,) * (values.ndim - 1 - dim))

    first = jax.random.permutation(rng, blocks)[block_of(target)]
    second = (block_of(target) + blocks // 2) % blocks
    return jnp.where((block_of(source) == first) | (block_of(source) == second), factor * values, values)


def block_scale(rng, dims, pieces, low, high):
    loudness, own = 1.0, jax.random.fold_in(rng, 6)
    for axis_at, parts in pieces:
        heights = jnp.exp(jax.random.uniform(jax.random.fold_in(own, axis_at), (parts,), jnp.float32, low / len(pieces), high / len(pieces)))
        loudness = loudness * jnp.repeat(heights, dims[axis_at] // parts).reshape([-1 if axis == axis_at else 1 for axis in range(len(dims))])
    return loudness


def shared_out(rng, own, number, rows, amount, top, bound, slope):
    order = jax.random.permutation(rng, amount)
    heavy_load, usual = load_shares(amount, rows * top, bound, slope, True), load_shares(amount, rows * top, bound, slope, False)
    places = jnp.arange(amount)

    def named(lengths, offset_by):
        used = int((lengths > 0).sum())
        fixed = max(1, used // 4)
        moved = fixed + (places - fixed + offset_by * (used - fixed)) % max(1, amount - fixed)
        return jnp.zeros((amount,), jnp.int32).at[order[jnp.where(places < fixed, places, moved)]].set(jnp.asarray(lengths, jnp.int32))

    lengths = jnp.where(number % 4 == 0, named(heavy_load, number // 4), named(usual, number - number // 4 - 1))
    mixed = jax.random.permutation(jax.random.fold_in(own, 3), amount)
    donor, receiver = mixed[0:amount // 2 * 2:2], mixed[1:amount // 2 * 2:2]
    slack = jnp.minimum(lengths[donor] - 1, bound - lengths[receiver]) // 2
    slack = jnp.where((donor == order[0]) | (receiver == order[0]) | (lengths[receiver] == 0), 0, jnp.maximum(slack, 0))
    moved = jax.random.randint(jax.random.fold_in(own, 4), (amount // 2,), 0, 1 << 20) % (slack + 1)
    lengths = lengths.at[donor].add(-moved).at[receiver].add(moved)
    labels = jnp.searchsorted(jnp.cumsum(lengths), jnp.arange(rows * top), side="right").astype(jnp.int32)
    table = labels.reshape(top, rows).T
    table = table[jax.random.permutation(jax.random.fold_in(own, 1), rows)]
    offset_by = jax.random.randint(jax.random.fold_in(own, 2), (rows, 1), 0, top)
    return jnp.take_along_axis(table, (jnp.arange(top)[None, :] + offset_by) % top, axis=1)


def load_shares(amount, total, bound, skew, full):
    portions = [(1 << 20) // math.isqrt(standing ** skew) + 1 for standing in range(1, amount + 1)]
    largest = bound if full else min(bound, max(-(-total // amount), total * portions[0] // sum(portions)))
    least = 1 if total - largest >= amount - 1 else 0
    counts, spare = [largest] + [least] * (amount - 1), total - largest - least * (amount - 1)
    while spare > 0:
        candidates = [i for i in range(1, amount) if counts[i] < largest] or [i for i in range(1, amount) if counts[i] < bound]
        whole, remaining = sum([portions[i] for i in candidates]), spare
        for i in candidates:
            addition = min(bound - counts[i], max(1, remaining * portions[i] // whole), spare)
            counts[i] = counts[i] + addition
            spare = spare - addition
    return np.array(counts)


def normal_values(rng, extent, deviation, limit, cuts=(), kind=jnp.bfloat16):
    loudness = block_scale(rng, extent, cuts, -0.22, 0.18) if cuts else 1.0
    drawn = jax.random.normal(rng, extent, jnp.float32) * deviation * loudness
    return jnp.minimum(jnp.maximum(drawn, -limit), limit).astype(kind)


def noise_with(rng, dims, width, limit, pieces, heavy, kind=jnp.bfloat16):
    drawn = width * jax.random.normal(rng, dims, jnp.float32)
    if pieces:
        drawn = drawn * block_scale(rng, dims, pieces, -0.22, 0.18)
    return jnp.clip(strengthened(drawn, jax.random.fold_in(rng, 3), *heavy), -limit, limit).astype(kind)


def setup_inputs(seed: int = 0) -> dict:
    splits = jax.random.split(jax.random.key(seed), 16)
    tokens = normal_values(splits[0], (MB, SEQ, D), 1.0, 6.0, ((1, 8),))
    cotangent = noise_with(splits[1], (MB, SEQ, D), 1.0, 6.0, ((1, 8),), (1, 2, 8, 2.0))
    expert_ids_keys = jax.random.split(jax.random.fold_in(splits[2], 1), MB * SEQ // TOK_DEV)
    expert_ids_turns = jax.random.permutation(jax.random.fold_in(splits[2], 3), MB * SEQ // TOK_DEV)
    expert_ids = jax.vmap(lambda own, number: shared_out(jax.random.fold_in(splits[2], 2), own, number, TOK_DEV, EXPERTS, TOP, CAP, 0))(expert_ids_keys, expert_ids_turns).reshape((MB, SEQ, TOP))
    attention_gain = jnp.clip(1.0 + 0.1 * jax.random.normal(splits[3], (D,), jnp.float32), 0.5, 1.5)
    query_gain = jnp.clip(1.0 + 0.1 * jax.random.normal(splits[4], (HEAD_DIM,), jnp.float32), 0.5, 1.5)
    key_gain = jnp.clip(1.0 + 0.1 * jax.random.normal(splits[5], (HEAD_DIM,), jnp.float32), 0.5, 1.5)
    query_weight = normal_values(splits[6], (D, HEADS * HEAD_DIM), D ** -0.5, 0.125, ((0, 8), (1, 4)))
    key_weight = normal_values(splits[7], (D, KV_HEADS * HEAD_DIM), D ** -0.5, 0.125, ((0, 8), (1, 4)))
    value_weight = normal_values(splits[8], (D, KV_HEADS * HEAD_DIM), D ** -0.5, 0.125, ((0, 8), (1, 4)))
    output_weight = normal_values(splits[9], (D, HEADS * HEAD_DIM), (max(1, HEADS * HEAD_DIM * 16 // SEQ)) ** -0.5, 0.75, ((0, 8), (1, 4)))
    expert_gain = jnp.clip(1.0 + 0.1 * jax.random.normal(splits[10], (D,), jnp.float32), 0.5, 1.5)
    router_weight = normal_values(splits[11], (D, EXPERTS), (4 * D) ** -0.5, 0.0625, ((0, 8),))
    gate_weight = normal_values(splits[12], (EXPERTS, FF, D), D ** -0.5, 0.125, ((0, 8), (1, 4)))
    up_weight = normal_values(splits[13], (EXPERTS, FF, D), D ** -0.5, 0.125, ((0, 8), (1, 4)))
    down_weight = normal_values(splits[14], (EXPERTS, FF, D), (FF // 16) ** -0.5, 0.875, ((0, 8), (1, 4)))
    return {"tokens": tokens, "cotangent": cotangent, "expert_ids": expert_ids, "attention_gain": attention_gain, "query_gain": query_gain, "key_gain": key_gain, "query_weight": query_weight, "key_weight": key_weight, "value_weight": value_weight, "output_weight": output_weight, "expert_gain": expert_gain, "router_weight": router_weight, "gate_weight": gate_weight, "up_weight": up_weight, "down_weight": down_weight}


norm_eps = 1e-06
rope_base = 1000000.0
highest = lax.Precision.HIGHEST

@jax.custom_vjp
def low(v):
    return lax.optimization_barrier(v.astype(jnp.bfloat16)).astype(jnp.float32)

@jax.custom_vjp
def low_back(v):
    return v

def low_keep(v):
    return (low(v), None)

def low_pass(kept, grad):
    return (grad,)

def back_keep(v):
    return (v, None)

def back_low(kept, grad):
    return (low(grad),)
low.defvjp(low_keep, low_pass)
low_back.defvjp(back_keep, back_low)

def rounded_both(values):
    return low(low_back(values))

def rms_scale(values, gain):
    factor = lax.rsqrt(lax.optimization_barrier(jnp.mean(values * values, axis=-1, keepdims=True)) + norm_eps)
    return values * factor * gain

def rotate_half(values):
    middle = values.shape[-1] // 2
    return jnp.concatenate([-values[..., middle:], values[..., :middle]], axis=-1)

def rope_tables(length):
    middle = HEAD_DIM // 2
    frequency = rope_base ** (-jnp.arange(middle, dtype=jnp.float32) * 2.0 / HEAD_DIM)
    angles = jnp.arange(length, dtype=jnp.float32)[:, None] * frequency[None, :]
    angles = jnp.concatenate([angles, angles], axis=1)
    return (jnp.cos(angles), jnp.sin(angles))

def attention(queries, key_rows, values):
    length = queries.shape[0]
    block_rows = math.gcd(length, 512)
    group_size = HEADS // KV_HEADS
    score_scale = 1.0 / math.sqrt(HEAD_DIM)
    key_pos = jnp.arange(length, dtype=jnp.int32)

    def one_block(block_index):
        start = (block_index * block_rows).astype(jnp.int32)
        picked = lax.dynamic_slice_in_dim(queries, start, block_rows, 0).reshape(block_rows, KV_HEADS, group_size, HEAD_DIM)
        raw_scores = jnp.einsum('qgrd,kgd->grqk', picked, key_rows, precision=highest) * score_scale
        scores = low_back(raw_scores)
        query_pos = start + jnp.arange(block_rows, dtype=jnp.int32)
        allowed = key_pos[None, :] <= query_pos[:, None]
        scores = jnp.where(allowed[None, None], scores, -1e+30)
        row_peak = lax.optimization_barrier(jnp.max(scores, axis=-1, keepdims=True))
        shifted = jnp.exp(scores - row_peak)
        probabilities = low(shifted / lax.optimization_barrier(jnp.sum(shifted, axis=-1, keepdims=True)))
        mixture = jnp.einsum('grqk,kgd->qgrd', probabilities, values, precision=highest)
        return mixture.reshape(block_rows, HEADS * HEAD_DIM)
    blocks = lax.map(jax.checkpoint(one_block), jnp.arange(length // block_rows, dtype=jnp.int32))
    return blocks.reshape(length, HEADS * HEAD_DIM)

def forward(tokens_row, routes, weights):
    attention_gain, query_gain, key_gain, query_weight, key_weight, value_weight, output_weight, expert_gain, router_weight, gate_weight, up_weight, down_weight = weights
    length = tokens_row.shape[0]
    group_cap = N_FSDP * CAP
    normed = low(rms_scale(tokens_row, attention_gain))
    queries = low_back(jnp.dot(normed, query_weight, precision=highest)).reshape(length, HEADS, HEAD_DIM)
    key_rows = low_back(jnp.dot(normed, key_weight, precision=highest)).reshape(length, KV_HEADS, HEAD_DIM)
    values = rounded_both(jnp.dot(normed, value_weight, precision=highest)).reshape(length, KV_HEADS, HEAD_DIM)
    cosine_table, sine_table = rope_tables(length)
    queries = rms_scale(queries, query_gain)
    queries = low(queries * cosine_table[:, None, :] + rotate_half(queries) * sine_table[:, None, :])
    key_rows = rms_scale(key_rows, key_gain)
    key_rows = low(key_rows * cosine_table[:, None, :] + rotate_half(key_rows) * sine_table[:, None, :])
    context = rounded_both(attention(queries, key_rows, values))
    hidden_state = tokens_row + low_back(jnp.einsum('th,dh->td', context, output_weight, precision=highest))
    expert_in = low(rms_scale(hidden_state, expert_gain))
    logits = low_back(jnp.dot(expert_in, router_weight, precision=highest))
    choose = (routes[:, :, None] == jnp.arange(EXPERTS, dtype=jnp.int32)[None, None, :]).astype(jnp.float32)
    picked = lax.optimization_barrier(jnp.sum(choose * logits[:, None, :], axis=-1))
    row_peak = lax.optimization_barrier(jnp.max(picked, axis=-1, keepdims=True))
    shifted = jnp.exp(picked - row_peak)
    gate_probs = shifted / lax.optimization_barrier(jnp.sum(shifted, axis=-1, keepdims=True))
    flat_routes = routes.reshape(-1).astype(jnp.int32)
    onehot = (flat_routes[:, None] == jnp.arange(EXPERTS, dtype=jnp.int32)[None, :]).astype(jnp.int32)
    rank_in = lax.optimization_barrier(jnp.sum((jnp.cumsum(onehot, axis=0) - onehot) * onehot, axis=1))
    slot_index = (flat_routes * group_cap + rank_in).astype(jnp.int32)
    route_rows = length * TOP
    slot_source = jnp.full((EXPERTS * group_cap,), route_rows, jnp.int32).at[slot_index].set(jnp.arange(route_rows, dtype=jnp.int32))
    copies = low_back(jnp.broadcast_to(expert_in[:, None, :], (length, TOP, D))).reshape(route_rows, D)
    padded = jnp.concatenate([copies, jnp.zeros((1, D), jnp.float32)], axis=0)
    batches = padded[slot_source].reshape(EXPERTS, group_cap, D)
    gate_pre = low_back(jnp.einsum('erd,efd->erf', batches, gate_weight, precision=highest))
    up_pre = low_back(jnp.einsum('erd,efd->erf', batches, up_weight, precision=highest))
    inner_act = low(jax.nn.silu(gate_pre) * up_pre)
    results = rounded_both(jnp.einsum('erf,efd->erd', inner_act, down_weight, precision=highest))
    routed = results.reshape(EXPERTS * group_cap, D)[slot_index].reshape(length, TOP, D)
    return hidden_state + lax.optimization_barrier(jnp.sum(gate_probs[:, :, None] * routed, axis=1))

def reference(tokens, cotangent, expert_ids, attention_gain, query_gain, key_gain, query_weight, key_weight, value_weight, output_weight, expert_gain, router_weight, gate_weight, up_weight, down_weight):
    weights = tuple((tensor.astype(jnp.float32) for tensor in (attention_gain, query_gain, key_gain, query_weight, key_weight, value_weight, output_weight, expert_gain, router_weight, gate_weight, up_weight, down_weight)))
    totals = tuple((jnp.zeros_like(tensor) for tensor in weights))
    outputs = []
    input_grads = []
    for micro_index in range(MB):
        routes = expert_ids[micro_index]

        def closed(tokens_row, *weight_list):
            return forward(tokens_row, routes, weight_list)
        result, pullback = jax.vjp(closed, tokens[micro_index].astype(jnp.float32), *weights)
        gradients = pullback(cotangent[micro_index].astype(jnp.float32))
        outputs.append(result.astype(jnp.bfloat16))
        input_grads.append(gradients[0].astype(jnp.bfloat16))
        totals = tuple((earlier + adding for earlier, adding in zip(totals, gradients[1:])))
    return (jnp.stack(outputs), jnp.stack(input_grads), totals[0], totals[1], totals[2], totals[3], totals[4], totals[5], totals[6], totals[7], totals[8], totals[9], totals[10], totals[11])
```

```python
import functools
import math

import jax
import jax.numpy as jnp
from jax import lax
from jax.experimental import pallas as pl
from jax.experimental.pallas import tpu as pltpu
from jax.sharding import PartitionSpec as P

norm_eps = 1e-06
rope_base = 1000000.0
masked_score = -1e30
MESH = pl.DeviceIdType.MESH
LOW = jnp.bfloat16
F32 = jnp.float32
VMEM_LIMIT = 60 * 2**20


def coords():
    f = lax.axis_index("fsdp")
    t = lax.axis_index("tp")
    return f // 2, f % 2, t // 2, t % 2


def place(z, x, y, c):
    return (2 * z + x, 2 * y + c)


def greet(z, x, y, c):
    barrier = pltpu.get_barrier_semaphore()
    peers = [place(z, 1 - x, y, c), place(z, x, 1 - y, c), place(z, x, y, 1 - c)]
    peers += [place((z + d) % 4, x, y, c) for d in (1, 2, 3)]
    for peer in peers:
        pl.semaphore_signal(barrier, inc=1, device_id=peer, device_id_type=MESH)
    pl.semaphore_wait(barrier, len(peers))


def push(src, dst, send_sem, recv_sem, device):
    copy = pltpu.make_async_remote_copy(
        src_ref=src, dst_ref=dst, send_sem=send_sem, recv_sem=recv_sem, device_id=device, device_id_type=MESH
    )
    copy.start()
    return copy


def landed(ref, sem, device):
    pltpu.make_async_remote_copy(
        src_ref=ref, dst_ref=ref, send_sem=sem, recv_sem=sem, device_id=device, device_id_type=MESH
    ).wait_recv()


def gather_kernel(whole, in_ref, out_ref, loc, sz, rz, sx, rx, sy, ry, sdx, rdx, sdy, rdy, sc, rc):
    z, x, y, c = coords()
    rows = in_ref.shape[1]
    cols = in_ref.shape[2] // 4
    half = rows // 2
    f = 2 * z + x
    t = 2 * y + c

    def block(z_, x_, y_, c_, h=None):
        first, count = ((2 * z_ + x_) * rows, rows) if h is None else ((2 * z_ + x_) * rows + h * half, half)
        return out_ref.at[:, pl.ds(first, count), pl.ds((2 * y_ + c_) * cols, cols)]

    def source(z_to, t_, first, count):
        seqs = slice(None) if whole else pl.ds(z_to // 2, 1)
        return in_ref.at[seqs, pl.ds(first, count), pl.ds(t_ * cols, cols)]

    greet(z, x, y, c)
    xn, yn, cn = place(z, 1 - x, y, c), place(z, x, 1 - y, c), place(z, x, y, 1 - c)
    own_src = in_ref if whole else in_ref.at[pl.ds(z // 2, 1)]
    own = pltpu.make_async_copy(own_src, out_ref.at[:, pl.ds(f * rows, rows), :], loc.at[0])
    own.start()
    order = (1, 3, 2)
    sends = []
    for d in order:
        zd = (z + d) % 4
        sends.append(push(source(zd, t, 0, rows), block(z, x, y, c), sz.at[d], rz.at[z], place(zd, x, y, c)))
    sends.append(push(source(z, t, 0, rows), block(z, x, y, c), sx.at[z], rx.at[z], xn))
    ty = 2 * (1 - y) + c
    sends.append(push(source(z, ty, 0, half), block(z, x, 1 - y, c, 0), sdx.at[z], rdx.at[z], xn))
    for d in order:
        zd = (z + d) % 4
        b = block(zd, x, y, c)
        landed(b, rz.at[zd], xn)
        sends.append(push(b, b, sx.at[zd], rx.at[zd], xn))
        sends.append(push(b, b, sy.at[zd], ry.at[zd], yn))
        sends.append(push(b, b, sc.at[0, zd], rc.at[0, zd], cn))
    for d in (0,) + order:
        zd = (z + d) % 4
        b = block(zd, 1 - x, y, c)
        landed(b, rx.at[zd], xn)
        bh = block(zd, 1 - x, y, c, 1)
        sends.append(push(bh, bh, sdy.at[zd], rdy.at[zd], yn))
        sends.append(push(b, b, sc.at[1, zd], rc.at[1, zd], cn))
        if d != 0:
            b = block(zd, x, 1 - y, c)
            landed(b, ry.at[zd], xn)
            bh = block(zd, x, 1 - y, c, 0)
            sends.append(push(bh, bh, sdx.at[zd], rdx.at[zd], xn))
            sends.append(push(b, b, sc.at[2, zd], rc.at[2, zd], cn))
    for d in (0,) + order:
        zd = (z + d) % 4
        landed(block(zd, 1 - x, 1 - y, c, 0), rdx.at[zd], xn)
        landed(block(zd, 1 - x, 1 - y, c, 1), rdy.at[zd], xn)
        b = block(zd, 1 - x, 1 - y, c)
        sends.append(push(b, b, sc.at[3, zd], rc.at[3, zd], cn))
    for d in (0,) + order:
        zd = (z + d) % 4
        if d != 0:
            landed(block(zd, x, y, 1 - c), rc.at[0, zd], xn)
            landed(block(zd, x, 1 - y, 1 - c), rc.at[2, zd], xn)
        landed(block(zd, 1 - x, y, 1 - c), rc.at[1, zd], xn)
        landed(block(zd, 1 - x, 1 - y, 1 - c), rc.at[3, zd], xn)
    for copy in sends:
        copy.wait_send()
    own.wait()


def gather_rows(value, whole):
    count, rows, width = value.shape
    dma = pltpu.SemaphoreType.DMA
    return pl.pallas_call(
        functools.partial(gather_kernel, whole),
        out_shape=jax.ShapeDtypeStruct((count if whole else 1, rows * 8, width), value.dtype),
        in_specs=[pl.BlockSpec(memory_space=pl.ANY)],
        out_specs=pl.BlockSpec(memory_space=pl.ANY),
        scratch_shapes=[dma((1,))] + [dma((4,))] * 10 + [dma((4, 4))] * 2,
        compiler_params=pltpu.CompilerParams(collective_id=0 if whole else 1, has_side_effects=True),
        name="gather_whole" if whole else "gather_half",
    )(value)


def add_into(target, *others):
    count, rows, _ = target.shape
    step = 32

    @pl.loop(0, count * rows // step)
    def _(i):
        n = i // (rows // step)
        r = pl.ds(pl.multiple_of((i % (rows // step)) * step, step), step)
        total = target[n, r, :].astype(F32)
        for other in others:
            total = total + other[n, r, :].astype(F32)
        target[n, r, :] = total.astype(target.dtype)


def sum_kernel(whole, in_ref, out_ref, acc, fc, f1x, f1y, f2x, f2y, fz, full, tmp,
               lsem, sc, rc, s1x, r1x, s1y, r1y, s2x, r2x, s2y, r2y, sz, rz, sg, rg, osem):
    z, x, y, c = coords()
    rows = out_ref.shape[1]
    cols = out_ref.shape[2] // 4
    half = rows // 2
    xn, yn, cn = place(z, 1 - x, y, c), place(z, x, 1 - y, c), place(z, x, y, 1 - c)
    lanes = ((x, y), (1 - x, y), (x, 1 - y), (1 - x, 1 - y))

    def block(z_, lane, c_):
        x_, y_ = lanes[lane]
        return in_ref.at[:, pl.ds((2 * z_ + x_) * rows, rows), pl.ds((2 * y_ + c_) * cols, cols)]

    greet(z, x, y, c)
    sends = []
    loads = {}
    order = (2, 1, 3, 0)
    for lane in (3, 1, 2, 0):
        for d in order:
            zd = (z + d) % 4
            sends.append(push(block(zd, lane, 1 - c), fc.at[lane, d], sc.at[lane, d], rc.at[lane, d], cn))
            loads[lane, d] = pltpu.make_async_copy(block(zd, lane, c), acc.at[lane, d], lsem.at[lane, d])
            loads[lane, d].start()

    def core_sum(lane, d):
        loads[lane, d].wait()
        landed(fc.at[lane, d], rc.at[lane, d], cn)
        add_into(acc.at[lane, d], fc.at[lane, d])

    top, low = pl.ds(0, half), pl.ds(half, half)
    for d in order:
        core_sum(3, d)
        sends.append(push(acc.at[3, d, :, top], f1x.at[d], s1x.at[d], r1x.at[d], xn))
        sends.append(push(acc.at[3, d, :, low], f1y.at[d], s1y.at[d], r1y.at[d], yn))
    for d in order:
        core_sum(1, d)
        core_sum(2, d)
        landed(f1y.at[d], r1y.at[d], yn)
        add_into(acc.at[1, d, :, low], f1y.at[d])
        sends.append(push(acc.at[1, d], f2x.at[d], s2x.at[d], r2x.at[d], xn))
        landed(f1x.at[d], r1x.at[d], xn)
        add_into(acc.at[2, d, :, top], f1x.at[d])
        sends.append(push(acc.at[2, d], f2y.at[d], s2y.at[d], r2y.at[d], yn))
    for d in order:
        core_sum(0, d)
        landed(f2x.at[d], r2x.at[d], xn)
        landed(f2y.at[d], r2y.at[d], yn)
        add_into(acc.at[0, d], f2x.at[d], f2y.at[d])
        if d != 0:
            zd = (z + d) % 4
            sends.append(push(acc.at[0, d], fz.at[(4 - d) % 4], sz.at[d], rz.at[(4 - d) % 4], place(zd, x, y, c)))
    t = 2 * y + c
    for d in (1, 2, 3):
        landed(fz.at[d], rz.at[d], cn)
    step = 32

    @pl.loop(0, 2 * rows // step)
    def _(i):
        n = i // (rows // step)
        r = pl.ds(pl.multiple_of((i % (rows // step)) * step, step), step)
        if whole:
            total = acc[0, 0, n, r, :].astype(F32)
            for d in (1, 2, 3):
                total = total + fz[d, n, r, :].astype(F32)
        else:
            total = jnp.where(z // 2 == n, acc[0, 0, 0, r, :].astype(F32), 0.0)
            for d in (1, 2, 3):
                total = total + jnp.where(((z + d) % 4) // 2 == n, fz[d, 0, r, :].astype(F32), 0.0)
        tmp[n, r, :] = total.astype(tmp.dtype)

    mine = full.at[t]
    keep = pltpu.make_async_copy(tmp, mine, osem.at[4])
    keep.start()
    sends.append(push(tmp, mine, sg.at[0], rg.at[0], yn))
    sends.append(push(tmp, mine, sg.at[1], rg.at[1], cn))
    ty, tc, td = 2 * (1 - y) + c, 2 * y + 1 - c, 2 * (1 - y) + 1 - c
    landed(full.at[ty], rg.at[0], yn)
    sends.append(push(full.at[ty], full.at[ty], sg.at[2], rg.at[2], cn))
    landed(full.at[tc], rg.at[1], cn)
    landed(full.at[td], rg.at[2], cn)
    keep.wait()
    outs = []
    for q in range(4):
        outs.append(pltpu.make_async_copy(full.at[q], out_ref.at[:, :, pl.ds(q * cols, cols)], osem.at[q]))
        outs[-1].start()
    for copy in sends:
        copy.wait_send()
    for copy in outs:
        copy.wait()


def sum_rows(value, whole):
    count, total_rows, width = value.shape
    rows, cols = total_rows // 8, width // 4
    dma = pltpu.SemaphoreType.DMA
    low = value.dtype
    vm = pltpu.VMEM
    return pl.pallas_call(
        functools.partial(sum_kernel, whole),
        out_shape=jax.ShapeDtypeStruct((2, rows, width), low),
        in_specs=[pl.BlockSpec(memory_space=pl.ANY)],
        out_specs=pl.BlockSpec(memory_space=pl.ANY),
        scratch_shapes=[
            vm((4, 4, count, rows, cols), low),
            vm((4, 4, count, rows, cols), low),
            vm((4, count, rows // 2, cols), low),
            vm((4, count, rows // 2, cols), low),
            vm((4, count, rows, cols), low),
            vm((4, count, rows, cols), low),
            vm((4, count, rows, cols), low),
            vm((4, 2, rows, cols), low),
            vm((2, rows, cols), low),
            dma((4, 4)), dma((4, 4)), dma((4, 4)),
        ] + [dma((4,))] * 10 + [dma((3,))] * 2 + [dma((5,))],
        compiler_params=pltpu.CompilerParams(
            collective_id=2 if whole else 3, has_side_effects=True, vmem_limit_bytes=VMEM_LIMIT
        ),
        name="sum_whole" if whole else "sum_half",
    )(value)


def dot_nn(a, b):
    return jnp.dot(a, b, preferred_element_type=F32)


def dot_nt(a, b):
    return lax.dot_general(a, b, (((1,), (1,)), ((), ())), preferred_element_type=F32)


def dot_tn(a, b):
    return lax.dot_general(a, b, (((0,), (0,)), ((), ())), preferred_element_type=F32)


def turn_half(values):
    width = values.shape[-1]
    lane = lax.broadcasted_iota(jnp.int32, values.shape, values.ndim - 1)
    rolled = pltpu.roll(values, width // 2, values.ndim - 1)
    return jnp.where(lane < width // 2, -rolled, rolled)


def attend_kernel(heads, xn_ref, w_ref, cos_ref, sin_ref, qg_ref, kg_ref,
                  pre_ref, qkv_ref, prob_ref, ctx_ref):
    seq = xn_ref.shape[0]
    hd = cos_ref.shape[1]
    tile = 256
    scale = 1.0 / math.sqrt(hd)
    for i in range(seq // tile):
        r = pl.ds(i * tile, tile)
        pre = dot_nn(xn_ref[r, :], w_ref[...])
        pre_ref[r, :] = pre[:, : (heads + 1) * hd]
        qkv_ref[r, pl.ds((heads + 1) * hd, hd)] = pre[:, (heads + 1) * hd :].astype(LOW)
        for a in range(heads + 1):
            one = pre[:, a * hd : (a + 1) * hd]
            factor = lax.rsqrt(jnp.mean(one * one, axis=-1, keepdims=True) + norm_eps)
            gained = one * factor * (qg_ref if a < heads else kg_ref)[...]
            turned = gained * cos_ref[r, :] + turn_half(gained) * sin_ref[r, :]
            qkv_ref[r, pl.ds(a * hd, hd)] = turned.astype(LOW)
    for a in range(heads):
        for i in range(seq // tile):
            r = pl.ds(i * tile, tile)
            n = (i + 1) * tile
            query = qkv_ref[r, pl.ds(a * hd, hd)]
            key = qkv_ref[pl.ds(0, n), pl.ds(heads * hd, hd)]
            value = qkv_ref[pl.ds(0, n), pl.ds((heads + 1) * hd, hd)]
            score = dot_nt(query, key) * scale
            row = lax.broadcasted_iota(jnp.int32, (tile, n), 0) + i * tile
            col = lax.broadcasted_iota(jnp.int32, (tile, n), 1)
            score = jnp.where(col <= row, score, masked_score)
            peak = jnp.max(score, axis=-1, keepdims=True)
            terms = jnp.exp(score - peak)
            prob = (terms * (1.0 / jnp.sum(terms, axis=-1, keepdims=True))).astype(LOW)
            prob_ref[a, r, pl.ds(0, n)] = prob
            ctx_ref[r, pl.ds(a * hd, hd)] = dot_nn(prob, value).astype(LOW)


def attend(xn, weights, cosine, sine, query_gain, key_gain):
    seq = xn.shape[0]
    hd = query_gain.shape[0]
    heads = weights.shape[1] // hd - 2
    return pl.pallas_call(
        functools.partial(attend_kernel, heads),
        out_shape=(
            jax.ShapeDtypeStruct((seq, (heads + 1) * hd), F32),
            jax.ShapeDtypeStruct((seq, (heads + 2) * hd), LOW),
            jax.ShapeDtypeStruct((heads, seq, seq), LOW),
            jax.ShapeDtypeStruct((seq, heads * hd), LOW),
        ),
        compiler_params=pltpu.CompilerParams(vmem_limit_bytes=VMEM_LIMIT),
        name="attend",
    )(xn, weights, cosine, sine, query_gain[None], key_gain[None])


def attend_back_kernel(heads, dctx_ref, pre_ref, qkv_ref, prob_ref, cos_ref, sin_ref, qg_ref, kg_ref,
                       dqkv_ref, gains_ref, dq_s, dk_s, dv_s):
    seq = dctx_ref.shape[0]
    hd = cos_ref.shape[1]
    tile = 256
    scale = 1.0 / math.sqrt(hd)
    dk_s[...] = jnp.zeros_like(dk_s)
    dv_s[...] = jnp.zeros_like(dv_s)
    for a in range(heads):
        for i in range(seq // tile):
            r = pl.ds(i * tile, tile)
            n = (i + 1) * tile
            query = qkv_ref[r, pl.ds(a * hd, hd)]
            key = qkv_ref[pl.ds(0, n), pl.ds(heads * hd, hd)]
            value = qkv_ref[pl.ds(0, n), pl.ds((heads + 1) * hd, hd)]
            dctx = dctx_ref[r, pl.ds(a * hd, hd)]
            prob = prob_ref[a, r, pl.ds(0, n)]
            wide = prob.astype(F32)
            dprob = dot_nt(dctx, value)
            delta = jnp.sum(wide * dprob, axis=-1, keepdims=True)
            dscore = (wide * (dprob - delta)).astype(LOW)
            dq_s[r, pl.ds(a * hd, hd)] = dot_nn(dscore, key) * scale
            dk_s[pl.ds(0, n), :] += dot_tn(dscore, query) * scale
            dv_s[pl.ds(0, n), :] += dot_tn(prob, dctx)
    gq = jnp.zeros((1, hd), F32)
    gk = jnp.zeros((1, hd), F32)
    for i in range(seq // tile):
        r = pl.ds(i * tile, tile)
        dqkv_ref[r, pl.ds((heads + 1) * hd, hd)] = dv_s[r, :].astype(LOW)
        for a in range(heads + 1):
            up = dq_s[r, pl.ds(a * hd, hd)] if a < heads else dk_s[r, :]
            one = pre_ref[r, pl.ds(a * hd, hd)]
            factor = lax.rsqrt(jnp.mean(one * one, axis=-1, keepdims=True) + norm_eps)
            hat = one * factor
            turned = up * cos_ref[r, :] - turn_half(up * sin_ref[r, :])
            part = jnp.sum(turned * hat, axis=0, keepdims=True)
            gained = turned * (qg_ref if a < heads else kg_ref)[...]
            back = factor * (gained - hat * jnp.mean(gained * hat, axis=-1, keepdims=True))
            dqkv_ref[r, pl.ds(a * hd, hd)] = back.astype(LOW)
            if a < heads:
                gq = gq + part
            else:
                gk = gk + part
    gains_ref[...] = jnp.concatenate([gq, gk], axis=0)


def attend_back(dctx, pre, qkv, prob, cosine, sine, query_gain, key_gain):
    seq = dctx.shape[0]
    hd = query_gain.shape[0]
    heads = prob.shape[0]
    return pl.pallas_call(
        functools.partial(attend_back_kernel, heads),
        out_shape=(
            jax.ShapeDtypeStruct((seq, (heads + 2) * hd), LOW),
            jax.ShapeDtypeStruct((2, hd), F32),
        ),
        scratch_shapes=[
            pltpu.VMEM((seq, heads * hd), F32),
            pltpu.VMEM((seq, hd), F32),
            pltpu.VMEM((seq, hd), F32),
        ],
        compiler_params=pltpu.CompilerParams(vmem_limit_bytes=VMEM_LIMIT),
        name="attend_back",
    )(dctx, pre, qkv, prob, cosine, sine, query_gain[None], key_gain[None])


def route_probs(logits, ids, count):
    lane = lax.broadcasted_iota(jnp.int32, logits.shape, 1)
    named = lane == ids[:, 0:1]
    for k in range(1, count):
        named = named | (lane == ids[:, k : k + 1])
    masked = jnp.where(named, logits, masked_score)
    terms = jnp.where(named, jnp.exp(masked - jnp.max(masked, axis=-1, keepdims=True)), 0.0)
    return terms / jnp.sum(terms, axis=-1, keepdims=True)


def experts_kernel(experts, route_count, first_ref, x_ref, og_ref, ids_ref, router_ref, g_ref, u_ref, d_ref,
                   out_ref, dx_ref, dgp_ref, dg_ref, du_ref, dd_ref, dg_s, du_s, dd_s, sem):
    i = pl.program_id(0)
    hidden = g_ref.shape[0]
    per = hidden // experts
    tile = x_ref.shape[0]

    @pl.when(i == 0)
    def _():
        dg_s[...] = jnp.zeros_like(dg_s)
        du_s[...] = jnp.zeros_like(du_s)
        dd_s[...] = jnp.zeros_like(dd_s)

    x = x_ref[...]
    og = og_ref[...]
    first = first_ref[0]
    probs = route_probs(dot_nn(x, router_ref[...]), ids_ref[...], route_count)
    lanes = probs.shape[1]
    row = lax.broadcasted_iota(jnp.int32, (lanes, hidden), 0)
    col = lax.broadcasted_iota(jnp.int32, (lanes, hidden), 1)
    spread = jnp.where(row == first + col // per, 1.0, 0.0).astype(LOW)
    high = probs.astype(LOW)
    rest = (probs - high.astype(F32)).astype(LOW)
    share = dot_nn(high, spread) + dot_nn(rest, spread)
    gate = dot_nt(x, g_ref[...])
    up = dot_nt(x, u_ref[...])
    raw = dot_nt(og, d_ref[...])
    sig = 1.0 / (1.0 + jnp.exp(-gate))
    act = gate * sig
    inner = act * up
    weighted = (inner * share).astype(LOW)
    product = jnp.where(share > 0.0, inner * raw, 0.0)
    product_high = product.astype(LOW)
    product_rest = (product - product_high.astype(F32)).astype(LOW)
    dgp_ref[...] = dot_nt(product_high, spread) + dot_nt(product_rest, spread)
    d_inner = raw * share
    d_up = (d_inner * act).astype(LOW)
    d_gate = (d_inner * up * sig * (1.0 + gate * (1.0 - sig))).astype(LOW)
    dx_ref[...] = (dot_nn(d_gate, g_ref[...]) + dot_nn(d_up, u_ref[...])).astype(LOW)
    out_ref[...] = dot_nn(weighted, d_ref[...]).astype(LOW)
    dg_s[...] += dot_tn(d_gate, x)
    du_s[...] += dot_tn(d_up, x)
    dd_s[...] += dot_tn(weighted, og)

    @pl.when(i == pl.num_programs(0) - 1)
    def _():
        copies = []
        for n, (src, dst) in enumerate(((dg_s, dg_ref), (du_s, du_ref), (dd_s, dd_ref))):
            copies.append(pltpu.make_async_copy(src, dst, sem.at[n]))
            copies[-1].start()
        for copy in copies:
            copy.wait()


def run_experts(first, x, og, ids, router, gate, up, down):
    tokens, width = x.shape
    experts, per, _ = gate.shape
    hidden = experts * per
    tile = 256
    lanes = router.shape[1]
    once = pl.Buffered(1)
    keep = lambda i, s: (0, 0)
    walk = lambda i, s: (i, 0)
    any_space = pl.BlockSpec(memory_space=pl.ANY)
    grads = jax.ShapeDtypeStruct((hidden, width), F32)
    return pl.pallas_call(
        functools.partial(experts_kernel, experts, ids.shape[1]),
        grid_spec=pltpu.PrefetchScalarGridSpec(
            num_scalar_prefetch=1,
            grid=(tokens // tile,),
            in_specs=[
                pl.BlockSpec((tile, width), walk),
                pl.BlockSpec((tile, width), walk),
                pl.BlockSpec((tile, ids.shape[1]), walk),
                pl.BlockSpec((width, lanes), keep, pipeline_mode=once),
                pl.BlockSpec((hidden, width), keep, pipeline_mode=once),
                pl.BlockSpec((hidden, width), keep, pipeline_mode=once),
                pl.BlockSpec((hidden, width), keep, pipeline_mode=once),
            ],
            out_specs=[
                pl.BlockSpec((tile, width), walk),
                pl.BlockSpec((tile, width), walk),
                pl.BlockSpec((tile, lanes), walk),
                any_space,
                any_space,
                any_space,
            ],
            scratch_shapes=[pltpu.VMEM((hidden, width), F32)] * 3 + [pltpu.SemaphoreType.DMA((3,))],
        ),
        out_shape=(
            jax.ShapeDtypeStruct((tokens, width), LOW),
            jax.ShapeDtypeStruct((tokens, width), LOW),
            jax.ShapeDtypeStruct((tokens, lanes), F32),
            grads,
            grads,
            grads,
        ),
        compiler_params=pltpu.CompilerParams(
            vmem_limit_bytes=VMEM_LIMIT, dimension_semantics=("arbitrary",)
        ),
        name="experts",
    )(first, x, og, ids, router, gate.reshape(hidden, width), up.reshape(hidden, width), down.reshape(hidden, width))


def rotate_half(values):
    middle = values.shape[-1] // 2
    return jnp.concatenate([-values[..., middle:], values[..., :middle]], axis=-1)


def rope_tables(positions, head_width):
    middle = head_width // 2
    frequency = rope_base ** (-jnp.arange(middle, dtype=jnp.float32) * 2.0 / head_width)
    angles = positions.astype(jnp.float32)[:, None] * frequency[None, :]
    angles = jnp.concatenate([angles, angles], axis=1)
    return (jnp.cos(angles), jnp.sin(angles))


def norm_parts(values):
    factor = lax.rsqrt(jnp.mean(values * values, axis=-1, keepdims=True) + norm_eps)
    return (values * factor, factor)


def norm_back(upstream, gain, normal, factor):
    scaled = upstream * gain
    return factor * (scaled - normal * jnp.mean(scaled * normal, axis=-1, keepdims=True))


def head_back(upstream, cosine_heads, sine_heads, gain, normal, factor):
    turned = upstream * cosine_heads - rotate_half(upstream * sine_heads)
    gain_part = jnp.sum(turned * normal, axis=(0, 1))
    return (norm_back(turned, gain, normal, factor), gain_part)


def fetch_weights(query_weight, key_weight, value_weight, output_weight, router_weight):
    return (
        lax.all_gather(query_weight, "fsdp", axis=0, tiled=True),
        lax.all_gather(key_weight, "fsdp", axis=0, tiled=True),
        lax.all_gather(value_weight, "fsdp", axis=0, tiled=True),
        lax.all_gather(output_weight, "fsdp", axis=0, tiled=True),
        lax.all_gather(router_weight, "fsdp", axis=0, tiled=True),
    )


def widen(summed):
    return lax.all_gather(summed, "tp", axis=3, tiled=True)


def carry_back(summed):
    return lax.all_to_all(summed, "fsdp", split_axis=0, concat_axis=0, tiled=True)


def send_home(summed):
    arrived_home = carry_back(widen(summed))
    return arrived_home


def general_device(
    tokens,
    cotangent,
    expert_ids,
    attention_gain,
    query_gain,
    key_gain,
    query_weight,
    key_weight,
    value_weight,
    output_weight,
    expert_gain,
    router_weight,
    gate_weight,
    up_weight,
    down_weight,
):
    micro_count = tokens.shape[0]
    tok_rows = tokens.shape[1]
    width = tokens.shape[2]
    route_count = expert_ids.shape[2]
    head_dim = query_gain.shape[0]
    local_heads = query_weight.shape[1] // head_dim
    local_groups = key_weight.shape[1] // head_dim
    group_size = local_heads // local_groups
    fsdp_count = lax.axis_size("fsdp")
    seq_len = tok_rows * fsdp_count
    experts_here = gate_weight.shape[0]
    expert_count = experts_here * fsdp_count
    capacity = max(2, 5 * tok_rows * route_count // (4 * expert_count))
    key_block = math.gcd(seq_len, 512)
    score_scale = 1.0 / math.sqrt(head_dim)
    query_count = tok_rows * group_size
    routed_total = tok_rows * route_count
    start_row = lax.axis_index("fsdp") * tok_rows
    positions = start_row + jnp.arange(tok_rows, dtype=jnp.int32)
    cosine_table, sine_table = rope_tables(positions, head_dim)
    cosine_heads = cosine_table[:, None, :]
    sine_heads = sine_table[:, None, :]
    query_pos = start_row + jnp.arange(query_count, dtype=jnp.int32) // group_size
    block_total = (start_row + tok_rows + key_block - 1) // key_block
    expert_range = jnp.arange(expert_count, dtype=jnp.int32)
    zero_row = jnp.zeros((1, width), jnp.bfloat16)

    def to_rows(tensor):
        return (
            tensor.reshape(tok_rows, local_groups, group_size, head_dim)
            .transpose(1, 0, 2, 3)
            .reshape(local_groups, query_count, head_dim)
        )

    def from_rows(tensor):
        return (
            tensor.reshape(local_groups, tok_rows, group_size, head_dim)
            .transpose(1, 0, 2, 3)
            .reshape(tok_rows, local_heads, head_dim)
        )

    acc_attention_gain = jnp.zeros((width,), jnp.float32)
    acc_head_gains = jnp.zeros((2, head_dim), jnp.float32)
    acc_query = jnp.zeros((width, local_heads * head_dim), jnp.float32)
    acc_key = jnp.zeros((width, local_groups * head_dim), jnp.float32)
    acc_value = jnp.zeros((width, local_groups * head_dim), jnp.float32)
    acc_output = jnp.zeros((width, local_heads * head_dim), jnp.float32)
    acc_expert_gain = jnp.zeros((width,), jnp.float32)
    acc_router = jnp.zeros((width, expert_count), jnp.float32)
    acc_gate = jnp.zeros(gate_weight.shape, jnp.float32)
    acc_up = jnp.zeros(up_weight.shape, jnp.float32)
    acc_down = jnp.zeros(down_weight.shape, jnp.float32)
    layer_rows = []
    input_rows = []
    for micro_index in range(micro_count):
        inputs = tokens[micro_index].astype(jnp.float32)
        query_full, key_full, value_full, output_full, router_full = fetch_weights(
            query_weight, key_weight, value_weight, output_weight, router_weight
        )
        input_hat, attention_factor = norm_parts(inputs)
        normed = (input_hat * attention_gain).astype(jnp.bfloat16)
        query_pre = jnp.dot(normed, query_full, preferred_element_type=jnp.float32).reshape(
            tok_rows, local_heads, head_dim
        )
        key_pre = jnp.dot(normed, key_full, preferred_element_type=jnp.float32).reshape(
            tok_rows, local_groups, head_dim
        )
        value_low = jnp.dot(normed, value_full, preferred_element_type=jnp.float32).astype(
            jnp.bfloat16
        )
        query_hat, query_factor = norm_parts(query_pre)
        key_hat, key_factor = norm_parts(key_pre)
        query_scaled = query_hat * query_gain
        key_scaled = key_hat * key_gain
        query_low = (query_scaled * cosine_heads + rotate_half(query_scaled) * sine_heads).astype(
            jnp.bfloat16
        )
        key_low = (key_scaled * cosine_heads + rotate_half(key_scaled) * sine_heads).astype(
            jnp.bfloat16
        )
        key_all, value_all = (
            lax.all_gather(
                key_low.reshape(tok_rows, local_groups * head_dim), "fsdp", axis=0, tiled=True
            ),
            lax.all_gather(value_low, "fsdp", axis=0, tiled=True),
        )
        key_heads = key_all.reshape(seq_len, local_groups, head_dim).transpose(1, 0, 2)
        value_heads = value_all.reshape(seq_len, local_groups, head_dim).transpose(1, 0, 2)
        query_rows = to_rows(query_low)

        def scores_at(block_index):
            block_start = block_index * key_block
            key_slice = lax.dynamic_slice_in_dim(key_heads, block_start, key_block, 1)
            raw_scores = (
                jnp.einsum(
                    "gqd,gkd->gqk", query_rows, key_slice, preferred_element_type=jnp.float32
                )
                * score_scale
            )
            allowed = (block_start + jnp.arange(key_block, dtype=jnp.int32))[None, :] <= query_pos[
                :, None
            ]
            return (jnp.where(allowed[None], raw_scores, masked_score), allowed, block_start)

        def stats_step(block_index, carried):
            run_peak, run_total = carried
            scores, allowed, block_start = scores_at(block_index)
            new_peak = jnp.maximum(run_peak, jnp.max(scores, axis=-1))
            terms = jnp.where(allowed[None], jnp.exp(scores - new_peak[..., None]), 0.0)
            return (new_peak, run_total * jnp.exp(run_peak - new_peak) + jnp.sum(terms, axis=-1))

        start_stats = (
            jnp.full((local_groups, query_count), masked_score, jnp.float32),
            jnp.zeros((local_groups, query_count), jnp.float32),
        )
        run_peak, run_total = lax.fori_loop(0, block_total, stats_step, start_stats)
        log_total = run_peak + jnp.log(run_total)

        def value_step(block_index, acc_context):
            scores, allowed, block_start = scores_at(block_index)
            probs_low = jnp.where(
                allowed[None], jnp.exp(scores - log_total[..., None]), 0.0
            ).astype(jnp.bfloat16)
            value_slice = lax.dynamic_slice_in_dim(value_heads, block_start, key_block, 1)
            return acc_context + jnp.einsum(
                "gqk,gkd->gqd", probs_low, value_slice, preferred_element_type=jnp.float32
            )

        context_rows = lax.fori_loop(
            0,
            block_total,
            value_step,
            jnp.zeros((local_groups, query_count, head_dim), jnp.float32),
        )
        context_low = (
            from_rows(context_rows).reshape(tok_rows, local_heads * head_dim).astype(jnp.bfloat16)
        )
        branch_part = jnp.einsum(
            "th,dh->td", context_low, output_full, preferred_element_type=jnp.float32
        )
        resid = inputs + lax.psum(branch_part.astype(jnp.bfloat16), "tp").astype(jnp.float32)
        resid_hat, expert_factor = norm_parts(resid)
        expert_in = (resid_hat * expert_gain).astype(jnp.bfloat16)
        logits = jnp.dot(expert_in, router_full, preferred_element_type=jnp.float32)
        routes_now = expert_ids[micro_index]
        choose = (routes_now[:, :, None] == expert_range[None, None, :]).astype(jnp.float32)
        picked = jnp.sum(choose * logits[:, None, :], axis=-1)
        shifted = jnp.exp(picked - jnp.max(picked, axis=-1, keepdims=True))
        gate_probs = shifted / jnp.sum(shifted, axis=-1, keepdims=True)
        flat_routes = routes_now.reshape(-1)
        onehot = (flat_routes[:, None] == expert_range[None, :]).astype(jnp.int32)
        rank_in = jnp.sum((jnp.cumsum(onehot, axis=0) - onehot) * onehot, axis=1)
        slot_index = flat_routes * capacity + rank_in
        slot_source = (
            jnp.full((expert_count * capacity,), routed_total, jnp.int32)
            .at[slot_index]
            .set(jnp.arange(routed_total, dtype=jnp.int32))
        )
        padded_in = jnp.concatenate([expert_in, zero_row], axis=0)
        outgoing = padded_in[slot_source // route_count].reshape(
            fsdp_count, experts_here, capacity, width
        )
        arrived = lax.all_to_all(outgoing, "fsdp", split_axis=0, concat_axis=0, tiled=True)
        gate_pre = jnp.einsum(
            "secd,efd->secf", arrived, gate_weight, preferred_element_type=jnp.float32
        )
        up_pre = jnp.einsum(
            "secd,efd->secf", arrived, up_weight, preferred_element_type=jnp.float32
        )
        gate_sigmoid = jax.nn.sigmoid(gate_pre)
        inner_low = (gate_pre * gate_sigmoid * up_pre).astype(jnp.bfloat16)
        result_part = jnp.einsum(
            "secf,efd->secd", inner_low, down_weight, preferred_element_type=jnp.float32
        )
        result_low = lax.psum_scatter(
            result_part.astype(jnp.bfloat16), "tp", scatter_dimension=3, tiled=True
        )
        result_home = send_home(result_low)
        routed = (
            result_home.reshape(expert_count * capacity, width)[slot_index]
            .astype(jnp.float32)
            .reshape(tok_rows, route_count, width)
        )
        layer_rows.append(
            (resid + jnp.sum(gate_probs[:, :, None] * routed, axis=1)).astype(jnp.bfloat16)
        )
        query_full, key_full, value_full, output_full, router_full = fetch_weights(
            query_weight, key_weight, value_weight, output_weight, router_weight
        )
        out_grad = cotangent[micro_index].astype(jnp.float32)
        d_route = (
            (gate_probs[:, :, None] * out_grad[:, None, :])
            .astype(jnp.bfloat16)
            .reshape(routed_total, width)
        )
        d_gate_probs = jnp.sum(out_grad[:, None, :] * routed, axis=-1)
        d_pick = gate_probs * (
            d_gate_probs - jnp.sum(gate_probs * d_gate_probs, axis=-1, keepdims=True)
        )
        d_logits = jnp.sum(choose * d_pick[:, :, None], axis=1).astype(jnp.bfloat16)
        grad_outgoing = jnp.concatenate([d_route, zero_row], axis=0)[slot_source].reshape(
            fsdp_count, experts_here, capacity, width
        )
        grad_arrived = lax.all_to_all(
            grad_outgoing, "fsdp", split_axis=0, concat_axis=0, tiled=True
        )
        d_inner = jnp.einsum(
            "secd,efd->secf", grad_arrived, down_weight, preferred_element_type=jnp.float32
        )
        acc_down = acc_down + jnp.einsum(
            "secf,secd->efd", inner_low, grad_arrived, preferred_element_type=jnp.float32
        )
        d_gate_low = (
            d_inner * up_pre * gate_sigmoid * (1.0 + gate_pre * (1.0 - gate_sigmoid))
        ).astype(jnp.bfloat16)
        d_up_low = (d_inner * gate_pre * gate_sigmoid).astype(jnp.bfloat16)
        acc_gate = acc_gate + jnp.einsum(
            "secf,secd->efd", d_gate_low, arrived, preferred_element_type=jnp.float32
        )
        acc_up = acc_up + jnp.einsum(
            "secf,secd->efd", d_up_low, arrived, preferred_element_type=jnp.float32
        )
        d_copy_part = jnp.einsum(
            "secf,efd->secd", d_gate_low, gate_weight, preferred_element_type=jnp.float32
        ) + jnp.einsum("secf,efd->secd", d_up_low, up_weight, preferred_element_type=jnp.float32)
        d_copy_low = lax.psum_scatter(
            d_copy_part.astype(jnp.bfloat16), "tp", scatter_dimension=3, tiled=True
        )
        d_copy_home = send_home(d_copy_low)
        d_copies = (
            d_copy_home.reshape(expert_count * capacity, width)[slot_index]
            .astype(jnp.float32)
            .reshape(tok_rows, route_count, width)
        )
        d_expert_in = jnp.sum(d_copies, axis=1) + jnp.dot(
            d_logits, router_full.T, preferred_element_type=jnp.float32
        )
        acc_router = acc_router + jnp.dot(expert_in.T, d_logits, preferred_element_type=jnp.float32)
        acc_expert_gain = acc_expert_gain + jnp.sum(d_expert_in * resid_hat, axis=0)
        d_resid = out_grad + norm_back(d_expert_in, expert_gain, resid_hat, expert_factor)
        d_branch = d_resid.astype(jnp.bfloat16)
        acc_output = acc_output + jnp.einsum(
            "td,th->dh", d_branch, context_low, preferred_element_type=jnp.float32
        )
        d_context = jnp.dot(d_branch, output_full, preferred_element_type=jnp.float32).astype(
            jnp.bfloat16
        )
        d_context_rows = to_rows(d_context.reshape(tok_rows, local_heads, head_dim))
        delta_rows = jnp.sum(d_context_rows.astype(jnp.float32) * context_rows, axis=-1)

        def grad_step(block_index, carried):
            d_query_rows, key_grads_all = carried
            scores, allowed, block_start = scores_at(block_index)
            probs = jnp.where(allowed[None], jnp.exp(scores - log_total[..., None]), 0.0)
            key_slice = lax.dynamic_slice_in_dim(key_heads, block_start, key_block, 1)
            value_slice = lax.dynamic_slice_in_dim(value_heads, block_start, key_block, 1)
            d_probs = jnp.einsum(
                "gqd,gkd->gqk", d_context_rows, value_slice, preferred_element_type=jnp.float32
            )
            d_scores = (probs * (d_probs - delta_rows[..., None])).astype(jnp.bfloat16)
            d_query_rows = (
                d_query_rows
                + jnp.einsum(
                    "gqk,gkd->gqd", d_scores, key_slice, preferred_element_type=jnp.float32
                )
                * score_scale
            )
            d_key_block = (
                jnp.einsum("gqk,gqd->kgd", d_scores, query_rows, preferred_element_type=jnp.float32)
                * score_scale
            )
            d_value_block = jnp.einsum(
                "gqk,gqd->kgd",
                probs.astype(jnp.bfloat16),
                d_context_rows,
                preferred_element_type=jnp.float32,
            )
            current = lax.dynamic_slice_in_dim(key_grads_all, block_start, key_block, 0)
            updated = current + jnp.concatenate([d_key_block, d_value_block], axis=-1)
            return (
                d_query_rows,
                lax.dynamic_update_slice_in_dim(key_grads_all, updated, block_start, 0),
            )

        start_grads = (
            jnp.zeros((local_groups, query_count, head_dim), jnp.float32),
            jnp.zeros((seq_len, local_groups, 2 * head_dim), jnp.float32),
        )
        d_query_rows, key_grads_all = lax.fori_loop(0, block_total, grad_step, start_grads)
        key_grads = (
            lax.psum_scatter(
                key_grads_all.reshape(seq_len, local_groups * 2 * head_dim).astype(jnp.bfloat16),
                "fsdp",
                scatter_dimension=0,
                tiled=True,
            )
            .astype(jnp.float32)
            .reshape(tok_rows, local_groups, 2 * head_dim)
        )
        d_value_low = (
            key_grads[..., head_dim:]
            .reshape(tok_rows, local_groups * head_dim)
            .astype(jnp.bfloat16)
        )
        d_key_pre, key_gain_part = head_back(
            key_grads[..., :head_dim], cosine_heads, sine_heads, key_gain, key_hat, key_factor
        )
        d_query_pre, query_gain_part = head_back(
            from_rows(d_query_rows), cosine_heads, sine_heads, query_gain, query_hat, query_factor
        )
        d_query_low = d_query_pre.astype(jnp.bfloat16).reshape(tok_rows, local_heads * head_dim)
        d_key_low = d_key_pre.astype(jnp.bfloat16).reshape(tok_rows, local_groups * head_dim)
        d_normed_part = jnp.dot(d_query_low, query_full.T, preferred_element_type=jnp.float32)
        d_normed_part = d_normed_part + jnp.dot(
            d_key_low, key_full.T, preferred_element_type=jnp.float32
        )
        d_normed_part = d_normed_part + jnp.dot(
            d_value_low, value_full.T, preferred_element_type=jnp.float32
        )
        acc_query = acc_query + jnp.dot(normed.T, d_query_low, preferred_element_type=jnp.float32)
        acc_key = acc_key + jnp.dot(normed.T, d_key_low, preferred_element_type=jnp.float32)
        acc_value = acc_value + jnp.dot(normed.T, d_value_low, preferred_element_type=jnp.float32)
        d_normed, head_gain_parts = (
            lax.psum(d_normed_part.astype(jnp.bfloat16), "tp").astype(jnp.float32),
            lax.psum(jnp.stack([query_gain_part, key_gain_part]).astype(jnp.bfloat16), "tp").astype(
                jnp.float32
            ),
        )
        acc_head_gains = acc_head_gains + head_gain_parts
        acc_attention_gain = acc_attention_gain + jnp.sum(d_normed * input_hat, axis=0)
        input_rows.append(
            (d_resid + norm_back(d_normed, attention_gain, input_hat, attention_factor)).astype(
                jnp.bfloat16
            )
        )
    summed = (
        lax.psum_scatter(
            acc_attention_gain.astype(jnp.bfloat16), "fsdp", scatter_dimension=0, tiled=True
        ).astype(jnp.float32),
        lax.psum_scatter(
            acc_head_gains[0].astype(jnp.bfloat16), "fsdp", scatter_dimension=0, tiled=True
        ).astype(jnp.float32),
        lax.psum_scatter(
            acc_head_gains[1].astype(jnp.bfloat16), "fsdp", scatter_dimension=0, tiled=True
        ).astype(jnp.float32),
        lax.psum_scatter(
            acc_query.astype(jnp.bfloat16), "fsdp", scatter_dimension=0, tiled=True
        ).astype(jnp.float32),
        lax.psum_scatter(
            acc_key.astype(jnp.bfloat16), "fsdp", scatter_dimension=0, tiled=True
        ).astype(jnp.float32),
        lax.psum_scatter(
            acc_value.astype(jnp.bfloat16), "fsdp", scatter_dimension=0, tiled=True
        ).astype(jnp.float32),
        lax.psum_scatter(
            acc_output.astype(jnp.bfloat16), "fsdp", scatter_dimension=0, tiled=True
        ).astype(jnp.float32),
        lax.psum_scatter(
            acc_expert_gain.astype(jnp.bfloat16), "fsdp", scatter_dimension=0, tiled=True
        ).astype(jnp.float32),
        lax.psum_scatter(
            acc_router.astype(jnp.bfloat16), "fsdp", scatter_dimension=0, tiled=True
        ).astype(jnp.float32),
    )
    return (
        jnp.stack(layer_rows),
        jnp.stack(input_rows),
        summed[0],
        summed[1],
        summed[2],
        summed[3],
        summed[4],
        summed[5],
        summed[6],
        summed[7],
        summed[8],
        acc_gate,
        acc_up,
        acc_down,
    )


def small_device(
    tokens,
    cotangent,
    expert_ids,
    attention_gain,
    query_gain,
    key_gain,
    query_weight,
    key_weight,
    value_weight,
    output_weight,
    expert_gain,
    router_weight,
    gate_weight,
    up_weight,
    down_weight,
):
    count, rows, width = tokens.shape
    hd = query_gain.shape[0]
    f = lax.axis_index("fsdp")
    n_fsdp = lax.axis_size("fsdp")
    seq = rows * n_fsdp
    experts = gate_weight.shape[0]
    expert_count = experts * n_fsdp
    local = query_weight.shape[1]
    pairs = n_fsdp // count
    part = local // pairs
    piece = query_weight.shape[0]

    cosine, sine = rope_tables(jnp.arange(seq, dtype=jnp.int32), hd)
    inputs = tokens.astype(F32)
    input_hat, attention_factor = norm_parts(inputs)
    normed = (input_hat * attention_gain).astype(LOW)

    def fetch(weight):
        cut = weight.reshape(piece, pairs, part).transpose(1, 0, 2)
        cut = jnp.concatenate([cut] * count, axis=0)
        return lax.all_to_all(cut, "fsdp", split_axis=0, concat_axis=0, tiled=True).reshape(width, part)

    def give_back(grad):
        cut = lax.all_to_all(
            grad.astype(LOW).reshape(n_fsdp, piece, part), "fsdp", split_axis=0, concat_axis=0, tiled=True
        ).astype(F32)
        cut = jnp.sum(cut.reshape(count, pairs, piece, part), axis=0)
        return cut.transpose(1, 0, 2).reshape(piece, local)

    query_pair = fetch(query_weight)
    output_pair = fetch(output_weight)
    key_value = lax.all_gather(
        jnp.concatenate([key_weight, value_weight], axis=1), "fsdp", axis=0, tiled=True
    )
    router_full = lax.all_gather(router_weight, "fsdp", axis=0, tiled=True)
    ids_all = lax.all_gather(expert_ids, "fsdp", axis=1, tiled=True)

    normed_all = gather_rows(normed, False)[0]
    weights = jnp.concatenate([query_pair, key_value], axis=1)
    pre, qkv, prob, context = attend(normed_all, weights, cosine, sine, query_gain, key_gain)
    branch_part = lax.dot_general(
        context, output_pair, (((1,), (1,)), ((), ())), preferred_element_type=F32
    ).astype(LOW)
    branch = sum_rows(branch_part[None], False)
    resid = inputs + branch.astype(F32)
    resid_hat, expert_factor = norm_parts(resid)
    expert_in = (resid_hat * expert_gain).astype(LOW)

    expert_all = gather_rows(expert_in, True).reshape(count * seq, width)
    grad_all = gather_rows(cotangent, True).reshape(count * seq, width)
    lanes = 128
    router_wide = jnp.pad(router_full, ((0, 0), (0, lanes - expert_count)))
    first = (f * experts).astype(jnp.int32).reshape(1)
    out_part, dx_part, dgp_part, d_gate, d_up, d_down = run_experts(
        first,
        expert_all,
        grad_all,
        ids_all.reshape(count * seq, -1),
        router_wide,
        gate_weight,
        up_weight,
        down_weight,
    )
    dgp_part = dgp_part[:, :expert_count].reshape(count, seq, expert_count)
    d_gate_probs = lax.psum(
        lax.psum_scatter(dgp_part, "fsdp", scatter_dimension=1, tiled=True), "tp"
    )
    dx_sum = sum_rows(dx_part.reshape(count, seq, width), True).astype(F32)
    out_sum = sum_rows(out_part.reshape(count, seq, width), True).astype(F32)
    layer_output = (resid + out_sum).astype(LOW)

    expert_range = jnp.arange(expert_count, dtype=jnp.int32)
    named = jnp.any(expert_ids[..., None] == expert_range, axis=2)
    logits = jnp.dot(expert_in, router_full, preferred_element_type=F32)
    masked = jnp.where(named, logits, masked_score)
    terms = jnp.where(named, jnp.exp(masked - jnp.max(masked, axis=-1, keepdims=True)), 0.0)
    gate_probs = terms / jnp.sum(terms, axis=-1, keepdims=True)
    d_logits = (
        gate_probs * (d_gate_probs - jnp.sum(gate_probs * d_gate_probs, axis=-1, keepdims=True))
    ).astype(LOW)
    d_expert_in = dx_sum + lax.dot_general(
        d_logits, router_full, (((2,), (1,)), ((), ())), preferred_element_type=F32
    )
    router_part = lax.dot_general(
        expert_in, d_logits, (((0, 1), (0, 1)), ((), ())), preferred_element_type=F32
    )
    expert_gain_part = jnp.sum(d_expert_in * resid_hat, axis=(0, 1))
    out_grad = cotangent.astype(F32)
    d_resid = out_grad + norm_back(d_expert_in, expert_gain, resid_hat, expert_factor)
    d_branch = d_resid.astype(LOW)

    branch_all = gather_rows(d_branch, False)[0]
    d_context = jnp.dot(branch_all, output_pair, preferred_element_type=F32).astype(LOW)
    d_output = lax.dot_general(branch_all, context, (((0,), (0,)), ((), ())), preferred_element_type=F32)
    d_qkv, head_gains = attend_back(d_context, pre, qkv, prob, cosine, sine, query_gain, key_gain)
    d_normed_part = lax.dot_general(
        d_qkv, weights, (((1,), (1,)), ((), ())), preferred_element_type=F32
    ).astype(LOW)
    d_weights = lax.dot_general(normed_all, d_qkv, (((0,), (0,)), ((), ())), preferred_element_type=F32)
    d_normed = sum_rows(d_normed_part[None], False).astype(F32)
    attention_gain_part = jnp.sum(d_normed * input_hat, axis=(0, 1))
    input_grad = (d_resid + norm_back(d_normed, attention_gain, input_hat, attention_factor)).astype(LOW)

    head_gains = lax.psum(head_gains, "tp")

    def scattered(value):
        return lax.psum_scatter(value, "fsdp", scatter_dimension=0, tiled=True)

    d_key_value = scattered(d_weights[:, part:].astype(LOW)).astype(F32)
    return (
        layer_output,
        input_grad,
        scattered(attention_gain_part),
        scattered(head_gains[0]),
        scattered(head_gains[1]),
        give_back(d_weights[:, :part]),
        d_key_value[:, :hd],
        d_key_value[:, hd:],
        give_back(d_output),
        scattered(expert_gain_part),
        scattered(router_part),
        d_gate.reshape(gate_weight.shape),
        d_up.reshape(up_weight.shape),
        d_down.reshape(down_weight.shape),
    )


def solution(mesh):
    body = small_device if (mesh.shape["fsdp"], mesh.shape["tp"]) == (8, 4) else general_device
    return jax.shard_map(
        body,
        mesh=mesh,
        in_specs=(
            P(None, "fsdp", None),
            P(None, "fsdp", None),
            P(None, "fsdp", None),
            P(),
            P(),
            P(),
            P("fsdp", "tp"),
            P("fsdp", "tp"),
            P("fsdp", "tp"),
            P("fsdp", "tp"),
            P(),
            P("fsdp", None),
            P("fsdp", "tp", None),
            P("fsdp", "tp", None),
            P("fsdp", "tp", None),
        ),
        out_specs=(
            P(None, "fsdp", None),
            P(None, "fsdp", None),
            P("fsdp"),
            P("fsdp"),
            P("fsdp"),
            P("fsdp", "tp"),
            P("fsdp", "tp"),
            P("fsdp", "tp"),
            P("fsdp", "tp"),
            P("fsdp"),
            P("fsdp", None),
            P("fsdp", "tp", None),
            P("fsdp", "tp", None),
            P("fsdp", "tp", None),
        ),
        check_vma=False,
    )
```

```python
import functools
import math

import jax
import jax.numpy as jnp
import numpy as np
from jax import lax
from jax.experimental import pallas as pl
from jax.experimental.pallas import tpu as pltpu
from jax.sharding import PartitionSpec as P

norm_eps = 1e-06
rope_base = 1000000.0
masked_score = -1e30
MESH = pl.DeviceIdType.MESH
LOW = jnp.bfloat16
F32 = jnp.float32
VMEM_LIMIT = 60 * 2**20


def coords():
    f = lax.axis_index("fsdp")
    t = lax.axis_index("tp")
    return f // 2, f % 2, t // 2, t % 2


def place(z, x, y, c):
    return (2 * z + x, 2 * y + c)


def span(first, count):
    return pl.ds(pl.multiple_of(first, count), count)


class Here:
    def __init__(self):
        z, x, y, c = coords()
        self.z, self.x, self.y, self.c = z, x, y, c
        self.f, self.t = 2 * z + x, 2 * y + c
        self.xn, self.yn, self.cn = place(z, 1 - x, y, c), place(z, x, 1 - y, c), place(z, x, y, 1 - c)
        self.lanes = ((x, y), (1 - x, y), (x, 1 - y), (1 - x, 1 - y))

    def zd(self, d):
        return (self.z + d) % 4

    def peer(self, d, e):
        return place(self.zd(d), (self.x + e) % 2, self.y, self.c)

    def greet(self):
        barrier = pltpu.get_barrier_semaphore()
        peers = [self.peer(d, e) for d in range(4) for e in range(2) if d or e] + [self.yn, self.cn]
        for peer in peers:
            pl.semaphore_signal(barrier, inc=1, device_id=peer, device_id_type=MESH)
        pl.semaphore_wait(barrier, len(peers))


def push(src, dst, send_sem, recv_sem, device):
    copy = pltpu.make_async_remote_copy(
        src_ref=src, dst_ref=dst, send_sem=send_sem, recv_sem=recv_sem, device_id=device, device_id_type=MESH
    )
    copy.start()
    return copy


def keep(src, dst, sem):
    copy = pltpu.make_async_copy(src, dst, sem)
    copy.start()
    return copy


ORDER = (1, 3, 2)
FAR_FIRST = (2, 1, 3, 0)


class Gather:
    scratch = staticmethod(
        lambda: [pltpu.SemaphoreType.DMA((1,))]
        + [pltpu.SemaphoreType.DMA((4,))] * 10
        + [pltpu.SemaphoreType.DMA((4, 4))] * 2
    )
    slots = 13

    def __init__(self, here, whole, src, dst, sems):
        self.here, self.whole, self.src, self.dst = here, whole, src, dst
        (self.loc, self.sz, self.rz, self.sx, self.rx, self.sy, self.ry,
         self.sdx, self.rdx, self.sdy, self.rdy, self.sc, self.rc) = sems
        self.rows, self.cols = src.shape[1], src.shape[2] // 4
        self.half = self.rows // 2
        self.sends = []

    def block(self, z, x, y, c, h=None):
        first = (2 * z + x) * self.rows
        rows = span(first, self.rows) if h is None else span(first + h * self.half, self.half)
        return self.dst.at[:, rows, span((2 * y + c) * self.cols, self.cols)]

    def source(self, z_to, t, first, count):
        seqs = slice(None) if self.whole else pl.ds(z_to // 2, 1)
        return self.src.at[seqs, pl.ds(first, count), span(t * self.cols, self.cols)]

    def push(self, *args):
        self.sends.append(push(*args))

    def landed(self, ref, sem):
        pltpu.make_async_remote_copy(
            src_ref=ref, dst_ref=ref, send_sem=sem, recv_sem=sem, device_id=self.here.xn, device_id_type=MESH
        ).wait_recv()

    def start(self):
        h = self.here
        own = self.src if self.whole else self.src.at[pl.ds(h.z // 2, 1)]
        self.own = keep(own, self.dst.at[:, span(h.f * self.rows, self.rows), :], self.loc.at[0])
        for d in ORDER:
            self.push(self.source(h.zd(d), h.t, 0, self.rows), self.block(h.z, h.x, h.y, h.c),
                      self.sz.at[d], self.rz.at[h.z], h.peer(d, 0))
        self.push(self.source(h.z, h.t, 0, self.rows), self.block(h.z, h.x, h.y, h.c),
                  self.sx.at[h.z], self.rx.at[h.z], h.xn)
        self.push(self.source(h.z, 2 * (1 - h.y) + h.c, 0, self.half), self.block(h.z, h.x, 1 - h.y, h.c, 0),
                  self.sdx.at[h.z], self.rdx.at[h.z], h.xn)

    def spread(self, d):
        h, zd = self.here, self.here.zd(d)
        b = self.block(zd, h.x, h.y, h.c)
        self.landed(b, self.rz.at[zd])
        self.push(b, b, self.sx.at[zd], self.rx.at[zd], h.xn)
        self.push(b, b, self.sy.at[zd], self.ry.at[zd], h.yn)
        self.push(b, b, self.sc.at[0, zd], self.rc.at[0, zd], h.cn)

    def cross(self, d):
        h, zd = self.here, self.here.zd(d)
        b = self.block(zd, 1 - h.x, h.y, h.c)
        self.landed(b, self.rx.at[zd])
        low = self.block(zd, 1 - h.x, h.y, h.c, 1)
        self.push(low, low, self.sdy.at[zd], self.rdy.at[zd], h.yn)
        self.push(b, b, self.sc.at[1, zd], self.rc.at[1, zd], h.cn)
        if d != 0:
            b = self.block(zd, h.x, 1 - h.y, h.c)
            self.landed(b, self.ry.at[zd])
            top = self.block(zd, h.x, 1 - h.y, h.c, 0)
            self.push(top, top, self.sdx.at[zd], self.rdx.at[zd], h.xn)
            self.push(b, b, self.sc.at[2, zd], self.rc.at[2, zd], h.cn)

    def close(self, d):
        h, zd = self.here, self.here.zd(d)
        self.landed(self.block(zd, 1 - h.x, 1 - h.y, h.c, 0), self.rdx.at[zd])
        self.landed(self.block(zd, 1 - h.x, 1 - h.y, h.c, 1), self.rdy.at[zd])
        b = self.block(zd, 1 - h.x, 1 - h.y, h.c)
        self.push(b, b, self.sc.at[3, zd], self.rc.at[3, zd], h.cn)

    def arrived(self, d, e):
        h, zd = self.here, self.here.zd(d)
        if e == 0:
            if d == 0:
                self.own.wait()
            else:
                self.landed(self.block(zd, h.x, h.y, 1 - h.c), self.rc.at[0, zd])
                self.landed(self.block(zd, h.x, 1 - h.y, 1 - h.c), self.rc.at[2, zd])
        else:
            self.landed(self.block(zd, 1 - h.x, h.y, 1 - h.c), self.rc.at[1, zd])
            self.landed(self.block(zd, 1 - h.x, 1 - h.y, 1 - h.c), self.rc.at[3, zd])

    def finish(self):
        for copy in self.sends:
            copy.wait_send()


def add_into(target, *others):
    count, rows, _ = target.shape
    step = 32

    @pl.loop(0, count * rows // step)
    def _(i):
        n = i // (rows // step)
        r = pl.ds(pl.multiple_of((i % (rows // step)) * step, step), step)
        total = target[n, r, :].astype(F32)
        for other in others:
            total = total + other[n, r, :].astype(F32)
        target[n, r, :] = total.astype(target.dtype)


class Sum:
    slots = 24

    @staticmethod
    def scratch(count, rows, width, low):
        dma = pltpu.SemaphoreType.DMA
        cols = width // 4
        vm = pltpu.VMEM
        return [
            vm((4, 4, count, rows, cols), low),
            vm((4, count, rows // 2, cols), low),
            vm((4, count, rows // 2, cols), low),
            vm((4, count, rows, cols), low),
            vm((4, count, rows, cols), low),
            vm((4, count, rows, cols), low),
            vm((4, 2, rows, cols), low),
            vm((2, rows, cols), low),
            vm((2, rows, cols), F32),
            dma((4, 4)), dma((4, 4)),
        ] + [dma((4,))] * 10 + [dma((3,))] * 2 + [dma((5,))]

    def __init__(self, here, whole, part, refs):
        self.here, self.whole, self.part = here, whole, part
        (self.fc, self.f1x, self.f1y, self.f2x, self.f2y, self.fz, self.full, self.tmp, self.wide, self.sc, self.rc,
         self.s1x, self.r1x, self.s1y, self.r1y, self.s2x, self.r2x, self.s2y, self.r2y, self.sz, self.rz,
         self.sg, self.rg, self.osem) = refs
        self.rows, self.cols = part.shape[1] // 8, part.shape[2] // 4
        self.top, self.low = pl.ds(0, self.rows // 2), pl.ds(self.rows // 2, self.rows // 2)
        self.sends = []

    def block(self, d, lane, c):
        x, y = self.here.lanes[lane]
        return self.part.at[:, span((2 * self.here.zd(d) + x) * self.rows, self.rows),
                            span((2 * y + c) * self.cols, self.cols)]

    def push(self, *args):
        self.sends.append(push(*args))

    def landed(self, ref, sem):
        pltpu.make_async_remote_copy(
            src_ref=ref, dst_ref=ref, send_sem=sem, recv_sem=sem, device_id=self.here.xn, device_id_type=MESH
        ).wait_recv()

    def give(self, d, e):
        for lane in ((1, 3) if e else (0, 2)):
            self.push(self.block(d, lane, 1 - self.here.c), self.fc.at[lane, d],
                      self.sc.at[lane, d], self.rc.at[lane, d], self.here.cn)

    def pair(self, lane, d):
        self.landed(self.fc.at[lane, d], self.rc.at[lane, d])
        add_into(self.block(d, lane, self.here.c), self.fc.at[lane, d])
        return self.block(d, lane, self.here.c)

    def corner(self, d):
        b = self.pair(3, d)
        self.push(b.at[:, self.top], self.f1x.at[d], self.s1x.at[d], self.r1x.at[d], self.here.xn)
        self.push(b.at[:, self.low], self.f1y.at[d], self.s1y.at[d], self.r1y.at[d], self.here.yn)

    def sides(self, d):
        b = self.pair(1, d)
        self.landed(self.f1y.at[d], self.r1y.at[d])
        add_into(b.at[:, self.low], self.f1y.at[d])
        self.push(b, self.f2x.at[d], self.s2x.at[d], self.r2x.at[d], self.here.xn)
        b = self.pair(2, d)
        self.landed(self.f1x.at[d], self.r1x.at[d])
        add_into(b.at[:, self.top], self.f1x.at[d])
        self.push(b, self.f2y.at[d], self.s2y.at[d], self.r2y.at[d], self.here.yn)

    def centre(self, d):
        b = self.pair(0, d)
        self.landed(self.f2x.at[d], self.r2x.at[d])
        self.landed(self.f2y.at[d], self.r2y.at[d])
        add_into(b, self.f2x.at[d], self.f2y.at[d])
        if d != 0:
            self.push(b, self.fz.at[(4 - d) % 4], self.sz.at[d], self.rz.at[(4 - d) % 4], self.here.peer(d, 0))

    def total(self):
        for d in (1, 2, 3):
            self.landed(self.fz.at[d], self.rz.at[d])
        b = self.block(0, 0, self.here.c)
        step = 32

        @pl.loop(0, 2 * self.rows // step)
        def _(i):
            n = i // (self.rows // step)
            r = pl.ds(pl.multiple_of((i % (self.rows // step)) * step, step), step)
            if self.whole:
                total = b[n, r, :].astype(F32)
                for d in (1, 2, 3):
                    total = total + self.fz[d, n, r, :].astype(F32)
            else:
                total = jnp.where(self.here.z // 2 == n, b[0, r, :].astype(F32), 0.0)
                for d in (1, 2, 3):
                    total = total + jnp.where(self.here.zd(d) // 2 == n, self.fz[d, 0, r, :].astype(F32), 0.0)
            self.tmp[n, r, :] = total.astype(self.tmp.dtype)

    def share(self, out):
        h = self.here
        mine = self.full.at[h.t]
        self.keeps = [keep(self.tmp, mine, self.osem.at[4])]
        self.push(self.tmp, mine, self.sg.at[0], self.rg.at[0], h.yn)
        self.push(self.tmp, mine, self.sg.at[1], self.rg.at[1], h.cn)
        ty, tc, td = 2 * (1 - h.y) + h.c, 2 * h.y + 1 - h.c, 2 * (1 - h.y) + 1 - h.c
        self.landed(self.full.at[ty], self.rg.at[0])
        self.push(self.full.at[ty], self.full.at[ty], self.sg.at[2], self.rg.at[2], h.cn)
        self.landed(self.full.at[tc], self.rg.at[1])
        self.landed(self.full.at[td], self.rg.at[2])
        self.keeps[0].wait()
        outs = [keep(self.full.at[q], out.at[:, :, pl.ds(q * self.cols, self.cols)], self.osem.at[q]) for q in range(4)]
        for copy in outs:
            copy.wait()

    def finish(self):
        for copy in self.sends:
            copy.wait_send()


def sum_kernel(whole, in_ref, out_ref, part, load, *refs):
    here = Here()
    here.greet()
    total = Sum(here, whole, part, refs)
    rows = total.rows
    copies = {}
    for e in (1, 0):
        for d in FAR_FIRST:
            at = span((2 * here.zd(d) + (here.x + e) % 2) * rows, rows)
            copies[d, e] = keep(in_ref.at[:, at, :], part.at[:, at, :], load.at[e, d])
    for e in (1, 0):
        for d in FAR_FIRST:
            copies[d, e].wait()
            total.give(d, e)
    for d in FAR_FIRST:
        total.corner(d)
    for d in FAR_FIRST:
        total.sides(d)
    for d in FAR_FIRST:
        total.centre(d)
    total.total()
    total.share(out_ref)
    total.finish()


def sum_rows(value, whole):
    count, total_rows, width = value.shape
    rows = total_rows // 8
    low = value.dtype
    return pl.pallas_call(
        functools.partial(sum_kernel, whole),
        out_shape=jax.ShapeDtypeStruct((2, rows, width), low),
        in_specs=[pl.BlockSpec(memory_space=pl.ANY)],
        out_specs=pl.BlockSpec(memory_space=pl.ANY),
        scratch_shapes=[pltpu.VMEM((count, total_rows, width), low), pltpu.SemaphoreType.DMA((2, 4))]
        + Sum.scratch(count, rows, width, low),
        compiler_params=pltpu.CompilerParams(
            collective_id=2 if whole else 3, has_side_effects=True, vmem_limit_bytes=VMEM_LIMIT
        ),
        name="sum_whole" if whole else "sum_half",
    )(value)


def gather_kernel(whole, in_ref, out_ref, *sems):
    here = Here()
    here.greet()
    rows = Gather(here, whole, in_ref, out_ref, sems)
    rows.start()
    for d in ORDER:
        rows.spread(d)
    for d in (0,) + ORDER:
        rows.cross(d)
    for d in (0,) + ORDER:
        rows.close(d)
    for d in (0,) + ORDER:
        rows.arrived(d, 0)
        rows.arrived(d, 1)
    rows.finish()


def gather_rows(value, whole):
    count, rows, width = value.shape
    return pl.pallas_call(
        functools.partial(gather_kernel, whole),
        out_shape=jax.ShapeDtypeStruct((count if whole else 1, rows * 8, width), value.dtype),
        in_specs=[pl.BlockSpec(memory_space=pl.ANY)],
        out_specs=pl.BlockSpec(memory_space=pl.ANY),
        scratch_shapes=Gather.scratch(),
        compiler_params=pltpu.CompilerParams(collective_id=0 if whole else 1, has_side_effects=True),
        name="gather_whole" if whole else "gather_half",
    )(value)


def signed_tables(length, width):
    middle = width // 2
    frequency = rope_base ** (-np.arange(middle) * 2.0 / width)
    angles = np.arange(length)[:, None] * frequency[None, :]
    cosine, sine = np.cos(angles), np.sin(angles)
    return (
        jnp.asarray(np.concatenate([cosine, cosine], axis=1), F32),
        jnp.asarray(np.concatenate([-sine, sine], axis=1), F32),
    )


def dot_nn(a, b):
    return jnp.dot(a, b, preferred_element_type=F32)


def dot_nt(a, b):
    return lax.dot_general(a, b, (((1,), (1,)), ((), ())), preferred_element_type=F32)


def dot_tn(a, b):
    return lax.dot_general(a, b, (((0,), (0,)), ((), ())), preferred_element_type=F32)


def attend_back_kernel(heads, dctx_ref, pre_ref, qkv_ref, prob_ref, cos_ref, sin_ref, qg_ref, kg_ref,
                       dqkv_ref, gains_ref, dq_s, dk_s, dv_s):
    seq = dctx_ref.shape[0]
    hd = cos_ref.shape[1]
    tile = 256
    scale = 1.0 / math.sqrt(hd)
    dk_s[...] = jnp.zeros_like(dk_s)
    dv_s[...] = jnp.zeros_like(dv_s)
    for a in range(heads):
        for i in range(seq // tile):
            r = pl.ds(i * tile, tile)
            n = (i + 1) * tile
            query = qkv_ref[r, pl.ds(a * hd, hd)]
            key = qkv_ref[pl.ds(0, n), pl.ds(heads * hd, hd)]
            value = qkv_ref[pl.ds(0, n), pl.ds((heads + 1) * hd, hd)]
            dctx = dctx_ref[r, pl.ds(a * hd, hd)]
            prob = prob_ref[a, r, pl.ds(0, n)]
            wide = prob.astype(F32)
            dprob = dot_nt(dctx, value)
            delta = jnp.sum(wide * dprob, axis=-1, keepdims=True)
            dscore = (wide * (dprob - delta)).astype(LOW)
            dq_s[r, pl.ds(a * hd, hd)] = dot_nn(dscore, key) * scale
            dk_s[pl.ds(0, n), :] += dot_tn(dscore, query) * scale
            dv_s[pl.ds(0, n), :] += dot_tn(prob, dctx)
    gq = jnp.zeros((1, hd), F32)
    gk = jnp.zeros((1, hd), F32)
    for i in range(seq // tile):
        r = pl.ds(i * tile, tile)
        dqkv_ref[r, pl.ds((heads + 1) * hd, hd)] = dv_s[r, :].astype(LOW)
        for a in range(heads + 1):
            up = dq_s[r, pl.ds(a * hd, hd)] if a < heads else dk_s[r, :]
            one = pre_ref[r, pl.ds(a * hd, hd)]
            factor = lax.rsqrt(jnp.mean(one * one, axis=-1, keepdims=True) + norm_eps)
            hat = one * factor
            turned = up * cos_ref[r, :] + pltpu.roll(up * sin_ref[r, :], hd // 2, 1)
            part = jnp.sum(turned * hat, axis=0, keepdims=True)
            gained = turned * (qg_ref if a < heads else kg_ref)[...]
            back = factor * (gained - hat * jnp.mean(gained * hat, axis=-1, keepdims=True))
            dqkv_ref[r, pl.ds(a * hd, hd)] = back.astype(LOW)
            if a < heads:
                gq = gq + part
            else:
                gk = gk + part
    gains_ref[...] = jnp.concatenate([gq, gk], axis=0)


def attend_back(dctx, pre, qkv, prob, cosine, sine, query_gain, key_gain):
    seq = dctx.shape[0]
    hd = query_gain.shape[0]
    heads = prob.shape[0]
    return pl.pallas_call(
        functools.partial(attend_back_kernel, heads),
        out_shape=(
            jax.ShapeDtypeStruct((seq, (heads + 2) * hd), LOW),
            jax.ShapeDtypeStruct((2, hd), F32),
        ),
        scratch_shapes=[
            pltpu.VMEM((seq, heads * hd), F32),
            pltpu.VMEM((seq, hd), F32),
            pltpu.VMEM((seq, hd), F32),
        ],
        compiler_params=pltpu.CompilerParams(vmem_limit_bytes=VMEM_LIMIT),
        name="attend_back",
    )(dctx, pre, qkv, prob, cosine, sine, query_gain[None], key_gain[None])


def route_probs(logits, ids, count):
    lane = lax.broadcasted_iota(jnp.int32, logits.shape, 1)
    named = lane == ids[:, 0:1]
    for k in range(1, count):
        named = named | (lane == ids[:, k : k + 1])
    masked = jnp.where(named, logits, masked_score)
    terms = jnp.where(named, jnp.exp(masked - jnp.max(masked, axis=-1, keepdims=True)), 0.0)
    return terms / jnp.sum(terms, axis=-1, keepdims=True)


def experts_kernel(experts, route_count, first_ref, x_ref, og_ref, ids_ref, router_ref, g_ref, u_ref, d_ref,
                   out_ref, dx_ref, dgp_ref, dg_ref, du_ref, dd_ref, dg_s, du_s, dd_s, sem):
    i = pl.program_id(0)
    hidden = g_ref.shape[0]
    per = hidden // experts
    tile = x_ref.shape[0]

    @pl.when(i == 0)
    def _():
        dg_s[...] = jnp.zeros_like(dg_s)
        du_s[...] = jnp.zeros_like(du_s)
        dd_s[...] = jnp.zeros_like(dd_s)

    x = x_ref[...]
    og = og_ref[...]
    first = first_ref[0]
    probs = route_probs(dot_nn(x, router_ref[...]), ids_ref[...], route_count)
    lanes = probs.shape[1]
    row = lax.broadcasted_iota(jnp.int32, (lanes, hidden), 0)
    col = lax.broadcasted_iota(jnp.int32, (lanes, hidden), 1)
    spread = jnp.where(row == first + col // per, 1.0, 0.0).astype(LOW)
    high = probs.astype(LOW)
    rest = (probs - high.astype(F32)).astype(LOW)
    share = dot_nn(high, spread) + dot_nn(rest, spread)
    gate = dot_nt(x, g_ref[...])
    up = dot_nt(x, u_ref[...])
    raw = dot_nt(og, d_ref[...])
    sig = 1.0 / (1.0 + jnp.exp(-gate))
    act = gate * sig
    inner = act * up
    weighted = (inner * share).astype(LOW)
    product = jnp.where(share > 0.0, inner * raw, 0.0)
    product_high = product.astype(LOW)
    product_rest = (product - product_high.astype(F32)).astype(LOW)
    dgp_ref[...] = dot_nt(product_high, spread) + dot_nt(product_rest, spread)
    d_inner = raw * share
    d_up = (d_inner * act).astype(LOW)
    d_gate = (d_inner * up * sig * (1.0 + gate * (1.0 - sig))).astype(LOW)
    dx_ref[...] = (dot_nn(d_gate, g_ref[...]) + dot_nn(d_up, u_ref[...])).astype(LOW)
    out_ref[...] = dot_nn(weighted, d_ref[...]).astype(LOW)
    dg_s[...] += dot_tn(d_gate, x)
    du_s[...] += dot_tn(d_up, x)
    dd_s[...] += dot_tn(weighted, og)

    @pl.when(i == pl.num_programs(0) - 1)
    def _():
        copies = []
        for n, (src, dst) in enumerate(((dg_s, dg_ref), (du_s, du_ref), (dd_s, dd_ref))):
            copies.append(pltpu.make_async_copy(src, dst, sem.at[n]))
            copies[-1].start()
        for copy in copies:
            copy.wait()


def run_experts(first, x, og, ids, router, gate, up, down):
    tokens, width = x.shape
    experts, per, _ = gate.shape
    hidden = experts * per
    tile = 256
    lanes = router.shape[1]
    once = pl.Buffered(1)
    keep = lambda i, s: (0, 0)
    walk = lambda i, s: (i, 0)
    any_space = pl.BlockSpec(memory_space=pl.ANY)
    grads = jax.ShapeDtypeStruct((hidden, width), F32)
    return pl.pallas_call(
        functools.partial(experts_kernel, experts, ids.shape[1]),
        grid_spec=pltpu.PrefetchScalarGridSpec(
            num_scalar_prefetch=1,
            grid=(tokens // tile,),
            in_specs=[
                pl.BlockSpec((tile, width), walk),
                pl.BlockSpec((tile, width), walk),
                pl.BlockSpec((tile, ids.shape[1]), walk),
                pl.BlockSpec((width, lanes), keep, pipeline_mode=once),
                pl.BlockSpec((hidden, width), keep, pipeline_mode=once),
                pl.BlockSpec((hidden, width), keep, pipeline_mode=once),
                pl.BlockSpec((hidden, width), keep, pipeline_mode=once),
            ],
            out_specs=[
                pl.BlockSpec((tile, width), walk),
                pl.BlockSpec((tile, width), walk),
                pl.BlockSpec((tile, lanes), walk),
                any_space,
                any_space,
                any_space,
            ],
            scratch_shapes=[pltpu.VMEM((hidden, width), F32)] * 3 + [pltpu.SemaphoreType.DMA((3,))],
        ),
        out_shape=(
            jax.ShapeDtypeStruct((tokens, width), LOW),
            jax.ShapeDtypeStruct((tokens, width), LOW),
            jax.ShapeDtypeStruct((tokens, lanes), F32),
            grads,
            grads,
            grads,
        ),
        compiler_params=pltpu.CompilerParams(
            vmem_limit_bytes=VMEM_LIMIT, dimension_semantics=("arbitrary",)
        ),
        name="experts",
    )(first, x, og, ids, router, gate.reshape(hidden, width), up.reshape(hidden, width), down.reshape(hidden, width))


class Weights:
    scratch = staticmethod(lambda: [pltpu.SemaphoreType.DMA((8, 4, 2))] * 4 + [pltpu.SemaphoreType.DMA((6,))])
    slots = 5

    def __init__(self, here, query, key, value, output, router, ids, w, wo, router_all, ids_all, sems):
        self.here = here
        self.query, self.output, self.w, self.wo = query, output, w, wo
        piece, part = query.shape[0], wo.shape[1]
        self.piece, self.part = piece, part
        hd = key.shape[1]
        self.shared = (
            (key, lambda f: w.at[span(f * piece, piece), pl.ds(part, hd)]),
            (value, lambda f: w.at[span(f * piece, piece), pl.ds(part + hd, hd)]),
            (router, lambda f: router_all.at[:, span(f * piece, piece)]),
            (ids, lambda f: ids_all.at[:, :, span(f * ids.shape[2], ids.shape[2])]),
        )
        self.qs, self.qr, self.ss, self.sr, self.loc = sems
        self.sends, self.keeps = [], []

    def landed(self, ref, sem):
        pltpu.make_async_remote_copy(
            src_ref=ref, dst_ref=ref, send_sem=sem, recv_sem=sem, device_id=self.here.xn, device_id_type=MESH
        ).wait_recv()

    def start_shared(self):
        h = self.here
        for n, (src, dst) in enumerate(self.shared):
            self.keeps.append(keep(src, dst(h.f), self.loc.at[n]))
            for d, e in ((2, 0), (1, 0), (3, 0), (0, 1)):
                self.sends.append(push(src, dst(h.f), self.ss.at[n, d, e], self.sr.at[n, (4 - d) % 4, e], h.peer(d, e)))

    def pass_shared(self, d):
        h = self.here
        for n, (_, dst) in enumerate(self.shared):
            ref = dst(2 * h.zd(d) + h.x)
            self.landed(ref, self.sr.at[n, d, 0])
            self.sends.append(push(ref, ref, self.ss.at[n, d, 1], self.sr.at[n, d, 1], h.xn))

    def wait_shared(self):
        h = self.here
        for n, (_, dst) in enumerate(self.shared):
            for d in range(4):
                self.landed(dst(2 * h.zd(d) + 1 - h.x), self.sr.at[n, d, 1])

    def start_pairs(self, n):
        h = self.here
        src, dst = ((self.query, self.w), (self.output, self.wo))[n]
        mine = lambda f: dst.at[span(f * self.piece, self.piece), pl.ds(0, self.part)]
        self.keeps.append(keep(src.at[:, span((h.f % 4) * self.part, self.part)], mine(h.f), self.loc.at[4 + n]))
        for d in FAR_FIRST:
            for e in (1, 0):
                if d or e:
                    f = 2 * h.zd(d) + (h.x + e) % 2
                    self.sends.append(push(src.at[:, span((f % 4) * self.part, self.part)], mine(h.f),
                                           self.qs.at[n, d, e], self.qr.at[n, (4 - d) % 4, e], h.peer(d, e)))

    def wait_pairs(self, n):
        h = self.here
        dst = (self.w, self.wo)[n]
        for d in range(4):
            for e in (1, 0):
                if d or e:
                    f = 2 * h.zd(d) + (h.x + e) % 2
                    self.landed(dst.at[span(f * self.piece, self.piece), pl.ds(0, self.part)], self.qr.at[n, d, e])

    def finish(self):
        for copy in self.sends:
            copy.wait_send()


def begin_kernel(heads, normed, cot, query, key, value, output, router, ids, cos_ref, sin_ref, qg_ref, kg_ref,
                 xn_out, w_out, wo_out, router_out, ids_out, cot_out, pre_out, qkv_out, prob_out, ctx_out, branch_out,
                 xn, w, wo, pre, qkv, prob, ctx, part, osem, *sems):
    here = Here()
    here.greet()
    at = 0
    x_rows = Gather(here, False, normed, xn, sems[at : at + Gather.slots])
    at += Gather.slots
    c_rows = Gather(here, True, cot, cot_out, sems[at : at + Gather.slots])
    at += Gather.slots
    moved = Weights(here, query, key, value, output, router, ids, w, wo, router_out, ids_out, sems[at : at + Weights.slots])
    at += Weights.slots
    total = Sum(here, False, part, sems[at:])

    x_rows.start()
    moved.start_shared()
    moved.start_pairs(0)
    for d in ORDER:
        x_rows.spread(d)
        moved.pass_shared(d)
    for d in (0,) + ORDER:
        x_rows.cross(d)
    for d in (0,) + ORDER:
        x_rows.close(d)
    for d in (0,) + ORDER:
        x_rows.arrived(d, 0)
        x_rows.arrived(d, 1)
    moved.wait_shared()
    moved.wait_pairs(0)
    for copy in moved.keeps:
        copy.wait()
    c_rows.start()
    moved.keeps = []
    moved.start_pairs(1)
    outs = [keep(xn, xn_out, osem.at[0]), keep(w, w_out, osem.at[1])]

    seq = xn.shape[1]
    hd = cos_ref.shape[1]
    tile = 256
    scale = 1.0 / math.sqrt(hd)
    for i in range(seq // tile):
        r = pl.ds(i * tile, tile)
        got = dot_nn(xn[0, r, :], w[...])
        pre[r, :] = got[:, : (heads + 1) * hd]
        qkv[r, pl.ds((heads + 1) * hd, hd)] = got[:, (heads + 1) * hd :].astype(LOW)
        for a in range(heads + 1):
            one = got[:, a * hd : (a + 1) * hd]
            factor = lax.rsqrt(jnp.mean(one * one, axis=-1, keepdims=True) + norm_eps)
            gained = one * factor * (qg_ref if a < heads else kg_ref)[...]
            turned = gained * cos_ref[r, :] + pltpu.roll(gained, hd // 2, 1) * sin_ref[r, :]
            qkv[r, pl.ds(a * hd, hd)] = turned.astype(LOW)
    outs += [keep(pre, pre_out, osem.at[2]), keep(qkv, qkv_out, osem.at[3])]
    for d in ORDER:
        c_rows.spread(d)
    for a in range(heads):
        for i in range(seq // tile):
            r = pl.ds(i * tile, tile)
            n = (i + 1) * tile
            score = dot_nt(qkv[r, pl.ds(a * hd, hd)], qkv[pl.ds(0, n), pl.ds(heads * hd, hd)]) * scale
            row = lax.broadcasted_iota(jnp.int32, (tile, n), 0) + i * tile
            col = lax.broadcasted_iota(jnp.int32, (tile, n), 1)
            score = jnp.where(col <= row, score, masked_score)
            terms = jnp.exp(score - jnp.max(score, axis=-1, keepdims=True))
            low = (terms * (1.0 / jnp.sum(terms, axis=-1, keepdims=True))).astype(LOW)
            prob[a, r, pl.ds(0, n)] = low
            ctx[r, pl.ds(a * hd, hd)] = dot_nn(low, qkv[pl.ds(0, n), pl.ds((heads + 1) * hd, hd)]).astype(LOW)
        if a == 0:
            for d in (0,) + ORDER:
                c_rows.cross(d)
    outs += [keep(prob, prob_out, osem.at[4]), keep(ctx, ctx_out, osem.at[5])]
    moved.wait_pairs(1)
    for copy in moved.keeps:
        copy.wait()
    outs.append(keep(wo, wo_out, osem.at[6]))
    rows = total.rows
    for e in (1, 0):
        for d in FAR_FIRST:
            at_f = span((2 * here.zd(d) + (here.x + e) % 2) * rows, rows)
            part[0, at_f, :] = dot_nt(ctx[at_f, :], wo[...]).astype(LOW)
            total.give(d, e)
    for d in FAR_FIRST:
        total.corner(d)
    for d in (0,) + ORDER:
        c_rows.close(d)
    for d in FAR_FIRST:
        total.sides(d)
    for d in FAR_FIRST:
        total.centre(d)
    total.total()
    total.share(branch_out)
    for d in (0,) + ORDER:
        c_rows.arrived(d, 0)
        c_rows.arrived(d, 1)
    for each in (x_rows, c_rows, moved, total):
        each.finish()
    for copy in outs:
        copy.wait()


def begin(normed, cot, query, key, value, output, router, ids, cosine, sine, query_gain, key_gain):
    count, rows, width = normed.shape
    seq = rows * 8
    hd = query_gain.shape[0]
    part = query.shape[1] // 4
    heads = part // hd
    vm = pltpu.VMEM
    hbm = pl.BlockSpec(memory_space=pl.ANY)
    near = pl.BlockSpec(memory_space=pltpu.VMEM)
    shape = jax.ShapeDtypeStruct
    local = [
        ((1, seq, width), LOW),
        ((width, part + 2 * hd), LOW),
        ((width, part), LOW),
        ((seq, (heads + 1) * hd), F32),
        ((seq, (heads + 2) * hd), LOW),
        ((heads, seq, seq), LOW),
        ((seq, heads * hd), LOW),
    ]
    return pl.pallas_call(
        functools.partial(begin_kernel, heads),
        out_shape=(
            shape(*local[0]),
            shape(*local[1]),
            shape(*local[2]),
            shape((router.shape[0], width), LOW),
            shape((count, ids.shape[1], seq), jnp.int32),
            shape((count, seq, width), LOW),
            shape(*local[3]),
            shape(*local[4]),
            shape(*local[5]),
            shape(*local[6]),
            shape((count, rows, width), LOW),
        ),
        in_specs=[hbm] * 8 + [near] * 4,
        out_specs=[hbm] * 11,
        scratch_shapes=[vm(*entry) for entry in local]
        + [vm((1, seq, width), LOW), pltpu.SemaphoreType.DMA((7,))]
        + Gather.scratch() + Gather.scratch() + Weights.scratch() + Sum.scratch(1, rows, width, LOW),
        compiler_params=pltpu.CompilerParams(
            collective_id=4, has_side_effects=True, vmem_limit_bytes=VMEM_LIMIT
        ),
        name="begin",
    )(normed, cot, query, key, value, output, router, ids, cosine, sine, query_gain[None], key_gain[None])


def rotate_half(values):
    middle = values.shape[-1] // 2
    return jnp.concatenate([-values[..., middle:], values[..., :middle]], axis=-1)


def rope_tables(positions, head_width):
    middle = head_width // 2
    frequency = rope_base ** (-jnp.arange(middle, dtype=jnp.float32) * 2.0 / head_width)
    angles = positions.astype(jnp.float32)[:, None] * frequency[None, :]
    angles = jnp.concatenate([angles, angles], axis=1)
    return (jnp.cos(angles), jnp.sin(angles))


def norm_parts(values):
    factor = lax.rsqrt(jnp.mean(values * values, axis=-1, keepdims=True) + norm_eps)
    return (values * factor, factor)


def norm_back(upstream, gain, normal, factor):
    scaled = upstream * gain
    return factor * (scaled - normal * jnp.mean(scaled * normal, axis=-1, keepdims=True))


def head_back(upstream, cosine_heads, sine_heads, gain, normal, factor):
    turned = upstream * cosine_heads - rotate_half(upstream * sine_heads)
    gain_part = jnp.sum(turned * normal, axis=(0, 1))
    return (norm_back(turned, gain, normal, factor), gain_part)


def fetch_weights(query_weight, key_weight, value_weight, output_weight, router_weight):
    return (
        lax.all_gather(query_weight, "fsdp", axis=0, tiled=True),
        lax.all_gather(key_weight, "fsdp", axis=0, tiled=True),
        lax.all_gather(value_weight, "fsdp", axis=0, tiled=True),
        lax.all_gather(output_weight, "fsdp", axis=0, tiled=True),
        lax.all_gather(router_weight, "fsdp", axis=0, tiled=True),
    )


def widen(summed):
    return lax.all_gather(summed, "tp", axis=3, tiled=True)


def carry_back(summed):
    return lax.all_to_all(summed, "fsdp", split_axis=0, concat_axis=0, tiled=True)


def send_home(summed):
    arrived_home = carry_back(widen(summed))
    return arrived_home


def general_device(
    tokens,
    cotangent,
    expert_ids,
    attention_gain,
    query_gain,
    key_gain,
    query_weight,
    key_weight,
    value_weight,
    output_weight,
    expert_gain,
    router_weight,
    gate_weight,
    up_weight,
    down_weight,
):
    micro_count = tokens.shape[0]
    tok_rows = tokens.shape[1]
    width = tokens.shape[2]
    route_count = expert_ids.shape[2]
    head_dim = query_gain.shape[0]
    local_heads = query_weight.shape[1] // head_dim
    local_groups = key_weight.shape[1] // head_dim
    group_size = local_heads // local_groups
    fsdp_count = lax.axis_size("fsdp")
    seq_len = tok_rows * fsdp_count
    experts_here = gate_weight.shape[0]
    expert_count = experts_here * fsdp_count
    capacity = max(2, 5 * tok_rows * route_count // (4 * expert_count))
    key_block = math.gcd(seq_len, 512)
    score_scale = 1.0 / math.sqrt(head_dim)
    query_count = tok_rows * group_size
    routed_total = tok_rows * route_count
    start_row = lax.axis_index("fsdp") * tok_rows
    positions = start_row + jnp.arange(tok_rows, dtype=jnp.int32)
    cosine_table, sine_table = rope_tables(positions, head_dim)
    cosine_heads = cosine_table[:, None, :]
    sine_heads = sine_table[:, None, :]
    query_pos = start_row + jnp.arange(query_count, dtype=jnp.int32) // group_size
    block_total = (start_row + tok_rows + key_block - 1) // key_block
    expert_range = jnp.arange(expert_count, dtype=jnp.int32)
    zero_row = jnp.zeros((1, width), jnp.bfloat16)

    def to_rows(tensor):
        return (
            tensor.reshape(tok_rows, local_groups, group_size, head_dim)
            .transpose(1, 0, 2, 3)
            .reshape(local_groups, query_count, head_dim)
        )

    def from_rows(tensor):
        return (
            tensor.reshape(local_groups, tok_rows, group_size, head_dim)
            .transpose(1, 0, 2, 3)
            .reshape(tok_rows, local_heads, head_dim)
        )

    acc_attention_gain = jnp.zeros((width,), jnp.float32)
    acc_head_gains = jnp.zeros((2, head_dim), jnp.float32)
    acc_query = jnp.zeros((width, local_heads * head_dim), jnp.float32)
    acc_key = jnp.zeros((width, local_groups * head_dim), jnp.float32)
    acc_value = jnp.zeros((width, local_groups * head_dim), jnp.float32)
    acc_output = jnp.zeros((width, local_heads * head_dim), jnp.float32)
    acc_expert_gain = jnp.zeros((width,), jnp.float32)
    acc_router = jnp.zeros((width, expert_count), jnp.float32)
    acc_gate = jnp.zeros(gate_weight.shape, jnp.float32)
    acc_up = jnp.zeros(up_weight.shape, jnp.float32)
    acc_down = jnp.zeros(down_weight.shape, jnp.float32)
    layer_rows = []
    input_rows = []
    for micro_index in range(micro_count):
        inputs = tokens[micro_index].astype(jnp.float32)
        query_full, key_full, value_full, output_full, router_full = fetch_weights(
            query_weight, key_weight, value_weight, output_weight, router_weight
        )
        input_hat, attention_factor = norm_parts(inputs)
        normed = (input_hat * attention_gain).astype(jnp.bfloat16)
        query_pre = jnp.dot(normed, query_full, preferred_element_type=jnp.float32).reshape(
            tok_rows, local_heads, head_dim
        )
        key_pre = jnp.dot(normed, key_full, preferred_element_type=jnp.float32).reshape(
            tok_rows, local_groups, head_dim
        )
        value_low = jnp.dot(normed, value_full, preferred_element_type=jnp.float32).astype(
            jnp.bfloat16
        )
        query_hat, query_factor = norm_parts(query_pre)
        key_hat, key_factor = norm_parts(key_pre)
        query_scaled = query_hat * query_gain
        key_scaled = key_hat * key_gain
        query_low = (query_scaled * cosine_heads + rotate_half(query_scaled) * sine_heads).astype(
            jnp.bfloat16
        )
        key_low = (key_scaled * cosine_heads + rotate_half(key_scaled) * sine_heads).astype(
            jnp.bfloat16
        )
        key_all, value_all = (
            lax.all_gather(
                key_low.reshape(tok_rows, local_groups * head_dim), "fsdp", axis=0, tiled=True
            ),
            lax.all_gather(value_low, "fsdp", axis=0, tiled=True),
        )
        key_heads = key_all.reshape(seq_len, local_groups, head_dim).transpose(1, 0, 2)
        value_heads = value_all.reshape(seq_len, local_groups, head_dim).transpose(1, 0, 2)
        query_rows = to_rows(query_low)

        def scores_at(block_index):
            block_start = block_index * key_block
            key_slice = lax.dynamic_slice_in_dim(key_heads, block_start, key_block, 1)
            raw_scores = (
                jnp.einsum(
                    "gqd,gkd->gqk", query_rows, key_slice, preferred_element_type=jnp.float32
                )
                * score_scale
            )
            allowed = (block_start + jnp.arange(key_block, dtype=jnp.int32))[None, :] <= query_pos[
                :, None
            ]
            return (jnp.where(allowed[None], raw_scores, masked_score), allowed, block_start)

        def stats_step(block_index, carried):
            run_peak, run_total = carried
            scores, allowed, block_start = scores_at(block_index)
            new_peak = jnp.maximum(run_peak, jnp.max(scores, axis=-1))
            terms = jnp.where(allowed[None], jnp.exp(scores - new_peak[..., None]), 0.0)
            return (new_peak, run_total * jnp.exp(run_peak - new_peak) + jnp.sum(terms, axis=-1))

        start_stats = (
            jnp.full((local_groups, query_count), masked_score, jnp.float32),
            jnp.zeros((local_groups, query_count), jnp.float32),
        )
        run_peak, run_total = lax.fori_loop(0, block_total, stats_step, start_stats)
        log_total = run_peak + jnp.log(run_total)

        def value_step(block_index, acc_context):
            scores, allowed, block_start = scores_at(block_index)
            probs_low = jnp.where(
                allowed[None], jnp.exp(scores - log_total[..., None]), 0.0
            ).astype(jnp.bfloat16)
            value_slice = lax.dynamic_slice_in_dim(value_heads, block_start, key_block, 1)
            return acc_context + jnp.einsum(
                "gqk,gkd->gqd", probs_low, value_slice, preferred_element_type=jnp.float32
            )

        context_rows = lax.fori_loop(
            0,
            block_total,
            value_step,
            jnp.zeros((local_groups, query_count, head_dim), jnp.float32),
        )
        context_low = (
            from_rows(context_rows).reshape(tok_rows, local_heads * head_dim).astype(jnp.bfloat16)
        )
        branch_part = jnp.einsum(
            "th,dh->td", context_low, output_full, preferred_element_type=jnp.float32
        )
        resid = inputs + lax.psum(branch_part.astype(jnp.bfloat16), "tp").astype(jnp.float32)
        resid_hat, expert_factor = norm_parts(resid)
        expert_in = (resid_hat * expert_gain).astype(jnp.bfloat16)
        logits = jnp.dot(expert_in, router_full, preferred_element_type=jnp.float32)
        routes_now = expert_ids[micro_index]
        choose = (routes_now[:, :, None] == expert_range[None, None, :]).astype(jnp.float32)
        picked = jnp.sum(choose * logits[:, None, :], axis=-1)
        shifted = jnp.exp(picked - jnp.max(picked, axis=-1, keepdims=True))
        gate_probs = shifted / jnp.sum(shifted, axis=-1, keepdims=True)
        flat_routes = routes_now.reshape(-1)
        onehot = (flat_routes[:, None] == expert_range[None, :]).astype(jnp.int32)
        rank_in = jnp.sum((jnp.cumsum(onehot, axis=0) - onehot) * onehot, axis=1)
        slot_index = flat_routes * capacity + rank_in
        slot_source = (
            jnp.full((expert_count * capacity,), routed_total, jnp.int32)
            .at[slot_index]
            .set(jnp.arange(routed_total, dtype=jnp.int32))
        )
        padded_in = jnp.concatenate([expert_in, zero_row], axis=0)
        outgoing = padded_in[slot_source // route_count].reshape(
            fsdp_count, experts_here, capacity, width
        )
        arrived = lax.all_to_all(outgoing, "fsdp", split_axis=0, concat_axis=0, tiled=True)
        gate_pre = jnp.einsum(
            "secd,efd->secf", arrived, gate_weight, preferred_element_type=jnp.float32
        )
        up_pre = jnp.einsum(
            "secd,efd->secf", arrived, up_weight, preferred_element_type=jnp.float32
        )
        gate_sigmoid = jax.nn.sigmoid(gate_pre)
        inner_low = (gate_pre * gate_sigmoid * up_pre).astype(jnp.bfloat16)
        result_part = jnp.einsum(
            "secf,efd->secd", inner_low, down_weight, preferred_element_type=jnp.float32
        )
        result_low = lax.psum_scatter(
            result_part.astype(jnp.bfloat16), "tp", scatter_dimension=3, tiled=True
        )
        result_home = send_home(result_low)
        routed = (
            result_home.reshape(expert_count * capacity, width)[slot_index]
            .astype(jnp.float32)
            .reshape(tok_rows, route_count, width)
        )
        layer_rows.append(
            (resid + jnp.sum(gate_probs[:, :, None] * routed, axis=1)).astype(jnp.bfloat16)
        )
        query_full, key_full, value_full, output_full, router_full = fetch_weights(
            query_weight, key_weight, value_weight, output_weight, router_weight
        )
        out_grad = cotangent[micro_index].astype(jnp.float32)
        d_route = (
            (gate_probs[:, :, None] * out_grad[:, None, :])
            .astype(jnp.bfloat16)
            .reshape(routed_total, width)
        )
        d_gate_probs = jnp.sum(out_grad[:, None, :] * routed, axis=-1)
        d_pick = gate_probs * (
            d_gate_probs - jnp.sum(gate_probs * d_gate_probs, axis=-1, keepdims=True)
        )
        d_logits = jnp.sum(choose * d_pick[:, :, None], axis=1).astype(jnp.bfloat16)
        grad_outgoing = jnp.concatenate([d_route, zero_row], axis=0)[slot_source].reshape(
            fsdp_count, experts_here, capacity, width
        )
        grad_arrived = lax.all_to_all(
            grad_outgoing, "fsdp", split_axis=0, concat_axis=0, tiled=True
        )
        d_inner = jnp.einsum(
            "secd,efd->secf", grad_arrived, down_weight, preferred_element_type=jnp.float32
        )
        acc_down = acc_down + jnp.einsum(
            "secf,secd->efd", inner_low, grad_arrived, preferred_element_type=jnp.float32
        )
        d_gate_low = (
            d_inner * up_pre * gate_sigmoid * (1.0 + gate_pre * (1.0 - gate_sigmoid))
        ).astype(jnp.bfloat16)
        d_up_low = (d_inner * gate_pre * gate_sigmoid).astype(jnp.bfloat16)
        acc_gate = acc_gate + jnp.einsum(
            "secf,secd->efd", d_gate_low, arrived, preferred_element_type=jnp.float32
        )
        acc_up = acc_up + jnp.einsum(
            "secf,secd->efd", d_up_low, arrived, preferred_element_type=jnp.float32
        )
        d_copy_part = jnp.einsum(
            "secf,efd->secd", d_gate_low, gate_weight, preferred_element_type=jnp.float32
        ) + jnp.einsum("secf,efd->secd", d_up_low, up_weight, preferred_element_type=jnp.float32)
        d_copy_low = lax.psum_scatter(
            d_copy_part.astype(jnp.bfloat16), "tp", scatter_dimension=3, tiled=True
        )
        d_copy_home = send_home(d_copy_low)
        d_copies = (
            d_copy_home.reshape(expert_count * capacity, width)[slot_index]
            .astype(jnp.float32)
            .reshape(tok_rows, route_count, width)
        )
        d_expert_in = jnp.sum(d_copies, axis=1) + jnp.dot(
            d_logits, router_full.T, preferred_element_type=jnp.float32
        )
        acc_router = acc_router + jnp.dot(expert_in.T, d_logits, preferred_element_type=jnp.float32)
        acc_expert_gain = acc_expert_gain + jnp.sum(d_expert_in * resid_hat, axis=0)
        d_resid = out_grad + norm_back(d_expert_in, expert_gain, resid_hat, expert_factor)
        d_branch = d_resid.astype(jnp.bfloat16)
        acc_output = acc_output + jnp.einsum(
            "td,th->dh", d_branch, context_low, preferred_element_type=jnp.float32
        )
        d_context = jnp.dot(d_branch, output_full, preferred_element_type=jnp.float32).astype(
            jnp.bfloat16
        )
        d_context_rows = to_rows(d_context.reshape(tok_rows, local_heads, head_dim))
        delta_rows = jnp.sum(d_context_rows.astype(jnp.float32) * context_rows, axis=-1)

        def grad_step(block_index, carried):
            d_query_rows, key_grads_all = carried
            scores, allowed, block_start = scores_at(block_index)
            probs = jnp.where(allowed[None], jnp.exp(scores - log_total[..., None]), 0.0)
            key_slice = lax.dynamic_slice_in_dim(key_heads, block_start, key_block, 1)
            value_slice = lax.dynamic_slice_in_dim(value_heads, block_start, key_block, 1)
            d_probs = jnp.einsum(
                "gqd,gkd->gqk", d_context_rows, value_slice, preferred_element_type=jnp.float32
            )
            d_scores = (probs * (d_probs - delta_rows[..., None])).astype(jnp.bfloat16)
            d_query_rows = (
                d_query_rows
                + jnp.einsum(
                    "gqk,gkd->gqd", d_scores, key_slice, preferred_element_type=jnp.float32
                )
                * score_scale
            )
            d_key_block = (
                jnp.einsum("gqk,gqd->kgd", d_scores, query_rows, preferred_element_type=jnp.float32)
                * score_scale
            )
            d_value_block = jnp.einsum(
                "gqk,gqd->kgd",
                probs.astype(jnp.bfloat16),
                d_context_rows,
                preferred_element_type=jnp.float32,
            )
            current = lax.dynamic_slice_in_dim(key_grads_all, block_start, key_block, 0)
            updated = current + jnp.concatenate([d_key_block, d_value_block], axis=-1)
            return (
                d_query_rows,
                lax.dynamic_update_slice_in_dim(key_grads_all, updated, block_start, 0),
            )

        start_grads = (
            jnp.zeros((local_groups, query_count, head_dim), jnp.float32),
            jnp.zeros((seq_len, local_groups, 2 * head_dim), jnp.float32),
        )
        d_query_rows, key_grads_all = lax.fori_loop(0, block_total, grad_step, start_grads)
        key_grads = (
            lax.psum_scatter(
                key_grads_all.reshape(seq_len, local_groups * 2 * head_dim).astype(jnp.bfloat16),
                "fsdp",
                scatter_dimension=0,
                tiled=True,
            )
            .astype(jnp.float32)
            .reshape(tok_rows, local_groups, 2 * head_dim)
        )
        d_value_low = (
            key_grads[..., head_dim:]
            .reshape(tok_rows, local_groups * head_dim)
            .astype(jnp.bfloat16)
        )
        d_key_pre, key_gain_part = head_back(
            key_grads[..., :head_dim], cosine_heads, sine_heads, key_gain, key_hat, key_factor
        )
        d_query_pre, query_gain_part = head_back(
            from_rows(d_query_rows), cosine_heads, sine_heads, query_gain, query_hat, query_factor
        )
        d_query_low = d_query_pre.astype(jnp.bfloat16).reshape(tok_rows, local_heads * head_dim)
        d_key_low = d_key_pre.astype(jnp.bfloat16).reshape(tok_rows, local_groups * head_dim)
        d_normed_part = jnp.dot(d_query_low, query_full.T, preferred_element_type=jnp.float32)
        d_normed_part = d_normed_part + jnp.dot(
            d_key_low, key_full.T, preferred_element_type=jnp.float32
        )
        d_normed_part = d_normed_part + jnp.dot(
            d_value_low, value_full.T, preferred_element_type=jnp.float32
        )
        acc_query = acc_query + jnp.dot(normed.T, d_query_low, preferred_element_type=jnp.float32)
        acc_key = acc_key + jnp.dot(normed.T, d_key_low, preferred_element_type=jnp.float32)
        acc_value = acc_value + jnp.dot(normed.T, d_value_low, preferred_element_type=jnp.float32)
        d_normed, head_gain_parts = (
            lax.psum(d_normed_part.astype(jnp.bfloat16), "tp").astype(jnp.float32),
            lax.psum(jnp.stack([query_gain_part, key_gain_part]).astype(jnp.bfloat16), "tp").astype(
                jnp.float32
            ),
        )
        acc_head_gains = acc_head_gains + head_gain_parts
        acc_attention_gain = acc_attention_gain + jnp.sum(d_normed * input_hat, axis=0)
        input_rows.append(
            (d_resid + norm_back(d_normed, attention_gain, input_hat, attention_factor)).astype(
                jnp.bfloat16
            )
        )
    summed = (
        lax.psum_scatter(
            acc_attention_gain.astype(jnp.bfloat16), "fsdp", scatter_dimension=0, tiled=True
        ).astype(jnp.float32),
        lax.psum_scatter(
            acc_head_gains[0].astype(jnp.bfloat16), "fsdp", scatter_dimension=0, tiled=True
        ).astype(jnp.float32),
        lax.psum_scatter(
            acc_head_gains[1].astype(jnp.bfloat16), "fsdp", scatter_dimension=0, tiled=True
        ).astype(jnp.float32),
        lax.psum_scatter(
            acc_query.astype(jnp.bfloat16), "fsdp", scatter_dimension=0, tiled=True
        ).astype(jnp.float32),
        lax.psum_scatter(
            acc_key.astype(jnp.bfloat16), "fsdp", scatter_dimension=0, tiled=True
        ).astype(jnp.float32),
        lax.psum_scatter(
            acc_value.astype(jnp.bfloat16), "fsdp", scatter_dimension=0, tiled=True
        ).astype(jnp.float32),
        lax.psum_scatter(
            acc_output.astype(jnp.bfloat16), "fsdp", scatter_dimension=0, tiled=True
        ).astype(jnp.float32),
        lax.psum_scatter(
            acc_expert_gain.astype(jnp.bfloat16), "fsdp", scatter_dimension=0, tiled=True
        ).astype(jnp.float32),
        lax.psum_scatter(
            acc_router.astype(jnp.bfloat16), "fsdp", scatter_dimension=0, tiled=True
        ).astype(jnp.float32),
    )
    return (
        jnp.stack(layer_rows),
        jnp.stack(input_rows),
        summed[0],
        summed[1],
        summed[2],
        summed[3],
        summed[4],
        summed[5],
        summed[6],
        summed[7],
        summed[8],
        acc_gate,
        acc_up,
        acc_down,
    )


def small_device(
    tokens,
    cotangent,
    expert_ids,
    attention_gain,
    query_gain,
    key_gain,
    query_weight,
    key_weight,
    value_weight,
    output_weight,
    expert_gain,
    router_weight,
    gate_weight,
    up_weight,
    down_weight,
):
    count, rows, width = tokens.shape
    hd = query_gain.shape[0]
    f = lax.axis_index("fsdp")
    n_fsdp = lax.axis_size("fsdp")
    seq = rows * n_fsdp
    experts = gate_weight.shape[0]
    expert_count = experts * n_fsdp
    local = query_weight.shape[1]
    pairs = n_fsdp // count
    part = local // pairs
    piece = query_weight.shape[0]

    cosine, sine = signed_tables(seq, hd)
    inputs = tokens.astype(F32)
    input_hat, attention_factor = norm_parts(inputs)
    normed = (input_hat * attention_gain).astype(LOW)

    def give_back(grad):
        cut = lax.all_to_all(
            grad.astype(LOW).reshape(n_fsdp, piece, part), "fsdp", split_axis=0, concat_axis=0, tiled=True
        ).astype(F32)
        cut = jnp.sum(cut.reshape(count, pairs, piece, part), axis=0)
        return cut.transpose(1, 0, 2).reshape(piece, local)

    (normed_all, weights, output_pair, router_all, ids_all, grad_all, pre, qkv, prob, context, branch) = begin(
        normed,
        cotangent,
        query_weight,
        key_weight,
        value_weight,
        output_weight,
        router_weight.T,
        expert_ids.transpose(0, 2, 1),
        cosine,
        sine,
        query_gain,
        key_gain,
    )
    normed_all = normed_all[0]
    router_full = router_all.T
    ids_all = ids_all.transpose(0, 2, 1)
    resid = inputs + branch.astype(F32)
    resid_hat, expert_factor = norm_parts(resid)
    expert_in = (resid_hat * expert_gain).astype(LOW)

    expert_all = gather_rows(expert_in, True).reshape(count * seq, width)
    lanes = 128
    router_wide = jnp.pad(router_full, ((0, 0), (0, lanes - expert_count)))
    first = (f * experts).astype(jnp.int32).reshape(1)
    out_part, dx_part, dgp_part, d_gate, d_up, d_down = run_experts(
        first,
        expert_all,
        grad_all.reshape(count * seq, width),
        ids_all.reshape(count * seq, -1),
        router_wide,
        gate_weight,
        up_weight,
        down_weight,
    )
    dgp_part = dgp_part[:, :expert_count].reshape(count, seq, expert_count)
    d_gate_probs = lax.psum(
        lax.psum_scatter(dgp_part, "fsdp", scatter_dimension=1, tiled=True), "tp"
    )
    dx_sum = sum_rows(dx_part.reshape(count, seq, width), True).astype(F32)
    out_sum = sum_rows(out_part.reshape(count, seq, width), True).astype(F32)
    layer_output = (resid + out_sum).astype(LOW)

    expert_range = jnp.arange(expert_count, dtype=jnp.int32)
    named = jnp.any(expert_ids[..., None] == expert_range, axis=2)
    logits = jnp.dot(expert_in, router_full, preferred_element_type=F32)
    masked = jnp.where(named, logits, masked_score)
    terms = jnp.where(named, jnp.exp(masked - jnp.max(masked, axis=-1, keepdims=True)), 0.0)
    gate_probs = terms / jnp.sum(terms, axis=-1, keepdims=True)
    d_logits = (
        gate_probs * (d_gate_probs - jnp.sum(gate_probs * d_gate_probs, axis=-1, keepdims=True))
    ).astype(LOW)
    d_expert_in = dx_sum + lax.dot_general(
        d_logits, router_full, (((2,), (1,)), ((), ())), preferred_element_type=F32
    )
    router_part = lax.dot_general(
        expert_in, d_logits, (((0, 1), (0, 1)), ((), ())), preferred_element_type=F32
    )
    expert_gain_part = jnp.sum(d_expert_in * resid_hat, axis=(0, 1))
    out_grad = cotangent.astype(F32)
    d_resid = out_grad + norm_back(d_expert_in, expert_gain, resid_hat, expert_factor)
    d_branch = d_resid.astype(LOW)

    branch_all = gather_rows(d_branch, False)[0]
    d_context = jnp.dot(branch_all, output_pair, preferred_element_type=F32).astype(LOW)
    d_output = lax.dot_general(branch_all, context, (((0,), (0,)), ((), ())), preferred_element_type=F32)
    d_qkv, head_gains = attend_back(d_context, pre, qkv, prob, cosine, sine, query_gain, key_gain)
    d_normed_part = lax.dot_general(
        d_qkv, weights, (((1,), (1,)), ((), ())), preferred_element_type=F32
    ).astype(LOW)
    d_weights = lax.dot_general(normed_all, d_qkv, (((0,), (0,)), ((), ())), preferred_element_type=F32)
    d_normed = sum_rows(d_normed_part[None], False).astype(F32)
    attention_gain_part = jnp.sum(d_normed * input_hat, axis=(0, 1))
    input_grad = (d_resid + norm_back(d_normed, attention_gain, input_hat, attention_factor)).astype(LOW)

    head_gains = lax.psum(head_gains, "tp")

    def scattered(value):
        return lax.psum_scatter(value, "fsdp", scatter_dimension=0, tiled=True)

    d_key_value = scattered(d_weights[:, part:].astype(LOW)).astype(F32)
    return (
        layer_output,
        input_grad,
        scattered(attention_gain_part),
        scattered(head_gains[0]),
        scattered(head_gains[1]),
        give_back(d_weights[:, :part]),
        d_key_value[:, :hd],
        d_key_value[:, hd:],
        give_back(d_output),
        scattered(expert_gain_part),
        scattered(router_part),
        d_gate.reshape(gate_weight.shape),
        d_up.reshape(up_weight.shape),
        d_down.reshape(down_weight.shape),
    )


def solution(mesh):
    body = small_device if (mesh.shape["fsdp"], mesh.shape["tp"]) == (8, 4) else general_device
    return jax.shard_map(
        body,
        mesh=mesh,
        in_specs=(
            P(None, "fsdp", None),
            P(None, "fsdp", None),
            P(None, "fsdp", None),
            P(),
            P(),
            P(),
            P("fsdp", "tp"),
            P("fsdp", "tp"),
            P("fsdp", "tp"),
            P("fsdp", "tp"),
            P(),
            P("fsdp", None),
            P("fsdp", "tp", None),
            P("fsdp", "tp", None),
            P("fsdp", "tp", None),
        ),
        out_specs=(
            P(None, "fsdp", None),
            P(None, "fsdp", None),
            P("fsdp"),
            P("fsdp"),
            P("fsdp"),
            P("fsdp", "tp"),
            P("fsdp", "tp"),
            P("fsdp", "tp"),
            P("fsdp", "tp"),
            P("fsdp"),
            P("fsdp", None),
            P("fsdp", "tp", None),
            P("fsdp", "tp", None),
            P("fsdp", "tp", None),
        ),
        check_vma=False,
    )
```

```python
import functools
import math

import jax
import jax.numpy as jnp
import numpy as np
from jax import lax
from jax.experimental import pallas as pl
from jax.experimental.pallas import tpu as pltpu
from jax.sharding import PartitionSpec as P

norm_eps = 1e-06
rope_base = 1000000.0
masked_score = -1e30
MESH = pl.DeviceIdType.MESH
LOW = jnp.bfloat16
F32 = jnp.float32
VMEM_LIMIT = 60 * 2**20


def coords():
    f = lax.axis_index("fsdp")
    t = lax.axis_index("tp")
    return f // 2, f % 2, t // 2, t % 2


def place(z, x, y, c):
    return (2 * z + x, 2 * y + c)


def span(first, count):
    return pl.ds(pl.multiple_of(first, count), count)


class Here:
    def __init__(self):
        z, x, y, c = coords()
        self.z, self.x, self.y, self.c = z, x, y, c
        self.f, self.t = 2 * z + x, 2 * y + c
        self.xn, self.yn, self.cn = place(z, 1 - x, y, c), place(z, x, 1 - y, c), place(z, x, y, 1 - c)
        self.lanes = ((x, y), (1 - x, y), (x, 1 - y), (1 - x, 1 - y))

    def zd(self, d):
        return (self.z + d) % 4

    def peer(self, d, e):
        return place(self.zd(d), (self.x + e) % 2, self.y, self.c)

    def greet(self):
        barrier = pltpu.get_barrier_semaphore()
        peers = [self.peer(d, e) for d in range(4) for e in range(2) if d or e] + [self.yn, self.cn]
        for peer in peers:
            pl.semaphore_signal(barrier, inc=1, device_id=peer, device_id_type=MESH)
        pl.semaphore_wait(barrier, len(peers))


def push(src, dst, send_sem, recv_sem, device):
    copy = pltpu.make_async_remote_copy(
        src_ref=src, dst_ref=dst, send_sem=send_sem, recv_sem=recv_sem, device_id=device, device_id_type=MESH
    )
    copy.start()
    return copy


def keep(src, dst, sem):
    copy = pltpu.make_async_copy(src, dst, sem)
    copy.start()
    return copy


ORDER = (1, 3, 2)
FAR_FIRST = (2, 1, 3, 0)


class Gather:
    scratch = staticmethod(
        lambda: [pltpu.SemaphoreType.DMA((1,))]
        + [pltpu.SemaphoreType.DMA((4,))] * 10
        + [pltpu.SemaphoreType.DMA((4, 4))] * 2
    )
    slots = 13

    def __init__(self, here, whole, src, dst, sems):
        self.here, self.whole, self.src, self.dst = here, whole, src, dst
        (self.loc, self.sz, self.rz, self.sx, self.rx, self.sy, self.ry,
         self.sdx, self.rdx, self.sdy, self.rdy, self.sc, self.rc) = sems
        self.rows, self.cols = src.shape[1], src.shape[2] // 4
        self.half = self.rows // 2
        self.sends = []

    def block(self, z, x, y, c, h=None):
        first = (2 * z + x) * self.rows
        rows = span(first, self.rows) if h is None else span(first + h * self.half, self.half)
        return self.dst.at[:, rows, span((2 * y + c) * self.cols, self.cols)]

    def source(self, z_to, t, first, count):
        seqs = slice(None) if self.whole else pl.ds(z_to // 2, 1)
        return self.src.at[seqs, pl.ds(first, count), span(t * self.cols, self.cols)]

    def push(self, *args):
        self.sends.append(push(*args))

    def landed(self, ref, sem):
        pltpu.make_async_remote_copy(
            src_ref=ref, dst_ref=ref, send_sem=sem, recv_sem=sem, device_id=self.here.xn, device_id_type=MESH
        ).wait_recv()

    def start(self):
        h = self.here
        own = self.src if self.whole else self.src.at[pl.ds(h.z // 2, 1)]
        self.own = keep(own, self.dst.at[:, span(h.f * self.rows, self.rows), :], self.loc.at[0])
        for d in ORDER:
            self.push(self.source(h.zd(d), h.t, 0, self.rows), self.block(h.z, h.x, h.y, h.c),
                      self.sz.at[d], self.rz.at[h.z], h.peer(d, 0))
        self.push(self.source(h.z, h.t, 0, self.rows), self.block(h.z, h.x, h.y, h.c),
                  self.sx.at[h.z], self.rx.at[h.z], h.xn)
        self.push(self.source(h.z, 2 * (1 - h.y) + h.c, 0, self.half), self.block(h.z, h.x, 1 - h.y, h.c, 0),
                  self.sdx.at[h.z], self.rdx.at[h.z], h.xn)

    def spread(self, d):
        h, zd = self.here, self.here.zd(d)
        b = self.block(zd, h.x, h.y, h.c)
        self.landed(b, self.rz.at[zd])
        self.push(b, b, self.sx.at[zd], self.rx.at[zd], h.xn)
        self.push(b, b, self.sy.at[zd], self.ry.at[zd], h.yn)
        self.push(b, b, self.sc.at[0, zd], self.rc.at[0, zd], h.cn)

    def cross(self, d):
        h, zd = self.here, self.here.zd(d)
        b = self.block(zd, 1 - h.x, h.y, h.c)
        self.landed(b, self.rx.at[zd])
        low = self.block(zd, 1 - h.x, h.y, h.c, 1)
        self.push(low, low, self.sdy.at[zd], self.rdy.at[zd], h.yn)
        self.push(b, b, self.sc.at[1, zd], self.rc.at[1, zd], h.cn)
        if d != 0:
            b = self.block(zd, h.x, 1 - h.y, h.c)
            self.landed(b, self.ry.at[zd])
            top = self.block(zd, h.x, 1 - h.y, h.c, 0)
            self.push(top, top, self.sdx.at[zd], self.rdx.at[zd], h.xn)
            self.push(b, b, self.sc.at[2, zd], self.rc.at[2, zd], h.cn)

    def close(self, d):
        h, zd = self.here, self.here.zd(d)
        self.landed(self.block(zd, 1 - h.x, 1 - h.y, h.c, 0), self.rdx.at[zd])
        self.landed(self.block(zd, 1 - h.x, 1 - h.y, h.c, 1), self.rdy.at[zd])
        b = self.block(zd, 1 - h.x, 1 - h.y, h.c)
        self.push(b, b, self.sc.at[3, zd], self.rc.at[3, zd], h.cn)

    def arrived(self, d, e):
        h, zd = self.here, self.here.zd(d)
        if e == 0:
            if d == 0:
                self.own.wait()
            else:
                self.landed(self.block(zd, h.x, h.y, 1 - h.c), self.rc.at[0, zd])
                self.landed(self.block(zd, h.x, 1 - h.y, 1 - h.c), self.rc.at[2, zd])
        else:
            self.landed(self.block(zd, 1 - h.x, h.y, 1 - h.c), self.rc.at[1, zd])
            self.landed(self.block(zd, 1 - h.x, 1 - h.y, 1 - h.c), self.rc.at[3, zd])

    def finish(self):
        for copy in self.sends:
            copy.wait_send()


def add_into(target, *others):
    count, rows, _ = target.shape
    step = 32

    @pl.loop(0, count * rows // step)
    def _(i):
        n = i // (rows // step)
        r = pl.ds(pl.multiple_of((i % (rows // step)) * step, step), step)
        total = target[n, r, :].astype(F32)
        for other in others:
            total = total + other[n, r, :].astype(F32)
        target[n, r, :] = total.astype(target.dtype)


class Sum:
    slots = 23

    @staticmethod
    def scratch(count, rows, width, low):
        dma = pltpu.SemaphoreType.DMA
        cols = width // 4
        vm = pltpu.VMEM
        return [
            vm((4, 4, count, rows, cols), low),
            vm((4, count, rows // 2, cols), low),
            vm((4, count, rows // 2, cols), low),
            vm((4, count, rows, cols), low),
            vm((4, count, rows, cols), low),
            vm((4, count, rows, cols), low),
            vm((4, 2, rows, cols), low),
            vm((2, rows, cols), low),
            dma((4, 4)), dma((4, 4)),
        ] + [dma((4,))] * 10 + [dma((3,))] * 2 + [dma((5,))]

    def __init__(self, here, whole, part, refs):
        self.here, self.whole, self.part = here, whole, part
        (self.fc, self.f1x, self.f1y, self.f2x, self.f2y, self.fz, self.full, self.tmp, self.sc, self.rc,
         self.s1x, self.r1x, self.s1y, self.r1y, self.s2x, self.r2x, self.s2y, self.r2y, self.sz, self.rz,
         self.sg, self.rg, self.osem) = refs
        self.rows, self.cols = part.shape[1] // 8, part.shape[2] // 4
        self.top, self.low = pl.ds(0, self.rows // 2), pl.ds(self.rows // 2, self.rows // 2)
        self.sends = []

    def block(self, d, lane, c):
        x, y = self.here.lanes[lane]
        return self.part.at[:, span((2 * self.here.zd(d) + x) * self.rows, self.rows),
                            span((2 * y + c) * self.cols, self.cols)]

    def push(self, *args):
        self.sends.append(push(*args))

    def landed(self, ref, sem):
        pltpu.make_async_remote_copy(
            src_ref=ref, dst_ref=ref, send_sem=sem, recv_sem=sem, device_id=self.here.xn, device_id_type=MESH
        ).wait_recv()

    def give(self, d, e):
        for lane in ((1, 3) if e else (0, 2)):
            self.push(self.block(d, lane, 1 - self.here.c), self.fc.at[lane, d],
                      self.sc.at[lane, d], self.rc.at[lane, d], self.here.cn)

    def pair(self, lane, d):
        self.landed(self.fc.at[lane, d], self.rc.at[lane, d])
        add_into(self.block(d, lane, self.here.c), self.fc.at[lane, d])
        return self.block(d, lane, self.here.c)

    def corner(self, d):
        b = self.pair(3, d)
        self.push(b.at[:, self.top], self.f1x.at[d], self.s1x.at[d], self.r1x.at[d], self.here.xn)
        self.push(b.at[:, self.low], self.f1y.at[d], self.s1y.at[d], self.r1y.at[d], self.here.yn)

    def sides(self, d):
        b = self.pair(1, d)
        self.landed(self.f1y.at[d], self.r1y.at[d])
        add_into(b.at[:, self.low], self.f1y.at[d])
        self.push(b, self.f2x.at[d], self.s2x.at[d], self.r2x.at[d], self.here.xn)
        b = self.pair(2, d)
        self.landed(self.f1x.at[d], self.r1x.at[d])
        add_into(b.at[:, self.top], self.f1x.at[d])
        self.push(b, self.f2y.at[d], self.s2y.at[d], self.r2y.at[d], self.here.yn)

    def centre(self, d):
        b = self.pair(0, d)
        self.landed(self.f2x.at[d], self.r2x.at[d])
        self.landed(self.f2y.at[d], self.r2y.at[d])
        add_into(b, self.f2x.at[d], self.f2y.at[d])
        if d != 0:
            self.push(b, self.fz.at[(4 - d) % 4], self.sz.at[d], self.rz.at[(4 - d) % 4], self.here.peer(d, 0))

    def total(self):
        for d in (1, 2, 3):
            self.landed(self.fz.at[d], self.rz.at[d])
        b = self.block(0, 0, self.here.c)
        step = 32

        @pl.loop(0, 2 * self.rows // step)
        def _(i):
            n = i // (self.rows // step)
            r = pl.ds(pl.multiple_of((i % (self.rows // step)) * step, step), step)
            if self.whole:
                total = b[n, r, :].astype(F32)
                for d in (1, 2, 3):
                    total = total + self.fz[d, n, r, :].astype(F32)
            else:
                total = jnp.where(self.here.z // 2 == n, b[0, r, :].astype(F32), 0.0)
                for d in (1, 2, 3):
                    total = total + jnp.where(self.here.zd(d) // 2 == n, self.fz[d, 0, r, :].astype(F32), 0.0)
            self.tmp[n, r, :] = total.astype(self.tmp.dtype)

    def share(self, out):
        h = self.here
        mine = self.full.at[h.t]
        self.keeps = [keep(self.tmp, mine, self.osem.at[4])]
        self.push(self.tmp, mine, self.sg.at[0], self.rg.at[0], h.yn)
        self.push(self.tmp, mine, self.sg.at[1], self.rg.at[1], h.cn)
        ty, tc, td = 2 * (1 - h.y) + h.c, 2 * h.y + 1 - h.c, 2 * (1 - h.y) + 1 - h.c
        self.landed(self.full.at[ty], self.rg.at[0])
        self.push(self.full.at[ty], self.full.at[ty], self.sg.at[2], self.rg.at[2], h.cn)
        self.landed(self.full.at[tc], self.rg.at[1])
        self.landed(self.full.at[td], self.rg.at[2])
        self.keeps[0].wait()
        outs = [keep(self.full.at[q], out.at[:, :, pl.ds(q * self.cols, self.cols)], self.osem.at[q]) for q in range(4)]
        for copy in outs:
            copy.wait()

    def finish(self):
        for copy in self.sends:
            copy.wait_send()


def sum_kernel(whole, in_ref, out_ref, part, load, *refs):
    here = Here()
    here.greet()
    total = Sum(here, whole, part, refs)
    rows = total.rows
    copies = {}
    for e in (1, 0):
        for d in FAR_FIRST:
            at = span((2 * here.zd(d) + (here.x + e) % 2) * rows, rows)
            copies[d, e] = keep(in_ref.at[:, at, :], part.at[:, at, :], load.at[e, d])
    for e in (1, 0):
        for d in FAR_FIRST:
            copies[d, e].wait()
            total.give(d, e)
    for d in FAR_FIRST:
        total.corner(d)
    for d in FAR_FIRST:
        total.sides(d)
    for d in FAR_FIRST:
        total.centre(d)
    total.total()
    total.share(out_ref)
    total.finish()


def sum_rows(value, whole):
    count, total_rows, width = value.shape
    rows = total_rows // 8
    low = value.dtype
    return pl.pallas_call(
        functools.partial(sum_kernel, whole),
        out_shape=jax.ShapeDtypeStruct((2, rows, width), low),
        in_specs=[pl.BlockSpec(memory_space=pl.ANY)],
        out_specs=pl.BlockSpec(memory_space=pl.ANY),
        scratch_shapes=[pltpu.VMEM((count, total_rows, width), low), pltpu.SemaphoreType.DMA((2, 4))]
        + Sum.scratch(count, rows, width, low),
        compiler_params=pltpu.CompilerParams(
            collective_id=2 if whole else 3, has_side_effects=True, vmem_limit_bytes=VMEM_LIMIT
        ),
        name="sum_whole" if whole else "sum_half",
    )(value)


def gather_kernel(whole, in_ref, out_ref, *sems):
    here = Here()
    here.greet()
    rows = Gather(here, whole, in_ref, out_ref, sems)
    rows.start()
    for d in ORDER:
        rows.spread(d)
    for d in (0,) + ORDER:
        rows.cross(d)
    for d in (0,) + ORDER:
        rows.close(d)
    for d in (0,) + ORDER:
        rows.arrived(d, 0)
        rows.arrived(d, 1)
    rows.finish()


def gather_rows(value, whole):
    count, rows, width = value.shape
    return pl.pallas_call(
        functools.partial(gather_kernel, whole),
        out_shape=jax.ShapeDtypeStruct((count if whole else 1, rows * 8, width), value.dtype),
        in_specs=[pl.BlockSpec(memory_space=pl.ANY)],
        out_specs=pl.BlockSpec(memory_space=pl.ANY),
        scratch_shapes=Gather.scratch(),
        compiler_params=pltpu.CompilerParams(collective_id=0 if whole else 1, has_side_effects=True),
        name="gather_whole" if whole else "gather_half",
    )(value)


def signed_tables(length, width):
    middle = width // 2
    frequency = rope_base ** (-np.arange(middle) * 2.0 / width)
    angles = np.arange(length)[:, None] * frequency[None, :]
    cosine, sine = np.cos(angles), np.sin(angles)
    return (
        jnp.asarray(np.concatenate([cosine, cosine], axis=1), F32),
        jnp.asarray(np.concatenate([-sine, sine], axis=1), F32),
    )


def dot_nn(a, b):
    return jnp.dot(a, b, preferred_element_type=F32)


def dot_nt(a, b):
    return lax.dot_general(a, b, (((1,), (1,)), ((), ())), preferred_element_type=F32)


def dot_tn(a, b):
    return lax.dot_general(a, b, (((0,), (0,)), ((), ())), preferred_element_type=F32)


def route_probs(logits, ids, count):
    lane = lax.broadcasted_iota(jnp.int32, logits.shape, 1)
    named = lane == ids[:, 0:1]
    for k in range(1, count):
        named = named | (lane == ids[:, k : k + 1])
    masked = jnp.where(named, logits, masked_score)
    terms = jnp.where(named, jnp.exp(masked - jnp.max(masked, axis=-1, keepdims=True)), 0.0)
    return terms / jnp.sum(terms, axis=-1, keepdims=True)


def experts_kernel(experts, route_count, first_ref, x_ref, og_ref, ids_ref, router_ref, g_ref, u_ref, d_ref,
                   out_ref, dx_ref, dgp_ref, dg_ref, du_ref, dd_ref, dg_s, du_s, dd_s, sem):
    i = pl.program_id(0)
    hidden = g_ref.shape[0]
    per = hidden // experts
    tile = x_ref.shape[0]

    @pl.when(i == 0)
    def _():
        dg_s[...] = jnp.zeros_like(dg_s)
        du_s[...] = jnp.zeros_like(du_s)
        dd_s[...] = jnp.zeros_like(dd_s)

    x = x_ref[...]
    og = og_ref[...]
    first = first_ref[0]
    probs = route_probs(dot_nn(x, router_ref[...]), ids_ref[...], route_count)
    lanes = probs.shape[1]
    row = lax.broadcasted_iota(jnp.int32, (lanes, hidden), 0)
    col = lax.broadcasted_iota(jnp.int32, (lanes, hidden), 1)
    spread = jnp.where(row == first + col // per, 1.0, 0.0).astype(LOW)
    high = probs.astype(LOW)
    rest = (probs - high.astype(F32)).astype(LOW)
    share = dot_nn(high, spread) + dot_nn(rest, spread)
    gate = dot_nt(x, g_ref[...])
    up = dot_nt(x, u_ref[...])
    raw = dot_nt(og, d_ref[...])
    sig = 1.0 / (1.0 + jnp.exp(-gate))
    act = gate * sig
    inner = act * up
    weighted = (inner * share).astype(LOW)
    product = jnp.where(share > 0.0, inner * raw, 0.0)
    product_high = product.astype(LOW)
    product_rest = (product - product_high.astype(F32)).astype(LOW)
    dgp_ref[...] = dot_nt(product_high, spread) + dot_nt(product_rest, spread)
    d_inner = raw * share
    d_up = (d_inner * act).astype(LOW)
    d_gate = (d_inner * up * sig * (1.0 + gate * (1.0 - sig))).astype(LOW)
    dx_ref[...] = (dot_nn(d_gate, g_ref[...]) + dot_nn(d_up, u_ref[...])).astype(LOW)
    out_ref[...] = dot_nn(weighted, d_ref[...]).astype(LOW)
    dg_s[...] += dot_tn(d_gate, x)
    du_s[...] += dot_tn(d_up, x)
    dd_s[...] += dot_tn(weighted, og)

    @pl.when(i == pl.num_programs(0) - 1)
    def _():
        copies = []
        for n, (src, dst) in enumerate(((dg_s, dg_ref), (du_s, du_ref), (dd_s, dd_ref))):
            copies.append(pltpu.make_async_copy(src, dst, sem.at[n]))
            copies[-1].start()
        for copy in copies:
            copy.wait()


def run_experts(first, x, og, ids, router, gate, up, down):
    tokens, width = x.shape
    experts, per, _ = gate.shape
    hidden = experts * per
    tile = 256
    lanes = router.shape[1]
    once = pl.Buffered(1)
    keep = lambda i, s: (0, 0)
    walk = lambda i, s: (i, 0)
    any_space = pl.BlockSpec(memory_space=pl.ANY)
    grads = jax.ShapeDtypeStruct((hidden, width), F32)
    return pl.pallas_call(
        functools.partial(experts_kernel, experts, ids.shape[1]),
        grid_spec=pltpu.PrefetchScalarGridSpec(
            num_scalar_prefetch=1,
            grid=(tokens // tile,),
            in_specs=[
                pl.BlockSpec((tile, width), walk),
                pl.BlockSpec((tile, width), walk),
                pl.BlockSpec((tile, ids.shape[1]), walk),
                pl.BlockSpec((width, lanes), keep, pipeline_mode=once),
                pl.BlockSpec((hidden, width), keep, pipeline_mode=once),
                pl.BlockSpec((hidden, width), keep, pipeline_mode=once),
                pl.BlockSpec((hidden, width), keep, pipeline_mode=once),
            ],
            out_specs=[
                pl.BlockSpec((tile, width), walk),
                pl.BlockSpec((tile, width), walk),
                pl.BlockSpec((tile, lanes), walk),
                any_space,
                any_space,
                any_space,
            ],
            scratch_shapes=[pltpu.VMEM((hidden, width), F32)] * 3 + [pltpu.SemaphoreType.DMA((3,))],
        ),
        out_shape=(
            jax.ShapeDtypeStruct((tokens, width), LOW),
            jax.ShapeDtypeStruct((tokens, width), LOW),
            jax.ShapeDtypeStruct((tokens, lanes), F32),
            grads,
            grads,
            grads,
        ),
        compiler_params=pltpu.CompilerParams(
            vmem_limit_bytes=VMEM_LIMIT, dimension_semantics=("arbitrary",)
        ),
        name="experts",
    )(first, x, og, ids, router, gate.reshape(hidden, width), up.reshape(hidden, width), down.reshape(hidden, width))


class Weights:
    scratch = staticmethod(lambda: [pltpu.SemaphoreType.DMA((8, 4, 2))] * 4 + [pltpu.SemaphoreType.DMA((6,))])
    slots = 5

    def __init__(self, here, query, key, value, output, router, ids, w, wo, router_all, ids_all, sems):
        self.here = here
        self.query, self.output, self.w, self.wo = query, output, w, wo
        piece, part = query.shape[0], wo.shape[1]
        self.piece, self.part = piece, part
        hd = key.shape[1]
        self.shared = (
            (key, lambda f: w.at[span(f * piece, piece), pl.ds(part, hd)]),
            (value, lambda f: w.at[span(f * piece, piece), pl.ds(part + hd, hd)]),
            (router, lambda f: router_all.at[:, span(f * piece, piece)]),
            (ids, lambda f: ids_all.at[:, :, span(f * ids.shape[2], ids.shape[2])]),
        )
        self.qs, self.qr, self.ss, self.sr, self.loc = sems
        self.sends, self.keeps = [], []

    def landed(self, ref, sem):
        pltpu.make_async_remote_copy(
            src_ref=ref, dst_ref=ref, send_sem=sem, recv_sem=sem, device_id=self.here.xn, device_id_type=MESH
        ).wait_recv()

    def start_shared(self):
        h = self.here
        for n, (src, dst) in enumerate(self.shared):
            self.keeps.append(keep(src, dst(h.f), self.loc.at[n]))
            for d, e in ((2, 0), (1, 0), (3, 0), (0, 1)):
                self.sends.append(push(src, dst(h.f), self.ss.at[n, d, e], self.sr.at[n, (4 - d) % 4, e], h.peer(d, e)))

    def pass_shared(self, d):
        h = self.here
        for n, (_, dst) in enumerate(self.shared):
            ref = dst(2 * h.zd(d) + h.x)
            self.landed(ref, self.sr.at[n, d, 0])
            self.sends.append(push(ref, ref, self.ss.at[n, d, 1], self.sr.at[n, d, 1], h.xn))

    def wait_shared(self):
        h = self.here
        for n, (_, dst) in enumerate(self.shared):
            for d in range(4):
                self.landed(dst(2 * h.zd(d) + 1 - h.x), self.sr.at[n, d, 1])

    def start_pairs(self, n):
        h = self.here
        src, dst = ((self.query, self.w), (self.output, self.wo))[n]
        mine = lambda f: dst.at[span(f * self.piece, self.piece), pl.ds(0, self.part)]
        self.keeps.append(keep(src.at[:, span((h.f % 4) * self.part, self.part)], mine(h.f), self.loc.at[4 + n]))
        for d in FAR_FIRST:
            for e in (1, 0):
                if d or e:
                    f = 2 * h.zd(d) + (h.x + e) % 2
                    self.sends.append(push(src.at[:, span((f % 4) * self.part, self.part)], mine(h.f),
                                           self.qs.at[n, d, e], self.qr.at[n, (4 - d) % 4, e], h.peer(d, e)))

    def wait_pairs(self, n):
        h = self.here
        dst = (self.w, self.wo)[n]
        for d in range(4):
            for e in (1, 0):
                if d or e:
                    f = 2 * h.zd(d) + (h.x + e) % 2
                    self.landed(dst.at[span(f * self.piece, self.piece), pl.ds(0, self.part)], self.qr.at[n, d, e])

    def finish(self):
        for copy in self.sends:
            copy.wait_send()


def begin_kernel(heads, normed, cot, query, key, value, output, router, ids, cos_ref, sin_ref, qg_ref, kg_ref,
                 xn_out, w_out, wo_out, router_out, ids_out, cot_out, pre_out, qkv_out, prob_out, ctx_out, branch_out,
                 xn, w, wo, pre, qkv, prob, ctx, part, osem, *sems):
    here = Here()
    here.greet()
    at = 0
    x_rows = Gather(here, False, normed, xn, sems[at : at + Gather.slots])
    at += Gather.slots
    c_rows = Gather(here, True, cot, cot_out, sems[at : at + Gather.slots])
    at += Gather.slots
    moved = Weights(here, query, key, value, output, router, ids, w, wo, router_out, ids_out, sems[at : at + Weights.slots])
    at += Weights.slots
    total = Sum(here, False, part, sems[at:])

    x_rows.start()
    moved.start_shared()
    moved.start_pairs(0)
    for d in ORDER:
        x_rows.spread(d)
        moved.pass_shared(d)
    for d in (0,) + ORDER:
        x_rows.cross(d)
    for d in (0,) + ORDER:
        x_rows.close(d)
    for d in (0,) + ORDER:
        x_rows.arrived(d, 0)
        x_rows.arrived(d, 1)
    moved.wait_shared()
    moved.wait_pairs(0)
    for copy in moved.keeps:
        copy.wait()
    c_rows.start()
    moved.keeps = []
    moved.start_pairs(1)
    outs = [keep(xn, xn_out, osem.at[0]), keep(w, w_out, osem.at[1])]

    seq = xn.shape[1]
    hd = cos_ref.shape[1]
    tile = 256
    scale = 1.0 / math.sqrt(hd)
    for i in range(seq // tile):
        r = pl.ds(i * tile, tile)
        got = dot_nn(xn[0, r, :], w[...])
        pre[r, :] = got[:, : (heads + 1) * hd]
        qkv[r, pl.ds((heads + 1) * hd, hd)] = got[:, (heads + 1) * hd :].astype(LOW)
        for a in range(heads + 1):
            one = got[:, a * hd : (a + 1) * hd]
            factor = lax.rsqrt(jnp.mean(one * one, axis=-1, keepdims=True) + norm_eps)
            gained = one * factor * (qg_ref if a < heads else kg_ref)[...]
            turned = gained * cos_ref[r, :] + pltpu.roll(gained, hd // 2, 1) * sin_ref[r, :]
            qkv[r, pl.ds(a * hd, hd)] = turned.astype(LOW)
    outs += [keep(pre, pre_out, osem.at[2]), keep(qkv, qkv_out, osem.at[3])]
    for d in ORDER:
        c_rows.spread(d)
    for a in range(heads):
        for i in range(seq // tile):
            r = pl.ds(i * tile, tile)
            n = (i + 1) * tile
            score = dot_nt(qkv[r, pl.ds(a * hd, hd)], qkv[pl.ds(0, n), pl.ds(heads * hd, hd)]) * scale
            row = lax.broadcasted_iota(jnp.int32, (tile, n), 0) + i * tile
            col = lax.broadcasted_iota(jnp.int32, (tile, n), 1)
            score = jnp.where(col <= row, score, masked_score)
            terms = jnp.exp(score - jnp.max(score, axis=-1, keepdims=True))
            low = (terms * (1.0 / jnp.sum(terms, axis=-1, keepdims=True))).astype(LOW)
            prob[a, r, pl.ds(0, n)] = low
            ctx[r, pl.ds(a * hd, hd)] = dot_nn(low, qkv[pl.ds(0, n), pl.ds((heads + 1) * hd, hd)]).astype(LOW)
        if a == 0:
            for d in (0,) + ORDER:
                c_rows.cross(d)
    outs += [keep(prob, prob_out, osem.at[4]), keep(ctx, ctx_out, osem.at[5])]
    moved.wait_pairs(1)
    for copy in moved.keeps:
        copy.wait()
    outs.append(keep(wo, wo_out, osem.at[6]))
    rows = total.rows
    for e in (1, 0):
        for d in FAR_FIRST:
            at_f = span((2 * here.zd(d) + (here.x + e) % 2) * rows, rows)
            part[0, at_f, :] = dot_nt(ctx[at_f, :], wo[...]).astype(LOW)
            total.give(d, e)
    for d in FAR_FIRST:
        total.corner(d)
    for d in (0,) + ORDER:
        c_rows.close(d)
    for d in FAR_FIRST:
        total.sides(d)
    for d in FAR_FIRST:
        total.centre(d)
    total.total()
    total.share(branch_out)
    for d in (0,) + ORDER:
        c_rows.arrived(d, 0)
        c_rows.arrived(d, 1)
    for each in (x_rows, c_rows, moved, total):
        each.finish()
    for copy in outs:
        copy.wait()


def begin(normed, cot, query, key, value, output, router, ids, cosine, sine, query_gain, key_gain):
    count, rows, width = normed.shape
    seq = rows * 8
    hd = query_gain.shape[0]
    part = query.shape[1] // 4
    heads = part // hd
    vm = pltpu.VMEM
    hbm = pl.BlockSpec(memory_space=pl.ANY)
    near = pl.BlockSpec(memory_space=pltpu.VMEM)
    shape = jax.ShapeDtypeStruct
    local = [
        ((1, seq, width), LOW),
        ((width, part + 2 * hd), LOW),
        ((width, part), LOW),
        ((seq, (heads + 1) * hd), F32),
        ((seq, (heads + 2) * hd), LOW),
        ((heads, seq, seq), LOW),
        ((seq, heads * hd), LOW),
    ]
    return pl.pallas_call(
        functools.partial(begin_kernel, heads),
        out_shape=(
            shape(*local[0]),
            shape(*local[1]),
            shape(*local[2]),
            shape((router.shape[0], width), LOW),
            shape((count, ids.shape[1], seq), jnp.int32),
            shape((count, seq, width), LOW),
            shape(*local[3]),
            shape(*local[4]),
            shape(*local[5]),
            shape(*local[6]),
            shape((count, rows, width), LOW),
        ),
        in_specs=[hbm] * 8 + [near] * 4,
        out_specs=[hbm] * 11,
        scratch_shapes=[vm(*entry) for entry in local]
        + [vm((1, seq, width), LOW), pltpu.SemaphoreType.DMA((7,))]
        + Gather.scratch() + Gather.scratch() + Weights.scratch() + Sum.scratch(1, rows, width, LOW),
        compiler_params=pltpu.CompilerParams(
            collective_id=4, has_side_effects=True, vmem_limit_bytes=VMEM_LIMIT
        ),
        name="begin",
    )(normed, cot, query, key, value, output, router, ids, cosine, sine, query_gain[None], key_gain[None])


def wait_for(ref, sem, device):
    pltpu.make_async_remote_copy(
        src_ref=ref, dst_ref=ref, send_sem=sem, recv_sem=sem, device_id=device, device_id_type=MESH
    ).wait_recv()


PEERS = tuple((d, e) for d in FAR_FIRST for e in (1, 0) if d or e)


def end_kernel(heads, d_branch, xn_in, w_in, wo_in, pre_in, qkv_in, prob_in, ctx_in, out_in, aux, query, key, value,
               cos_ref, sin_ref, qg_ref, kg_ref,
               out_sum, dn_sum, dq_out, dk_out, dv_out, do_out, aux_out, gains_out,
               db, xn, w, wo, pre, qkv, prob, ctx, dctx, dq_s, dk_s, dv_s, dqkv, dwo, dw, dwo_got, dwq_got, kv_x, kv_z,
               aux_got, head_part, head_got, line, line_c, line_y, wide_q, wide_o, wide_kv, out_part,
               lsem, psem, rsem, kxs, kxr, kzs, kzr, tsem, usem, osem, *rest):
    here = Here()
    here.greet()
    sends, outs = [], []
    rows_db = Gather(here, False, d_branch, db, rest[: Gather.slots])
    at = Gather.slots
    out = Sum(here, True, out_part, rest[at : at + Sum.slots])
    dn = Sum(here, False, db, rest[at + Sum.slots :])
    rows = out.rows
    piece, part = query.shape[0], wo.shape[1]
    seq = xn.shape[1]
    hd = cos_ref.shape[1]
    tile = 256
    scale = 1.0 / math.sqrt(hd)

    def number(d, e):
        return 2 * here.zd(d) + (here.x + e) % 2

    def send(n, d, e, src, got):
        sends.append(push(src, got.at[(4 - d) % 4, e], psem.at[n, d, e], rsem.at[n, (4 - d) % 4, e], here.peer(d, e)))

    def got_from(n, d, e, got):
        wait_for(got.at[d, e], rsem.at[n, d, e], here.xn)
        return got[d, e]

    rows_db.start()
    loads = {}
    for n, (src, dst) in enumerate(((wo_in, wo), (ctx_in, ctx), (qkv_in, qkv), (prob_in, prob), (pre_in, pre),
                                    (xn_in, xn), (w_in, w))):
        loads[n] = keep(src, dst, lsem.at[n])
    tiles = {}
    for n, (e, d) in enumerate((e, d) for e in (1, 0) for d in FAR_FIRST):
        at_f = span(number(d, e) * rows, rows)
        tiles[d, e] = keep(out_in.at[:, at_f, :], out_part.at[:, at_f, :], lsem.at[7 + n])
    for d, e in PEERS:
        send(0, d, e, aux.at[number(d, e)], aux_got)
    for e in (1, 0):
        for d in FAR_FIRST:
            tiles[d, e].wait()
            out.give(d, e)
    for d in ORDER:
        rows_db.spread(d)
    for d in (0,) + ORDER:
        rows_db.cross(d)
    for d in (0,) + ORDER:
        rows_db.close(d)
    for d in FAR_FIRST:
        out.corner(d)
    for d in (0,) + ORDER:
        rows_db.arrived(d, 0)
        rows_db.arrived(d, 1)
    for n in range(7):
        loads[n].wait()

    for i in range(seq // tile):
        r = pl.ds(i * tile, tile)
        dctx[r, :] = dot_nn(db[0, r, :], wo[...]).astype(LOW)
    for d, e in PEERS + ((0, 0),):
        r = span(number(d, e) * piece, piece)
        dwo[r, :] = dot_tn(db[0, :, r], ctx[...]).astype(LOW)
        if d or e:
            send(1, d, e, dwo.at[r, :], dwo_got)
    dk_s[...] = jnp.zeros_like(dk_s)
    dv_s[...] = jnp.zeros_like(dv_s)
    for a in range(heads):
        for i in range(seq // tile):
            r = pl.ds(i * tile, tile)
            n = (i + 1) * tile
            q_tile = qkv[r, pl.ds(a * hd, hd)]
            k_rows = qkv[pl.ds(0, n), pl.ds(heads * hd, hd)]
            v_rows = qkv[pl.ds(0, n), pl.ds((heads + 1) * hd, hd)]
            up = dctx[r, pl.ds(a * hd, hd)]
            low = prob[a, r, pl.ds(0, n)]
            wide = low.astype(F32)
            dprob = dot_nt(up, v_rows)
            delta = jnp.sum(wide * dprob, axis=-1, keepdims=True)
            dscore = (wide * (dprob - delta)).astype(LOW)
            dq_s[r, pl.ds(a * hd, hd)] = dot_nn(dscore, k_rows) * scale
            dk_s[pl.ds(0, n), :] += dot_tn(dscore, q_tile) * scale
            dv_s[pl.ds(0, n), :] += dot_tn(low, up)
        for d in FAR_FIRST[2 * a : 2 * a + 2]:
            out.sides(d)
    gq = jnp.zeros((1, hd), F32)
    gk = jnp.zeros((1, hd), F32)
    for i in range(seq // tile):
        r = pl.ds(i * tile, tile)
        dqkv[r, pl.ds((heads + 1) * hd, hd)] = dv_s[r, :].astype(LOW)
        for a in range(heads + 1):
            up = dq_s[r, pl.ds(a * hd, hd)] if a < heads else dk_s[r, :]
            one = pre[r, pl.ds(a * hd, hd)]
            factor = lax.rsqrt(jnp.mean(one * one, axis=-1, keepdims=True) + norm_eps)
            hat = one * factor
            turned = up * cos_ref[r, :] + pltpu.roll(up * sin_ref[r, :], hd // 2, 1)
            gain_part = jnp.sum(turned * hat, axis=0, keepdims=True)
            gained = turned * (qg_ref if a < heads else kg_ref)[...]
            back = factor * (gained - hat * jnp.mean(gained * hat, axis=-1, keepdims=True))
            dqkv[r, pl.ds(a * hd, hd)] = back.astype(LOW)
            if a < heads:
                gq = gq + gain_part
            else:
                gk = gk + gain_part
    head_part[...] = jnp.concatenate([gq, gk, jnp.zeros((6, hd), F32)], axis=0)
    for d, e in PEERS:
        send(3, d, e, head_part, head_got)
    for d, e in PEERS + ((0, 0),):
        r = span(number(d, e) * piece, piece)
        dw[r, :] = dot_tn(xn[0, :, r], dqkv[...]).astype(LOW)
        if d or e:
            send(2, d, e, dw.at[r, pl.ds(0, part)], dwq_got)
        if e:
            sends.append(push(dw.at[r, pl.ds(part, 2 * hd)], kv_x.at[d], kxs.at[d], kxr.at[d], here.xn))
    rows_db.finish()
    for e in (1, 0):
        for d in FAR_FIRST:
            r = span(number(d, e) * rows, rows)
            db[0, r, :] = dot_nt(dqkv[r, :], w[...]).astype(LOW)
            dn.give(d, e)
    for d in FAR_FIRST:
        dn.corner(d)
    for d in FAR_FIRST:
        out.centre(d)
    for d in FAR_FIRST:
        r = span(number(d, 0) * piece, piece)
        wait_for(kv_x.at[d], kxr.at[d], here.xn)
        both = dw[r, pl.ds(part, 2 * hd)].astype(F32) + kv_x[d].astype(F32)
        dw[r, pl.ds(part, 2 * hd)] = both.astype(LOW)
        if d:
            there = (4 - d) % 4
            sends.append(push(dw.at[r, pl.ds(part, 2 * hd)], kv_z.at[there], kzs.at[d], kzr.at[there], here.peer(d, 0)))
    for d in FAR_FIRST:
        dn.sides(d)
    out.total()
    out.share(out_sum)
    for d in FAR_FIRST:
        dn.centre(d)

    def merged(n, wide, got, mine):
        for d in (0, 1):
            for e in (0, 1):
                first = mine if (d, e) == (0, 0) else got_from(n, d, e, got)
                both = first.astype(F32) + got_from(n, d + 2, e, got).astype(F32)
                wide[:, span((number(d, e) % 4) * part, part)] = both

    own = span(here.f * piece, piece)
    merged(1, wide_o, dwo_got, dwo[own, :])
    outs.append(keep(wide_o, do_out, osem.at[0]))
    aux_total = aux[here.f].astype(F32)
    for d, e in PEERS:
        aux_total = aux_total + got_from(0, d, e, aux_got).astype(F32)
    aux_out[...] = aux_total
    head_total = head_part[...]
    for d, e in PEERS:
        head_total = head_total + got_from(3, d, e, head_got)
    line[:, pl.ds(piece, hd)] = head_total
    dn.total()
    dn.share(dn_sum)
    merged(2, wide_q, dwq_got, dw[own, pl.ds(0, part)])
    outs.append(keep(wide_q, dq_out, osem.at[1]))
    kv = dw[own, pl.ds(part, 2 * hd)].astype(F32)
    for d in (1, 2, 3):
        wait_for(kv_z.at[d], kzr.at[d], here.xn)
        kv = kv + kv_z[d].astype(F32)
    wide_kv[...] = kv
    outs.append(keep(wide_kv.at[:, pl.ds(0, hd)], dk_out, osem.at[2]))
    outs.append(keep(wide_kv.at[:, pl.ds(hd, hd)], dv_out, osem.at[3]))

    def row_sums(product):
        high = product.astype(LOW)
        rest_ = (product - high.astype(F32)).astype(LOW)
        ones = jnp.ones((8, product.shape[1]), LOW)
        return dot_nt(ones, high) + dot_nt(ones, rest_)

    line[:, pl.ds(0, piece)] = (
        row_sums(query[...].astype(F32) * wide_q[...])
        + row_sums(key[...].astype(F32) * kv[:, :hd])
        + row_sums(value[...].astype(F32) * kv[:, hd:])
    )
    first = push(line, line_c, tsem.at[0], usem.at[0], here.cn)
    wait_for(line_c, usem.at[0], here.cn)
    first.wait_send()
    line[...] = line[...] + line_c[...]
    second = push(line, line_y, tsem.at[1], usem.at[1], here.yn)
    wait_for(line_y, usem.at[1], here.yn)
    gains_out[...] = line[...] + line_y[...]
    second.wait_send()
    for each in (out, dn):
        each.finish()
    for copy in sends:
        copy.wait_send()
    for copy in outs:
        copy.wait()


def end(d_branch, xn, w, wo, pre, qkv, prob, ctx, out_part, aux, query, key, value, cosine, sine, query_gain, key_gain):
    count, rows, width = d_branch.shape
    seq = rows * 8
    hd = query_gain.shape[0]
    piece, local = query.shape
    part = local // 4
    heads = part // hd
    vm = pltpu.VMEM
    dma = pltpu.SemaphoreType.DMA
    hbm = pl.BlockSpec(memory_space=pl.ANY)
    near = pl.BlockSpec(memory_space=pltpu.VMEM)
    shape = jax.ShapeDtypeStruct
    return pl.pallas_call(
        functools.partial(end_kernel, heads),
        out_shape=(
            shape((count, rows, width), LOW),
            shape((count, rows, width), LOW),
            shape((piece, local), F32),
            shape((piece, hd), F32),
            shape((piece, hd), F32),
            shape((piece, local), F32),
            shape(aux.shape[1:], F32),
            shape((8, piece + hd), F32),
        ),
        in_specs=[hbm] * 9 + [near] * 8,
        out_specs=[hbm] * 6 + [near] * 2,
        scratch_shapes=[
            vm((1, seq, width), LOW),
            vm((1, seq, width), LOW),
            vm(w.shape, LOW),
            vm(wo.shape, LOW),
            vm(pre.shape, F32),
            vm(qkv.shape, LOW),
            vm(prob.shape, LOW),
            vm(ctx.shape, LOW),
            vm(ctx.shape, LOW),
            vm((seq, heads * hd), F32),
            vm((seq, hd), F32),
            vm((seq, hd), F32),
            vm((seq, (heads + 2) * hd), LOW),
            vm((width, part), LOW),
            vm((width, part + 2 * hd), LOW),
            vm((4, 2, piece, part), LOW),
            vm((4, 2, piece, part), LOW),
            vm((4, piece, 2 * hd), LOW),
            vm((4, piece, 2 * hd), LOW),
            vm((4, 2) + aux.shape[1:], LOW),
            vm((8, hd), F32),
            vm((4, 2, 8, hd), F32),
            vm((8, piece + hd), F32),
            vm((8, piece + hd), F32),
            vm((8, piece + hd), F32),
            vm((piece, local), F32),
            vm((piece, local), F32),
            vm((piece, 2 * hd), F32),
            vm((count, seq, width), LOW),
            dma((15,)),
            dma((4, 4, 2)),
            dma((4, 4, 2)),
            dma((4,)),
            dma((4,)),
            dma((4,)),
            dma((4,)),
            dma((2,)),
            dma((2,)),
            dma((4,)),
        ]
        + Gather.scratch()
        + Sum.scratch(count, rows, width, LOW)
        + Sum.scratch(1, rows, width, LOW),
        compiler_params=pltpu.CompilerParams(
            collective_id=5, has_side_effects=True, vmem_limit_bytes=VMEM_LIMIT
        ),
        name="end",
    )(d_branch, xn, w, wo, pre, qkv, prob, ctx, out_part, aux, query, key, value, cosine, sine,
      query_gain[None], key_gain[None])


def rotate_half(values):
    middle = values.shape[-1] // 2
    return jnp.concatenate([-values[..., middle:], values[..., :middle]], axis=-1)


def rope_tables(positions, head_width):
    middle = head_width // 2
    frequency = rope_base ** (-jnp.arange(middle, dtype=jnp.float32) * 2.0 / head_width)
    angles = positions.astype(jnp.float32)[:, None] * frequency[None, :]
    angles = jnp.concatenate([angles, angles], axis=1)
    return (jnp.cos(angles), jnp.sin(angles))


def norm_parts(values):
    factor = lax.rsqrt(jnp.mean(values * values, axis=-1, keepdims=True) + norm_eps)
    return (values * factor, factor)


def norm_back(upstream, gain, normal, factor):
    scaled = upstream * gain
    return factor * (scaled - normal * jnp.mean(scaled * normal, axis=-1, keepdims=True))


def head_back(upstream, cosine_heads, sine_heads, gain, normal, factor):
    turned = upstream * cosine_heads - rotate_half(upstream * sine_heads)
    gain_part = jnp.sum(turned * normal, axis=(0, 1))
    return (norm_back(turned, gain, normal, factor), gain_part)


def fetch_weights(query_weight, key_weight, value_weight, output_weight, router_weight):
    return (
        lax.all_gather(query_weight, "fsdp", axis=0, tiled=True),
        lax.all_gather(key_weight, "fsdp", axis=0, tiled=True),
        lax.all_gather(value_weight, "fsdp", axis=0, tiled=True),
        lax.all_gather(output_weight, "fsdp", axis=0, tiled=True),
        lax.all_gather(router_weight, "fsdp", axis=0, tiled=True),
    )


def widen(summed):
    return lax.all_gather(summed, "tp", axis=3, tiled=True)


def carry_back(summed):
    return lax.all_to_all(summed, "fsdp", split_axis=0, concat_axis=0, tiled=True)


def send_home(summed):
    arrived_home = carry_back(widen(summed))
    return arrived_home


def general_device(
    tokens,
    cotangent,
    expert_ids,
    attention_gain,
    query_gain,
    key_gain,
    query_weight,
    key_weight,
    value_weight,
    output_weight,
    expert_gain,
    router_weight,
    gate_weight,
    up_weight,
    down_weight,
):
    micro_count = tokens.shape[0]
    tok_rows = tokens.shape[1]
    width = tokens.shape[2]
    route_count = expert_ids.shape[2]
    head_dim = query_gain.shape[0]
    local_heads = query_weight.shape[1] // head_dim
    local_groups = key_weight.shape[1] // head_dim
    group_size = local_heads // local_groups
    fsdp_count = lax.axis_size("fsdp")
    seq_len = tok_rows * fsdp_count
    experts_here = gate_weight.shape[0]
    expert_count = experts_here * fsdp_count
    capacity = max(2, 5 * tok_rows * route_count // (4 * expert_count))
    key_block = math.gcd(seq_len, 512)
    score_scale = 1.0 / math.sqrt(head_dim)
    query_count = tok_rows * group_size
    routed_total = tok_rows * route_count
    start_row = lax.axis_index("fsdp") * tok_rows
    positions = start_row + jnp.arange(tok_rows, dtype=jnp.int32)
    cosine_table, sine_table = rope_tables(positions, head_dim)
    cosine_heads = cosine_table[:, None, :]
    sine_heads = sine_table[:, None, :]
    query_pos = start_row + jnp.arange(query_count, dtype=jnp.int32) // group_size
    block_total = (start_row + tok_rows + key_block - 1) // key_block
    expert_range = jnp.arange(expert_count, dtype=jnp.int32)
    zero_row = jnp.zeros((1, width), jnp.bfloat16)

    def to_rows(tensor):
        return (
            tensor.reshape(tok_rows, local_groups, group_size, head_dim)
            .transpose(1, 0, 2, 3)
            .reshape(local_groups, query_count, head_dim)
        )

    def from_rows(tensor):
        return (
            tensor.reshape(local_groups, tok_rows, group_size, head_dim)
            .transpose(1, 0, 2, 3)
            .reshape(tok_rows, local_heads, head_dim)
        )

    acc_attention_gain = jnp.zeros((width,), jnp.float32)
    acc_head_gains = jnp.zeros((2, head_dim), jnp.float32)
    acc_query = jnp.zeros((width, local_heads * head_dim), jnp.float32)
    acc_key = jnp.zeros((width, local_groups * head_dim), jnp.float32)
    acc_value = jnp.zeros((width, local_groups * head_dim), jnp.float32)
    acc_output = jnp.zeros((width, local_heads * head_dim), jnp.float32)
    acc_expert_gain = jnp.zeros((width,), jnp.float32)
    acc_router = jnp.zeros((width, expert_count), jnp.float32)
    acc_gate = jnp.zeros(gate_weight.shape, jnp.float32)
    acc_up = jnp.zeros(up_weight.shape, jnp.float32)
    acc_down = jnp.zeros(down_weight.shape, jnp.float32)
    layer_rows = []
    input_rows = []
    for micro_index in range(micro_count):
        inputs = tokens[micro_index].astype(jnp.float32)
        query_full, key_full, value_full, output_full, router_full = fetch_weights(
            query_weight, key_weight, value_weight, output_weight, router_weight
        )
        input_hat, attention_factor = norm_parts(inputs)
        normed = (input_hat * attention_gain).astype(jnp.bfloat16)
        query_pre = jnp.dot(normed, query_full, preferred_element_type=jnp.float32).reshape(
            tok_rows, local_heads, head_dim
        )
        key_pre = jnp.dot(normed, key_full, preferred_element_type=jnp.float32).reshape(
            tok_rows, local_groups, head_dim
        )
        value_low = jnp.dot(normed, value_full, preferred_element_type=jnp.float32).astype(
            jnp.bfloat16
        )
        query_hat, query_factor = norm_parts(query_pre)
        key_hat, key_factor = norm_parts(key_pre)
        query_scaled = query_hat * query_gain
        key_scaled = key_hat * key_gain
        query_low = (query_scaled * cosine_heads + rotate_half(query_scaled) * sine_heads).astype(
            jnp.bfloat16
        )
        key_low = (key_scaled * cosine_heads + rotate_half(key_scaled) * sine_heads).astype(
            jnp.bfloat16
        )
        key_all, value_all = (
            lax.all_gather(
                key_low.reshape(tok_rows, local_groups * head_dim), "fsdp", axis=0, tiled=True
            ),
            lax.all_gather(value_low, "fsdp", axis=0, tiled=True),
        )
        key_heads = key_all.reshape(seq_len, local_groups, head_dim).transpose(1, 0, 2)
        value_heads = value_all.reshape(seq_len, local_groups, head_dim).transpose(1, 0, 2)
        query_rows = to_rows(query_low)

        def scores_at(block_index):
            block_start = block_index * key_block
            key_slice = lax.dynamic_slice_in_dim(key_heads, block_start, key_block, 1)
            raw_scores = (
                jnp.einsum(
                    "gqd,gkd->gqk", query_rows, key_slice, preferred_element_type=jnp.float32
                )
                * score_scale
            )
            allowed = (block_start + jnp.arange(key_block, dtype=jnp.int32))[None, :] <= query_pos[
                :, None
            ]
            return (jnp.where(allowed[None], raw_scores, masked_score), allowed, block_start)

        def stats_step(block_index, carried):
            run_peak, run_total = carried
            scores, allowed, block_start = scores_at(block_index)
            new_peak = jnp.maximum(run_peak, jnp.max(scores, axis=-1))
            terms = jnp.where(allowed[None], jnp.exp(scores - new_peak[..., None]), 0.0)
            return (new_peak, run_total * jnp.exp(run_peak - new_peak) + jnp.sum(terms, axis=-1))

        start_stats = (
            jnp.full((local_groups, query_count), masked_score, jnp.float32),
            jnp.zeros((local_groups, query_count), jnp.float32),
        )
        run_peak, run_total = lax.fori_loop(0, block_total, stats_step, start_stats)
        log_total = run_peak + jnp.log(run_total)

        def value_step(block_index, acc_context):
            scores, allowed, block_start = scores_at(block_index)
            probs_low = jnp.where(
                allowed[None], jnp.exp(scores - log_total[..., None]), 0.0
            ).astype(jnp.bfloat16)
            value_slice = lax.dynamic_slice_in_dim(value_heads, block_start, key_block, 1)
            return acc_context + jnp.einsum(
                "gqk,gkd->gqd", probs_low, value_slice, preferred_element_type=jnp.float32
            )

        context_rows = lax.fori_loop(
            0,
            block_total,
            value_step,
            jnp.zeros((local_groups, query_count, head_dim), jnp.float32),
        )
        context_low = (
            from_rows(context_rows).reshape(tok_rows, local_heads * head_dim).astype(jnp.bfloat16)
        )
        branch_part = jnp.einsum(
            "th,dh->td", context_low, output_full, preferred_element_type=jnp.float32
        )
        resid = inputs + lax.psum(branch_part.astype(jnp.bfloat16), "tp").astype(jnp.float32)
        resid_hat, expert_factor = norm_parts(resid)
        expert_in = (resid_hat * expert_gain).astype(jnp.bfloat16)
        logits = jnp.dot(expert_in, router_full, preferred_element_type=jnp.float32)
        routes_now = expert_ids[micro_index]
        choose = (routes_now[:, :, None] == expert_range[None, None, :]).astype(jnp.float32)
        picked = jnp.sum(choose * logits[:, None, :], axis=-1)
        shifted = jnp.exp(picked - jnp.max(picked, axis=-1, keepdims=True))
        gate_probs = shifted / jnp.sum(shifted, axis=-1, keepdims=True)
        flat_routes = routes_now.reshape(-1)
        onehot = (flat_routes[:, None] == expert_range[None, :]).astype(jnp.int32)
        rank_in = jnp.sum((jnp.cumsum(onehot, axis=0) - onehot) * onehot, axis=1)
        slot_index = flat_routes * capacity + rank_in
        slot_source = (
            jnp.full((expert_count * capacity,), routed_total, jnp.int32)
            .at[slot_index]
            .set(jnp.arange(routed_total, dtype=jnp.int32))
        )
        padded_in = jnp.concatenate([expert_in, zero_row], axis=0)
        outgoing = padded_in[slot_source // route_count].reshape(
            fsdp_count, experts_here, capacity, width
        )
        arrived = lax.all_to_all(outgoing, "fsdp", split_axis=0, concat_axis=0, tiled=True)
        gate_pre = jnp.einsum(
            "secd,efd->secf", arrived, gate_weight, preferred_element_type=jnp.float32
        )
        up_pre = jnp.einsum(
            "secd,efd->secf", arrived, up_weight, preferred_element_type=jnp.float32
        )
        gate_sigmoid = jax.nn.sigmoid(gate_pre)
        inner_low = (gate_pre * gate_sigmoid * up_pre).astype(jnp.bfloat16)
        result_part = jnp.einsum(
            "secf,efd->secd", inner_low, down_weight, preferred_element_type=jnp.float32
        )
        result_low = lax.psum_scatter(
            result_part.astype(jnp.bfloat16), "tp", scatter_dimension=3, tiled=True
        )
        result_home = send_home(result_low)
        routed = (
            result_home.reshape(expert_count * capacity, width)[slot_index]
            .astype(jnp.float32)
            .reshape(tok_rows, route_count, width)
        )
        layer_rows.append(
            (resid + jnp.sum(gate_probs[:, :, None] * routed, axis=1)).astype(jnp.bfloat16)
        )
        query_full, key_full, value_full, output_full, router_full = fetch_weights(
            query_weight, key_weight, value_weight, output_weight, router_weight
        )
        out_grad = cotangent[micro_index].astype(jnp.float32)
        d_route = (
            (gate_probs[:, :, None] * out_grad[:, None, :])
            .astype(jnp.bfloat16)
            .reshape(routed_total, width)
        )
        d_gate_probs = jnp.sum(out_grad[:, None, :] * routed, axis=-1)
        d_pick = gate_probs * (
            d_gate_probs - jnp.sum(gate_probs * d_gate_probs, axis=-1, keepdims=True)
        )
        d_logits = jnp.sum(choose * d_pick[:, :, None], axis=1).astype(jnp.bfloat16)
        grad_outgoing = jnp.concatenate([d_route, zero_row], axis=0)[slot_source].reshape(
            fsdp_count, experts_here, capacity, width
        )
        grad_arrived = lax.all_to_all(
            grad_outgoing, "fsdp", split_axis=0, concat_axis=0, tiled=True
        )
        d_inner = jnp.einsum(
            "secd,efd->secf", grad_arrived, down_weight, preferred_element_type=jnp.float32
        )
        acc_down = acc_down + jnp.einsum(
            "secf,secd->efd", inner_low, grad_arrived, preferred_element_type=jnp.float32
        )
        d_gate_low = (
            d_inner * up_pre * gate_sigmoid * (1.0 + gate_pre * (1.0 - gate_sigmoid))
        ).astype(jnp.bfloat16)
        d_up_low = (d_inner * gate_pre * gate_sigmoid).astype(jnp.bfloat16)
        acc_gate = acc_gate + jnp.einsum(
            "secf,secd->efd", d_gate_low, arrived, preferred_element_type=jnp.float32
        )
        acc_up = acc_up + jnp.einsum(
            "secf,secd->efd", d_up_low, arrived, preferred_element_type=jnp.float32
        )
        d_copy_part = jnp.einsum(
            "secf,efd->secd", d_gate_low, gate_weight, preferred_element_type=jnp.float32
        ) + jnp.einsum("secf,efd->secd", d_up_low, up_weight, preferred_element_type=jnp.float32)
        d_copy_low = lax.psum_scatter(
            d_copy_part.astype(jnp.bfloat16), "tp", scatter_dimension=3, tiled=True
        )
        d_copy_home = send_home(d_copy_low)
        d_copies = (
            d_copy_home.reshape(expert_count * capacity, width)[slot_index]
            .astype(jnp.float32)
            .reshape(tok_rows, route_count, width)
        )
        d_expert_in = jnp.sum(d_copies, axis=1) + jnp.dot(
            d_logits, router_full.T, preferred_element_type=jnp.float32
        )
        acc_router = acc_router + jnp.dot(expert_in.T, d_logits, preferred_element_type=jnp.float32)
        acc_expert_gain = acc_expert_gain + jnp.sum(d_expert_in * resid_hat, axis=0)
        d_resid = out_grad + norm_back(d_expert_in, expert_gain, resid_hat, expert_factor)
        d_branch = d_resid.astype(jnp.bfloat16)
        acc_output = acc_output + jnp.einsum(
            "td,th->dh", d_branch, context_low, preferred_element_type=jnp.float32
        )
        d_context = jnp.dot(d_branch, output_full, preferred_element_type=jnp.float32).astype(
            jnp.bfloat16
        )
        d_context_rows = to_rows(d_context.reshape(tok_rows, local_heads, head_dim))
        delta_rows = jnp.sum(d_context_rows.astype(jnp.float32) * context_rows, axis=-1)

        def grad_step(block_index, carried):
            d_query_rows, key_grads_all = carried
            scores, allowed, block_start = scores_at(block_index)
            probs = jnp.where(allowed[None], jnp.exp(scores - log_total[..., None]), 0.0)
            key_slice = lax.dynamic_slice_in_dim(key_heads, block_start, key_block, 1)
            value_slice = lax.dynamic_slice_in_dim(value_heads, block_start, key_block, 1)
            d_probs = jnp.einsum(
                "gqd,gkd->gqk", d_context_rows, value_slice, preferred_element_type=jnp.float32
            )
            d_scores = (probs * (d_probs - delta_rows[..., None])).astype(jnp.bfloat16)
            d_query_rows = (
                d_query_rows
                + jnp.einsum(
                    "gqk,gkd->gqd", d_scores, key_slice, preferred_element_type=jnp.float32
                )
                * score_scale
            )
            d_key_block = (
                jnp.einsum("gqk,gqd->kgd", d_scores, query_rows, preferred_element_type=jnp.float32)
                * score_scale
            )
            d_value_block = jnp.einsum(
                "gqk,gqd->kgd",
                probs.astype(jnp.bfloat16),
                d_context_rows,
                preferred_element_type=jnp.float32,
            )
            current = lax.dynamic_slice_in_dim(key_grads_all, block_start, key_block, 0)
            updated = current + jnp.concatenate([d_key_block, d_value_block], axis=-1)
            return (
                d_query_rows,
                lax.dynamic_update_slice_in_dim(key_grads_all, updated, block_start, 0),
            )

        start_grads = (
            jnp.zeros((local_groups, query_count, head_dim), jnp.float32),
            jnp.zeros((seq_len, local_groups, 2 * head_dim), jnp.float32),
        )
        d_query_rows, key_grads_all = lax.fori_loop(0, block_total, grad_step, start_grads)
        key_grads = (
            lax.psum_scatter(
                key_grads_all.reshape(seq_len, local_groups * 2 * head_dim).astype(jnp.bfloat16),
                "fsdp",
                scatter_dimension=0,
                tiled=True,
            )
            .astype(jnp.float32)
            .reshape(tok_rows, local_groups, 2 * head_dim)
        )
        d_value_low = (
            key_grads[..., head_dim:]
            .reshape(tok_rows, local_groups * head_dim)
            .astype(jnp.bfloat16)
        )
        d_key_pre, key_gain_part = head_back(
            key_grads[..., :head_dim], cosine_heads, sine_heads, key_gain, key_hat, key_factor
        )
        d_query_pre, query_gain_part = head_back(
            from_rows(d_query_rows), cosine_heads, sine_heads, query_gain, query_hat, query_factor
        )
        d_query_low = d_query_pre.astype(jnp.bfloat16).reshape(tok_rows, local_heads * head_dim)
        d_key_low = d_key_pre.astype(jnp.bfloat16).reshape(tok_rows, local_groups * head_dim)
        d_normed_part = jnp.dot(d_query_low, query_full.T, preferred_element_type=jnp.float32)
        d_normed_part = d_normed_part + jnp.dot(
            d_key_low, key_full.T, preferred_element_type=jnp.float32
        )
        d_normed_part = d_normed_part + jnp.dot(
            d_value_low, value_full.T, preferred_element_type=jnp.float32
        )
        acc_query = acc_query + jnp.dot(normed.T, d_query_low, preferred_element_type=jnp.float32)
        acc_key = acc_key + jnp.dot(normed.T, d_key_low, preferred_element_type=jnp.float32)
        acc_value = acc_value + jnp.dot(normed.T, d_value_low, preferred_element_type=jnp.float32)
        d_normed, head_gain_parts = (
            lax.psum(d_normed_part.astype(jnp.bfloat16), "tp").astype(jnp.float32),
            lax.psum(jnp.stack([query_gain_part, key_gain_part]).astype(jnp.bfloat16), "tp").astype(
                jnp.float32
            ),
        )
        acc_head_gains = acc_head_gains + head_gain_parts
        acc_attention_gain = acc_attention_gain + jnp.sum(d_normed * input_hat, axis=0)
        input_rows.append(
            (d_resid + norm_back(d_normed, attention_gain, input_hat, attention_factor)).astype(
                jnp.bfloat16
            )
        )
    summed = (
        lax.psum_scatter(
            acc_attention_gain.astype(jnp.bfloat16), "fsdp", scatter_dimension=0, tiled=True
        ).astype(jnp.float32),
        lax.psum_scatter(
            acc_head_gains[0].astype(jnp.bfloat16), "fsdp", scatter_dimension=0, tiled=True
        ).astype(jnp.float32),
        lax.psum_scatter(
            acc_head_gains[1].astype(jnp.bfloat16), "fsdp", scatter_dimension=0, tiled=True
        ).astype(jnp.float32),
        lax.psum_scatter(
            acc_query.astype(jnp.bfloat16), "fsdp", scatter_dimension=0, tiled=True
        ).astype(jnp.float32),
        lax.psum_scatter(
            acc_key.astype(jnp.bfloat16), "fsdp", scatter_dimension=0, tiled=True
        ).astype(jnp.float32),
        lax.psum_scatter(
            acc_value.astype(jnp.bfloat16), "fsdp", scatter_dimension=0, tiled=True
        ).astype(jnp.float32),
        lax.psum_scatter(
            acc_output.astype(jnp.bfloat16), "fsdp", scatter_dimension=0, tiled=True
        ).astype(jnp.float32),
        lax.psum_scatter(
            acc_expert_gain.astype(jnp.bfloat16), "fsdp", scatter_dimension=0, tiled=True
        ).astype(jnp.float32),
        lax.psum_scatter(
            acc_router.astype(jnp.bfloat16), "fsdp", scatter_dimension=0, tiled=True
        ).astype(jnp.float32),
    )
    return (
        jnp.stack(layer_rows),
        jnp.stack(input_rows),
        summed[0],
        summed[1],
        summed[2],
        summed[3],
        summed[4],
        summed[5],
        summed[6],
        summed[7],
        summed[8],
        acc_gate,
        acc_up,
        acc_down,
    )


def small_device(
    tokens,
    cotangent,
    expert_ids,
    attention_gain,
    query_gain,
    key_gain,
    query_weight,
    key_weight,
    value_weight,
    output_weight,
    expert_gain,
    router_weight,
    gate_weight,
    up_weight,
    down_weight,
):
    count, rows, width = tokens.shape
    hd = query_gain.shape[0]
    f = lax.axis_index("fsdp")
    n_fsdp = lax.axis_size("fsdp")
    seq = rows * n_fsdp
    experts = gate_weight.shape[0]
    expert_count = experts * n_fsdp
    piece = query_weight.shape[0]

    cosine, sine = signed_tables(seq, hd)
    inputs = tokens.astype(F32)
    input_hat, attention_factor = norm_parts(inputs)
    normed = (input_hat * attention_gain).astype(LOW)

    (normed_all, weights, output_pair, router_all, ids_all, grad_all, pre, qkv, prob, context, branch) = begin(
        normed,
        cotangent,
        query_weight,
        key_weight,
        value_weight,
        output_weight,
        router_weight.T,
        expert_ids.transpose(0, 2, 1),
        cosine,
        sine,
        query_gain,
        key_gain,
    )
    router_full = router_all.T
    ids_all = ids_all.transpose(0, 2, 1)
    resid = inputs + branch.astype(F32)
    resid_hat, expert_factor = norm_parts(resid)
    expert_in = (resid_hat * expert_gain).astype(LOW)

    expert_all = gather_rows(expert_in, True).reshape(count * seq, width)
    lanes = 128
    router_wide = jnp.pad(router_full, ((0, 0), (0, lanes - expert_count)))
    first = (f * experts).astype(jnp.int32).reshape(1)
    out_part, dx_part, dgp_part, d_gate, d_up, d_down = run_experts(
        first,
        expert_all,
        grad_all.reshape(count * seq, width),
        ids_all.reshape(count * seq, -1),
        router_wide,
        gate_weight,
        up_weight,
        down_weight,
    )
    dgp_part = dgp_part[:, :expert_count].reshape(count, seq, expert_count)
    d_gate_probs = lax.psum(
        lax.psum_scatter(dgp_part, "fsdp", scatter_dimension=1, tiled=True), "tp"
    )
    dx_sum = sum_rows(dx_part.reshape(count, seq, width), True).astype(F32)
    expert_range = jnp.arange(expert_count, dtype=jnp.int32)
    named = jnp.any(expert_ids[..., None] == expert_range, axis=2)
    logits = jnp.dot(expert_in, router_full, preferred_element_type=F32)
    masked = jnp.where(named, logits, masked_score)
    terms = jnp.where(named, jnp.exp(masked - jnp.max(masked, axis=-1, keepdims=True)), 0.0)
    gate_probs = terms / jnp.sum(terms, axis=-1, keepdims=True)
    d_logits = (
        gate_probs * (d_gate_probs - jnp.sum(gate_probs * d_gate_probs, axis=-1, keepdims=True))
    ).astype(LOW)
    d_expert_in = dx_sum + lax.dot_general(
        d_logits, router_full, (((2,), (1,)), ((), ())), preferred_element_type=F32
    )
    router_part = lax.dot_general(
        expert_in, d_logits, (((0, 1), (0, 1)), ((), ())), preferred_element_type=F32
    )
    expert_gain_part = jnp.sum(d_expert_in * resid_hat, axis=(0, 1))
    out_grad = cotangent.astype(F32)
    d_resid = out_grad + norm_back(d_expert_in, expert_gain, resid_hat, expert_factor)
    d_branch = d_resid.astype(LOW)

    aux = jnp.concatenate(
        [
            router_part.T.reshape(expert_count, n_fsdp, piece).transpose(1, 0, 2),
            expert_gain_part.reshape(n_fsdp, 1, piece),
            jnp.zeros((n_fsdp, -(expert_count + 1) % 16, piece), F32),
        ],
        axis=1,
    ).astype(LOW)
    out_sum, d_normed, d_query, d_key, d_value, d_output, aux_sum, line = end(
        d_branch,
        normed_all,
        weights,
        output_pair,
        pre,
        qkv,
        prob,
        context,
        out_part.reshape(count, seq, width),
        aux,
        query_weight,
        key_weight,
        value_weight,
        cosine,
        sine,
        query_gain,
        key_gain,
    )
    layer_output = (resid + out_sum.astype(F32)).astype(LOW)
    input_grad = (
        d_resid + norm_back(d_normed.astype(F32), attention_gain, input_hat, attention_factor)
    ).astype(LOW)
    own_gain = lax.dynamic_slice_in_dim(attention_gain, f * piece, piece, 0)
    head_piece = hd // n_fsdp
    head_gains = lax.dynamic_slice_in_dim(line[:2, piece:], f * head_piece, head_piece, 1)
    return (
        layer_output,
        input_grad,
        line[0, :piece] / own_gain,
        head_gains[0],
        head_gains[1],
        d_query,
        d_key,
        d_value,
        d_output,
        aux_sum[expert_count],
        aux_sum[:expert_count].T,
        d_gate.reshape(gate_weight.shape),
        d_up.reshape(up_weight.shape),
        d_down.reshape(down_weight.shape),
    )


def solution(mesh):
    body = small_device if (mesh.shape["fsdp"], mesh.shape["tp"]) == (8, 4) else general_device
    return jax.shard_map(
        body,
        mesh=mesh,
        in_specs=(
            P(None, "fsdp", None),
            P(None, "fsdp", None),
            P(None, "fsdp", None),
            P(),
            P(),
            P(),
            P("fsdp", "tp"),
            P("fsdp", "tp"),
            P("fsdp", "tp"),
            P("fsdp", "tp"),
            P(),
            P("fsdp", None),
            P("fsdp", "tp", None),
            P("fsdp", "tp", None),
            P("fsdp", "tp", None),
        ),
        out_specs=(
            P(None, "fsdp", None),
            P(None, "fsdp", None),
            P("fsdp"),
            P("fsdp"),
            P("fsdp"),
            P("fsdp", "tp"),
            P("fsdp", "tp"),
            P("fsdp", "tp"),
            P("fsdp", "tp"),
            P("fsdp"),
            P("fsdp", None),
            P("fsdp", "tp", None),
            P("fsdp", "tp", None),
            P("fsdp", "tp", None),
        ),
        check_vma=False,
    )
```

```python
import functools
import math

import jax
import jax.numpy as jnp
import numpy as np
from jax import lax
from jax.experimental import pallas as pl
from jax.experimental.pallas import tpu as pltpu
from jax.sharding import PartitionSpec as P

norm_eps = 1e-06
rope_base = 1000000.0
masked_score = -1e30
MESH = pl.DeviceIdType.MESH
LOW = jnp.bfloat16
F32 = jnp.float32
VMEM_LIMIT = 60 * 2**20


def coords():
    f = lax.axis_index("fsdp")
    t = lax.axis_index("tp")
    return f // 2, f % 2, t // 2, t % 2


def place(z, x, y, c):
    return (2 * z + x, 2 * y + c)


def span(first, count):
    return pl.ds(pl.multiple_of(first, count), count)


class Here:
    def __init__(self):
        z, x, y, c = coords()
        self.z, self.x, self.y, self.c = z, x, y, c
        self.f, self.t = 2 * z + x, 2 * y + c
        self.xn, self.yn, self.cn = place(z, 1 - x, y, c), place(z, x, 1 - y, c), place(z, x, y, 1 - c)
        self.lanes = ((x, y), (1 - x, y), (x, 1 - y), (1 - x, 1 - y))

    def zr(self, d):
        return (self.z + d) % 4

    def flip(self, k):
        return (self.z // 2 + k // 2) % 2 * 2 + (self.z % 2 + k % 2) % 2

    def zd(self, j):
        inner = (self.z % 3 + 1) // 2
        return self.flip(j + inner * (j // 2) * (1 - 2 * (j % 2)))

    def at_z(self, z):
        return place(z, self.x, self.y, self.c)

    def number(self, j, e):
        return 2 * self.zd(j) + (self.x + e) % 2

    def peer(self, d, e):
        return place(self.zr(d), (self.x + e) % 2, self.y, self.c)

    def greet(self):
        barrier = pltpu.get_barrier_semaphore()
        peers = [self.peer(d, e) for d in range(4) for e in range(2) if d or e] + [self.yn, self.cn]
        for peer in peers:
            pl.semaphore_signal(barrier, inc=1, device_id=peer, device_id_type=MESH)
        pl.semaphore_wait(barrier, len(peers))


def remote(src, dst, send_sem, recv_sem, device):
    return pltpu.make_async_remote_copy(
        src_ref=src, dst_ref=dst, send_sem=send_sem, recv_sem=recv_sem, device_id=device, device_id_type=MESH
    )


def push(src, dst, send_sem, recv_sem, device):
    copy = remote(src, dst, send_sem, recv_sem, device)
    copy.start()
    return copy


def keep(src, dst, sem):
    copy = pltpu.make_async_copy(src, dst, sem)
    copy.start()
    return copy


ORDER = (1, 2, 3)
FAR_FIRST = (3, 2, 1, 0)


class Gather:
    scratch = staticmethod(
        lambda: [pltpu.SemaphoreType.DMA((1,)), pltpu.SemaphoreType.DMA((6,))]
        + [pltpu.SemaphoreType.DMA((4,))] * 9
        + [pltpu.SemaphoreType.DMA((4, 4))] * 2
    )
    slots = 13

    def __init__(self, here, whole, src, dst, sems, by_x, own=None):
        self.here, self.whole, self.src, self.dst, self.own_rows = here, whole, src, dst, own
        (self.loc, self.sz, self.rz, self.sx, self.rx, self.sy, self.ry,
         self.sdx, self.rdx, self.sdy, self.rdy, self.sc, self.rc) = sems
        self.rows, self.cols = src.shape[1], src.shape[2] // 4
        self.half = by_x
        self.sends = []

    def block(self, z, x, y, c, h=None):
        first = (2 * z + x) * self.rows
        rows = span(first, self.rows)
        if h is not None:
            start, count = ((0, self.half), (self.half, self.rows - self.half))[h]
            rows = pl.ds(pl.multiple_of(first + start, 16), count)
        return self.dst.at[:, rows, span((2 * y + c) * self.cols, self.cols)]

    def source(self, z_to, t, first, count):
        seqs = slice(None) if self.whole else pl.ds(z_to // 2, 1)
        return self.src.at[seqs, pl.ds(first, count), span(t * self.cols, self.cols)]

    def push(self, make, when=None):
        if when is None:
            push(*make())
        else:
            pl.when(when)(lambda: push(*make()) and None)
        self.sends.append((make, when))

    def landed(self, ref, sem):
        pltpu.make_async_remote_copy(
            src_ref=ref, dst_ref=ref, send_sem=sem, recv_sem=sem, device_id=self.here.xn, device_id_type=MESH
        ).wait_recv()

    def start(self):
        h = self.here
        self.inner = h.z % 3 > 0
        self.along(0, h.flip(1), True)
        self.along(1, h.flip(3), self.inner)
        if not self.whole:
            self.along(2, h.flip(2), h.z % 3 == 0)
        self.push(lambda: (self.source(h.z, h.t, 0, self.rows), self.block(h.z, h.x, h.y, h.c),
                           self.sx.at[h.z], self.rx.at[h.z], h.xn))
        if self.half:
            self.push(lambda: (self.source(h.z, 2 * (1 - h.y) + h.c, 0, self.half),
                               self.block(h.z, h.x, 1 - h.y, h.c, 0), self.sdx.at[h.z], self.rdx.at[h.z], h.xn))
        own = self.src if self.whole else self.src.at[pl.ds(h.z // 2, 1)]
        if self.own_rows is not None:
            own = self.own_rows
            pltpu.make_async_copy(self.src, own, self.loc.at[0]).start()
            pltpu.make_async_copy(self.src, own, self.loc.at[0]).wait()
        self.own = keep(own, self.dst.at[:, span(h.f * self.rows, self.rows), :], self.loc.at[0])

    def along(self, n, z_to, when):
        h = self.here
        self.push(lambda: (self.source(z_to, h.t, 0, self.rows), self.block(h.z, h.x, h.y, h.c),
                           self.sz.at[n], self.rz.at[h.z], h.at_z(z_to)), None if when is True else when)

    def relay(self, j):
        h, zd = self.here, self.here.zd(j)
        self.landed(self.block(zd, h.x, h.y, h.c), self.rz.at[zd])
        if j > 1 or self.whole:

            def make():
                b = self.block(h.zd(j), h.x, h.y, h.c)
                return b, b, self.sz.at[2 + j], self.rz.at[h.zd(j)], h.at_z(h.flip(3 if j == 1 else 1))

            self.push(make, self.inner)

    def pass_on(self, d, lane, sends, recvs, device, h=None):
        x, y = self.here.lanes[lane]

        def make():
            zd = self.here.zd(d)
            b = self.block(zd, x, y, self.here.c, h)
            return b, b, sends(zd), recvs(zd), device

        self.push(make)

    def spread(self, d):
        h = self.here
        self.pass_on(d, 0, lambda k: self.sx.at[k], lambda k: self.rx.at[k], h.xn)
        self.pass_on(d, 0, lambda k: self.sy.at[k], lambda k: self.ry.at[k], h.yn)
        self.pass_on(d, 0, lambda k: self.sc.at[0, k], lambda k: self.rc.at[0, k], h.cn)

    def cross(self, d):
        h, zd = self.here, self.here.zd(d)
        self.landed(self.block(zd, 1 - h.x, h.y, h.c), self.rx.at[zd])
        self.pass_on(d, 1, lambda k: self.sdy.at[k], lambda k: self.rdy.at[k], h.yn, 1)
        self.pass_on(d, 1, lambda k: self.sc.at[1, k], lambda k: self.rc.at[1, k], h.cn)
        if d != 0:
            self.landed(self.block(zd, h.x, 1 - h.y, h.c), self.ry.at[zd])
            if self.half:
                self.pass_on(d, 2, lambda k: self.sdx.at[k], lambda k: self.rdx.at[k], h.xn, 0)
            self.pass_on(d, 2, lambda k: self.sc.at[2, k], lambda k: self.rc.at[2, k], h.cn)

    def close(self, d):
        h, zd = self.here, self.here.zd(d)
        if self.half:
            self.landed(self.block(zd, 1 - h.x, 1 - h.y, h.c, 0), self.rdx.at[zd])
        self.landed(self.block(zd, 1 - h.x, 1 - h.y, h.c, 1), self.rdy.at[zd])
        self.pass_on(d, 3, lambda k: self.sc.at[3, k], lambda k: self.rc.at[3, k], h.cn)

    def first_steps(self):
        for j in ORDER:
            self.relay(j)
            self.spread(j)
            if j < 3:
                self.cross(j - 1)

    def last_steps(self):
        self.close(0)
        for j in (2, 3):
            self.cross(j)
            self.close(j - 1)
        self.close(3)

    def arrived(self, d, e):
        h, zd = self.here, self.here.zd(d)
        if e == 0:
            if d == 0:
                self.own.wait()
            else:
                self.landed(self.block(zd, h.x, h.y, 1 - h.c), self.rc.at[0, zd])
                self.landed(self.block(zd, h.x, 1 - h.y, 1 - h.c), self.rc.at[2, zd])
        else:
            self.landed(self.block(zd, 1 - h.x, h.y, 1 - h.c), self.rc.at[1, zd])
            self.landed(self.block(zd, 1 - h.x, 1 - h.y, 1 - h.c), self.rc.at[3, zd])

    def finish(self):
        for make, when in self.sends:
            if when is None:
                remote(*make()).wait_send()
            else:
                pl.when(when)(lambda make=make: remote(*make()).wait_send())


def add_into(target, *others):
    count, rows, _ = target.shape
    step = 32

    @pl.loop(0, count * rows // step)
    def _(i):
        n = i // (rows // step)
        r = pl.ds(pl.multiple_of((i % (rows // step)) * step, step), step)
        total = target[n, r, :].astype(F32)
        for other in others:
            total = total + other[n, r, :].astype(F32)
        target[n, r, :] = total.astype(target.dtype)


class Sum:
    slots = 23

    @staticmethod
    def scratch(count, rows, width, low, by_x):
        dma = pltpu.SemaphoreType.DMA
        cols = width // 4
        vm = pltpu.VMEM
        return [
            vm((4, 4, count, rows, cols), low),
            vm((4, count, max(by_x, 16), cols), low),
            vm((4, count, rows - by_x, cols), low),
            vm((4, count, rows, cols), low),
            vm((4, count, rows, cols), low),
            vm((4, count, rows, cols), low),
            vm((4, 2, rows, cols), low),
            vm((2, rows, cols), low),
            dma((4, 4)), dma((4, 4)),
        ] + [dma((4,))] * 10 + [dma((3,))] * 2 + [dma((5,))]

    def __init__(self, here, whole, part, refs, by_x):
        self.here, self.whole, self.part, self.by_x = here, whole, part, by_x
        (self.fc, self.f1x, self.f1y, self.f2x, self.f2y, self.fz, self.full, self.tmp, self.sc, self.rc,
         self.s1x, self.r1x, self.s1y, self.r1y, self.s2x, self.r2x, self.s2y, self.r2y, self.sz, self.rz,
         self.sg, self.rg, self.osem) = refs
        self.rows, self.cols = part.shape[1] // 8, part.shape[2] // 4
        self.top, self.low = pl.ds(0, by_x), pl.ds(by_x, self.rows - by_x)
        self.sends = []

    def block(self, d, lane, c):
        x, y = self.here.lanes[lane]
        return self.part.at[:, span((2 * self.here.zd(d) + x) * self.rows, self.rows),
                            span((2 * y + c) * self.cols, self.cols)]

    def push(self, make):
        push(*make())
        self.sends.append(make)

    def landed(self, ref, sem):
        pltpu.make_async_remote_copy(
            src_ref=ref, dst_ref=ref, send_sem=sem, recv_sem=sem, device_id=self.here.xn, device_id_type=MESH
        ).wait_recv()

    def giving(self, d, e):
        h = self.here
        for q in (0, 1):
            lane = 2 * q + e
            at = self.part.at[:, span((2 * h.zd(d) + (h.x + e) % 2) * self.rows, self.rows),
                              span((2 * ((h.y + q) % 2) + 1 - h.c) * self.cols, self.cols)]
            yield at, self.fc.at[lane, d], self.sc.at[lane, d], self.rc.at[lane, d], h.cn

    def give(self, d, e):
        for args in self.giving(d, e):
            push(*args)

    def pair(self, lane, d):
        self.landed(self.fc.at[lane, d], self.rc.at[lane, d])
        add_into(self.block(d, lane, self.here.c), self.fc.at[lane, d])

    def mine(self, d, lane, rows=slice(None)):
        return self.block(d, lane, self.here.c).at[:, rows]

    def corner(self, d):
        self.pair(3, d)
        if self.by_x:
            self.push(lambda: (self.mine(d, 3, self.top), self.f1x.at[d], self.s1x.at[d], self.r1x.at[d], self.here.xn))
        self.push(lambda: (self.mine(d, 3, self.low), self.f1y.at[d], self.s1y.at[d], self.r1y.at[d], self.here.yn))

    def sides(self, d):
        self.pair(1, d)
        self.landed(self.f1y.at[d], self.r1y.at[d])
        add_into(self.mine(d, 1, self.low), self.f1y.at[d])
        self.push(lambda: (self.mine(d, 1), self.f2x.at[d], self.s2x.at[d], self.r2x.at[d], self.here.xn))
        self.pair(2, d)
        if self.by_x:
            self.landed(self.f1x.at[d], self.r1x.at[d])
            add_into(self.mine(d, 2, self.top), self.f1x.at[d])
        self.push(lambda: (self.mine(d, 2), self.f2y.at[d], self.s2y.at[d], self.r2y.at[d], self.here.yn))

    def centre(self, d):
        self.pair(0, d)
        self.landed(self.f2x.at[d], self.r2x.at[d])
        self.landed(self.f2y.at[d], self.r2y.at[d])
        add_into(self.mine(d, 0), self.f2x.at[d], self.f2y.at[d])
        if d != 0:
            h = self.here
            self.push(lambda: (self.mine(d, 0), self.fz.at[h.z], self.sz.at[d], self.rz.at[h.z], h.at_z(h.zd(d))))

    def total(self):
        for d in (1, 2, 3):
            self.landed(self.fz.at[self.here.zd(d)], self.rz.at[self.here.zd(d)])
        b = self.block(0, 0, self.here.c)
        step = 32

        @pl.loop(0, 2 * self.rows // step)
        def _(i):
            n = i // (self.rows // step)
            r = pl.ds(pl.multiple_of((i % (self.rows // step)) * step, step), step)
            if self.whole:
                total = b[n, r, :].astype(F32)
                for d in (1, 2, 3):
                    total = total + self.fz[self.here.zd(d), n, r, :].astype(F32)
            else:
                total = jnp.where(self.here.z // 2 == n, b[0, r, :].astype(F32), 0.0)
                for d in (1, 2, 3):
                    total = total + jnp.where(self.here.zd(d) // 2 == n, self.fz[self.here.zd(d), 0, r, :].astype(F32), 0.0)
            self.tmp[n, r, :] = total.astype(self.tmp.dtype)

    def share(self, out):
        self.share_start()
        self.share_cross()
        self.share_end(out)

    def share_start(self):
        h = self.here
        self.keeps = [keep(self.tmp, self.full.at[h.t], self.osem.at[4])]
        self.push(lambda: (self.tmp, self.full.at[h.t], self.sg.at[0], self.rg.at[0], h.yn))
        self.push(lambda: (self.tmp, self.full.at[h.t], self.sg.at[1], self.rg.at[1], h.cn))

    def share_cross(self):
        h = self.here
        ty = 2 * (1 - h.y) + h.c
        self.landed(self.full.at[ty], self.rg.at[0])
        self.push(lambda: (self.full.at[ty], self.full.at[ty], self.sg.at[2], self.rg.at[2], h.cn))

    def share_end(self, out):
        h = self.here
        self.landed(self.full.at[2 * h.y + 1 - h.c], self.rg.at[1])
        self.landed(self.full.at[2 * (1 - h.y) + 1 - h.c], self.rg.at[2])
        self.keeps[0].wait()
        outs = [keep(self.full.at[q], out.at[:, :, pl.ds(q * self.cols, self.cols)], self.osem.at[q]) for q in range(4)]
        for copy in outs:
            copy.wait()

    def finish(self):
        for make in self.sends:
            remote(*make()).wait_send()
        for d in range(4):
            for e in range(2):
                for args in self.giving(d, e):
                    remote(*args).wait_send()


def wait_for(ref, sem, device):
    pltpu.make_async_remote_copy(
        src_ref=ref, dst_ref=ref, send_sem=sem, recv_sem=sem, device_id=device, device_id_type=MESH
    ).wait_recv()


def signed_tables(length, width):
    middle = width // 2
    frequency = rope_base ** (-np.arange(middle) * 2.0 / width)
    angles = np.arange(length)[:, None] * frequency[None, :]
    cosine, sine = np.cos(angles), np.sin(angles)
    return (
        jnp.asarray(np.concatenate([cosine, cosine], axis=1), F32),
        jnp.asarray(np.concatenate([-sine, sine], axis=1), F32),
    )


def dot_nn(a, b):
    return jnp.dot(a, b, preferred_element_type=F32)


def dot_nt(a, b):
    return lax.dot_general(a, b, (((1,), (1,)), ((), ())), preferred_element_type=F32)


def dot_tn(a, b):
    return lax.dot_general(a, b, (((0,), (0,)), ((), ())), preferred_element_type=F32)


BY_X = 64


class Weights:
    scratch = staticmethod(lambda: [pltpu.SemaphoreType.DMA((8, 4, 2))] * 4 + [pltpu.SemaphoreType.DMA((6,))])
    slots = 5

    def __init__(self, here, query, key, value, output, router, ids, w, wo, router_all, ids_all, sems):
        self.here = here
        self.query, self.output, self.w, self.wo = query, output, w, wo
        piece, part = query.shape[0], wo.shape[1]
        self.piece, self.part = piece, part
        hd = key.shape[1]
        self.shared = (
            (key, lambda f: w.at[span(f * piece, piece), pl.ds(part, hd)]),
            (value, lambda f: w.at[span(f * piece, piece), pl.ds(part + hd, hd)]),
            (router, lambda f: router_all.at[:, span(f * piece, piece)]),
            (ids, lambda f: ids_all.at[:, :, span(f * ids.shape[2], ids.shape[2])]),
        )
        self.qs, self.qr, self.ss, self.sr, self.loc = sems
        self.sends, self.keeps = [], []

    def landed(self, ref, sem):
        pltpu.make_async_remote_copy(
            src_ref=ref, dst_ref=ref, send_sem=sem, recv_sem=sem, device_id=self.here.xn, device_id_type=MESH
        ).wait_recv()

    def start_shared(self):
        h = self.here
        for n, (src, dst) in enumerate(self.shared):
            self.keeps.append(keep(src, dst(h.f), self.loc.at[n]))
            for d, e in ((2, 0), (1, 0), (3, 0), (0, 1)):
                self.sends.append(push(src, dst(h.f), self.ss.at[n, d, e], self.sr.at[n, (4 - d) % 4, e], h.peer(d, e)))

    def pass_shared(self, d):
        h = self.here
        for n, (_, dst) in enumerate(self.shared):
            ref = dst(2 * h.zr(d) + h.x)
            self.landed(ref, self.sr.at[n, d, 0])
            self.sends.append(push(ref, ref, self.ss.at[n, d, 1], self.sr.at[n, d, 1], h.xn))

    def wait_shared(self):
        h = self.here
        for n, (_, dst) in enumerate(self.shared):
            for d in range(4):
                self.landed(dst(2 * h.zr(d) + 1 - h.x), self.sr.at[n, d, 1])

    def start_pairs(self, n):
        h = self.here
        src, dst = ((self.query, self.w), (self.output, self.wo))[n]
        mine = lambda f: dst.at[span(f * self.piece, self.piece), pl.ds(0, self.part)]
        self.keeps.append(keep(src.at[:, span((h.f % 4) * self.part, self.part)], mine(h.f), self.loc.at[4 + n]))
        for d in (2, 1, 3, 0):
            for e in (1, 0):
                if d or e:
                    f = 2 * h.zr(d) + (h.x + e) % 2
                    self.sends.append(push(src.at[:, span((f % 4) * self.part, self.part)], mine(h.f),
                                           self.qs.at[n, d, e], self.qr.at[n, (4 - d) % 4, e], h.peer(d, e)))

    def wait_pairs(self, n, far=range(4)):
        h = self.here
        dst = (self.w, self.wo)[n]
        for d in far:
            for e in (1, 0):
                if d or e:
                    f = 2 * h.zr(d) + (h.x + e) % 2
                    self.landed(dst.at[span(f * self.piece, self.piece), pl.ds(0, self.part)], self.qr.at[n, d, e])

    def finish(self):
        for copy in self.sends:
            copy.wait_send()


def begin_kernel(heads, normed, cot, query, key, value, output, router, ids, cos_ref, sin_ref, qg_ref, kg_ref,
                 xn_out, w_out, wo_out, router_out, ids_out, cot_out, pre_out, qkv_out, prob_out, ctx_out, branch_out,
                 xn, w, wo, pre, qkv, prob, ctx, part, own, osem, *sems):
    here = Here()
    here.greet()
    at = 0
    x_rows = Gather(here, False, normed, xn, sems[at : at + Gather.slots], BY_X)
    at += Gather.slots
    c_rows = Gather(here, True, cot, cot_out, sems[at : at + Gather.slots], BY_X + 32, own)
    at += Gather.slots
    moved = Weights(here, query, key, value, output, router, ids, w, wo, router_out, ids_out, sems[at : at + Weights.slots])
    at += Weights.slots
    total = Sum(here, False, part, sems[at:], BY_X)

    x_rows.start()
    moved.start_shared()
    moved.start_pairs(0)
    x_rows.first_steps()
    for d in (1, 3, 2):
        moved.pass_shared(d)
    x_rows.last_steps()
    for d in (0,) + ORDER:
        x_rows.arrived(d, 0)
        x_rows.arrived(d, 1)
    moved.wait_shared()
    moved.wait_pairs(0, (2,))
    moved.start_pairs(1)
    moved.wait_pairs(0, (0, 1, 3))
    for copy in moved.keeps:
        copy.wait()
    outs = [keep(xn, xn_out, osem.at[0]), keep(w, w_out, osem.at[1])]

    seq = xn.shape[1]
    hd = cos_ref.shape[1]
    tile = 256
    scale = 1.0 / math.sqrt(hd)
    for i in range(seq // tile):
        r = pl.ds(i * tile, tile)
        got = dot_nn(xn[0, r, :], w[...])
        pre[r, :] = got[:, : (heads + 1) * hd]
        qkv[r, pl.ds((heads + 1) * hd, hd)] = got[:, (heads + 1) * hd :].astype(LOW)
        for a in range(heads + 1):
            one = got[:, a * hd : (a + 1) * hd]
            factor = lax.rsqrt(jnp.mean(one * one, axis=-1, keepdims=True) + norm_eps)
            gained = one * factor * (qg_ref if a < heads else kg_ref)[...]
            turned = gained * cos_ref[r, :] + pltpu.roll(gained, hd // 2, 1) * sin_ref[r, :]
            qkv[r, pl.ds(a * hd, hd)] = turned.astype(LOW)
    c_rows.start()
    outs += [keep(pre, pre_out, osem.at[2]), keep(qkv, qkv_out, osem.at[3])]
    for a in range(heads):
        for i in range(seq // tile):
            r = pl.ds(i * tile, tile)
            n = (i + 1) * tile
            score = dot_nt(qkv[r, pl.ds(a * hd, hd)], qkv[pl.ds(0, n), pl.ds(heads * hd, hd)]) * scale
            row = lax.broadcasted_iota(jnp.int32, (tile, n), 0) + i * tile
            col = lax.broadcasted_iota(jnp.int32, (tile, n), 1)
            score = jnp.where(col <= row, score, masked_score)
            terms = jnp.exp(score - jnp.max(score, axis=-1, keepdims=True))
            low = (terms * (1.0 / jnp.sum(terms, axis=-1, keepdims=True))).astype(LOW)
            prob[a, r, pl.ds(0, n)] = low
            ctx[r, pl.ds(a * hd, hd)] = dot_nn(low, qkv[pl.ds(0, n), pl.ds((heads + 1) * hd, hd)]).astype(LOW)
        if a == 0:
            c_rows.relay(1)
            c_rows.spread(1)
    outs += [keep(prob, prob_out, osem.at[4]), keep(ctx, ctx_out, osem.at[5])]
    moved.wait_pairs(1)
    outs.append(keep(wo, wo_out, osem.at[6]))
    rows = total.rows
    for e in (1, 0):
        for d in FAR_FIRST:
            at_f = span(here.number(d, e) * rows, rows)
            part[0, at_f, :] = dot_nt(ctx[at_f, :], wo[...]).astype(LOW)
            total.give(d, e)
    for d in FAR_FIRST:
        total.corner(d)
    c_rows.cross(0)
    c_rows.relay(2)
    c_rows.spread(2)
    for d in FAR_FIRST:
        total.sides(d)
    c_rows.cross(1)
    c_rows.relay(3)
    c_rows.spread(3)
    for d in FAR_FIRST:
        total.centre(d)
    c_rows.close(0)
    c_rows.cross(2)
    c_rows.close(1)
    total.total()
    total.share_start()
    c_rows.cross(3)
    c_rows.close(2)
    total.share_cross()
    c_rows.close(3)
    total.share_end(branch_out)
    for d in (0,) + ORDER:
        c_rows.arrived(d, 0)
        c_rows.arrived(d, 1)
    for each in (x_rows, c_rows, moved, total):
        each.finish()
    for copy in outs:
        copy.wait()


def begin(normed, cot, query, key, value, output, router, ids, cosine, sine, query_gain, key_gain):
    count, rows, width = normed.shape
    seq = rows * 8
    hd = query_gain.shape[0]
    part = query.shape[1] // 4
    heads = part // hd
    vm = pltpu.VMEM
    hbm = pl.BlockSpec(memory_space=pl.ANY)
    near = pl.BlockSpec(memory_space=pltpu.VMEM)
    shape = jax.ShapeDtypeStruct
    local = [
        ((1, seq, width), LOW),
        ((width, part + 2 * hd), LOW),
        ((width, part), LOW),
        ((seq, (heads + 1) * hd), F32),
        ((seq, (heads + 2) * hd), LOW),
        ((heads, seq, seq), LOW),
        ((seq, heads * hd), LOW),
    ]
    return pl.pallas_call(
        functools.partial(begin_kernel, heads),
        out_shape=(
            shape(*local[0]),
            shape(*local[1]),
            shape(*local[2]),
            shape((router.shape[0], width), LOW),
            shape((count, ids.shape[1], seq), jnp.int32),
            shape((count, seq, width), LOW),
            shape(*local[3]),
            shape(*local[4]),
            shape(*local[5]),
            shape(*local[6]),
            shape((count, rows, width), LOW),
        ),
        in_specs=[hbm] * 8 + [near] * 4,
        out_specs=[hbm] * 11,
        scratch_shapes=[vm(*entry) for entry in local]
        + [vm((1, seq, width), LOW), vm((count, rows, width), LOW), pltpu.SemaphoreType.DMA((7,))]
        + Gather.scratch() + Gather.scratch() + Weights.scratch() + Sum.scratch(1, rows, width, LOW, BY_X),
        compiler_params=pltpu.CompilerParams(
            collective_id=4, has_side_effects=True, vmem_limit_bytes=VMEM_LIMIT
        ),
        name="begin",
    )(normed, cot, query, key, value, output, router, ids, cosine, sine, query_gain[None], key_gain[None])


def experts_kernel(experts, expert_in, og_in, ids, router, g_in, u_in, d_in,
                   x_out, act_out, dx_sum, out_sum, probs_out, dgp_out,
                   x_t, g, u, dn, og_t, raw_s, act_t, dx, out, stage, share_s, dgp_t, dgp_got, dgp_all, dgp_c, dgp_y,
                   wsem, ogsem, xsem, actsem, psem, rsem, tsem, usem, *rest):
    here = Here()
    here.greet()
    by_x = expert_in.shape[1] // 2
    rows_x = Gather(here, True, expert_in, x_out, rest[: Gather.slots], by_x, x_t)
    sums = (
        Sum(here, True, dx, rest[Gather.slots : Gather.slots + Sum.slots], by_x),
        Sum(here, True, out, rest[Gather.slots + Sum.slots :], by_x),
    )
    number = here.number
    count, rows, width = expert_in.shape
    hidden = g.shape[0]
    per = hidden // experts
    tokens = count * rows
    lanes = router.shape[0]
    part = stage.shape[2]
    chunk = width // 4
    rows_x.start()
    loads = [keep(src, dst, wsem.at[n]) for n, (src, dst) in enumerate(((d_in, dn), (g_in, g), (u_in, u)))]

    def tile(i):
        return span(number(i // 2, i % 2) * rows, rows)

    def og_load(i):
        return pltpu.make_async_copy(og_in.at[:, tile(i), :], og_t.at[i % 2], ogsem.at[i % 2])

    def x_load(i):
        return pltpu.make_async_copy(x_out.at[:, tile(i), :], x_t, xsem.at[0])

    def act_store(i):
        return pltpu.make_async_copy(act_t.at[i % 2], act_out.at[:, :, tile(i), :], actsem.at[i % 2])

    def dgp_send(i):
        to = place(here.zd(i // 2), (here.x + i % 2) % 2, here.y, here.c)
        return remote(dgp_t.at[i], dgp_got.at[here.f], psem.at[i], rsem.at[here.f], to)

    def both(step, j):
        for each in sums:
            getattr(each, step)(j)

    early = {
        2: lambda: (rows_x.relay(1), rows_x.spread(1)),
        4: lambda: (rows_x.cross(0),),
        6: lambda: (rows_x.relay(2), rows_x.spread(2)),
        7: lambda: (rows_x.cross(1), rows_x.close(0)),
    }
    before = {
        1: lambda: (rows_x.relay(3), rows_x.spread(3), rows_x.arrived(0, 1)),
        2: lambda: (rows_x.arrived(1, 0), rows_x.arrived(1, 1)),
        3: lambda: (both("corner", 0),),
        4: lambda: (rows_x.arrived(2, 0), rows_x.arrived(2, 1)),
        5: lambda: (both("sides", 0), both("corner", 1)),
        6: lambda: (rows_x.arrived(3, 0), rows_x.arrived(3, 1)),
        7: lambda: (both("sides", 1), both("corner", 2), both("centre", 0)),
    }
    middle = {
        1: lambda: (rows_x.cross(2), rows_x.close(1)),
        2: lambda: (rows_x.cross(3), rows_x.close(2)),
        3: lambda: (rows_x.close(3),),
    }

    def hooks(table, i):
        for key, run in table.items():
            @pl.when(i == key)
            def _(run=run):
                run()

    row = lax.broadcasted_iota(jnp.int32, (lanes, hidden), 0)
    col = lax.broadcasted_iota(jnp.int32, (lanes, hidden), 1)
    spread = jnp.where(row == here.f * experts + col // per, 1.0, 0.0).astype(LOW)
    row8 = lax.broadcasted_iota(jnp.int32, (8, hidden), 0)
    col8 = lax.broadcasted_iota(jnp.int32, (8, hidden), 1)
    gather8 = jnp.where(row8 == col8 // per, 1.0, 0.0).astype(LOW)

    def first_half(i):
        x_tile = x_t[...].reshape(tokens, width)
        for n, right in enumerate((g, u)):
            for k in range(hidden // part):
                stage[n, pl.ds(k * tokens, tokens), :] = dot_nt(x_tile, right[pl.ds(k * part, part), :])
        logits = dot_nt(router[...], x_tile)
        named_ids = jnp.concatenate([ids[m, :, tile(i)] for m in range(count)], axis=1)
        lane = lax.broadcasted_iota(jnp.int32, logits.shape, 0)
        named = lane == named_ids[0:1, :]
        for k in range(1, named_ids.shape[0]):
            named = named | (lane == named_ids[k : k + 1, :])
        masked = jnp.where(named, logits, masked_score)
        terms = jnp.where(named, jnp.exp(masked - jnp.max(masked, axis=0, keepdims=True)), 0.0)
        probs = terms / jnp.sum(terms, axis=0, keepdims=True)
        high = probs.astype(LOW)
        low = (probs - high.astype(F32)).astype(LOW)
        share_s[...] = dot_tn(high, spread) + dot_tn(low, spread)
        return probs

    def between(i, m):
        r = pl.ds(m * rows, rows)
        gate, up = (
            jnp.concatenate([stage[n, pl.ds(k * tokens + m * rows, rows), :] for k in range(hidden // part)], axis=1)
            for n in range(2)
        )
        raw = raw_s[i, r, :].astype(F32)
        share = share_s[r, :]
        sig = 1.0 / (1.0 + jnp.exp(-gate))
        silu = gate * sig
        inner = silu * up
        product = inner * raw
        product_high = product.astype(LOW)
        product_low = (product - product_high.astype(F32)).astype(LOW)
        dgp_t[i, :, r] = dot_nt(gather8, product_high) + dot_nt(gather8, product_low)
        d_inner = raw * share
        act_t[i % 2, 0, m] = (d_inner * up * (sig + silu * (1.0 - sig))).astype(LOW)
        act_t[i % 2, 1, m] = (d_inner * silu).astype(LOW)
        act_t[i % 2, 2, m] = (inner * share).astype(LOW)

    def second_half(i, q):
        d_gate, d_up, weighted = (act_t[i % 2, n].reshape(tokens, hidden) for n in range(3))
        cols = pl.ds(q * chunk, chunk)
        got = dot_nn(d_gate, g[:, cols]) + dot_nn(d_up, u[:, cols])
        dx[:, tile(i), cols] = got.astype(LOW).reshape(count, rows, chunk)
        out[:, tile(i), cols] = dot_nn(weighted, dn[:, cols]).astype(LOW).reshape(count, rows, chunk)

    def sent(i):
        for each in sums:
            each.give(i // 2, i % 2)

        @pl.when(i > 0)
        def _():
            dgp_send(i).start()

    og_load(0).start()
    loads[0].wait()

    @pl.loop(0, 8)
    def _(i):
        @pl.when(i + 1 < 8)
        def _():
            og_load(i + 1).start()

        hooks(early, i)
        og_load(i).wait()
        raw_s[i] = dot_nt(og_t[i % 2].reshape(tokens, width), dn[...]).astype(LOW)

    loads[1].wait()
    loads[2].wait()
    rows_x.arrived(0, 0)
    probs_out[...] = first_half(0)
    for m in range(count):
        between(0, m)
    act_store(0).start()

    @pl.loop(1, 8)
    def _(i):
        hooks(before, i)
        x_load(i).start()

        @pl.when(i >= 2)
        def _():
            act_store(i - 2).wait()

        x_load(i).wait()
        first_half(i)
        hooks(middle, i)
        for m in range(count):
            second_half(i - 1, 2 * m)
            between(i, m)
            second_half(i - 1, 2 * m + 1)
        act_store(i).start()
        sent(i - 1)

    for q in range(4):
        second_half(7, q)
    sent(7)
    both("corner", 3)
    both("sides", 2)
    both("centre", 1)
    both("sides", 3)
    both("centre", 2)
    both("centre", 3)
    for d in range(4):
        for e in range(2):
            if d or e:
                n = number(d, e)
                wait_for(dgp_got.at[n], rsem.at[n], here.xn)
                dgp_all[n] = dgp_got[n]
    dgp_all[here.f] = dgp_t[0]
    first = push(dgp_all, dgp_c, tsem.at[0], usem.at[0], here.cn)
    sums[0].total()
    wait_for(dgp_c, usem.at[0], here.cn)
    first.wait_send()
    dgp_all[...] = dgp_all[...] + dgp_c[...]
    second = push(dgp_all, dgp_y, tsem.at[1], usem.at[1], here.yn)
    sums[0].share_start()
    sums[1].total()
    sums[1].share_start()
    sums[0].share_cross()
    sums[1].share_cross()
    sums[0].share_end(dx_sum)
    sums[1].share_end(out_sum)
    wait_for(dgp_y, usem.at[1], here.yn)
    dgp_out[...] = dgp_all[...] + dgp_y[...]
    second.wait_send()
    act_store(6).wait()
    act_store(7).wait()
    for i in range(1, 8):
        dgp_send(i).wait_send()
    rows_x.finish()
    for each in sums:
        each.finish()


def run_experts(expert_in, og, ids, router, gate, up, down):
    count, rows, width = expert_in.shape
    seq = rows * 8
    experts, per, _ = gate.shape
    hidden = experts * per
    tokens = count * rows
    lanes = router.shape[0]
    vm = pltpu.VMEM
    dma = pltpu.SemaphoreType.DMA
    hbm = pl.BlockSpec(memory_space=pl.ANY)
    near = pl.BlockSpec(memory_space=pltpu.VMEM)
    shape = jax.ShapeDtypeStruct
    total = Sum.scratch(count, rows, width, LOW, rows // 2)
    return pl.pallas_call(
        functools.partial(experts_kernel, experts),
        out_shape=(
            shape((count, seq, width), LOW),
            shape((3, count, seq, hidden), LOW),
            shape((count, rows, width), LOW),
            shape((count, rows, width), LOW),
            shape((lanes, tokens), F32),
            shape((8, 8, tokens), F32),
        ),
        in_specs=[hbm, hbm, near, near, hbm, hbm, hbm],
        out_specs=[hbm, hbm, hbm, hbm, near, near],
        scratch_shapes=[
            vm((count, rows, width), LOW),
            vm((hidden, width), LOW),
            vm((hidden, width), LOW),
            vm((hidden, width), LOW),
            vm((2, count, rows, width), LOW),
            vm((8, tokens, hidden), LOW),
            vm((2, 3, count, rows, hidden), LOW),
            vm((count, seq, width), LOW),
            vm((count, seq, width), LOW),
            vm((2, hidden // 256 * tokens, 256), F32),
            vm((tokens, hidden), F32),
            vm((8, 8, tokens), F32),
            vm((8, 8, tokens), F32),
            vm((8, 8, tokens), F32),
            vm((8, 8, tokens), F32),
            vm((8, 8, tokens), F32),
            dma((3,)),
            dma((2,)),
            dma((1,)),
            dma((2,)),
            dma((8,)),
            dma((8,)),
            dma((2,)),
            dma((2,)),
        ]
        + Gather.scratch()
        + total
        + total,
        compiler_params=pltpu.CompilerParams(
            collective_id=6, has_side_effects=True, vmem_limit_bytes=VMEM_LIMIT
        ),
        name="experts",
    )(expert_in, og, ids, router, gate.reshape(hidden, width), up.reshape(hidden, width), down.reshape(hidden, width))


def expert_grads_kernel(act, x, og, dg, du, dd):
    tokens = act.shape[1] * act.shape[2]
    x_cols = x[...].reshape(tokens, x.shape[2])
    og_cols = og[...].reshape(tokens, og.shape[2])
    for n, (right, out) in enumerate(((x_cols, dg), (x_cols, du), (og_cols, dd))):
        out[...] = dot_tn(act[n].reshape(tokens, act.shape[3]), right)


def expert_grads(act, x, og):
    _, count, seq, hidden = act.shape
    width = x.shape[2]
    block = min(512, width)
    cols = pl.BlockSpec((count, seq, block), lambda i: (0, 0, i))
    out = pl.BlockSpec((hidden, block), lambda i: (0, i))
    grads = jax.ShapeDtypeStruct((hidden, width), F32)
    return pl.pallas_call(
        expert_grads_kernel,
        grid=(width // block,),
        in_specs=[
            pl.BlockSpec(act.shape, lambda i: (0, 0, 0, 0), pipeline_mode=pl.Buffered(1)),
            cols,
            cols,
        ],
        out_specs=[out, out, out],
        out_shape=(grads, grads, grads),
        compiler_params=pltpu.CompilerParams(vmem_limit_bytes=VMEM_LIMIT),
        name="expert_grads",
    )(act, x, og)


PEERS = tuple((d, e) for d in (2, 1, 3, 0) for e in (1, 0) if d or e)


def end_kernel(heads, d_branch, xn_in, w_in, wo_in, pre_in, qkv_in, prob_in, ctx_in, aux, query, key, value,
               cos_ref, sin_ref, qg_ref, kg_ref,
               dn_sum, dq_out, dk_out, dv_out, do_out, aux_out, gains_out,
               db, xn, w, wo, pre, qkv, prob, ctx, dctx, dq_s, dk_s, dv_s, dqkv, dwo, dw, dwo_got, dwq_got, kv_x, kv_z,
               aux_got, head_part, head_got, line, line_c, line_y, wide_q, wide_o, wide_kv,
               lsem, psem, rsem, kxs, kxr, kzs, kzr, tsem, usem, osem, *rest):
    here = Here()
    here.greet()
    sends, outs = [], []
    rows_db = Gather(here, False, d_branch, db, rest[: Gather.slots], BY_X)
    at = Gather.slots
    dn = Sum(here, False, db, rest[at:], BY_X)
    rows = dn.rows
    piece, part = query.shape[0], wo.shape[1]
    seq = xn.shape[1]
    hd = cos_ref.shape[1]
    tile = 256
    scale = 1.0 / math.sqrt(hd)

    def number(d, e):
        return 2 * here.zr(d) + (here.x + e) % 2

    def send(n, d, e, src, got):
        sends.append(push(src, got.at[(4 - d) % 4, e], psem.at[n, d, e], rsem.at[n, (4 - d) % 4, e], here.peer(d, e)))

    def got_from(n, d, e, got):
        wait_for(got.at[d, e], rsem.at[n, d, e], here.xn)
        return got[d, e]

    rows_db.start()
    loads = {}
    for n, (src, dst) in enumerate(((wo_in, wo), (ctx_in, ctx), (qkv_in, qkv), (prob_in, prob), (pre_in, pre),
                                    (xn_in, xn), (w_in, w))):
        loads[n] = keep(src, dst, lsem.at[n])
    for d, e in PEERS:
        send(0, d, e, aux.at[number(d, e)], aux_got)
    rows_db.first_steps()
    rows_db.last_steps()
    for d in (0,) + ORDER:
        rows_db.arrived(d, 0)
        rows_db.arrived(d, 1)
    for n in range(7):
        loads[n].wait()

    for i in range(seq // tile):
        r = pl.ds(i * tile, tile)
        dctx[r, :] = dot_nn(db[0, r, :], wo[...]).astype(LOW)
    for d, e in PEERS + ((0, 0),):
        r = span(number(d, e) * piece, piece)
        dwo[r, :] = dot_tn(db[0, :, r], ctx[...]).astype(LOW)
        if d or e:
            send(1, d, e, dwo.at[r, :], dwo_got)
    dk_s[...] = jnp.zeros_like(dk_s)
    dv_s[...] = jnp.zeros_like(dv_s)
    for a in range(heads):
        for i in range(seq // tile):
            r = pl.ds(i * tile, tile)
            n = (i + 1) * tile
            q_tile = qkv[r, pl.ds(a * hd, hd)]
            k_rows = qkv[pl.ds(0, n), pl.ds(heads * hd, hd)]
            v_rows = qkv[pl.ds(0, n), pl.ds((heads + 1) * hd, hd)]
            up = dctx[r, pl.ds(a * hd, hd)]
            low = prob[a, r, pl.ds(0, n)]
            wide = low.astype(F32)
            dprob = dot_nt(up, v_rows)
            delta = jnp.sum(wide * dprob, axis=-1, keepdims=True)
            dscore = (wide * (dprob - delta)).astype(LOW)
            dq_s[r, pl.ds(a * hd, hd)] = dot_nn(dscore, k_rows) * scale
            dk_s[pl.ds(0, n), :] += dot_tn(dscore, q_tile) * scale
            dv_s[pl.ds(0, n), :] += dot_tn(low, up)
    gq = jnp.zeros((1, hd), F32)
    gk = jnp.zeros((1, hd), F32)
    for i in range(seq // tile):
        r = pl.ds(i * tile, tile)
        dqkv[r, pl.ds((heads + 1) * hd, hd)] = dv_s[r, :].astype(LOW)
        for a in range(heads + 1):
            up = dq_s[r, pl.ds(a * hd, hd)] if a < heads else dk_s[r, :]
            one = pre[r, pl.ds(a * hd, hd)]
            factor = lax.rsqrt(jnp.mean(one * one, axis=-1, keepdims=True) + norm_eps)
            hat = one * factor
            turned = up * cos_ref[r, :] + pltpu.roll(up * sin_ref[r, :], hd // 2, 1)
            gain_part = jnp.sum(turned * hat, axis=0, keepdims=True)
            gained = turned * (qg_ref if a < heads else kg_ref)[...]
            back = factor * (gained - hat * jnp.mean(gained * hat, axis=-1, keepdims=True))
            dqkv[r, pl.ds(a * hd, hd)] = back.astype(LOW)
            if a < heads:
                gq = gq + gain_part
            else:
                gk = gk + gain_part
    head_part[...] = jnp.concatenate([gq, gk, jnp.zeros((6, hd), F32)], axis=0)
    for d, e in PEERS:
        send(3, d, e, head_part, head_got)
    rows_db.finish()
    for e in (1, 0):
        for d in FAR_FIRST:
            r = span(here.number(d, e) * rows, rows)
            db[0, r, :] = dot_nt(dqkv[r, :], w[...]).astype(LOW)
            dn.give(d, e)
    for d, e in PEERS + ((0, 0),):
        r = span(number(d, e) * piece, piece)
        dw[r, :] = dot_tn(xn[0, :, r], dqkv[...]).astype(LOW)
        if d or e:
            send(2, d, e, dw.at[r, pl.ds(0, part)], dwq_got)
        if e:
            sends.append(push(dw.at[r, pl.ds(part, 2 * hd)], kv_x.at[d], kxs.at[d], kxr.at[d], here.xn))
    for d in FAR_FIRST:
        dn.corner(d)
    for d in (2, 1, 3, 0):
        r = span(number(d, 0) * piece, piece)
        wait_for(kv_x.at[d], kxr.at[d], here.xn)
        both = dw[r, pl.ds(part, 2 * hd)].astype(F32) + kv_x[d].astype(F32)
        dw[r, pl.ds(part, 2 * hd)] = both.astype(LOW)
        if d:
            there = (4 - d) % 4
            sends.append(push(dw.at[r, pl.ds(part, 2 * hd)], kv_z.at[there], kzs.at[d], kzr.at[there], here.peer(d, 0)))
    for d in FAR_FIRST:
        dn.sides(d)
    for d in FAR_FIRST:
        dn.centre(d)

    def merged(n, wide, got, mine):
        for d in (0, 1):
            for e in (0, 1):
                first = mine if (d, e) == (0, 0) else got_from(n, d, e, got)
                both = first.astype(F32) + got_from(n, d + 2, e, got).astype(F32)
                wide[:, span((number(d, e) % 4) * part, part)] = both

    own = span(here.f * piece, piece)
    merged(1, wide_o, dwo_got, dwo[own, :])
    outs.append(keep(wide_o, do_out, osem.at[0]))
    aux_total = aux[here.f].astype(F32)
    for d, e in PEERS:
        aux_total = aux_total + got_from(0, d, e, aux_got).astype(F32)
    aux_out[...] = aux_total
    head_total = head_part[...]
    for d, e in PEERS:
        head_total = head_total + got_from(3, d, e, head_got)
    line[:, pl.ds(piece, hd)] = head_total
    dn.total()
    dn.share(dn_sum)
    merged(2, wide_q, dwq_got, dw[own, pl.ds(0, part)])
    outs.append(keep(wide_q, dq_out, osem.at[1]))
    kv = dw[own, pl.ds(part, 2 * hd)].astype(F32)
    for d in (1, 2, 3):
        wait_for(kv_z.at[d], kzr.at[d], here.xn)
        kv = kv + kv_z[d].astype(F32)
    wide_kv[...] = kv
    outs.append(keep(wide_kv.at[:, pl.ds(0, hd)], dk_out, osem.at[2]))
    outs.append(keep(wide_kv.at[:, pl.ds(hd, hd)], dv_out, osem.at[3]))

    def row_sums(product):
        high = product.astype(LOW)
        rest_ = (product - high.astype(F32)).astype(LOW)
        ones = jnp.ones((8, product.shape[1]), LOW)
        return dot_nt(ones, high) + dot_nt(ones, rest_)

    line[:, pl.ds(0, piece)] = (
        row_sums(query[...].astype(F32) * wide_q[...])
        + row_sums(key[...].astype(F32) * kv[:, :hd])
        + row_sums(value[...].astype(F32) * kv[:, hd:])
    )
    first = push(line, line_c, tsem.at[0], usem.at[0], here.cn)
    wait_for(line_c, usem.at[0], here.cn)
    first.wait_send()
    line[...] = line[...] + line_c[...]
    second = push(line, line_y, tsem.at[1], usem.at[1], here.yn)
    wait_for(line_y, usem.at[1], here.yn)
    gains_out[...] = line[...] + line_y[...]
    second.wait_send()
    dn.finish()
    for copy in sends:
        copy.wait_send()
    for copy in outs:
        copy.wait()


def end(d_branch, xn, w, wo, pre, qkv, prob, ctx, aux, query, key, value, cosine, sine, query_gain, key_gain):
    count, rows, width = d_branch.shape
    seq = rows * 8
    hd = query_gain.shape[0]
    piece, local = query.shape
    part = local // 4
    heads = part // hd
    vm = pltpu.VMEM
    dma = pltpu.SemaphoreType.DMA
    hbm = pl.BlockSpec(memory_space=pl.ANY)
    near = pl.BlockSpec(memory_space=pltpu.VMEM)
    shape = jax.ShapeDtypeStruct
    return pl.pallas_call(
        functools.partial(end_kernel, heads),
        out_shape=(
            shape((count, rows, width), LOW),
            shape((piece, local), F32),
            shape((piece, hd), F32),
            shape((piece, hd), F32),
            shape((piece, local), F32),
            shape(aux.shape[1:], F32),
            shape((8, piece + hd), F32),
        ),
        in_specs=[hbm] * 8 + [near] * 8,
        out_specs=[hbm] * 5 + [near] * 2,
        scratch_shapes=[
            vm((1, seq, width), LOW),
            vm((1, seq, width), LOW),
            vm(w.shape, LOW),
            vm(wo.shape, LOW),
            vm(pre.shape, F32),
            vm(qkv.shape, LOW),
            vm(prob.shape, LOW),
            vm(ctx.shape, LOW),
            vm(ctx.shape, LOW),
            vm((seq, heads * hd), F32),
            vm((seq, hd), F32),
            vm((seq, hd), F32),
            vm((seq, (heads + 2) * hd), LOW),
            vm((width, part), LOW),
            vm((width, part + 2 * hd), LOW),
            vm((4, 2, piece, part), LOW),
            vm((4, 2, piece, part), LOW),
            vm((4, piece, 2 * hd), LOW),
            vm((4, piece, 2 * hd), LOW),
            vm((4, 2) + aux.shape[1:], LOW),
            vm((8, hd), F32),
            vm((4, 2, 8, hd), F32),
            vm((8, piece + hd), F32),
            vm((8, piece + hd), F32),
            vm((8, piece + hd), F32),
            vm((piece, local), F32),
            vm((piece, local), F32),
            vm((piece, 2 * hd), F32),
            dma((7,)),
            dma((4, 4, 2)),
            dma((4, 4, 2)),
            dma((4,)),
            dma((4,)),
            dma((4,)),
            dma((4,)),
            dma((2,)),
            dma((2,)),
            dma((4,)),
        ]
        + Gather.scratch()
        + Sum.scratch(1, rows, width, LOW, BY_X),
        compiler_params=pltpu.CompilerParams(
            collective_id=5, has_side_effects=True, vmem_limit_bytes=VMEM_LIMIT
        ),
        name="end",
    )(d_branch, xn, w, wo, pre, qkv, prob, ctx, aux, query, key, value, cosine, sine,
      query_gain[None], key_gain[None])


def rotate_half(values):
    middle = values.shape[-1] // 2
    return jnp.concatenate([-values[..., middle:], values[..., :middle]], axis=-1)


def rope_tables(positions, head_width):
    middle = head_width // 2
    frequency = rope_base ** (-jnp.arange(middle, dtype=jnp.float32) * 2.0 / head_width)
    angles = positions.astype(jnp.float32)[:, None] * frequency[None, :]
    angles = jnp.concatenate([angles, angles], axis=1)
    return (jnp.cos(angles), jnp.sin(angles))


def norm_parts(values):
    factor = lax.rsqrt(jnp.mean(values * values, axis=-1, keepdims=True) + norm_eps)
    return (values * factor, factor)


def norm_back(upstream, gain, normal, factor):
    scaled = upstream * gain
    return factor * (scaled - normal * jnp.mean(scaled * normal, axis=-1, keepdims=True))


def head_back(upstream, cosine_heads, sine_heads, gain, normal, factor):
    turned = upstream * cosine_heads - rotate_half(upstream * sine_heads)
    gain_part = jnp.sum(turned * normal, axis=(0, 1))
    return (norm_back(turned, gain, normal, factor), gain_part)


def fetch_weights(query_weight, key_weight, value_weight, output_weight, router_weight):
    return (
        lax.all_gather(query_weight, "fsdp", axis=0, tiled=True),
        lax.all_gather(key_weight, "fsdp", axis=0, tiled=True),
        lax.all_gather(value_weight, "fsdp", axis=0, tiled=True),
        lax.all_gather(output_weight, "fsdp", axis=0, tiled=True),
        lax.all_gather(router_weight, "fsdp", axis=0, tiled=True),
    )


def widen(summed):
    return lax.all_gather(summed, "tp", axis=3, tiled=True)


def carry_back(summed):
    return lax.all_to_all(summed, "fsdp", split_axis=0, concat_axis=0, tiled=True)


def send_home(summed):
    arrived_home = carry_back(widen(summed))
    return arrived_home


def general_device(
    tokens,
    cotangent,
    expert_ids,
    attention_gain,
    query_gain,
    key_gain,
    query_weight,
    key_weight,
    value_weight,
    output_weight,
    expert_gain,
    router_weight,
    gate_weight,
    up_weight,
    down_weight,
):
    micro_count = tokens.shape[0]
    tok_rows = tokens.shape[1]
    width = tokens.shape[2]
    route_count = expert_ids.shape[2]
    head_dim = query_gain.shape[0]
    local_heads = query_weight.shape[1] // head_dim
    local_groups = key_weight.shape[1] // head_dim
    group_size = local_heads // local_groups
    fsdp_count = lax.axis_size("fsdp")
    seq_len = tok_rows * fsdp_count
    experts_here = gate_weight.shape[0]
    expert_count = experts_here * fsdp_count
    capacity = max(2, 5 * tok_rows * route_count // (4 * expert_count))
    key_block = math.gcd(seq_len, 512)
    score_scale = 1.0 / math.sqrt(head_dim)
    query_count = tok_rows * group_size
    routed_total = tok_rows * route_count
    start_row = lax.axis_index("fsdp") * tok_rows
    positions = start_row + jnp.arange(tok_rows, dtype=jnp.int32)
    cosine_table, sine_table = rope_tables(positions, head_dim)
    cosine_heads = cosine_table[:, None, :]
    sine_heads = sine_table[:, None, :]
    query_pos = start_row + jnp.arange(query_count, dtype=jnp.int32) // group_size
    block_total = (start_row + tok_rows + key_block - 1) // key_block
    expert_range = jnp.arange(expert_count, dtype=jnp.int32)
    zero_row = jnp.zeros((1, width), jnp.bfloat16)

    def to_rows(tensor):
        return (
            tensor.reshape(tok_rows, local_groups, group_size, head_dim)
            .transpose(1, 0, 2, 3)
            .reshape(local_groups, query_count, head_dim)
        )

    def from_rows(tensor):
        return (
            tensor.reshape(local_groups, tok_rows, group_size, head_dim)
            .transpose(1, 0, 2, 3)
            .reshape(tok_rows, local_heads, head_dim)
        )

    acc_attention_gain = jnp.zeros((width,), jnp.float32)
    acc_head_gains = jnp.zeros((2, head_dim), jnp.float32)
    acc_query = jnp.zeros((width, local_heads * head_dim), jnp.float32)
    acc_key = jnp.zeros((width, local_groups * head_dim), jnp.float32)
    acc_value = jnp.zeros((width, local_groups * head_dim), jnp.float32)
    acc_output = jnp.zeros((width, local_heads * head_dim), jnp.float32)
    acc_expert_gain = jnp.zeros((width,), jnp.float32)
    acc_router = jnp.zeros((width, expert_count), jnp.float32)
    acc_gate = jnp.zeros(gate_weight.shape, jnp.float32)
    acc_up = jnp.zeros(up_weight.shape, jnp.float32)
    acc_down = jnp.zeros(down_weight.shape, jnp.float32)
    layer_rows = []
    input_rows = []
    for micro_index in range(micro_count):
        inputs = tokens[micro_index].astype(jnp.float32)
        query_full, key_full, value_full, output_full, router_full = fetch_weights(
            query_weight, key_weight, value_weight, output_weight, router_weight
        )
        input_hat, attention_factor = norm_parts(inputs)
        normed = (input_hat * attention_gain).astype(jnp.bfloat16)
        query_pre = jnp.dot(normed, query_full, preferred_element_type=jnp.float32).reshape(
            tok_rows, local_heads, head_dim
        )
        key_pre = jnp.dot(normed, key_full, preferred_element_type=jnp.float32).reshape(
            tok_rows, local_groups, head_dim
        )
        value_low = jnp.dot(normed, value_full, preferred_element_type=jnp.float32).astype(
            jnp.bfloat16
        )
        query_hat, query_factor = norm_parts(query_pre)
        key_hat, key_factor = norm_parts(key_pre)
        query_scaled = query_hat * query_gain
        key_scaled = key_hat * key_gain
        query_low = (query_scaled * cosine_heads + rotate_half(query_scaled) * sine_heads).astype(
            jnp.bfloat16
        )
        key_low = (key_scaled * cosine_heads + rotate_half(key_scaled) * sine_heads).astype(
            jnp.bfloat16
        )
        key_all, value_all = (
            lax.all_gather(
                key_low.reshape(tok_rows, local_groups * head_dim), "fsdp", axis=0, tiled=True
            ),
            lax.all_gather(value_low, "fsdp", axis=0, tiled=True),
        )
        key_heads = key_all.reshape(seq_len, local_groups, head_dim).transpose(1, 0, 2)
        value_heads = value_all.reshape(seq_len, local_groups, head_dim).transpose(1, 0, 2)
        query_rows = to_rows(query_low)

        def scores_at(block_index):
            block_start = block_index * key_block
            key_slice = lax.dynamic_slice_in_dim(key_heads, block_start, key_block, 1)
            raw_scores = (
                jnp.einsum(
                    "gqd,gkd->gqk", query_rows, key_slice, preferred_element_type=jnp.float32
                )
                * score_scale
            )
            allowed = (block_start + jnp.arange(key_block, dtype=jnp.int32))[None, :] <= query_pos[
                :, None
            ]
            return (jnp.where(allowed[None], raw_scores, masked_score), allowed, block_start)

        def stats_step(block_index, carried):
            run_peak, run_total = carried
            scores, allowed, block_start = scores_at(block_index)
            new_peak = jnp.maximum(run_peak, jnp.max(scores, axis=-1))
            terms = jnp.where(allowed[None], jnp.exp(scores - new_peak[..., None]), 0.0)
            return (new_peak, run_total * jnp.exp(run_peak - new_peak) + jnp.sum(terms, axis=-1))

        start_stats = (
            jnp.full((local_groups, query_count), masked_score, jnp.float32),
            jnp.zeros((local_groups, query_count), jnp.float32),
        )
        run_peak, run_total = lax.fori_loop(0, block_total, stats_step, start_stats)
        log_total = run_peak + jnp.log(run_total)

        def value_step(block_index, acc_context):
            scores, allowed, block_start = scores_at(block_index)
            probs_low = jnp.where(
                allowed[None], jnp.exp(scores - log_total[..., None]), 0.0
            ).astype(jnp.bfloat16)
            value_slice = lax.dynamic_slice_in_dim(value_heads, block_start, key_block, 1)
            return acc_context + jnp.einsum(
                "gqk,gkd->gqd", probs_low, value_slice, preferred_element_type=jnp.float32
            )

        context_rows = lax.fori_loop(
            0,
            block_total,
            value_step,
            jnp.zeros((local_groups, query_count, head_dim), jnp.float32),
        )
        context_low = (
            from_rows(context_rows).reshape(tok_rows, local_heads * head_dim).astype(jnp.bfloat16)
        )
        branch_part = jnp.einsum(
            "th,dh->td", context_low, output_full, preferred_element_type=jnp.float32
        )
        resid = inputs + lax.psum(branch_part.astype(jnp.bfloat16), "tp").astype(jnp.float32)
        resid_hat, expert_factor = norm_parts(resid)
        expert_in = (resid_hat * expert_gain).astype(jnp.bfloat16)
        logits = jnp.dot(expert_in, router_full, preferred_element_type=jnp.float32)
        routes_now = expert_ids[micro_index]
        choose = (routes_now[:, :, None] == expert_range[None, None, :]).astype(jnp.float32)
        picked = jnp.sum(choose * logits[:, None, :], axis=-1)
        shifted = jnp.exp(picked - jnp.max(picked, axis=-1, keepdims=True))
        gate_probs = shifted / jnp.sum(shifted, axis=-1, keepdims=True)
        flat_routes = routes_now.reshape(-1)
        onehot = (flat_routes[:, None] == expert_range[None, :]).astype(jnp.int32)
        rank_in = jnp.sum((jnp.cumsum(onehot, axis=0) - onehot) * onehot, axis=1)
        slot_index = flat_routes * capacity + rank_in
        slot_source = (
            jnp.full((expert_count * capacity,), routed_total, jnp.int32)
            .at[slot_index]
            .set(jnp.arange(routed_total, dtype=jnp.int32))
        )
        padded_in = jnp.concatenate([expert_in, zero_row], axis=0)
        outgoing = padded_in[slot_source // route_count].reshape(
            fsdp_count, experts_here, capacity, width
        )
        arrived = lax.all_to_all(outgoing, "fsdp", split_axis=0, concat_axis=0, tiled=True)
        gate_pre = jnp.einsum(
            "secd,efd->secf", arrived, gate_weight, preferred_element_type=jnp.float32
        )
        up_pre = jnp.einsum(
            "secd,efd->secf", arrived, up_weight, preferred_element_type=jnp.float32
        )
        gate_sigmoid = jax.nn.sigmoid(gate_pre)
        inner_low = (gate_pre * gate_sigmoid * up_pre).astype(jnp.bfloat16)
        result_part = jnp.einsum(
            "secf,efd->secd", inner_low, down_weight, preferred_element_type=jnp.float32
        )
        result_low = lax.psum_scatter(
            result_part.astype(jnp.bfloat16), "tp", scatter_dimension=3, tiled=True
        )
        result_home = send_home(result_low)
        routed = (
            result_home.reshape(expert_count * capacity, width)[slot_index]
            .astype(jnp.float32)
            .reshape(tok_rows, route_count, width)
        )
        layer_rows.append(
            (resid + jnp.sum(gate_probs[:, :, None] * routed, axis=1)).astype(jnp.bfloat16)
        )
        query_full, key_full, value_full, output_full, router_full = fetch_weights(
            query_weight, key_weight, value_weight, output_weight, router_weight
        )
        out_grad = cotangent[micro_index].astype(jnp.float32)
        d_route = (
            (gate_probs[:, :, None] * out_grad[:, None, :])
            .astype(jnp.bfloat16)
            .reshape(routed_total, width)
        )
        d_gate_probs = jnp.sum(out_grad[:, None, :] * routed, axis=-1)
        d_pick = gate_probs * (
            d_gate_probs - jnp.sum(gate_probs * d_gate_probs, axis=-1, keepdims=True)
        )
        d_logits = jnp.sum(choose * d_pick[:, :, None], axis=1).astype(jnp.bfloat16)
        grad_outgoing = jnp.concatenate([d_route, zero_row], axis=0)[slot_source].reshape(
            fsdp_count, experts_here, capacity, width
        )
        grad_arrived = lax.all_to_all(
            grad_outgoing, "fsdp", split_axis=0, concat_axis=0, tiled=True
        )
        d_inner = jnp.einsum(
            "secd,efd->secf", grad_arrived, down_weight, preferred_element_type=jnp.float32
        )
        acc_down = acc_down + jnp.einsum(
            "secf,secd->efd", inner_low, grad_arrived, preferred_element_type=jnp.float32
        )
        d_gate_low = (
            d_inner * up_pre * gate_sigmoid * (1.0 + gate_pre * (1.0 - gate_sigmoid))
        ).astype(jnp.bfloat16)
        d_up_low = (d_inner * gate_pre * gate_sigmoid).astype(jnp.bfloat16)
        acc_gate = acc_gate + jnp.einsum(
            "secf,secd->efd", d_gate_low, arrived, preferred_element_type=jnp.float32
        )
        acc_up = acc_up + jnp.einsum(
            "secf,secd->efd", d_up_low, arrived, preferred_element_type=jnp.float32
        )
        d_copy_part = jnp.einsum(
            "secf,efd->secd", d_gate_low, gate_weight, preferred_element_type=jnp.float32
        ) + jnp.einsum("secf,efd->secd", d_up_low, up_weight, preferred_element_type=jnp.float32)
        d_copy_low = lax.psum_scatter(
            d_copy_part.astype(jnp.bfloat16), "tp", scatter_dimension=3, tiled=True
        )
        d_copy_home = send_home(d_copy_low)
        d_copies = (
            d_copy_home.reshape(expert_count * capacity, width)[slot_index]
            .astype(jnp.float32)
            .reshape(tok_rows, route_count, width)
        )
        d_expert_in = jnp.sum(d_copies, axis=1) + jnp.dot(
            d_logits, router_full.T, preferred_element_type=jnp.float32
        )
        acc_router = acc_router + jnp.dot(expert_in.T, d_logits, preferred_element_type=jnp.float32)
        acc_expert_gain = acc_expert_gain + jnp.sum(d_expert_in * resid_hat, axis=0)
        d_resid = out_grad + norm_back(d_expert_in, expert_gain, resid_hat, expert_factor)
        d_branch = d_resid.astype(jnp.bfloat16)
        acc_output = acc_output + jnp.einsum(
            "td,th->dh", d_branch, context_low, preferred_element_type=jnp.float32
        )
        d_context = jnp.dot(d_branch, output_full, preferred_element_type=jnp.float32).astype(
            jnp.bfloat16
        )
        d_context_rows = to_rows(d_context.reshape(tok_rows, local_heads, head_dim))
        delta_rows = jnp.sum(d_context_rows.astype(jnp.float32) * context_rows, axis=-1)

        def grad_step(block_index, carried):
            d_query_rows, key_grads_all = carried
            scores, allowed, block_start = scores_at(block_index)
            probs = jnp.where(allowed[None], jnp.exp(scores - log_total[..., None]), 0.0)
            key_slice = lax.dynamic_slice_in_dim(key_heads, block_start, key_block, 1)
            value_slice = lax.dynamic_slice_in_dim(value_heads, block_start, key_block, 1)
            d_probs = jnp.einsum(
                "gqd,gkd->gqk", d_context_rows, value_slice, preferred_element_type=jnp.float32
            )
            d_scores = (probs * (d_probs - delta_rows[..., None])).astype(jnp.bfloat16)
            d_query_rows = (
                d_query_rows
                + jnp.einsum(
                    "gqk,gkd->gqd", d_scores, key_slice, preferred_element_type=jnp.float32
                )
                * score_scale
            )
            d_key_block = (
                jnp.einsum("gqk,gqd->kgd", d_scores, query_rows, preferred_element_type=jnp.float32)
                * score_scale
            )
            d_value_block = jnp.einsum(
                "gqk,gqd->kgd",
                probs.astype(jnp.bfloat16),
                d_context_rows,
                preferred_element_type=jnp.float32,
            )
            current = lax.dynamic_slice_in_dim(key_grads_all, block_start, key_block, 0)
            updated = current + jnp.concatenate([d_key_block, d_value_block], axis=-1)
            return (
                d_query_rows,
                lax.dynamic_update_slice_in_dim(key_grads_all, updated, block_start, 0),
            )

        start_grads = (
            jnp.zeros((local_groups, query_count, head_dim), jnp.float32),
            jnp.zeros((seq_len, local_groups, 2 * head_dim), jnp.float32),
        )
        d_query_rows, key_grads_all = lax.fori_loop(0, block_total, grad_step, start_grads)
        key_grads = (
            lax.psum_scatter(
                key_grads_all.reshape(seq_len, local_groups * 2 * head_dim).astype(jnp.bfloat16),
                "fsdp",
                scatter_dimension=0,
                tiled=True,
            )
            .astype(jnp.float32)
            .reshape(tok_rows, local_groups, 2 * head_dim)
        )
        d_value_low = (
            key_grads[..., head_dim:]
            .reshape(tok_rows, local_groups * head_dim)
            .astype(jnp.bfloat16)
        )
        d_key_pre, key_gain_part = head_back(
            key_grads[..., :head_dim], cosine_heads, sine_heads, key_gain, key_hat, key_factor
        )
        d_query_pre, query_gain_part = head_back(
            from_rows(d_query_rows), cosine_heads, sine_heads, query_gain, query_hat, query_factor
        )
        d_query_low = d_query_pre.astype(jnp.bfloat16).reshape(tok_rows, local_heads * head_dim)
        d_key_low = d_key_pre.astype(jnp.bfloat16).reshape(tok_rows, local_groups * head_dim)
        d_normed_part = jnp.dot(d_query_low, query_full.T, preferred_element_type=jnp.float32)
        d_normed_part = d_normed_part + jnp.dot(
            d_key_low, key_full.T, preferred_element_type=jnp.float32
        )
        d_normed_part = d_normed_part + jnp.dot(
            d_value_low, value_full.T, preferred_element_type=jnp.float32
        )
        acc_query = acc_query + jnp.dot(normed.T, d_query_low, preferred_element_type=jnp.float32)
        acc_key = acc_key + jnp.dot(normed.T, d_key_low, preferred_element_type=jnp.float32)
        acc_value = acc_value + jnp.dot(normed.T, d_value_low, preferred_element_type=jnp.float32)
        d_normed, head_gain_parts = (
            lax.psum(d_normed_part.astype(jnp.bfloat16), "tp").astype(jnp.float32),
            lax.psum(jnp.stack([query_gain_part, key_gain_part]).astype(jnp.bfloat16), "tp").astype(
                jnp.float32
            ),
        )
        acc_head_gains = acc_head_gains + head_gain_parts
        acc_attention_gain = acc_attention_gain + jnp.sum(d_normed * input_hat, axis=0)
        input_rows.append(
            (d_resid + norm_back(d_normed, attention_gain, input_hat, attention_factor)).astype(
                jnp.bfloat16
            )
        )
    summed = (
        lax.psum_scatter(
            acc_attention_gain.astype(jnp.bfloat16), "fsdp", scatter_dimension=0, tiled=True
        ).astype(jnp.float32),
        lax.psum_scatter(
            acc_head_gains[0].astype(jnp.bfloat16), "fsdp", scatter_dimension=0, tiled=True
        ).astype(jnp.float32),
        lax.psum_scatter(
            acc_head_gains[1].astype(jnp.bfloat16), "fsdp", scatter_dimension=0, tiled=True
        ).astype(jnp.float32),
        lax.psum_scatter(
            acc_query.astype(jnp.bfloat16), "fsdp", scatter_dimension=0, tiled=True
        ).astype(jnp.float32),
        lax.psum_scatter(
            acc_key.astype(jnp.bfloat16), "fsdp", scatter_dimension=0, tiled=True
        ).astype(jnp.float32),
        lax.psum_scatter(
            acc_value.astype(jnp.bfloat16), "fsdp", scatter_dimension=0, tiled=True
        ).astype(jnp.float32),
        lax.psum_scatter(
            acc_output.astype(jnp.bfloat16), "fsdp", scatter_dimension=0, tiled=True
        ).astype(jnp.float32),
        lax.psum_scatter(
            acc_expert_gain.astype(jnp.bfloat16), "fsdp", scatter_dimension=0, tiled=True
        ).astype(jnp.float32),
        lax.psum_scatter(
            acc_router.astype(jnp.bfloat16), "fsdp", scatter_dimension=0, tiled=True
        ).astype(jnp.float32),
    )
    return (
        jnp.stack(layer_rows),
        jnp.stack(input_rows),
        summed[0],
        summed[1],
        summed[2],
        summed[3],
        summed[4],
        summed[5],
        summed[6],
        summed[7],
        summed[8],
        acc_gate,
        acc_up,
        acc_down,
    )


def small_device(
    tokens,
    cotangent,
    expert_ids,
    attention_gain,
    query_gain,
    key_gain,
    query_weight,
    key_weight,
    value_weight,
    output_weight,
    expert_gain,
    router_weight,
    gate_weight,
    up_weight,
    down_weight,
):
    count, rows, width = tokens.shape
    hd = query_gain.shape[0]
    f = lax.axis_index("fsdp")
    n_fsdp = lax.axis_size("fsdp")
    seq = rows * n_fsdp
    experts = gate_weight.shape[0]
    expert_count = experts * n_fsdp
    piece = query_weight.shape[0]

    cosine, sine = signed_tables(seq, hd)
    inputs = tokens.astype(F32)
    input_hat, attention_factor = norm_parts(inputs)
    normed = (input_hat * attention_gain).astype(LOW)

    (normed_all, weights, output_pair, router_all, ids_all, grad_all, pre, qkv, prob, context, branch) = begin(
        normed,
        cotangent,
        query_weight,
        key_weight,
        value_weight,
        output_weight,
        router_weight.T,
        expert_ids.transpose(0, 2, 1),
        cosine,
        sine,
        query_gain,
        key_gain,
    )
    resid = inputs + branch.astype(F32)
    resid_hat, expert_factor = norm_parts(resid)
    expert_in = (resid_hat * expert_gain).astype(LOW)

    expert_all, act, dx_sum, out_sum, probs, dgp = run_experts(
        expert_in, grad_all, ids_all, router_all, gate_weight, up_weight, down_weight
    )
    layer_output = (resid + out_sum.astype(F32)).astype(LOW)
    dgp = dgp[:, :experts].reshape(expert_count, count * rows)
    d_logits = (probs * (dgp - jnp.sum(probs * dgp, axis=0, keepdims=True))).astype(LOW)
    d_expert_in = dx_sum.astype(F32) + lax.dot_general(
        d_logits, router_all, (((0,), (0,)), ((), ())), preferred_element_type=F32
    ).reshape(dx_sum.shape)
    router_part = jnp.dot(
        d_logits, expert_in.reshape(count * rows, width), preferred_element_type=F32
    )
    expert_gain_part = jnp.sum(d_expert_in * resid_hat, axis=(0, 1))
    out_grad = cotangent.astype(F32)
    d_resid = out_grad + norm_back(d_expert_in, expert_gain, resid_hat, expert_factor)
    d_branch = d_resid.astype(LOW)

    aux = jnp.concatenate(
        [
            router_part.reshape(expert_count, n_fsdp, piece).transpose(1, 0, 2),
            expert_gain_part.reshape(n_fsdp, 1, piece),
            jnp.zeros((n_fsdp, -(expert_count + 1) % 16, piece), F32),
        ],
        axis=1,
    ).astype(LOW)
    d_normed, d_query, d_key, d_value, d_output, aux_sum, line = end(
        d_branch,
        normed_all,
        weights,
        output_pair,
        pre,
        qkv,
        prob,
        context,
        aux,
        query_weight,
        key_weight,
        value_weight,
        cosine,
        sine,
        query_gain,
        key_gain,
    )
    input_grad = (
        d_resid + norm_back(d_normed.astype(F32), attention_gain, input_hat, attention_factor)
    ).astype(LOW)
    d_gate, d_up, d_down = expert_grads(act, expert_all, grad_all)
    own_gain = lax.dynamic_slice_in_dim(attention_gain, f * piece, piece, 0)
    head_piece = hd // n_fsdp
    head_gains = lax.dynamic_slice_in_dim(line[:2, piece:], f * head_piece, head_piece, 1)
    return (
        layer_output,
        input_grad,
        line[0, :piece] / own_gain,
        head_gains[0],
        head_gains[1],
        d_query,
        d_key,
        d_value,
        d_output,
        aux_sum[expert_count],
        aux_sum[:expert_count].T,
        d_gate.reshape(gate_weight.shape),
        d_up.reshape(up_weight.shape),
        d_down.reshape(down_weight.shape),
    )


def solution(mesh):
    body = small_device if (mesh.shape["fsdp"], mesh.shape["tp"]) == (8, 4) else general_device
    return jax.shard_map(
        body,
        mesh=mesh,
        in_specs=(
            P(None, "fsdp", None),
            P(None, "fsdp", None),
            P(None, "fsdp", None),
            P(),
            P(),
            P(),
            P("fsdp", "tp"),
            P("fsdp", "tp"),
            P("fsdp", "tp"),
            P("fsdp", "tp"),
            P(),
            P("fsdp", None),
            P("fsdp", "tp", None),
            P("fsdp", "tp", None),
            P("fsdp", "tp", None),
        ),
        out_specs=(
            P(None, "fsdp", None),
            P(None, "fsdp", None),
            P("fsdp"),
            P("fsdp"),
            P("fsdp"),
            P("fsdp", "tp"),
            P("fsdp", "tp"),
            P("fsdp", "tp"),
            P("fsdp", "tp"),
            P("fsdp"),
            P("fsdp", None),
            P("fsdp", "tp", None),
            P("fsdp", "tp", None),
            P("fsdp", "tp", None),
        ),
        check_vma=False,
    )
```

```python
import functools
import math

import jax
import jax.numpy as jnp
import numpy as np
from jax import lax
from jax.experimental import pallas as pl
from jax.experimental.pallas import tpu as pltpu
from jax.sharding import PartitionSpec as P

norm_eps = 1e-06
rope_base = 1000000.0
masked_score = -1e30
MESH = pl.DeviceIdType.MESH
LOW = jnp.bfloat16
F32 = jnp.float32
VMEM_LIMIT = 62 * 2**20


def coords():
    f = lax.axis_index("fsdp")
    t = lax.axis_index("tp")
    return f // 2, f % 2, t // 2, t % 2


def place(z, x, y, c):
    return (2 * z + x, 2 * y + c)


def span(first, count):
    return pl.ds(pl.multiple_of(first, count), count)


class Here:
    def __init__(self):
        z, x, y, c = coords()
        self.z, self.x, self.y, self.c = z, x, y, c
        self.f, self.t = 2 * z + x, 2 * y + c
        self.xn, self.yn, self.cn = place(z, 1 - x, y, c), place(z, x, 1 - y, c), place(z, x, y, 1 - c)
        self.lanes = ((x, y), (1 - x, y), (x, 1 - y), (1 - x, 1 - y))

    def zr(self, d):
        return (self.z + d) % 4

    def flip(self, k):
        return (self.z // 2 + k // 2) % 2 * 2 + (self.z % 2 + k % 2) % 2

    def zd(self, j):
        inner = (self.z % 3 + 1) // 2
        return self.flip(j + inner * (j // 2) * (1 - 2 * (j % 2)))

    def at_z(self, z):
        return place(z, self.x, self.y, self.c)

    def number(self, j, e):
        return 2 * self.zd(j) + (self.x + e) % 2

    def peer(self, d, e):
        return place(self.zr(d), (self.x + e) % 2, self.y, self.c)

    def greet(self):
        barrier = pltpu.get_barrier_semaphore()
        peers = [self.peer(d, e) for d in range(4) for e in range(2) if d or e] + [self.yn, self.cn]
        for peer in peers:
            pl.semaphore_signal(barrier, inc=1, device_id=peer, device_id_type=MESH)
        pl.semaphore_wait(barrier, len(peers))


def remote(src, dst, send_sem, recv_sem, device):
    return pltpu.make_async_remote_copy(
        src_ref=src, dst_ref=dst, send_sem=send_sem, recv_sem=recv_sem, device_id=device, device_id_type=MESH
    )


def push(src, dst, send_sem, recv_sem, device):
    copy = remote(src, dst, send_sem, recv_sem, device)
    copy.start()
    return copy


def keep(src, dst, sem):
    copy = pltpu.make_async_copy(src, dst, sem)
    copy.start()
    return copy


ORDER = (1, 2, 3)
FAR_FIRST = (3, 2, 1, 0)


class Gather:
    scratch = staticmethod(
        lambda: [pltpu.SemaphoreType.DMA((1,)), pltpu.SemaphoreType.DMA((6,))]
        + [pltpu.SemaphoreType.DMA((4,))] * 9
        + [pltpu.SemaphoreType.DMA((4, 4))] * 2
    )
    slots = 13

    def __init__(self, here, whole, src, dst, sems, by_x, own=None):
        self.here, self.whole, self.src, self.dst, self.own_rows = here, whole, src, dst, own
        (self.loc, self.sz, self.rz, self.sx, self.rx, self.sy, self.ry,
         self.sdx, self.rdx, self.sdy, self.rdy, self.sc, self.rc) = sems
        self.rows, self.cols = src.shape[1], src.shape[2] // 4
        self.half = by_x
        self.sends = []

    def block(self, z, x, y, c, h=None):
        first = (2 * z + x) * self.rows
        rows = span(first, self.rows)
        if h is not None:
            start, count = ((0, self.half), (self.half, self.rows - self.half))[h]
            rows = pl.ds(pl.multiple_of(first + start, 16), count)
        return self.dst.at[:, rows, span((2 * y + c) * self.cols, self.cols)]

    def source(self, z_to, t, first, count):
        seqs = slice(None) if self.whole else pl.ds(z_to // 2, 1)
        return self.src.at[seqs, pl.ds(first, count), span(t * self.cols, self.cols)]

    def push(self, make, when=None):
        if when is None:
            push(*make())
        else:
            pl.when(when)(lambda: push(*make()) and None)
        self.sends.append((make, when))

    def landed(self, ref, sem):
        pltpu.make_async_remote_copy(
            src_ref=ref, dst_ref=ref, send_sem=sem, recv_sem=sem, device_id=self.here.xn, device_id_type=MESH
        ).wait_recv()

    def start(self):
        h = self.here
        self.inner = h.z % 3 > 0
        self.along(0, h.flip(1), True)
        self.along(1, h.flip(3), self.inner)
        if not self.whole:
            self.along(2, h.flip(2), h.z % 3 == 0)
        self.push(lambda: (self.source(h.z, h.t, 0, self.rows), self.block(h.z, h.x, h.y, h.c),
                           self.sx.at[h.z], self.rx.at[h.z], h.xn))
        if self.half:
            self.push(lambda: (self.source(h.z, 2 * (1 - h.y) + h.c, 0, self.half),
                               self.block(h.z, h.x, 1 - h.y, h.c, 0), self.sdx.at[h.z], self.rdx.at[h.z], h.xn))
        own = self.src if self.whole else self.src.at[pl.ds(h.z // 2, 1)]
        if self.own_rows is not None:
            own = self.own_rows
            pltpu.make_async_copy(self.src, own, self.loc.at[0]).start()
            pltpu.make_async_copy(self.src, own, self.loc.at[0]).wait()
        self.own = keep(own, self.dst.at[:, span(h.f * self.rows, self.rows), :], self.loc.at[0])

    def along(self, n, z_to, when):
        h = self.here
        self.push(lambda: (self.source(z_to, h.t, 0, self.rows), self.block(h.z, h.x, h.y, h.c),
                           self.sz.at[n], self.rz.at[h.z], h.at_z(z_to)), None if when is True else when)

    def relay(self, j):
        h, zd = self.here, self.here.zd(j)
        self.landed(self.block(zd, h.x, h.y, h.c), self.rz.at[zd])
        if j > 1 or self.whole:

            def make():
                b = self.block(h.zd(j), h.x, h.y, h.c)
                return b, b, self.sz.at[2 + j], self.rz.at[h.zd(j)], h.at_z(h.flip(3 if j == 1 else 1))

            self.push(make, self.inner)

    def pass_on(self, d, lane, sends, recvs, device, h=None):
        x, y = self.here.lanes[lane]

        def make():
            zd = self.here.zd(d)
            b = self.block(zd, x, y, self.here.c, h)
            return b, b, sends(zd), recvs(zd), device

        self.push(make)

    def spread(self, d):
        h = self.here
        self.pass_on(d, 0, lambda k: self.sx.at[k], lambda k: self.rx.at[k], h.xn)
        self.pass_on(d, 0, lambda k: self.sy.at[k], lambda k: self.ry.at[k], h.yn)
        self.pass_on(d, 0, lambda k: self.sc.at[0, k], lambda k: self.rc.at[0, k], h.cn)

    def cross(self, d):
        h, zd = self.here, self.here.zd(d)
        self.landed(self.block(zd, 1 - h.x, h.y, h.c), self.rx.at[zd])
        self.pass_on(d, 1, lambda k: self.sdy.at[k], lambda k: self.rdy.at[k], h.yn, 1)
        self.pass_on(d, 1, lambda k: self.sc.at[1, k], lambda k: self.rc.at[1, k], h.cn)
        if d != 0:
            self.landed(self.block(zd, h.x, 1 - h.y, h.c), self.ry.at[zd])
            if self.half:
                self.pass_on(d, 2, lambda k: self.sdx.at[k], lambda k: self.rdx.at[k], h.xn, 0)
            self.pass_on(d, 2, lambda k: self.sc.at[2, k], lambda k: self.rc.at[2, k], h.cn)

    def close(self, d):
        h, zd = self.here, self.here.zd(d)
        if self.half:
            self.landed(self.block(zd, 1 - h.x, 1 - h.y, h.c, 0), self.rdx.at[zd])
        self.landed(self.block(zd, 1 - h.x, 1 - h.y, h.c, 1), self.rdy.at[zd])
        self.pass_on(d, 3, lambda k: self.sc.at[3, k], lambda k: self.rc.at[3, k], h.cn)

    def first_steps(self):
        for j in ORDER:
            self.relay(j)
            self.spread(j)
            if j < 3:
                self.cross(j - 1)

    def last_steps(self):
        self.close(0)
        for j in (2, 3):
            self.cross(j)
            self.close(j - 1)
        self.close(3)

    def arrived(self, d, e):
        h, zd = self.here, self.here.zd(d)
        if e == 0:
            if d == 0:
                self.own.wait()
            else:
                self.landed(self.block(zd, h.x, h.y, 1 - h.c), self.rc.at[0, zd])
                self.landed(self.block(zd, h.x, 1 - h.y, 1 - h.c), self.rc.at[2, zd])
        else:
            self.landed(self.block(zd, 1 - h.x, h.y, 1 - h.c), self.rc.at[1, zd])
            self.landed(self.block(zd, 1 - h.x, 1 - h.y, 1 - h.c), self.rc.at[3, zd])

    def finish(self):
        for make, when in self.sends:
            if when is None:
                remote(*make()).wait_send()
            else:
                pl.when(when)(lambda make=make: remote(*make()).wait_send())


def add_into(target, *others):
    count, rows, _ = target.shape
    step = 32
    wide = target.dtype if len(others) == 1 else F32

    @pl.loop(0, count * rows // step)
    def _(i):
        n = i // (rows // step)
        r = pl.ds(pl.multiple_of((i % (rows // step)) * step, step), step)
        total = target[n, r, :].astype(wide)
        for other in others:
            total = total + other[n, r, :].astype(wide)
        target[n, r, :] = total.astype(target.dtype)


class Sum:
    slots = 23

    @staticmethod
    def scratch(count, rows, width, low, by_x):
        dma = pltpu.SemaphoreType.DMA
        cols = width // 4
        vm = pltpu.VMEM
        return [
            vm((4, 4, count, rows, cols), low),
            vm((4, count, max(by_x, 16), cols), low),
            vm((4, count, rows - by_x, cols), low),
            vm((4, count, rows, cols), low),
            vm((4, count, rows, cols), low),
            vm((4, count, rows, cols), low),
            vm((4, 2, rows, cols), low),
            vm((2, rows, cols), low),
            dma((4, 4)), dma((4, 4)),
        ] + [dma((4,))] * 10 + [dma((3,))] * 2 + [dma((5,))]

    def __init__(self, here, whole, part, refs, by_x):
        self.here, self.whole, self.part, self.by_x = here, whole, part, by_x
        (self.fc, self.f1x, self.f1y, self.f2x, self.f2y, self.fz, self.full, self.tmp, self.sc, self.rc,
         self.s1x, self.r1x, self.s1y, self.r1y, self.s2x, self.r2x, self.s2y, self.r2y, self.sz, self.rz,
         self.sg, self.rg, self.osem) = refs
        self.rows, self.cols = part.shape[1] // 8, part.shape[2] // 4
        self.top, self.low = pl.ds(0, by_x), pl.ds(by_x, self.rows - by_x)
        self.sends = []

    def block(self, d, lane, c):
        x, y = self.here.lanes[lane]
        return self.part.at[:, span((2 * self.here.zd(d) + x) * self.rows, self.rows),
                            span((2 * y + c) * self.cols, self.cols)]

    def push(self, make):
        push(*make())
        self.sends.append(make)

    def landed(self, ref, sem):
        pltpu.make_async_remote_copy(
            src_ref=ref, dst_ref=ref, send_sem=sem, recv_sem=sem, device_id=self.here.xn, device_id_type=MESH
        ).wait_recv()

    def giving(self, d, e):
        h = self.here
        for q in (0, 1):
            lane = 2 * q + e
            at = self.part.at[:, span((2 * h.zd(d) + (h.x + e) % 2) * self.rows, self.rows),
                              span((2 * ((h.y + q) % 2) + 1 - h.c) * self.cols, self.cols)]
            yield at, self.fc.at[lane, d], self.sc.at[lane, d], self.rc.at[lane, d], h.cn

    def give(self, d, e):
        for args in self.giving(d, e):
            push(*args)

    def pair(self, lane, d):
        self.landed(self.fc.at[lane, d], self.rc.at[lane, d])
        add_into(self.block(d, lane, self.here.c), self.fc.at[lane, d])

    def mine(self, d, lane, rows=slice(None)):
        return self.block(d, lane, self.here.c).at[:, rows]

    def corner(self, d):
        self.pair(3, d)
        if self.by_x:
            self.push(lambda: (self.mine(d, 3, self.top), self.f1x.at[d], self.s1x.at[d], self.r1x.at[d], self.here.xn))
        self.push(lambda: (self.mine(d, 3, self.low), self.f1y.at[d], self.s1y.at[d], self.r1y.at[d], self.here.yn))

    def sides(self, d):
        self.pair(1, d)
        self.landed(self.f1y.at[d], self.r1y.at[d])
        add_into(self.mine(d, 1, self.low), self.f1y.at[d])
        self.push(lambda: (self.mine(d, 1), self.f2x.at[d], self.s2x.at[d], self.r2x.at[d], self.here.xn))
        self.pair(2, d)
        if self.by_x:
            self.landed(self.f1x.at[d], self.r1x.at[d])
            add_into(self.mine(d, 2, self.top), self.f1x.at[d])
        self.push(lambda: (self.mine(d, 2), self.f2y.at[d], self.s2y.at[d], self.r2y.at[d], self.here.yn))

    def centre(self, d):
        self.pair(0, d)
        self.landed(self.f2x.at[d], self.r2x.at[d])
        self.landed(self.f2y.at[d], self.r2y.at[d])
        add_into(self.mine(d, 0), self.f2x.at[d], self.f2y.at[d])
        if d != 0:
            h = self.here
            self.push(lambda: (self.mine(d, 0), self.fz.at[h.z], self.sz.at[d], self.rz.at[h.z], h.at_z(h.zd(d))))

    def total(self):
        for d in (1, 2, 3):
            self.landed(self.fz.at[self.here.zd(d)], self.rz.at[self.here.zd(d)])
        b = self.block(0, 0, self.here.c)
        step = 32

        @pl.loop(0, 2 * self.rows // step)
        def _(i):
            n = i // (self.rows // step)
            r = pl.ds(pl.multiple_of((i % (self.rows // step)) * step, step), step)
            if self.whole:
                total = b[n, r, :].astype(F32)
                for d in (1, 2, 3):
                    total = total + self.fz[self.here.zd(d), n, r, :].astype(F32)
            else:
                total = jnp.where(self.here.z // 2 == n, b[0, r, :].astype(F32), 0.0)
                for d in (1, 2, 3):
                    total = total + jnp.where(self.here.zd(d) // 2 == n, self.fz[self.here.zd(d), 0, r, :].astype(F32), 0.0)
            self.tmp[n, r, :] = total.astype(self.tmp.dtype)

    def share(self, out):
        self.share_start()
        self.share_cross()
        self.share_end(out)

    def share_start(self):
        h = self.here
        self.keeps = [keep(self.tmp, self.full.at[h.t], self.osem.at[4])]
        self.push(lambda: (self.tmp, self.full.at[h.t], self.sg.at[0], self.rg.at[0], h.yn))
        self.push(lambda: (self.tmp, self.full.at[h.t], self.sg.at[1], self.rg.at[1], h.cn))

    def share_cross(self):
        h = self.here
        ty = 2 * (1 - h.y) + h.c
        self.landed(self.full.at[ty], self.rg.at[0])
        self.push(lambda: (self.full.at[ty], self.full.at[ty], self.sg.at[2], self.rg.at[2], h.cn))

    def share_end(self, out):
        h = self.here
        self.landed(self.full.at[2 * h.y + 1 - h.c], self.rg.at[1])
        self.landed(self.full.at[2 * (1 - h.y) + 1 - h.c], self.rg.at[2])
        self.keeps[0].wait()
        if out is None:
            return
        outs = [keep(self.full.at[q], out.at[:, :, pl.ds(q * self.cols, self.cols)], self.osem.at[q]) for q in range(4)]
        for copy in outs:
            copy.wait()

    def finish(self):
        for make in self.sends:
            remote(*make()).wait_send()
        for d in range(4):
            for e in range(2):
                for args in self.giving(d, e):
                    remote(*args).wait_send()


def wait_for(ref, sem, device):
    pltpu.make_async_remote_copy(
        src_ref=ref, dst_ref=ref, send_sem=sem, recv_sem=sem, device_id=device, device_id_type=MESH
    ).wait_recv()


def signed_tables(length, width):
    middle = width // 2
    frequency = rope_base ** (-np.arange(middle) * 2.0 / width)
    angles = np.arange(length)[:, None] * frequency[None, :]
    cosine, sine = np.cos(angles), np.sin(angles)
    return (
        jnp.asarray(np.concatenate([cosine, cosine], axis=1), F32),
        jnp.asarray(np.concatenate([-sine, sine], axis=1), F32),
    )


def dot_nn(a, b):
    return jnp.dot(a, b, preferred_element_type=F32)


def dot_nt(a, b):
    return lax.dot_general(a, b, (((1,), (1,)), ((), ())), preferred_element_type=F32)


def dot_tn(a, b):
    return lax.dot_general(a, b, (((0,), (0,)), ((), ())), preferred_element_type=F32)


BY_X = 64


class Weights:
    scratch = staticmethod(lambda: [pltpu.SemaphoreType.DMA((8, 4, 2))] * 4 + [pltpu.SemaphoreType.DMA((6,))])
    slots = 5

    def __init__(self, here, query, key, value, output, router, ids, w, wo, router_all, ids_all, sems):
        self.here = here
        self.query, self.output, self.w, self.wo = query, output, w, wo
        piece, part = query.shape[0], wo.shape[1]
        self.piece, self.part = piece, part
        hd = key.shape[1]
        self.shared = (
            (key, lambda f: w.at[span(f * piece, piece), pl.ds(part, hd)]),
            (value, lambda f: w.at[span(f * piece, piece), pl.ds(part + hd, hd)]),
            (router, lambda f: router_all.at[:, span(f * piece, piece)]),
            (ids, lambda f: ids_all.at[:, :, span(f * ids.shape[2], ids.shape[2])]),
        )
        self.qs, self.qr, self.ss, self.sr, self.loc = sems
        self.sends, self.keeps = [], []

    def landed(self, ref, sem):
        pltpu.make_async_remote_copy(
            src_ref=ref, dst_ref=ref, send_sem=sem, recv_sem=sem, device_id=self.here.xn, device_id_type=MESH
        ).wait_recv()

    def start_shared(self):
        h = self.here
        for n, (src, dst) in enumerate(self.shared):
            self.keeps.append(keep(src, dst(h.f), self.loc.at[n]))
            for d, e in ((2, 0), (1, 0), (3, 0), (0, 1)):
                self.sends.append(push(src, dst(h.f), self.ss.at[n, d, e], self.sr.at[n, (4 - d) % 4, e], h.peer(d, e)))

    def pass_shared(self, d):
        h = self.here
        for n, (_, dst) in enumerate(self.shared):
            ref = dst(2 * h.zr(d) + h.x)
            self.landed(ref, self.sr.at[n, d, 0])
            self.sends.append(push(ref, ref, self.ss.at[n, d, 1], self.sr.at[n, d, 1], h.xn))

    def wait_shared(self):
        h = self.here
        for n, (_, dst) in enumerate(self.shared):
            for d in range(4):
                self.landed(dst(2 * h.zr(d) + 1 - h.x), self.sr.at[n, d, 1])

    def start_pairs(self, n):
        h = self.here
        src, dst = ((self.query, self.w), (self.output, self.wo))[n]
        mine = lambda f: dst.at[span(f * self.piece, self.piece), pl.ds(0, self.part)]
        self.keeps.append(keep(src.at[:, span((h.f % 4) * self.part, self.part)], mine(h.f), self.loc.at[4 + n]))
        for d in (2, 1, 3, 0):
            for e in (1, 0):
                if d or e:
                    f = 2 * h.zr(d) + (h.x + e) % 2
                    self.sends.append(push(src.at[:, span((f % 4) * self.part, self.part)], mine(h.f),
                                           self.qs.at[n, d, e], self.qr.at[n, (4 - d) % 4, e], h.peer(d, e)))

    def wait_pairs(self, n, far=range(4)):
        h = self.here
        dst = (self.w, self.wo)[n]
        for d in far:
            for e in (1, 0):
                if d or e:
                    f = 2 * h.zr(d) + (h.x + e) % 2
                    self.landed(dst.at[span(f * self.piece, self.piece), pl.ds(0, self.part)], self.qr.at[n, d, e])

    def finish(self):
        for copy in self.sends:
            copy.wait_send()


def unit(values):
    factor = lax.rsqrt(jnp.mean(values * values, axis=-1, keepdims=True) + norm_eps)
    return values * factor, factor


def begin_kernel(heads, cot, query, key, value, output, router, ids, tokens, ag_ref, eg_ref,
                 cos_ref, sin_ref, qg_ref, kg_ref, xn_out, w_out, wo_out, router_out, ids_out, cot_out, pre_out, qkv_out, prob_out, ctx_out, resid_out, expert_out,
                 normed, resid, xn, w, wo, pre, qkv, prob, ctx, part, own, osem, *sems):
    here = Here()
    count, rows, _ = tokens.shape
    step = 32
    steps = rows // step

    def chunk_of(i):
        return i // steps, pl.ds(pl.multiple_of(i % steps * step, step), step)

    @pl.loop(0, count * steps)
    def _(i):
        n, r = chunk_of(i)
        normed[n, r, :] = (unit(tokens[n, r, :].astype(F32))[0] * ag_ref[...]).astype(LOW)

    here.greet()
    at = 0
    x_rows = Gather(here, False, normed, xn, sems[at : at + Gather.slots], BY_X)
    at += Gather.slots
    c_rows = Gather(here, True, cot, cot_out, sems[at : at + Gather.slots], BY_X + 32, own)
    at += Gather.slots
    moved = Weights(here, query, key, value, output, router, ids, w, wo, router_out, ids_out, sems[at : at + Weights.slots])
    at += Weights.slots
    total = Sum(here, False, part, sems[at:], BY_X)

    x_rows.start()
    moved.start_shared()
    moved.start_pairs(0)
    x_rows.first_steps()
    for d in (1, 3, 2):
        moved.pass_shared(d)
    x_rows.last_steps()
    for d in (0,) + ORDER:
        x_rows.arrived(d, 0)
        x_rows.arrived(d, 1)
    moved.wait_shared()
    moved.wait_pairs(0, (2,))
    moved.start_pairs(1)
    moved.wait_pairs(0, (0, 1, 3))
    for copy in moved.keeps:
        copy.wait()
    outs = [keep(xn, xn_out, osem.at[0]), keep(w, w_out, osem.at[1])]

    seq = xn.shape[1]
    hd = cos_ref.shape[1]
    tile = 256
    scale = 1.0 / math.sqrt(hd)
    for i in range(seq // tile):
        r = pl.ds(i * tile, tile)
        got = dot_nn(xn[0, r, :], w[...])
        pre[r, :] = got[:, : (heads + 1) * hd]
        qkv[r, pl.ds((heads + 1) * hd, hd)] = got[:, (heads + 1) * hd :].astype(LOW)
        for a in range(heads + 1):
            one = got[:, a * hd : (a + 1) * hd]
            factor = lax.rsqrt(jnp.mean(one * one, axis=-1, keepdims=True) + norm_eps)
            gained = one * factor * (qg_ref if a < heads else kg_ref)[...]
            turned = gained * cos_ref[r, :] + pltpu.roll(gained, hd // 2, 1) * sin_ref[r, :]
            qkv[r, pl.ds(a * hd, hd)] = turned.astype(LOW)
    c_rows.start()
    outs += [keep(pre, pre_out, osem.at[2]), keep(qkv, qkv_out, osem.at[3])]
    for a in range(heads):
        for i in range(seq // tile):
            r = pl.ds(i * tile, tile)
            n = (i + 1) * tile
            score = dot_nt(qkv[r, pl.ds(a * hd, hd)], qkv[pl.ds(0, n), pl.ds(heads * hd, hd)]) * scale
            row = lax.broadcasted_iota(jnp.int32, (tile, n), 0) + i * tile
            col = lax.broadcasted_iota(jnp.int32, (tile, n), 1)
            score = jnp.where(col <= row, score, masked_score)
            terms = jnp.exp(score - jnp.max(score, axis=-1, keepdims=True))
            low = (terms * (1.0 / jnp.sum(terms, axis=-1, keepdims=True))).astype(LOW)
            prob[a, r, pl.ds(0, n)] = low
            ctx[r, pl.ds(a * hd, hd)] = dot_nn(low, qkv[pl.ds(0, n), pl.ds((heads + 1) * hd, hd)]).astype(LOW)
        if a == 0:
            c_rows.relay(1)
            c_rows.spread(1)
    outs += [keep(prob, prob_out, osem.at[4]), keep(ctx, ctx_out, osem.at[5])]
    moved.wait_pairs(1)
    outs.append(keep(wo, wo_out, osem.at[6]))
    for e in (1, 0):
        for d in FAR_FIRST:
            at_f = span(here.number(d, e) * rows, rows)
            part[0, at_f, :] = dot_nt(ctx[at_f, :], wo[...]).astype(LOW)
            total.give(d, e)
    for d in FAR_FIRST:
        total.corner(d)
    c_rows.cross(0)
    c_rows.relay(2)
    c_rows.spread(2)
    for d in FAR_FIRST:
        total.sides(d)
    c_rows.cross(1)
    c_rows.relay(3)
    c_rows.spread(3)
    for d in FAR_FIRST:
        total.centre(d)
    c_rows.close(0)
    c_rows.cross(2)
    c_rows.close(1)
    total.total()
    total.share_start()
    c_rows.cross(3)
    c_rows.close(2)
    total.share_cross()
    c_rows.close(3)
    total.share_end(None)
    x_rows.finish()

    @pl.loop(0, count * steps)
    def _(i):
        n, r = chunk_of(i)
        branch = jnp.concatenate([total.full[q, n, r, :] for q in range(4)], axis=1).astype(F32)
        summed = tokens[n, r, :].astype(F32) + branch
        resid[n, r, :] = summed
        normed[n, r, :] = (unit(summed)[0] * eg_ref[...]).astype(LOW)

    outs += [keep(resid, resid_out, osem.at[7]), keep(normed, expert_out, osem.at[8])]
    for d in (0,) + ORDER:
        c_rows.arrived(d, 0)
        c_rows.arrived(d, 1)
    for each in (c_rows, moved, total):
        each.finish()
    for copy in outs:
        copy.wait()


def begin(cot, query, key, value, output, router, ids, tokens, attention_gain, expert_gain,
          cosine, sine, query_gain, key_gain):
    count, rows, width = tokens.shape
    seq = rows * 8
    hd = query_gain.shape[0]
    part = query.shape[1] // 4
    heads = part // hd
    vm = pltpu.VMEM
    hbm = pl.BlockSpec(memory_space=pl.ANY)
    near = pl.BlockSpec(memory_space=pltpu.VMEM)
    shape = jax.ShapeDtypeStruct
    local = [
        ((1, seq, width), LOW),
        ((width, part + 2 * hd), LOW),
        ((width, part), LOW),
        ((seq, (heads + 1) * hd), F32),
        ((seq, (heads + 2) * hd), LOW),
        ((heads, seq, seq), LOW),
        ((seq, heads * hd), LOW),
    ]
    return pl.pallas_call(
        functools.partial(begin_kernel, heads),
        out_shape=(
            shape(*local[0]),
            shape(*local[1]),
            shape(*local[2]),
            shape((router.shape[0], width), LOW),
            shape((count, ids.shape[1], seq), jnp.int32),
            shape((count, seq, width), LOW),
            shape(*local[3]),
            shape(*local[4]),
            shape(*local[5]),
            shape(*local[6]),
            shape((count, rows, width), F32),
            shape((count, rows, width), LOW),
        ),
        in_specs=[hbm] * 7 + [near] * 7,
        out_specs=[hbm] * 12,
        scratch_shapes=[vm((count, rows, width), LOW), vm((count, rows, width), F32)]
        + [vm(*entry) for entry in local]
        + [vm((1, seq, width), LOW), vm((count, rows, width), LOW), pltpu.SemaphoreType.DMA((9,))]
        + Gather.scratch() + Gather.scratch() + Weights.scratch() + Sum.scratch(1, rows, width, LOW, BY_X),
        compiler_params=pltpu.CompilerParams(
            collective_id=4, has_side_effects=True, vmem_limit_bytes=VMEM_LIMIT
        ),
        name="begin",
    )(cot, query, key, value, output, router, ids, tokens, attention_gain[None], expert_gain[None],
      cosine, sine, query_gain[None], key_gain[None])


def experts_kernel(experts, expert_in, og_in, ids, router, g_in, u_in, d_in,
                   x_out, act_out, dx_sum, out_sum, probs_out, dgp_out,
                   x_t, g, u, dn, og_t, raw_s, act_t, dx, out, stage, share_s, dgp_t, dgp_got, dgp_all, dgp_c, dgp_y,
                   wsem, ogsem, xsem, actsem, psem, rsem, tsem, usem, *rest):
    here = Here()
    here.greet()
    by_x = expert_in.shape[1] // 2
    rows_x = Gather(here, True, expert_in, x_out, rest[: Gather.slots], by_x, x_t.at[0])
    sums = (
        Sum(here, True, dx, rest[Gather.slots : Gather.slots + Sum.slots], by_x),
        Sum(here, True, out, rest[Gather.slots + Sum.slots :], by_x),
    )
    number = here.number
    count, rows, width = expert_in.shape
    hidden = g.shape[0]
    per = hidden // experts
    tokens = count * rows
    lanes = router.shape[0]
    part = stage.shape[2]
    chunk = width // 4
    rows_x.start()
    loads = [keep(src, dst, wsem.at[n]) for n, (src, dst) in enumerate(((d_in, dn), (g_in, g), (u_in, u)))]

    def plane(i):
        k = i // 2
        return k + (k + 2) // 3 - 3 * (k // 3)

    def tile(i):
        return span(number(plane(i), i % 2) * rows, rows)

    def og_load(i):
        return pltpu.make_async_copy(og_in.at[:, tile(i), :], og_t.at[i % 2], ogsem.at[i % 2])

    def x_load(i):
        return pltpu.make_async_copy(x_out.at[:, tile(i), :], x_t.at[i % 2], xsem.at[i % 2])

    def act_store(i):
        return pltpu.make_async_copy(act_t.at[i % 2], act_out.at[:, :, tile(i), :], actsem.at[i % 2])

    def dgp_send(i):
        to = place(here.zd(plane(i)), (here.x + i % 2) % 2, here.y, here.c)
        return remote(dgp_t.at[i], dgp_got.at[here.f], psem.at[i], rsem.at[here.f], to)

    def both(step, j):
        for each in sums:
            getattr(each, step)(j)

    first = {2: lambda: (rows_x.relay(1), rows_x.spread(1))}
    early = {
        3: lambda: (rows_x.cross(0),),
        5: lambda: (rows_x.relay(2), rows_x.spread(2)),
        7: lambda: (rows_x.cross(1), rows_x.close(0)),
    }
    before = {
        1: lambda: (rows_x.relay(3), rows_x.spread(3), rows_x.arrived(0, 1)),
        2: lambda: (rows_x.close(2), rows_x.arrived(2, 0), rows_x.arrived(2, 1)),
        3: lambda: (both("corner", 0),),
        5: lambda: (both("corner", 2),),
        7: lambda: (both("corner", 3),),
    }
    middle = {
        1: lambda: (rows_x.cross(2), rows_x.close(1)),
        2: lambda: (rows_x.cross(3),),
        3: lambda: (rows_x.close(3), rows_x.arrived(3, 0), rows_x.arrived(3, 1)),
        4: lambda: (both("sides", 0),),
        5: lambda: (rows_x.arrived(1, 0), rows_x.arrived(1, 1)),
        6: lambda: (both("sides", 2), both("centre", 0)),
    }

    def hooks(table, i):
        for key, run in table.items():
            @pl.when(i == key)
            def _(run=run):
                run()

    row = lax.broadcasted_iota(jnp.int32, (lanes, hidden), 0)
    col = lax.broadcasted_iota(jnp.int32, (lanes, hidden), 1)
    spread = jnp.where(row == here.f * experts + col // per, 1.0, 0.0).astype(LOW)
    row8 = lax.broadcasted_iota(jnp.int32, (8, hidden), 0)
    col8 = lax.broadcasted_iota(jnp.int32, (8, hidden), 1)
    gather8 = jnp.where(row8 == col8 // per, 1.0, 0.0).astype(LOW)

    def first_half(i):
        x_tile = x_t[i % 2].reshape(tokens, width)
        for n, right in enumerate((g, u)):
            for k in range(hidden // part):
                stage[n, pl.ds(k * tokens, tokens), :] = dot_nt(x_tile, right[pl.ds(k * part, part), :])
        logits = dot_nt(router[...], x_tile)
        named_ids = jnp.concatenate([ids[m, :, tile(i)] for m in range(count)], axis=1)
        lane = lax.broadcasted_iota(jnp.int32, logits.shape, 0)
        named = lane == named_ids[0:1, :]
        for k in range(1, named_ids.shape[0]):
            named = named | (lane == named_ids[k : k + 1, :])
        masked = jnp.where(named, logits, masked_score)
        terms = jnp.where(named, jnp.exp(masked - jnp.max(masked, axis=0, keepdims=True)), 0.0)
        probs = terms / jnp.sum(terms, axis=0, keepdims=True)
        share_s[...] = dot_tn(probs.astype(LOW), spread)
        return probs

    def between(i, m):
        r = pl.ds(m * rows, rows)
        gate, up = (
            jnp.concatenate([stage[n, pl.ds(k * tokens + m * rows, rows), :] for k in range(hidden // part)], axis=1)
            for n in range(2)
        )
        raw = raw_s[i, r, :].astype(F32)
        share = share_s[r, :]
        sig = 1.0 / (1.0 + jnp.exp(-gate))
        silu = gate * sig
        inner = silu * up
        dgp_t[i, :, r] = dot_nt(gather8, (inner * raw).astype(LOW))
        d_inner = raw * share
        act_t[i % 2, 0, m] = (d_inner * up * (sig + silu * (1.0 - sig))).astype(LOW)
        act_t[i % 2, 1, m] = (d_inner * silu).astype(LOW)
        act_t[i % 2, 2, m] = (inner * share).astype(LOW)

    def second_half(i, q):
        d_gate, d_up, weighted = (act_t[i % 2, n].reshape(tokens, hidden) for n in range(3))
        cols = pl.ds(q * chunk, chunk)
        got = dot_nn(d_gate, g[:, cols]) + dot_nn(d_up, u[:, cols])
        dx[:, tile(i), cols] = got.astype(LOW).reshape(count, rows, chunk)
        out[:, tile(i), cols] = dot_nn(weighted, dn[:, cols]).astype(LOW).reshape(count, rows, chunk)

    def sent(i):
        for each in sums:
            each.give(plane(i), i % 2)

        @pl.when(i > 0)
        def _():
            dgp_send(i).start()

    og_load(0).start()
    loads[0].wait()

    def raw_step(table, i):
        @pl.when(i + 1 < 8)
        def _():
            og_load(i + 1).start()

        hooks(table, i)
        og_load(i).wait()
        raw_s[i] = dot_nt(og_t[i % 2].reshape(tokens, width), dn[...]).astype(LOW)

    pl.loop(0, 3)(functools.partial(raw_step, first))
    loads[1].wait()
    loads[2].wait()
    rows_x.arrived(0, 0)
    probs_out[...] = first_half(0)
    for m in range(count):
        between(0, m)
    act_store(0).start()
    pl.loop(3, 8)(functools.partial(raw_step, early))

    @pl.loop(1, 8)
    def _(i):
        hooks(before, i)

        @pl.when(i < 3)
        def _():
            x_load(i).start()

        @pl.when(i >= 2)
        def _():
            act_store(i - 2).wait()

        x_load(i).wait()
        first_half(i)
        hooks(middle, i)

        @pl.when((i >= 2) & (i < 7))
        def _():
            x_load(i + 1).start()

        for m in range(count):
            second_half(i - 1, 2 * m)
            between(i, m)
            second_half(i - 1, 2 * m + 1)
        act_store(i).start()
        sent(i - 1)

    for q in range(4):
        second_half(7, q)
    sent(7)
    ahead, behind = sums
    ahead.corner(1)
    ahead.sides(3)
    ahead.centre(2)
    behind.corner(1)
    behind.sides(3)
    ahead.sides(1)
    ahead.centre(3)
    behind.centre(2)
    behind.sides(1)
    ahead.centre(1)
    behind.centre(3)
    for d in range(4):
        for e in range(2):
            if d or e:
                n = number(d, e)
                wait_for(dgp_got.at[n], rsem.at[n], here.xn)
                dgp_all[n] = dgp_got[n]
    dgp_all[here.f] = dgp_t[0]
    across = push(dgp_all, dgp_c, tsem.at[0], usem.at[0], here.cn)
    ahead.total()
    ahead.share_start()
    behind.centre(1)
    wait_for(dgp_c, usem.at[0], here.cn)
    across.wait_send()
    dgp_all[...] = dgp_all[...] + dgp_c[...]
    second = push(dgp_all, dgp_y, tsem.at[1], usem.at[1], here.yn)
    ahead.share_cross()
    behind.total()
    behind.share_start()
    ahead.share_end(dx_sum)
    behind.share_cross()
    behind.share_end(out_sum)
    wait_for(dgp_y, usem.at[1], here.yn)
    dgp_out[...] = dgp_all[...] + dgp_y[...]
    second.wait_send()
    act_store(6).wait()
    act_store(7).wait()
    for i in range(1, 8):
        dgp_send(i).wait_send()
    rows_x.finish()
    for each in sums:
        each.finish()


def run_experts(expert_in, og, ids, router, gate, up, down):
    count, rows, width = expert_in.shape
    seq = rows * 8
    experts, per, _ = gate.shape
    hidden = experts * per
    tokens = count * rows
    lanes = router.shape[0]
    vm = pltpu.VMEM
    dma = pltpu.SemaphoreType.DMA
    hbm = pl.BlockSpec(memory_space=pl.ANY)
    near = pl.BlockSpec(memory_space=pltpu.VMEM)
    shape = jax.ShapeDtypeStruct
    total = Sum.scratch(count, rows, width, LOW, rows // 2)
    return pl.pallas_call(
        functools.partial(experts_kernel, experts),
        out_shape=(
            shape((count, seq, width), LOW),
            shape((3, count, seq, hidden), LOW),
            shape((count, rows, width), LOW),
            shape((count, rows, width), LOW),
            shape((lanes, tokens), F32),
            shape((8, 8, tokens), F32),
        ),
        in_specs=[hbm, hbm, near, near, hbm, hbm, hbm],
        out_specs=[hbm, hbm, hbm, hbm, near, near],
        scratch_shapes=[
            vm((2, count, rows, width), LOW),
            vm((hidden, width), LOW),
            vm((hidden, width), LOW),
            vm((hidden, width), LOW),
            vm((2, count, rows, width), LOW),
            vm((8, tokens, hidden), LOW),
            vm((2, 3, count, rows, hidden), LOW),
            vm((count, seq, width), LOW),
            vm((count, seq, width), LOW),
            vm((2, hidden // 256 * tokens, 256), F32),
            vm((tokens, hidden), F32),
            vm((8, 8, tokens), F32),
            vm((8, 8, tokens), F32),
            vm((8, 8, tokens), F32),
            vm((8, 8, tokens), F32),
            vm((8, 8, tokens), F32),
            dma((3,)),
            dma((2,)),
            dma((2,)),
            dma((2,)),
            dma((8,)),
            dma((8,)),
            dma((2,)),
            dma((2,)),
        ]
        + Gather.scratch()
        + total
        + total,
        compiler_params=pltpu.CompilerParams(
            collective_id=6, has_side_effects=True, vmem_limit_bytes=VMEM_LIMIT
        ),
        name="experts",
    )(expert_in, og, ids, router, gate.reshape(hidden, width), up.reshape(hidden, width), down.reshape(hidden, width))


def expert_grads_kernel(act, x, og, *refs):
    kept = (len(refs) - 3) // 2
    tokens = act.shape[1] * act.shape[2]
    x_cols = x[...].reshape(tokens, x.shape[2])
    og_cols = og[...].reshape(tokens, og.shape[2])
    for n, right in enumerate((x_cols, x_cols, og_cols)):
        refs[kept + n][...] = dot_tn(act[n].reshape(tokens, act.shape[3]), right)
    for src, dst in zip(refs[:kept], refs[kept + 3 :]):
        dst[...] = src[...]


def expert_grads(act, x, og, *others):
    _, count, seq, hidden = act.shape
    width = x.shape[2]
    block = min(512, width)
    steps = width // block
    cols = pl.BlockSpec((count, seq, block), lambda i: (0, 0, i))
    out = pl.BlockSpec((hidden, block), lambda i: (0, i))

    def pieces(value):
        shape = value.shape[:-2] + (value.shape[-2] // steps, value.shape[-1])
        zeros = (0,) * (len(shape) - 2)
        return pl.BlockSpec(shape, lambda i: zeros + (i, 0))

    grads = jax.ShapeDtypeStruct((hidden, width), F32)
    kept = [pieces(value) for value in others]
    return pl.pallas_call(
        expert_grads_kernel,
        grid=(steps,),
        in_specs=[
            pl.BlockSpec(act.shape, lambda i: (0, 0, 0, 0), pipeline_mode=pl.Buffered(1)),
            cols,
            cols,
        ]
        + kept,
        out_specs=[out, out, out] + kept,
        out_shape=[grads] * 3 + [jax.ShapeDtypeStruct(value.shape, value.dtype) for value in others],
        compiler_params=pltpu.CompilerParams(vmem_limit_bytes=VMEM_LIMIT),
        name="expert_grads",
    )(act, x, og, *others)


PEERS = tuple((d, e) for d in (2, 1, 3, 0) for e in (1, 0) if d or e)


def end_kernel(heads, xn_in, w_in, wo_in, pre_in, qkv_in, prob_in, ctx_in, tokens_in, out_in,
               resid, cot, dx_sum, expert_in, probs, dgp, router, eg_ref, ag_ref, query, key, value,
               cos_ref, sin_ref, qg_ref, kg_ref,
               layer_out, input_out, dq_out, dk_out, dv_out, do_out, aux_out, gains_out,
               tokens, out_sum, d_res, low_rows, layer, aux, db, xn, w, wo, pre, qkv, prob, ctx, dctx, dq_s, dk_s, dv_s, dqkv, dwo, dw, dwo_got, dwq_got, kv_x, kv_z,
               aux_got, head_part, head_got, line, line_c, line_y, wide_q, wide_o, wide_kv,
               lsem, psem, rsem, kxs, kxr, kzs, kzr, tsem, usem, osem, *rest):
    here = Here()
    here.greet()
    sends, outs = [], []
    rows_db = Gather(here, False, low_rows, db, rest[: Gather.slots], BY_X)
    at = Gather.slots
    dn = Sum(here, False, db, rest[at:], BY_X)
    rows = dn.rows
    piece, part = query.shape[0], wo.shape[1]
    seq = xn.shape[1]
    hd = cos_ref.shape[1]
    tile = 256
    scale = 1.0 / math.sqrt(hd)

    def number(d, e):
        return 2 * here.zr(d) + (here.x + e) % 2

    def send(n, d, e, src, got):
        sends.append(push(src, got.at[(4 - d) % 4, e], psem.at[n, d, e], rsem.at[n, (4 - d) % 4, e], here.peer(d, e)))

    def got_from(n, d, e, got):
        wait_for(got.at[d, e], rsem.at[n, d, e], here.xn)
        return got[d, e]

    loads = {}
    for n, (src, dst) in enumerate(((wo_in, wo), (ctx_in, ctx), (qkv_in, qkv), (prob_in, prob), (pre_in, pre),
                                    (xn_in, xn), (w_in, w), (tokens_in, tokens), (out_in, out_sum))):
        loads[n] = keep(src, dst, lsem.at[n])
    count, lanes, width = resid.shape[0], probs.shape[0], resid.shape[2]
    experts = lanes // 8
    step = 32
    steps = rows // step

    def chunk_of(i):
        return i // steps, pl.ds(pl.multiple_of(i % steps * step, step), step)

    def unit_back(up, gain, hat, factor):
        gained = up * gain
        return factor * (gained - hat * jnp.mean(gained * hat, axis=-1, keepdims=True))

    d_probs = jnp.concatenate([dgp[k, :experts, :] for k in range(8)], axis=0)
    mixed = probs[...] * d_probs
    d_logits = (mixed - probs[...] * jnp.sum(mixed, axis=0, keepdims=True)).astype(LOW)
    for n in range(count):
        d_res[n] = dot_tn(d_logits[:, n * rows : (n + 1) * rows], router[...])

    def back(i, gain_part):
        n, r = chunk_of(i)
        hat, factor = unit(resid[n, r, :])
        d_in = d_res[n, r, :] + dx_sum[n, r, :].astype(F32)
        total = cot[n, r, :].astype(F32) + unit_back(d_in, eg_ref[...], hat, factor)
        d_res[n, r, :] = total
        low_rows[n, r, :] = total.astype(LOW)
        return gain_part + jnp.sum(d_in * hat, axis=0, keepdims=True)

    gain_part = lax.fori_loop(0, count * steps, back, jnp.zeros((1, width), F32))
    rows_db.start()
    router_part = dot_nn(d_logits, expert_in[...].reshape(count * rows, width)).astype(LOW)
    first_row = lax.broadcasted_iota(jnp.int32, (16, piece), 0) == 0
    for k in range(8):
        cols = slice(k * piece, (k + 1) * piece)
        aux[k, pl.ds(0, lanes), :] = router_part[:, cols]
        aux[k, pl.ds(lanes, 16), :] = jnp.where(first_row, gain_part[:, cols], 0.0).astype(LOW)
    for d, e in PEERS:
        send(0, d, e, aux.at[number(d, e)], aux_got)
    rows_db.first_steps()
    rows_db.last_steps()
    for d in (0,) + ORDER:
        rows_db.arrived(d, 0)
        rows_db.arrived(d, 1)
    for n in range(9):
        loads[n].wait()

    for i in range(seq // tile):
        r = pl.ds(i * tile, tile)
        dctx[r, :] = dot_nn(db[0, r, :], wo[...]).astype(LOW)
    for d, e in PEERS + ((0, 0),):
        r = span(number(d, e) * piece, piece)
        dwo[r, :] = dot_tn(db[0, :, r], ctx[...]).astype(LOW)
        if d or e:
            send(1, d, e, dwo.at[r, :], dwo_got)
    @pl.loop(0, count * steps)
    def _(i):
        n, r = chunk_of(i)
        layer[n, r, :] = (resid[n, r, :] + out_sum[n, r, :].astype(F32)).astype(LOW)

    outs.append(keep(layer, layer_out, osem.at[4]))
    dk_s[...] = jnp.zeros_like(dk_s)
    dv_s[...] = jnp.zeros_like(dv_s)
    for a in range(heads):
        for i in range(seq // tile):
            r = pl.ds(i * tile, tile)
            n = (i + 1) * tile
            q_tile = qkv[r, pl.ds(a * hd, hd)]
            k_rows = qkv[pl.ds(0, n), pl.ds(heads * hd, hd)]
            v_rows = qkv[pl.ds(0, n), pl.ds((heads + 1) * hd, hd)]
            up = dctx[r, pl.ds(a * hd, hd)]
            low = prob[a, r, pl.ds(0, n)]
            wide = low.astype(F32)
            dprob = dot_nt(up, v_rows)
            delta = jnp.sum(wide * dprob, axis=-1, keepdims=True)
            dscore = (wide * (dprob - delta)).astype(LOW)
            dq_s[r, pl.ds(a * hd, hd)] = dot_nn(dscore, k_rows) * scale
            dk_s[pl.ds(0, n), :] += dot_tn(dscore, q_tile) * scale
            dv_s[pl.ds(0, n), :] += dot_tn(low, up)
    gq = jnp.zeros((1, hd), F32)
    gk = jnp.zeros((1, hd), F32)
    for i in range(seq // tile):
        r = pl.ds(i * tile, tile)
        dqkv[r, pl.ds((heads + 1) * hd, hd)] = dv_s[r, :].astype(LOW)
        for a in range(heads + 1):
            up = dq_s[r, pl.ds(a * hd, hd)] if a < heads else dk_s[r, :]
            one = pre[r, pl.ds(a * hd, hd)]
            factor = lax.rsqrt(jnp.mean(one * one, axis=-1, keepdims=True) + norm_eps)
            hat = one * factor
            turned = up * cos_ref[r, :] + pltpu.roll(up * sin_ref[r, :], hd // 2, 1)
            gain_part = jnp.sum(turned * hat, axis=0, keepdims=True)
            gained = turned * (qg_ref if a < heads else kg_ref)[...]
            back = factor * (gained - hat * jnp.mean(gained * hat, axis=-1, keepdims=True))
            dqkv[r, pl.ds(a * hd, hd)] = back.astype(LOW)
            if a < heads:
                gq = gq + gain_part
            else:
                gk = gk + gain_part
    head_part[...] = jnp.concatenate([gq, gk, jnp.zeros((6, hd), F32)], axis=0)
    for d, e in PEERS:
        send(3, d, e, head_part, head_got)
    rows_db.finish()
    for e in (1, 0):
        for d in FAR_FIRST:
            r = span(here.number(d, e) * rows, rows)
            db[0, r, :] = dot_nt(dqkv[r, :], w[...]).astype(LOW)
            dn.give(d, e)
    for d, e in PEERS + ((0, 0),):
        r = span(number(d, e) * piece, piece)
        dw[r, :] = dot_tn(xn[0, :, r], dqkv[...]).astype(LOW)
        if d or e:
            send(2, d, e, dw.at[r, pl.ds(0, part)], dwq_got)
        if e:
            sends.append(push(dw.at[r, pl.ds(part, 2 * hd)], kv_x.at[d], kxs.at[d], kxr.at[d], here.xn))
    for d in FAR_FIRST:
        dn.corner(d)
    for d in (2, 1, 3, 0):
        r = span(number(d, 0) * piece, piece)
        wait_for(kv_x.at[d], kxr.at[d], here.xn)
        both = dw[r, pl.ds(part, 2 * hd)].astype(F32) + kv_x[d].astype(F32)
        dw[r, pl.ds(part, 2 * hd)] = both.astype(LOW)
        if d:
            there = (4 - d) % 4
            sends.append(push(dw.at[r, pl.ds(part, 2 * hd)], kv_z.at[there], kzs.at[d], kzr.at[there], here.peer(d, 0)))
    for d in FAR_FIRST:
        dn.sides(d)
    for d in FAR_FIRST:
        dn.centre(d)

    def merged(n, wide, got, mine):
        for d in (0, 1):
            for e in (0, 1):
                first = mine if (d, e) == (0, 0) else got_from(n, d, e, got)
                both = first.astype(F32) + got_from(n, d + 2, e, got).astype(F32)
                wide[:, span((number(d, e) % 4) * part, part)] = both

    own = span(here.f * piece, piece)
    merged(1, wide_o, dwo_got, dwo[own, :])
    outs.append(keep(wide_o, do_out, osem.at[0]))
    aux_total = aux[here.f].astype(F32)
    for d, e in PEERS:
        aux_total = aux_total + got_from(0, d, e, aux_got).astype(F32)
    aux_out[...] = aux_total
    head_total = head_part[...]
    for d, e in PEERS:
        head_total = head_total + got_from(3, d, e, head_got)
    line[:, pl.ds(piece, hd)] = head_total
    dn.total()
    dn.share_start()
    dn.share_cross()
    dn.share_end(None)

    @pl.loop(0, count * steps)
    def _(i):
        n, r = chunk_of(i)
        hat, factor = unit(tokens[n, r, :].astype(F32))
        up = jnp.concatenate([dn.full[q, n, r, :] for q in range(4)], axis=1).astype(F32)
        low_rows[n, r, :] = (d_res[n, r, :] + unit_back(up, ag_ref[...], hat, factor)).astype(LOW)

    outs.append(keep(low_rows, input_out, osem.at[5]))
    merged(2, wide_q, dwq_got, dw[own, pl.ds(0, part)])
    outs.append(keep(wide_q, dq_out, osem.at[1]))
    kv = dw[own, pl.ds(part, 2 * hd)].astype(F32)
    for d in (1, 2, 3):
        wait_for(kv_z.at[d], kzr.at[d], here.xn)
        kv = kv + kv_z[d].astype(F32)
    wide_kv[...] = kv
    outs.append(keep(wide_kv.at[:, pl.ds(0, hd)], dk_out, osem.at[2]))
    outs.append(keep(wide_kv.at[:, pl.ds(hd, hd)], dv_out, osem.at[3]))

    def row_sums(product):
        high = product.astype(LOW)
        rest_ = (product - high.astype(F32)).astype(LOW)
        ones = jnp.ones((8, product.shape[1]), LOW)
        return dot_nt(ones, high) + dot_nt(ones, rest_)

    line[:, pl.ds(0, piece)] = (
        row_sums(query[...].astype(F32) * wide_q[...])
        + row_sums(key[...].astype(F32) * kv[:, :hd])
        + row_sums(value[...].astype(F32) * kv[:, hd:])
    )
    first = push(line, line_c, tsem.at[0], usem.at[0], here.cn)
    wait_for(line_c, usem.at[0], here.cn)
    first.wait_send()
    line[...] = line[...] + line_c[...]
    second = push(line, line_y, tsem.at[1], usem.at[1], here.yn)
    wait_for(line_y, usem.at[1], here.yn)
    gains_out[...] = line[...] + line_y[...]
    second.wait_send()
    dn.finish()
    for copy in sends:
        copy.wait_send()
    for copy in outs:
        copy.wait()


def end(xn, w, wo, pre, qkv, prob, ctx, tokens, out_sum, resid, cot, dx_sum, expert_in, probs, dgp, router,
        expert_gain, attention_gain, query, key, value, cosine, sine, query_gain, key_gain):
    count, rows, width = tokens.shape
    seq = rows * 8
    lanes = probs.shape[0]
    hd = query_gain.shape[0]
    piece, local = query.shape
    part = local // 4
    heads = part // hd
    vm = pltpu.VMEM
    dma = pltpu.SemaphoreType.DMA
    hbm = pl.BlockSpec(memory_space=pl.ANY)
    near = pl.BlockSpec(memory_space=pltpu.VMEM)
    shape = jax.ShapeDtypeStruct
    return pl.pallas_call(
        functools.partial(end_kernel, heads),
        out_shape=(
            shape((count, rows, width), LOW),
            shape((count, rows, width), LOW),
            shape((piece, local), F32),
            shape((piece, hd), F32),
            shape((piece, hd), F32),
            shape((piece, local), F32),
            shape((lanes + 16, piece), F32),
            shape((8, piece + hd), F32),
        ),
        in_specs=[hbm] * 9 + [near] * 16,
        out_specs=[hbm] * 6 + [near] * 2,
        scratch_shapes=[
            vm((count, rows, width), LOW),
            vm((count, rows, width), LOW),
            vm((count, rows, width), F32),
            vm((count, rows, width), LOW),
            vm((count, rows, width), LOW),
            vm((8, lanes + 16, piece), LOW),
            vm((1, seq, width), LOW),
            vm((1, seq, width), LOW),
            vm(w.shape, LOW),
            vm(wo.shape, LOW),
            vm(pre.shape, F32),
            vm(qkv.shape, LOW),
            vm(prob.shape, LOW),
            vm(ctx.shape, LOW),
            vm(ctx.shape, LOW),
            vm((seq, heads * hd), F32),
            vm((seq, hd), F32),
            vm((seq, hd), F32),
            vm((seq, (heads + 2) * hd), LOW),
            vm((width, part), LOW),
            vm((width, part + 2 * hd), LOW),
            vm((4, 2, piece, part), LOW),
            vm((4, 2, piece, part), LOW),
            vm((4, piece, 2 * hd), LOW),
            vm((4, piece, 2 * hd), LOW),
            vm((4, 2, lanes + 16, piece), LOW),
            vm((8, hd), F32),
            vm((4, 2, 8, hd), F32),
            vm((8, piece + hd), F32),
            vm((8, piece + hd), F32),
            vm((8, piece + hd), F32),
            vm((piece, local), F32),
            vm((piece, local), F32),
            vm((piece, 2 * hd), F32),
            dma((9,)),
            dma((4, 4, 2)),
            dma((4, 4, 2)),
            dma((4,)),
            dma((4,)),
            dma((4,)),
            dma((4,)),
            dma((2,)),
            dma((2,)),
            dma((6,)),
        ]
        + Gather.scratch()
        + Sum.scratch(1, rows, width, LOW, BY_X),
        compiler_params=pltpu.CompilerParams(
            collective_id=5, has_side_effects=True, vmem_limit_bytes=VMEM_LIMIT
        ),
        name="end",
    )(xn, w, wo, pre, qkv, prob, ctx, tokens, out_sum, resid, cot, dx_sum, expert_in, probs, dgp, router,
      expert_gain[None], attention_gain[None], query, key, value, cosine, sine, query_gain[None], key_gain[None])


def rotate_half(values):
    middle = values.shape[-1] // 2
    return jnp.concatenate([-values[..., middle:], values[..., :middle]], axis=-1)


def rope_tables(positions, head_width):
    middle = head_width // 2
    frequency = rope_base ** (-jnp.arange(middle, dtype=jnp.float32) * 2.0 / head_width)
    angles = positions.astype(jnp.float32)[:, None] * frequency[None, :]
    angles = jnp.concatenate([angles, angles], axis=1)
    return (jnp.cos(angles), jnp.sin(angles))


def norm_parts(values):
    factor = lax.rsqrt(jnp.mean(values * values, axis=-1, keepdims=True) + norm_eps)
    return (values * factor, factor)


def norm_back(upstream, gain, normal, factor):
    scaled = upstream * gain
    return factor * (scaled - normal * jnp.mean(scaled * normal, axis=-1, keepdims=True))


def head_back(upstream, cosine_heads, sine_heads, gain, normal, factor):
    turned = upstream * cosine_heads - rotate_half(upstream * sine_heads)
    gain_part = jnp.sum(turned * normal, axis=(0, 1))
    return (norm_back(turned, gain, normal, factor), gain_part)


def fetch_weights(query_weight, key_weight, value_weight, output_weight, router_weight):
    return (
        lax.all_gather(query_weight, "fsdp", axis=0, tiled=True),
        lax.all_gather(key_weight, "fsdp", axis=0, tiled=True),
        lax.all_gather(value_weight, "fsdp", axis=0, tiled=True),
        lax.all_gather(output_weight, "fsdp", axis=0, tiled=True),
        lax.all_gather(router_weight, "fsdp", axis=0, tiled=True),
    )


def widen(summed):
    return lax.all_gather(summed, "tp", axis=3, tiled=True)


def carry_back(summed):
    return lax.all_to_all(summed, "fsdp", split_axis=0, concat_axis=0, tiled=True)


def send_home(summed):
    arrived_home = carry_back(widen(summed))
    return arrived_home


def general_device(
    tokens,
    cotangent,
    expert_ids,
    attention_gain,
    query_gain,
    key_gain,
    query_weight,
    key_weight,
    value_weight,
    output_weight,
    expert_gain,
    router_weight,
    gate_weight,
    up_weight,
    down_weight,
):
    micro_count = tokens.shape[0]
    tok_rows = tokens.shape[1]
    width = tokens.shape[2]
    route_count = expert_ids.shape[2]
    head_dim = query_gain.shape[0]
    local_heads = query_weight.shape[1] // head_dim
    local_groups = key_weight.shape[1] // head_dim
    group_size = local_heads // local_groups
    fsdp_count = lax.axis_size("fsdp")
    seq_len = tok_rows * fsdp_count
    experts_here = gate_weight.shape[0]
    expert_count = experts_here * fsdp_count
    capacity = max(2, 5 * tok_rows * route_count // (4 * expert_count))
    key_block = math.gcd(seq_len, 512)
    score_scale = 1.0 / math.sqrt(head_dim)
    query_count = tok_rows * group_size
    routed_total = tok_rows * route_count
    start_row = lax.axis_index("fsdp") * tok_rows
    positions = start_row + jnp.arange(tok_rows, dtype=jnp.int32)
    cosine_table, sine_table = rope_tables(positions, head_dim)
    cosine_heads = cosine_table[:, None, :]
    sine_heads = sine_table[:, None, :]
    query_pos = start_row + jnp.arange(query_count, dtype=jnp.int32) // group_size
    block_total = (start_row + tok_rows + key_block - 1) // key_block
    expert_range = jnp.arange(expert_count, dtype=jnp.int32)
    zero_row = jnp.zeros((1, width), jnp.bfloat16)

    def to_rows(tensor):
        return (
            tensor.reshape(tok_rows, local_groups, group_size, head_dim)
            .transpose(1, 0, 2, 3)
            .reshape(local_groups, query_count, head_dim)
        )

    def from_rows(tensor):
        return (
            tensor.reshape(local_groups, tok_rows, group_size, head_dim)
            .transpose(1, 0, 2, 3)
            .reshape(tok_rows, local_heads, head_dim)
        )

    acc_attention_gain = jnp.zeros((width,), jnp.float32)
    acc_head_gains = jnp.zeros((2, head_dim), jnp.float32)
    acc_query = jnp.zeros((width, local_heads * head_dim), jnp.float32)
    acc_key = jnp.zeros((width, local_groups * head_dim), jnp.float32)
    acc_value = jnp.zeros((width, local_groups * head_dim), jnp.float32)
    acc_output = jnp.zeros((width, local_heads * head_dim), jnp.float32)
    acc_expert_gain = jnp.zeros((width,), jnp.float32)
    acc_router = jnp.zeros((width, expert_count), jnp.float32)
    acc_gate = jnp.zeros(gate_weight.shape, jnp.float32)
    acc_up = jnp.zeros(up_weight.shape, jnp.float32)
    acc_down = jnp.zeros(down_weight.shape, jnp.float32)
    layer_rows = []
    input_rows = []
    for micro_index in range(micro_count):
        inputs = tokens[micro_index].astype(jnp.float32)
        query_full, key_full, value_full, output_full, router_full = fetch_weights(
            query_weight, key_weight, value_weight, output_weight, router_weight
        )
        input_hat, attention_factor = norm_parts(inputs)
        normed = (input_hat * attention_gain).astype(jnp.bfloat16)
        query_pre = jnp.dot(normed, query_full, preferred_element_type=jnp.float32).reshape(
            tok_rows, local_heads, head_dim
        )
        key_pre = jnp.dot(normed, key_full, preferred_element_type=jnp.float32).reshape(
            tok_rows, local_groups, head_dim
        )
        value_low = jnp.dot(normed, value_full, preferred_element_type=jnp.float32).astype(
            jnp.bfloat16
        )
        query_hat, query_factor = norm_parts(query_pre)
        key_hat, key_factor = norm_parts(key_pre)
        query_scaled = query_hat * query_gain
        key_scaled = key_hat * key_gain
        query_low = (query_scaled * cosine_heads + rotate_half(query_scaled) * sine_heads).astype(
            jnp.bfloat16
        )
        key_low = (key_scaled * cosine_heads + rotate_half(key_scaled) * sine_heads).astype(
            jnp.bfloat16
        )
        key_all, value_all = (
            lax.all_gather(
                key_low.reshape(tok_rows, local_groups * head_dim), "fsdp", axis=0, tiled=True
            ),
            lax.all_gather(value_low, "fsdp", axis=0, tiled=True),
        )
        key_heads = key_all.reshape(seq_len, local_groups, head_dim).transpose(1, 0, 2)
        value_heads = value_all.reshape(seq_len, local_groups, head_dim).transpose(1, 0, 2)
        query_rows = to_rows(query_low)

        def scores_at(block_index):
            block_start = block_index * key_block
            key_slice = lax.dynamic_slice_in_dim(key_heads, block_start, key_block, 1)
            raw_scores = (
                jnp.einsum(
                    "gqd,gkd->gqk", query_rows, key_slice, preferred_element_type=jnp.float32
                )
                * score_scale
            )
            allowed = (block_start + jnp.arange(key_block, dtype=jnp.int32))[None, :] <= query_pos[
                :, None
            ]
            return (jnp.where(allowed[None], raw_scores, masked_score), allowed, block_start)

        def stats_step(block_index, carried):
            run_peak, run_total = carried
            scores, allowed, block_start = scores_at(block_index)
            new_peak = jnp.maximum(run_peak, jnp.max(scores, axis=-1))
            terms = jnp.where(allowed[None], jnp.exp(scores - new_peak[..., None]), 0.0)
            return (new_peak, run_total * jnp.exp(run_peak - new_peak) + jnp.sum(terms, axis=-1))

        start_stats = (
            jnp.full((local_groups, query_count), masked_score, jnp.float32),
            jnp.zeros((local_groups, query_count), jnp.float32),
        )
        run_peak, run_total = lax.fori_loop(0, block_total, stats_step, start_stats)
        log_total = run_peak + jnp.log(run_total)

        def value_step(block_index, acc_context):
            scores, allowed, block_start = scores_at(block_index)
            probs_low = jnp.where(
                allowed[None], jnp.exp(scores - log_total[..., None]), 0.0
            ).astype(jnp.bfloat16)
            value_slice = lax.dynamic_slice_in_dim(value_heads, block_start, key_block, 1)
            return acc_context + jnp.einsum(
                "gqk,gkd->gqd", probs_low, value_slice, preferred_element_type=jnp.float32
            )

        context_rows = lax.fori_loop(
            0,
            block_total,
            value_step,
            jnp.zeros((local_groups, query_count, head_dim), jnp.float32),
        )
        context_low = (
            from_rows(context_rows).reshape(tok_rows, local_heads * head_dim).astype(jnp.bfloat16)
        )
        branch_part = jnp.einsum(
            "th,dh->td", context_low, output_full, preferred_element_type=jnp.float32
        )
        resid = inputs + lax.psum(branch_part.astype(jnp.bfloat16), "tp").astype(jnp.float32)
        resid_hat, expert_factor = norm_parts(resid)
        expert_in = (resid_hat * expert_gain).astype(jnp.bfloat16)
        logits = jnp.dot(expert_in, router_full, preferred_element_type=jnp.float32)
        routes_now = expert_ids[micro_index]
        choose = (routes_now[:, :, None] == expert_range[None, None, :]).astype(jnp.float32)
        picked = jnp.sum(choose * logits[:, None, :], axis=-1)
        shifted = jnp.exp(picked - jnp.max(picked, axis=-1, keepdims=True))
        gate_probs = shifted / jnp.sum(shifted, axis=-1, keepdims=True)
        flat_routes = routes_now.reshape(-1)
        onehot = (flat_routes[:, None] == expert_range[None, :]).astype(jnp.int32)
        rank_in = jnp.sum((jnp.cumsum(onehot, axis=0) - onehot) * onehot, axis=1)
        slot_index = flat_routes * capacity + rank_in
        slot_source = (
            jnp.full((expert_count * capacity,), routed_total, jnp.int32)
            .at[slot_index]
            .set(jnp.arange(routed_total, dtype=jnp.int32))
        )
        padded_in = jnp.concatenate([expert_in, zero_row], axis=0)
        outgoing = padded_in[slot_source // route_count].reshape(
            fsdp_count, experts_here, capacity, width
        )
        arrived = lax.all_to_all(outgoing, "fsdp", split_axis=0, concat_axis=0, tiled=True)
        gate_pre = jnp.einsum(
            "secd,efd->secf", arrived, gate_weight, preferred_element_type=jnp.float32
        )
        up_pre = jnp.einsum(
            "secd,efd->secf", arrived, up_weight, preferred_element_type=jnp.float32
        )
        gate_sigmoid = jax.nn.sigmoid(gate_pre)
        inner_low = (gate_pre * gate_sigmoid * up_pre).astype(jnp.bfloat16)
        result_part = jnp.einsum(
            "secf,efd->secd", inner_low, down_weight, preferred_element_type=jnp.float32
        )
        result_low = lax.psum_scatter(
            result_part.astype(jnp.bfloat16), "tp", scatter_dimension=3, tiled=True
        )
        result_home = send_home(result_low)
        routed = (
            result_home.reshape(expert_count * capacity, width)[slot_index]
            .astype(jnp.float32)
            .reshape(tok_rows, route_count, width)
        )
        layer_rows.append(
            (resid + jnp.sum(gate_probs[:, :, None] * routed, axis=1)).astype(jnp.bfloat16)
        )
        query_full, key_full, value_full, output_full, router_full = fetch_weights(
            query_weight, key_weight, value_weight, output_weight, router_weight
        )
        out_grad = cotangent[micro_index].astype(jnp.float32)
        d_route = (
            (gate_probs[:, :, None] * out_grad[:, None, :])
            .astype(jnp.bfloat16)
            .reshape(routed_total, width)
        )
        d_gate_probs = jnp.sum(out_grad[:, None, :] * routed, axis=-1)
        d_pick = gate_probs * (
            d_gate_probs - jnp.sum(gate_probs * d_gate_probs, axis=-1, keepdims=True)
        )
        d_logits = jnp.sum(choose * d_pick[:, :, None], axis=1).astype(jnp.bfloat16)
        grad_outgoing = jnp.concatenate([d_route, zero_row], axis=0)[slot_source].reshape(
            fsdp_count, experts_here, capacity, width
        )
        grad_arrived = lax.all_to_all(
            grad_outgoing, "fsdp", split_axis=0, concat_axis=0, tiled=True
        )
        d_inner = jnp.einsum(
            "secd,efd->secf", grad_arrived, down_weight, preferred_element_type=jnp.float32
        )
        acc_down = acc_down + jnp.einsum(
            "secf,secd->efd", inner_low, grad_arrived, preferred_element_type=jnp.float32
        )
        d_gate_low = (
            d_inner * up_pre * gate_sigmoid * (1.0 + gate_pre * (1.0 - gate_sigmoid))
        ).astype(jnp.bfloat16)
        d_up_low = (d_inner * gate_pre * gate_sigmoid).astype(jnp.bfloat16)
        acc_gate = acc_gate + jnp.einsum(
            "secf,secd->efd", d_gate_low, arrived, preferred_element_type=jnp.float32
        )
        acc_up = acc_up + jnp.einsum(
            "secf,secd->efd", d_up_low, arrived, preferred_element_type=jnp.float32
        )
        d_copy_part = jnp.einsum(
            "secf,efd->secd", d_gate_low, gate_weight, preferred_element_type=jnp.float32
        ) + jnp.einsum("secf,efd->secd", d_up_low, up_weight, preferred_element_type=jnp.float32)
        d_copy_low = lax.psum_scatter(
            d_copy_part.astype(jnp.bfloat16), "tp", scatter_dimension=3, tiled=True
        )
        d_copy_home = send_home(d_copy_low)
        d_copies = (
            d_copy_home.reshape(expert_count * capacity, width)[slot_index]
            .astype(jnp.float32)
            .reshape(tok_rows, route_count, width)
        )
        d_expert_in = jnp.sum(d_copies, axis=1) + jnp.dot(
            d_logits, router_full.T, preferred_element_type=jnp.float32
        )
        acc_router = acc_router + jnp.dot(expert_in.T, d_logits, preferred_element_type=jnp.float32)
        acc_expert_gain = acc_expert_gain + jnp.sum(d_expert_in * resid_hat, axis=0)
        d_resid = out_grad + norm_back(d_expert_in, expert_gain, resid_hat, expert_factor)
        d_branch = d_resid.astype(jnp.bfloat16)
        acc_output = acc_output + jnp.einsum(
            "td,th->dh", d_branch, context_low, preferred_element_type=jnp.float32
        )
        d_context = jnp.dot(d_branch, output_full, preferred_element_type=jnp.float32).astype(
            jnp.bfloat16
        )
        d_context_rows = to_rows(d_context.reshape(tok_rows, local_heads, head_dim))
        delta_rows = jnp.sum(d_context_rows.astype(jnp.float32) * context_rows, axis=-1)

        def grad_step(block_index, carried):
            d_query_rows, key_grads_all = carried
            scores, allowed, block_start = scores_at(block_index)
            probs = jnp.where(allowed[None], jnp.exp(scores - log_total[..., None]), 0.0)
            key_slice = lax.dynamic_slice_in_dim(key_heads, block_start, key_block, 1)
            value_slice = lax.dynamic_slice_in_dim(value_heads, block_start, key_block, 1)
            d_probs = jnp.einsum(
                "gqd,gkd->gqk", d_context_rows, value_slice, preferred_element_type=jnp.float32
            )
            d_scores = (probs * (d_probs - delta_rows[..., None])).astype(jnp.bfloat16)
            d_query_rows = (
                d_query_rows
                + jnp.einsum(
                    "gqk,gkd->gqd", d_scores, key_slice, preferred_element_type=jnp.float32
                )
                * score_scale
            )
            d_key_block = (
                jnp.einsum("gqk,gqd->kgd", d_scores, query_rows, preferred_element_type=jnp.float32)
                * score_scale
            )
            d_value_block = jnp.einsum(
                "gqk,gqd->kgd",
                probs.astype(jnp.bfloat16),
                d_context_rows,
                preferred_element_type=jnp.float32,
            )
            current = lax.dynamic_slice_in_dim(key_grads_all, block_start, key_block, 0)
            updated = current + jnp.concatenate([d_key_block, d_value_block], axis=-1)
            return (
                d_query_rows,
                lax.dynamic_update_slice_in_dim(key_grads_all, updated, block_start, 0),
            )

        start_grads = (
            jnp.zeros((local_groups, query_count, head_dim), jnp.float32),
            jnp.zeros((seq_len, local_groups, 2 * head_dim), jnp.float32),
        )
        d_query_rows, key_grads_all = lax.fori_loop(0, block_total, grad_step, start_grads)
        key_grads = (
            lax.psum_scatter(
                key_grads_all.reshape(seq_len, local_groups * 2 * head_dim).astype(jnp.bfloat16),
                "fsdp",
                scatter_dimension=0,
                tiled=True,
            )
            .astype(jnp.float32)
            .reshape(tok_rows, local_groups, 2 * head_dim)
        )
        d_value_low = (
            key_grads[..., head_dim:]
            .reshape(tok_rows, local_groups * head_dim)
            .astype(jnp.bfloat16)
        )
        d_key_pre, key_gain_part = head_back(
            key_grads[..., :head_dim], cosine_heads, sine_heads, key_gain, key_hat, key_factor
        )
        d_query_pre, query_gain_part = head_back(
            from_rows(d_query_rows), cosine_heads, sine_heads, query_gain, query_hat, query_factor
        )
        d_query_low = d_query_pre.astype(jnp.bfloat16).reshape(tok_rows, local_heads * head_dim)
        d_key_low = d_key_pre.astype(jnp.bfloat16).reshape(tok_rows, local_groups * head_dim)
        d_normed_part = jnp.dot(d_query_low, query_full.T, preferred_element_type=jnp.float32)
        d_normed_part = d_normed_part + jnp.dot(
            d_key_low, key_full.T, preferred_element_type=jnp.float32
        )
        d_normed_part = d_normed_part + jnp.dot(
            d_value_low, value_full.T, preferred_element_type=jnp.float32
        )
        acc_query = acc_query + jnp.dot(normed.T, d_query_low, preferred_element_type=jnp.float32)
        acc_key = acc_key + jnp.dot(normed.T, d_key_low, preferred_element_type=jnp.float32)
        acc_value = acc_value + jnp.dot(normed.T, d_value_low, preferred_element_type=jnp.float32)
        d_normed, head_gain_parts = (
            lax.psum(d_normed_part.astype(jnp.bfloat16), "tp").astype(jnp.float32),
            lax.psum(jnp.stack([query_gain_part, key_gain_part]).astype(jnp.bfloat16), "tp").astype(
                jnp.float32
            ),
        )
        acc_head_gains = acc_head_gains + head_gain_parts
        acc_attention_gain = acc_attention_gain + jnp.sum(d_normed * input_hat, axis=0)
        input_rows.append(
            (d_resid + norm_back(d_normed, attention_gain, input_hat, attention_factor)).astype(
                jnp.bfloat16
            )
        )
    summed = (
        lax.psum_scatter(
            acc_attention_gain.astype(jnp.bfloat16), "fsdp", scatter_dimension=0, tiled=True
        ).astype(jnp.float32),
        lax.psum_scatter(
            acc_head_gains[0].astype(jnp.bfloat16), "fsdp", scatter_dimension=0, tiled=True
        ).astype(jnp.float32),
        lax.psum_scatter(
            acc_head_gains[1].astype(jnp.bfloat16), "fsdp", scatter_dimension=0, tiled=True
        ).astype(jnp.float32),
        lax.psum_scatter(
            acc_query.astype(jnp.bfloat16), "fsdp", scatter_dimension=0, tiled=True
        ).astype(jnp.float32),
        lax.psum_scatter(
            acc_key.astype(jnp.bfloat16), "fsdp", scatter_dimension=0, tiled=True
        ).astype(jnp.float32),
        lax.psum_scatter(
            acc_value.astype(jnp.bfloat16), "fsdp", scatter_dimension=0, tiled=True
        ).astype(jnp.float32),
        lax.psum_scatter(
            acc_output.astype(jnp.bfloat16), "fsdp", scatter_dimension=0, tiled=True
        ).astype(jnp.float32),
        lax.psum_scatter(
            acc_expert_gain.astype(jnp.bfloat16), "fsdp", scatter_dimension=0, tiled=True
        ).astype(jnp.float32),
        lax.psum_scatter(
            acc_router.astype(jnp.bfloat16), "fsdp", scatter_dimension=0, tiled=True
        ).astype(jnp.float32),
    )
    return (
        jnp.stack(layer_rows),
        jnp.stack(input_rows),
        summed[0],
        summed[1],
        summed[2],
        summed[3],
        summed[4],
        summed[5],
        summed[6],
        summed[7],
        summed[8],
        acc_gate,
        acc_up,
        acc_down,
    )


def small_device(
    tokens,
    cotangent,
    expert_ids,
    attention_gain,
    query_gain,
    key_gain,
    query_weight,
    key_weight,
    value_weight,
    output_weight,
    expert_gain,
    router_weight,
    gate_weight,
    up_weight,
    down_weight,
):
    count, rows, width = tokens.shape
    hd = query_gain.shape[0]
    f = lax.axis_index("fsdp")
    n_fsdp = lax.axis_size("fsdp")
    seq = rows * n_fsdp
    experts = gate_weight.shape[0]
    expert_count = experts * n_fsdp
    piece = query_weight.shape[0]

    cosine, sine = signed_tables(seq, hd)
    (normed_all, weights, output_pair, router_all, ids_all, grad_all, pre, qkv, prob, context, resid, expert_in) = begin(
        cotangent,
        query_weight,
        key_weight,
        value_weight,
        output_weight,
        router_weight.T,
        expert_ids.transpose(0, 2, 1),
        tokens,
        attention_gain,
        expert_gain,
        cosine,
        sine,
        query_gain,
        key_gain,
    )
    expert_all, act, dx_sum, out_sum, probs, dgp = run_experts(
        expert_in, grad_all, ids_all, router_all, gate_weight, up_weight, down_weight
    )
    layer_output, input_grad, d_query, d_key, d_value, d_output, aux_sum, line = end(
        normed_all,
        weights,
        output_pair,
        pre,
        qkv,
        prob,
        context,
        tokens,
        out_sum,
        resid,
        cotangent,
        dx_sum,
        expert_in,
        probs,
        dgp,
        router_all,
        expert_gain,
        attention_gain,
        query_weight,
        key_weight,
        value_weight,
        cosine,
        sine,
        query_gain,
        key_gain,
    )
    d_gate, d_up, d_down, layer_output, input_grad, d_query, d_output = expert_grads(
        act, expert_all, grad_all, layer_output, input_grad, d_query, d_output
    )
    own_gain = lax.dynamic_slice_in_dim(attention_gain, f * piece, piece, 0)
    head_piece = hd // n_fsdp
    head_gains = lax.dynamic_slice_in_dim(line[:2, piece:], f * head_piece, head_piece, 1)
    return (
        layer_output,
        input_grad,
        line[0, :piece] / own_gain,
        head_gains[0],
        head_gains[1],
        d_query,
        d_key,
        d_value,
        d_output,
        aux_sum[expert_count],
        aux_sum[:expert_count].T,
        d_gate.reshape(gate_weight.shape),
        d_up.reshape(up_weight.shape),
        d_down.reshape(down_weight.shape),
    )


def solution(mesh):
    body = small_device if (mesh.shape["fsdp"], mesh.shape["tp"]) == (8, 4) else general_device
    return jax.shard_map(
        body,
        mesh=mesh,
        in_specs=(
            P(None, "fsdp", None),
            P(None, "fsdp", None),
            P(None, "fsdp", None),
            P(),
            P(),
            P(),
            P("fsdp", "tp"),
            P("fsdp", "tp"),
            P("fsdp", "tp"),
            P("fsdp", "tp"),
            P(),
            P("fsdp", None),
            P("fsdp", "tp", None),
            P("fsdp", "tp", None),
            P("fsdp", "tp", None),
        ),
        out_specs=(
            P(None, "fsdp", None),
            P(None, "fsdp", None),
            P("fsdp"),
            P("fsdp"),
            P("fsdp"),
            P("fsdp", "tp"),
            P("fsdp", "tp"),
            P("fsdp", "tp"),
            P("fsdp", "tp"),
            P("fsdp"),
            P("fsdp", None),
            P("fsdp", "tp", None),
            P("fsdp", "tp", None),
            P("fsdp", "tp", None),
        ),
        check_vma=False,
    )
```

```python
import functools
import math

import jax
import jax.numpy as jnp
import numpy as np
from jax import lax
from jax.experimental import pallas as pl
from jax.experimental.pallas import tpu as pltpu
from jax.sharding import PartitionSpec as P

norm_eps = 1e-06
rope_base = 1000000.0
masked_score = -1e30
MESH = pl.DeviceIdType.MESH
LOW = jnp.bfloat16
F32 = jnp.float32
VMEM_LIMIT = 62 * 2**20


def coords():
    f = lax.axis_index("fsdp")
    t = lax.axis_index("tp")
    return f // 2, f % 2, t // 2, t % 2


def place(z, x, y, c):
    return (2 * z + x, 2 * y + c)


def span(first, count):
    return pl.ds(pl.multiple_of(first, count), count)


class Here:
    def __init__(self):
        z, x, y, c = coords()
        self.z, self.x, self.y, self.c = z, x, y, c
        self.f, self.t = 2 * z + x, 2 * y + c
        self.xn, self.yn, self.cn = place(z, 1 - x, y, c), place(z, x, 1 - y, c), place(z, x, y, 1 - c)
        self.lanes = ((x, y), (1 - x, y), (x, 1 - y), (1 - x, 1 - y))

    def zr(self, d):
        return (self.z + d) % 4

    def flip(self, k):
        return (self.z // 2 + k // 2) % 2 * 2 + (self.z % 2 + k % 2) % 2

    def zd(self, j):
        inner = (self.z % 3 + 1) // 2
        return self.flip(j + inner * (j // 2) * (1 - 2 * (j % 2)))

    def at_z(self, z):
        return place(z, self.x, self.y, self.c)

    def number(self, j, e):
        return 2 * self.zd(j) + (self.x + e) % 2

    def peer(self, d, e):
        return place(self.zr(d), (self.x + e) % 2, self.y, self.c)

    def greet(self):
        self.say()
        self.hear()

    def say(self):
        peers = [self.peer(d, e) for d in range(4) for e in range(2) if d or e] + [self.yn, self.cn]
        for peer in peers:
            pl.semaphore_signal(pltpu.get_barrier_semaphore(), inc=1, device_id=peer, device_id_type=MESH)

    def hear(self):
        pl.semaphore_wait(pltpu.get_barrier_semaphore(), 9)


def remote(src, dst, send_sem, recv_sem, device):
    return pltpu.make_async_remote_copy(
        src_ref=src, dst_ref=dst, send_sem=send_sem, recv_sem=recv_sem, device_id=device, device_id_type=MESH
    )


def push(src, dst, send_sem, recv_sem, device):
    copy = remote(src, dst, send_sem, recv_sem, device)
    copy.start()
    return copy


def keep(src, dst, sem):
    copy = pltpu.make_async_copy(src, dst, sem)
    copy.start()
    return copy


ORDER = (1, 2, 3)
FAR_FIRST = (3, 2, 1, 0)


class Gather:
    scratch = staticmethod(
        lambda: [pltpu.SemaphoreType.DMA((1,)), pltpu.SemaphoreType.DMA((6,))]
        + [pltpu.SemaphoreType.DMA((4,))] * 9
        + [pltpu.SemaphoreType.DMA((4, 4))] * 2
    )
    slots = 13

    def __init__(self, here, whole, src, dst, sems, by_x, own=None):
        self.here, self.whole, self.src, self.dst, self.own_rows = here, whole, src, dst, own
        (self.loc, self.sz, self.rz, self.sx, self.rx, self.sy, self.ry,
         self.sdx, self.rdx, self.sdy, self.rdy, self.sc, self.rc) = sems
        self.rows, self.cols = src.shape[1], src.shape[2] // 4
        self.half = by_x
        self.sends = []

    def block(self, z, x, y, c, h=None):
        first = (2 * z + x) * self.rows
        rows = span(first, self.rows)
        if h is not None:
            start, count = ((0, self.half), (self.half, self.rows - self.half))[h]
            rows = pl.ds(pl.multiple_of(first + start, 16), count)
        return self.dst.at[:, rows, span((2 * y + c) * self.cols, self.cols)]

    def source(self, z_to, t, first, count):
        seqs = slice(None) if self.whole else pl.ds(z_to // 2, 1)
        return self.src.at[seqs, pl.ds(first, count), span(t * self.cols, self.cols)]

    def push(self, make, when=None):
        if when is None:
            push(*make())
        else:
            pl.when(when)(lambda: push(*make()) and None)
        self.sends.append((make, when))

    def landed(self, ref, sem):
        pltpu.make_async_remote_copy(
            src_ref=ref, dst_ref=ref, send_sem=sem, recv_sem=sem, device_id=self.here.xn, device_id_type=MESH
        ).wait_recv()

    def start(self):
        h = self.here
        self.inner = h.z % 3 > 0
        self.along(0, h.flip(1), True)
        self.along(1, h.flip(3), self.inner)
        if not self.whole:
            self.along(2, h.flip(2), h.z % 3 == 0)
        self.push(lambda: (self.source(h.z, h.t, 0, self.rows), self.block(h.z, h.x, h.y, h.c),
                           self.sx.at[h.z], self.rx.at[h.z], h.xn))
        if self.half:
            self.push(lambda: (self.source(h.z, 2 * (1 - h.y) + h.c, 0, self.half),
                               self.block(h.z, h.x, 1 - h.y, h.c, 0), self.sdx.at[h.z], self.rdx.at[h.z], h.xn))
        own = self.src if self.whole else self.src.at[pl.ds(h.z // 2, 1)]
        if self.own_rows is not None:
            own = self.own_rows
            pltpu.make_async_copy(self.src, own, self.loc.at[0]).start()
            pltpu.make_async_copy(self.src, own, self.loc.at[0]).wait()
        self.own = keep(own, self.dst.at[:, span(h.f * self.rows, self.rows), :], self.loc.at[0])

    def along(self, n, z_to, when):
        h = self.here
        self.push(lambda: (self.source(z_to, h.t, 0, self.rows), self.block(h.z, h.x, h.y, h.c),
                           self.sz.at[n], self.rz.at[h.z], h.at_z(z_to)), None if when is True else when)

    def relay(self, j):
        h, zd = self.here, self.here.zd(j)
        self.landed(self.block(zd, h.x, h.y, h.c), self.rz.at[zd])
        if j > 1 or self.whole:

            def make():
                b = self.block(h.zd(j), h.x, h.y, h.c)
                return b, b, self.sz.at[2 + j], self.rz.at[h.zd(j)], h.at_z(h.flip(3 if j == 1 else 1))

            self.push(make, self.inner)

    def pass_on(self, d, lane, sends, recvs, device, h=None):
        x, y = self.here.lanes[lane]

        def make():
            zd = self.here.zd(d)
            b = self.block(zd, x, y, self.here.c, h)
            return b, b, sends(zd), recvs(zd), device

        self.push(make)

    def spread(self, d):
        h = self.here
        self.pass_on(d, 0, lambda k: self.sx.at[k], lambda k: self.rx.at[k], h.xn)
        self.pass_on(d, 0, lambda k: self.sy.at[k], lambda k: self.ry.at[k], h.yn)
        self.pass_on(d, 0, lambda k: self.sc.at[0, k], lambda k: self.rc.at[0, k], h.cn)

    def cross(self, d):
        h, zd = self.here, self.here.zd(d)
        self.landed(self.block(zd, 1 - h.x, h.y, h.c), self.rx.at[zd])
        self.pass_on(d, 1, lambda k: self.sdy.at[k], lambda k: self.rdy.at[k], h.yn, 1)
        self.pass_on(d, 1, lambda k: self.sc.at[1, k], lambda k: self.rc.at[1, k], h.cn)
        if d != 0:
            self.landed(self.block(zd, h.x, 1 - h.y, h.c), self.ry.at[zd])
            if self.half:
                self.pass_on(d, 2, lambda k: self.sdx.at[k], lambda k: self.rdx.at[k], h.xn, 0)
            self.pass_on(d, 2, lambda k: self.sc.at[2, k], lambda k: self.rc.at[2, k], h.cn)

    def close(self, d):
        h, zd = self.here, self.here.zd(d)
        if self.half:
            self.landed(self.block(zd, 1 - h.x, 1 - h.y, h.c, 0), self.rdx.at[zd])
        self.landed(self.block(zd, 1 - h.x, 1 - h.y, h.c, 1), self.rdy.at[zd])
        self.pass_on(d, 3, lambda k: self.sc.at[3, k], lambda k: self.rc.at[3, k], h.cn)

    def first_steps(self):
        for j in ORDER:
            self.relay(j)
            self.spread(j)
            if j < 3:
                self.cross(j - 1)

    def last_steps(self):
        self.close(0)
        for j in (2, 3):
            self.cross(j)
            self.close(j - 1)
        self.close(3)

    def arrived(self, d, e):
        h, zd = self.here, self.here.zd(d)
        if e == 0:
            if d == 0:
                self.own.wait()
            else:
                self.landed(self.block(zd, h.x, h.y, 1 - h.c), self.rc.at[0, zd])
                self.landed(self.block(zd, h.x, 1 - h.y, 1 - h.c), self.rc.at[2, zd])
        else:
            self.landed(self.block(zd, 1 - h.x, h.y, 1 - h.c), self.rc.at[1, zd])
            self.landed(self.block(zd, 1 - h.x, 1 - h.y, 1 - h.c), self.rc.at[3, zd])

    def finish(self):
        for make, when in self.sends:
            if when is None:
                remote(*make()).wait_send()
            else:
                pl.when(when)(lambda make=make: remote(*make()).wait_send())


def add_into(target, *others):
    count, rows, _ = target.shape
    step = 32
    wide = target.dtype if len(others) == 1 else F32

    @pl.loop(0, count * rows // step)
    def _(i):
        n = i // (rows // step)
        r = pl.ds(pl.multiple_of((i % (rows // step)) * step, step), step)
        total = target[n, r, :].astype(wide)
        for other in others:
            total = total + other[n, r, :].astype(wide)
        target[n, r, :] = total.astype(target.dtype)


class Sum:
    slots = 23

    @staticmethod
    def scratch(count, rows, width, low, by_x):
        dma = pltpu.SemaphoreType.DMA
        cols = width // 4
        vm = pltpu.VMEM
        return [
            vm((4, 4, count, rows, cols), low),
            vm((4, count, max(by_x, 16), cols), low),
            vm((4, count, rows - by_x, cols), low),
            vm((4, count, rows, cols), low),
            vm((4, count, rows, cols), low),
            vm((4, count, rows, cols), low),
            vm((4, 2, rows, cols), low),
            vm((2, rows, cols), low),
            dma((4, 4)), dma((4, 4)),
        ] + [dma((4,))] * 10 + [dma((3,))] * 2 + [dma((5,))]

    def __init__(self, here, whole, part, refs, by_x):
        self.here, self.whole, self.part, self.by_x = here, whole, part, by_x
        (self.fc, self.f1x, self.f1y, self.f2x, self.f2y, self.fz, self.full, self.tmp, self.sc, self.rc,
         self.s1x, self.r1x, self.s1y, self.r1y, self.s2x, self.r2x, self.s2y, self.r2y, self.sz, self.rz,
         self.sg, self.rg, self.osem) = refs
        self.rows, self.cols = part.shape[1] // 8, part.shape[2] // 4
        self.top, self.low = pl.ds(0, by_x), pl.ds(by_x, self.rows - by_x)
        self.sends = []

    def block(self, d, lane, c):
        x, y = self.here.lanes[lane]
        return self.part.at[:, span((2 * self.here.zd(d) + x) * self.rows, self.rows),
                            span((2 * y + c) * self.cols, self.cols)]

    def push(self, make):
        push(*make())
        self.sends.append(make)

    def landed(self, ref, sem):
        pltpu.make_async_remote_copy(
            src_ref=ref, dst_ref=ref, send_sem=sem, recv_sem=sem, device_id=self.here.xn, device_id_type=MESH
        ).wait_recv()

    def giving(self, d, e):
        h = self.here
        for q in (0, 1):
            lane = 2 * q + e
            at = self.part.at[:, span((2 * h.zd(d) + (h.x + e) % 2) * self.rows, self.rows),
                              span((2 * ((h.y + q) % 2) + 1 - h.c) * self.cols, self.cols)]
            yield at, self.fc.at[lane, d], self.sc.at[lane, d], self.rc.at[lane, d], h.cn

    def give(self, d, e):
        for args in self.giving(d, e):
            push(*args)

    def pair(self, lane, d):
        self.landed(self.fc.at[lane, d], self.rc.at[lane, d])
        add_into(self.block(d, lane, self.here.c), self.fc.at[lane, d])

    def mine(self, d, lane, rows=slice(None)):
        return self.block(d, lane, self.here.c).at[:, rows]

    def corner(self, d):
        self.pair(3, d)
        if self.by_x:
            self.push(lambda: (self.mine(d, 3, self.top), self.f1x.at[d], self.s1x.at[d], self.r1x.at[d], self.here.xn))
        self.push(lambda: (self.mine(d, 3, self.low), self.f1y.at[d], self.s1y.at[d], self.r1y.at[d], self.here.yn))

    def sides(self, d):
        self.pair(1, d)
        self.landed(self.f1y.at[d], self.r1y.at[d])
        add_into(self.mine(d, 1, self.low), self.f1y.at[d])
        self.push(lambda: (self.mine(d, 1), self.f2x.at[d], self.s2x.at[d], self.r2x.at[d], self.here.xn))
        self.pair(2, d)
        if self.by_x:
            self.landed(self.f1x.at[d], self.r1x.at[d])
            add_into(self.mine(d, 2, self.top), self.f1x.at[d])
        self.push(lambda: (self.mine(d, 2), self.f2y.at[d], self.s2y.at[d], self.r2y.at[d], self.here.yn))

    def centre(self, d):
        self.pair(0, d)
        self.landed(self.f2x.at[d], self.r2x.at[d])
        self.landed(self.f2y.at[d], self.r2y.at[d])
        add_into(self.mine(d, 0), self.f2x.at[d], self.f2y.at[d])
        if d != 0:
            h = self.here
            self.push(lambda: (self.mine(d, 0), self.fz.at[h.z], self.sz.at[d], self.rz.at[h.z], h.at_z(h.zd(d))))

    def total(self):
        for d in (1, 2, 3):
            self.landed(self.fz.at[self.here.zd(d)], self.rz.at[self.here.zd(d)])
        b = self.block(0, 0, self.here.c)
        step = 32

        @pl.loop(0, 2 * self.rows // step)
        def _(i):
            n = i // (self.rows // step)
            r = pl.ds(pl.multiple_of((i % (self.rows // step)) * step, step), step)
            if self.whole:
                total = b[n, r, :].astype(F32)
                for d in (1, 2, 3):
                    total = total + self.fz[self.here.zd(d), n, r, :].astype(F32)
            else:
                total = jnp.where(self.here.z // 2 == n, b[0, r, :].astype(F32), 0.0)
                for d in (1, 2, 3):
                    total = total + jnp.where(self.here.zd(d) // 2 == n, self.fz[self.here.zd(d), 0, r, :].astype(F32), 0.0)
            self.tmp[n, r, :] = total.astype(self.tmp.dtype)

    def share(self, out):
        self.share_start()
        self.share_cross()
        self.share_end(out)

    def share_start(self):
        h = self.here
        self.keeps = [keep(self.tmp, self.full.at[h.t], self.osem.at[4])]
        self.push(lambda: (self.tmp, self.full.at[h.t], self.sg.at[0], self.rg.at[0], h.yn))
        self.push(lambda: (self.tmp, self.full.at[h.t], self.sg.at[1], self.rg.at[1], h.cn))

    def share_cross(self):
        h = self.here
        ty = 2 * (1 - h.y) + h.c
        self.landed(self.full.at[ty], self.rg.at[0])
        self.push(lambda: (self.full.at[ty], self.full.at[ty], self.sg.at[2], self.rg.at[2], h.cn))

    def share_end(self, out):
        h = self.here
        self.landed(self.full.at[2 * h.y + 1 - h.c], self.rg.at[1])
        self.landed(self.full.at[2 * (1 - h.y) + 1 - h.c], self.rg.at[2])
        self.keeps[0].wait()
        if out is None:
            return
        outs = [keep(self.full.at[q], out.at[:, :, pl.ds(q * self.cols, self.cols)], self.osem.at[q]) for q in range(4)]
        for copy in outs:
            copy.wait()

    def finish(self):
        for make in self.sends:
            remote(*make()).wait_send()
        for d in range(4):
            for e in range(2):
                for args in self.giving(d, e):
                    remote(*args).wait_send()


def wait_for(ref, sem, device):
    pltpu.make_async_remote_copy(
        src_ref=ref, dst_ref=ref, send_sem=sem, recv_sem=sem, device_id=device, device_id_type=MESH
    ).wait_recv()


def signed_tables(length, width):
    middle = width // 2
    frequency = rope_base ** (-np.arange(middle) * 2.0 / width)
    angles = np.arange(length)[:, None] * frequency[None, :]
    cosine, sine = np.cos(angles), np.sin(angles)
    return (
        jnp.asarray(np.concatenate([cosine, cosine], axis=1), F32),
        jnp.asarray(np.concatenate([-sine, sine], axis=1), F32),
    )


def dot_nn(a, b):
    return jnp.dot(a, b, preferred_element_type=F32)


def dot_nt(a, b):
    return lax.dot_general(a, b, (((1,), (1,)), ((), ())), preferred_element_type=F32)


def dot_tn(a, b):
    return lax.dot_general(a, b, (((0,), (0,)), ((), ())), preferred_element_type=F32)


BY_X = 64


class Weights:
    scratch = staticmethod(lambda: [pltpu.SemaphoreType.DMA((8, 4, 2))] * 4 + [pltpu.SemaphoreType.DMA((6,))])
    slots = 5

    def __init__(self, here, query, key, value, output, router, ids, w, wo, router_all, ids_all, sems):
        self.here = here
        self.query, self.output, self.w, self.wo = query, output, w, wo
        piece, part = query.shape[0], wo.shape[1]
        self.piece, self.part = piece, part
        hd = key.shape[1]
        self.shared = (
            (key, lambda f: w.at[span(f * piece, piece), pl.ds(part, hd)]),
            (value, lambda f: w.at[span(f * piece, piece), pl.ds(part + hd, hd)]),
            (router, lambda f: router_all.at[:, span(f * piece, piece)]),
            (ids, lambda f: ids_all.at[:, :, span(f * ids.shape[2], ids.shape[2])]),
        )
        self.qs, self.qr, self.ss, self.sr, self.loc = sems
        self.sends, self.keeps = [], []

    def landed(self, ref, sem):
        pltpu.make_async_remote_copy(
            src_ref=ref, dst_ref=ref, send_sem=sem, recv_sem=sem, device_id=self.here.xn, device_id_type=MESH
        ).wait_recv()

    def start_shared(self):
        h = self.here
        for n, (src, dst) in enumerate(self.shared):
            self.keeps.append(keep(src, dst(h.f), self.loc.at[n]))
            for d, e in ((2, 0), (1, 0), (3, 0), (0, 1)):
                self.sends.append(push(src, dst(h.f), self.ss.at[n, d, e], self.sr.at[n, (4 - d) % 4, e], h.peer(d, e)))

    def pass_shared(self, d):
        h = self.here
        for n, (_, dst) in enumerate(self.shared):
            ref = dst(2 * h.zr(d) + h.x)
            self.landed(ref, self.sr.at[n, d, 0])
            self.sends.append(push(ref, ref, self.ss.at[n, d, 1], self.sr.at[n, d, 1], h.xn))

    def wait_shared(self):
        h = self.here
        for n, (_, dst) in enumerate(self.shared):
            for d in range(4):
                self.landed(dst(2 * h.zr(d) + 1 - h.x), self.sr.at[n, d, 1])

    def start_pairs(self, n):
        h = self.here
        src, dst = ((self.query, self.w), (self.output, self.wo))[n]
        mine = lambda f: dst.at[span(f * self.piece, self.piece), pl.ds(0, self.part)]
        self.keeps.append(keep(src.at[:, span((h.f % 4) * self.part, self.part)], mine(h.f), self.loc.at[4 + n]))
        for d in (2, 1, 3, 0):
            for e in (1, 0):
                if d or e:
                    f = 2 * h.zr(d) + (h.x + e) % 2
                    self.sends.append(push(src.at[:, span((f % 4) * self.part, self.part)], mine(h.f),
                                           self.qs.at[n, d, e], self.qr.at[n, (4 - d) % 4, e], h.peer(d, e)))

    def wait_pairs(self, n, far=range(4)):
        h = self.here
        dst = (self.w, self.wo)[n]
        for d in far:
            for e in (1, 0):
                if d or e:
                    f = 2 * h.zr(d) + (h.x + e) % 2
                    self.landed(dst.at[span(f * self.piece, self.piece), pl.ds(0, self.part)], self.qr.at[n, d, e])

    def finish(self):
        for copy in self.sends:
            copy.wait_send()


def unit(values):
    factor = lax.rsqrt(jnp.mean(values * values, axis=-1, keepdims=True) + norm_eps)
    return values * factor, factor


def begin_kernel(heads, cot, query, key, value, output, router, ids, tokens, ag_ref, eg_ref,
                 cos_ref, sin_ref, qg_ref, kg_ref, xn_out, w_out, wo_out, router_out, ids_out, cot_out, pre_out, qkv_out, prob_out, ctx_out, resid_out, expert_out,
                 normed, resid, xn, w, wo, pre, qkv, prob, ctx, part, own, osem, *sems):
    here = Here()
    here.say()
    count, rows, _ = tokens.shape
    step = 32
    steps = rows // step

    def chunk_of(i):
        return i // steps, pl.ds(pl.multiple_of(i % steps * step, step), step)

    @pl.loop(0, count * steps)
    def _(i):
        n, r = chunk_of(i)
        normed[n, r, :] = (unit(tokens[n, r, :].astype(F32))[0] * ag_ref[...]).astype(LOW)

    here.hear()
    at = 0
    x_rows = Gather(here, False, normed, xn, sems[at : at + Gather.slots], BY_X)
    at += Gather.slots
    c_rows = Gather(here, True, cot, cot_out, sems[at : at + Gather.slots], BY_X + 32, own)
    at += Gather.slots
    moved = Weights(here, query, key, value, output, router, ids, w, wo, router_out, ids_out, sems[at : at + Weights.slots])
    at += Weights.slots
    total = Sum(here, False, part, sems[at:], BY_X)

    x_rows.start()
    moved.start_shared()
    moved.start_pairs(0)
    x_rows.first_steps()
    for d in (1, 3, 2):
        moved.pass_shared(d)
    x_rows.last_steps()
    for d in (0,) + ORDER:
        x_rows.arrived(d, 0)
        x_rows.arrived(d, 1)
    moved.wait_shared()
    moved.wait_pairs(0, (2,))
    moved.start_pairs(1)
    moved.wait_pairs(0, (0, 1, 3))
    for copy in moved.keeps:
        copy.wait()
    outs = [keep(xn, xn_out, osem.at[0]), keep(w, w_out, osem.at[1])]

    seq = xn.shape[1]
    hd = cos_ref.shape[1]
    tile = 256
    scale = 1.0 / math.sqrt(hd)
    for i in range(seq // tile):
        r = pl.ds(i * tile, tile)
        got = dot_nn(xn[0, r, :], w[...])
        pre[r, :] = got[:, : (heads + 1) * hd]
        qkv[r, pl.ds((heads + 1) * hd, hd)] = got[:, (heads + 1) * hd :].astype(LOW)
        for a in range(heads + 1):
            one = got[:, a * hd : (a + 1) * hd]
            factor = lax.rsqrt(jnp.mean(one * one, axis=-1, keepdims=True) + norm_eps)
            gained = one * factor * (qg_ref if a < heads else kg_ref)[...]
            turned = gained * cos_ref[r, :] + pltpu.roll(gained, hd // 2, 1) * sin_ref[r, :]
            qkv[r, pl.ds(a * hd, hd)] = turned.astype(LOW)
    c_rows.start()
    outs += [keep(pre, pre_out, osem.at[2]), keep(qkv, qkv_out, osem.at[3])]
    for a in range(heads):
        for i in range(seq // tile):
            r = pl.ds(i * tile, tile)
            n = (i + 1) * tile
            score = dot_nt(qkv[r, pl.ds(a * hd, hd)], qkv[pl.ds(0, n), pl.ds(heads * hd, hd)]) * scale
            row = lax.broadcasted_iota(jnp.int32, (tile, n), 0) + i * tile
            col = lax.broadcasted_iota(jnp.int32, (tile, n), 1)
            score = jnp.where(col <= row, score, masked_score)
            terms = jnp.exp(score - jnp.max(score, axis=-1, keepdims=True))
            low = (terms * (1.0 / jnp.sum(terms, axis=-1, keepdims=True))).astype(LOW)
            prob[a, r, pl.ds(0, n)] = low
            ctx[r, pl.ds(a * hd, hd)] = dot_nn(low, qkv[pl.ds(0, n), pl.ds((heads + 1) * hd, hd)]).astype(LOW)
        if a == 0:
            c_rows.relay(1)
            c_rows.spread(1)
    outs += [keep(prob, prob_out, osem.at[4]), keep(ctx, ctx_out, osem.at[5])]
    moved.wait_pairs(1)
    outs.append(keep(wo, wo_out, osem.at[6]))
    for e in (1, 0):
        for d in FAR_FIRST:
            at_f = span(here.number(d, e) * rows, rows)
            part[0, at_f, :] = dot_nt(ctx[at_f, :], wo[...]).astype(LOW)
            total.give(d, e)
    for d in FAR_FIRST:
        total.corner(d)
    c_rows.cross(0)
    c_rows.relay(2)
    c_rows.spread(2)
    for d in FAR_FIRST:
        total.sides(d)
    c_rows.cross(1)
    c_rows.relay(3)
    c_rows.spread(3)
    for d in FAR_FIRST:
        total.centre(d)
    c_rows.close(0)
    c_rows.cross(2)
    c_rows.close(1)
    total.total()
    total.share_start()
    c_rows.cross(3)
    c_rows.close(2)
    total.share_cross()
    c_rows.close(3)
    total.share_end(None)
    x_rows.finish()

    @pl.loop(0, count * steps)
    def _(i):
        n, r = chunk_of(i)
        branch = jnp.concatenate([total.full[q, n, r, :] for q in range(4)], axis=1).astype(F32)
        summed = tokens[n, r, :].astype(F32) + branch
        resid[n, r, :] = summed
        normed[n, r, :] = (unit(summed)[0] * eg_ref[...]).astype(LOW)

    outs += [keep(resid, resid_out, osem.at[7]), keep(normed, expert_out, osem.at[8])]
    for d in (0,) + ORDER:
        c_rows.arrived(d, 0)
        c_rows.arrived(d, 1)
    for each in (c_rows, moved, total):
        each.finish()
    for copy in outs:
        copy.wait()


def begin(cot, query, key, value, output, router, ids, tokens, attention_gain, expert_gain,
          cosine, sine, query_gain, key_gain):
    count, rows, width = tokens.shape
    seq = rows * 8
    hd = query_gain.shape[0]
    part = query.shape[1] // 4
    heads = part // hd
    vm = pltpu.VMEM
    hbm = pl.BlockSpec(memory_space=pl.ANY)
    near = pl.BlockSpec(memory_space=pltpu.VMEM)
    shape = jax.ShapeDtypeStruct
    local = [
        ((1, seq, width), LOW),
        ((width, part + 2 * hd), LOW),
        ((width, part), LOW),
        ((seq, (heads + 1) * hd), F32),
        ((seq, (heads + 2) * hd), LOW),
        ((heads, seq, seq), LOW),
        ((seq, heads * hd), LOW),
    ]
    return pl.pallas_call(
        functools.partial(begin_kernel, heads),
        out_shape=(
            shape(*local[0]),
            shape(*local[1]),
            shape(*local[2]),
            shape((router.shape[0], width), LOW),
            shape((count, ids.shape[1], seq), jnp.int32),
            shape((count, seq, width), LOW),
            shape(*local[3]),
            shape(*local[4]),
            shape(*local[5]),
            shape(*local[6]),
            shape((count, rows, width), F32),
            shape((count, rows, width), LOW),
        ),
        in_specs=[hbm] * 7 + [near] * 7,
        out_specs=[hbm] * 12,
        scratch_shapes=[vm((count, rows, width), LOW), vm((count, rows, width), F32)]
        + [vm(*entry) for entry in local]
        + [vm((1, seq, width), LOW), vm((count, rows, width), LOW), pltpu.SemaphoreType.DMA((9,))]
        + Gather.scratch() + Gather.scratch() + Weights.scratch() + Sum.scratch(1, rows, width, LOW, BY_X),
        compiler_params=pltpu.CompilerParams(
            collective_id=4, has_side_effects=True, vmem_limit_bytes=VMEM_LIMIT
        ),
        name="begin",
    )(cot, query, key, value, output, router, ids, tokens, attention_gain[None], expert_gain[None],
      cosine, sine, query_gain[None], key_gain[None])


def experts_kernel(experts, expert_in, og_in, ids, router, g_in, u_in, d_in,
                   x_out, act_out, dx_sum, out_sum, probs_out, dgp_out,
                   x_t, g, u, dn, og_t, raw_s, act_t, dx, out, stage, share_s, dgp_t, dgp_got, dgp_all, dgp_c, dgp_y,
                   wsem, ogsem, xsem, actsem, psem, rsem, tsem, usem, *rest):
    here = Here()
    here.greet()
    by_x = expert_in.shape[1] // 2
    rows_x = Gather(here, True, expert_in, x_out, rest[: Gather.slots], by_x, x_t.at[0])
    sums = (
        Sum(here, True, dx, rest[Gather.slots : Gather.slots + Sum.slots], by_x),
        Sum(here, True, out, rest[Gather.slots + Sum.slots :], by_x),
    )
    number = here.number
    count, rows, width = expert_in.shape
    hidden = g.shape[0]
    per = hidden // experts
    tokens = count * rows
    lanes = router.shape[0]
    part = stage.shape[2]
    chunk = width // 4
    rows_x.start()
    loads = [keep(src, dst, wsem.at[n]) for n, (src, dst) in enumerate(((d_in, dn), (g_in, g), (u_in, u)))]

    def plane(i):
        k = i // 2
        return k + (k + 2) // 3 - 3 * (k // 3)

    def tile(i):
        return span(number(plane(i), i % 2) * rows, rows)

    def og_load(i):
        return pltpu.make_async_copy(og_in.at[:, tile(i), :], og_t.at[i % 2], ogsem.at[i % 2])

    def x_load(i):
        return pltpu.make_async_copy(x_out.at[:, tile(i), :], x_t.at[i % 2], xsem.at[i % 2])

    def act_store(i):
        return pltpu.make_async_copy(act_t.at[i % 2], act_out.at[:, :, tile(i), :], actsem.at[i % 2])

    def dgp_send(i):
        to = place(here.zd(plane(i)), (here.x + i % 2) % 2, here.y, here.c)
        return remote(dgp_t.at[i], dgp_got.at[here.f], psem.at[i], rsem.at[here.f], to)

    def both(step, j):
        for each in sums:
            getattr(each, step)(j)

    first = {2: lambda: (rows_x.relay(1), rows_x.spread(1))}
    early = {
        3: lambda: (rows_x.cross(0),),
        5: lambda: (rows_x.relay(2), rows_x.spread(2)),
        7: lambda: (rows_x.cross(1), rows_x.close(0)),
    }
    before = {
        1: lambda: (rows_x.relay(3), rows_x.spread(3), rows_x.arrived(0, 1)),
        2: lambda: (rows_x.close(2), rows_x.arrived(2, 0), rows_x.arrived(2, 1)),
        3: lambda: (both("corner", 0),),
        5: lambda: (both("corner", 2),),
        7: lambda: (both("corner", 3),),
    }
    middle = {
        1: lambda: (rows_x.cross(2), rows_x.close(1)),
        2: lambda: (rows_x.cross(3),),
        3: lambda: (rows_x.close(3), rows_x.arrived(3, 0), rows_x.arrived(3, 1)),
        4: lambda: (both("sides", 0),),
        5: lambda: (rows_x.arrived(1, 0), rows_x.arrived(1, 1)),
        6: lambda: (both("sides", 2), both("centre", 0)),
    }

    def hooks(table, i):
        for key, run in table.items():
            @pl.when(i == key)
            def _(run=run):
                run()

    row = lax.broadcasted_iota(jnp.int32, (lanes, hidden), 0)
    col = lax.broadcasted_iota(jnp.int32, (lanes, hidden), 1)
    spread = jnp.where(row == here.f * experts + col // per, 1.0, 0.0).astype(LOW)
    row8 = lax.broadcasted_iota(jnp.int32, (8, hidden), 0)
    col8 = lax.broadcasted_iota(jnp.int32, (8, hidden), 1)
    gather8 = jnp.where(row8 == col8 // per, 1.0, 0.0).astype(LOW)

    def first_half(i):
        x_tile = x_t[i % 2].reshape(tokens, width)
        for n, right in enumerate((g, u)):
            for k in range(hidden // part):
                stage[n, pl.ds(k * tokens, tokens), :] = dot_nt(x_tile, right[pl.ds(k * part, part), :])
        logits = dot_nt(router[...], x_tile)
        named_ids = jnp.concatenate([ids[m, :, tile(i)] for m in range(count)], axis=1)
        lane = lax.broadcasted_iota(jnp.int32, logits.shape, 0)
        named = lane == named_ids[0:1, :]
        for k in range(1, named_ids.shape[0]):
            named = named | (lane == named_ids[k : k + 1, :])
        masked = jnp.where(named, logits, masked_score)
        terms = jnp.where(named, jnp.exp(masked - jnp.max(masked, axis=0, keepdims=True)), 0.0)
        probs = terms / jnp.sum(terms, axis=0, keepdims=True)
        share_s[...] = dot_tn(probs.astype(LOW), spread)
        return probs

    def between(i, m):
        r = pl.ds(m * rows, rows)
        gate, up = (
            jnp.concatenate([stage[n, pl.ds(k * tokens + m * rows, rows), :] for k in range(hidden // part)], axis=1)
            for n in range(2)
        )
        raw = raw_s[i, r, :].astype(F32)
        share = share_s[r, :]
        sig = 1.0 / (1.0 + jnp.exp(-gate))
        silu = gate * sig
        inner = silu * up
        dgp_t[i, :, r] = dot_nt(gather8, (inner * raw).astype(LOW))
        d_inner = raw * share
        act_t[i % 2, 0, m] = (d_inner * up * (sig + silu * (1.0 - sig))).astype(LOW)
        act_t[i % 2, 1, m] = (d_inner * silu).astype(LOW)
        act_t[i % 2, 2, m] = (inner * share).astype(LOW)

    def second_half(i, q):
        d_gate, d_up, weighted = (act_t[i % 2, n].reshape(tokens, hidden) for n in range(3))
        cols = pl.ds(q * chunk, chunk)
        got = dot_nn(d_gate, g[:, cols]) + dot_nn(d_up, u[:, cols])
        dx[:, tile(i), cols] = got.astype(LOW).reshape(count, rows, chunk)
        out[:, tile(i), cols] = dot_nn(weighted, dn[:, cols]).astype(LOW).reshape(count, rows, chunk)

    def sent(i):
        for each in sums:
            each.give(plane(i), i % 2)

        @pl.when(i > 0)
        def _():
            dgp_send(i).start()

    og_load(0).start()
    loads[0].wait()

    def raw_step(table, i):
        @pl.when(i + 1 < 8)
        def _():
            og_load(i + 1).start()

        hooks(table, i)
        og_load(i).wait()
        raw_s[i] = dot_nt(og_t[i % 2].reshape(tokens, width), dn[...]).astype(LOW)

    pl.loop(0, 3)(functools.partial(raw_step, first))
    loads[1].wait()
    loads[2].wait()
    rows_x.arrived(0, 0)
    probs_out[...] = first_half(0)
    for m in range(count):
        between(0, m)
    act_store(0).start()
    pl.loop(3, 8)(functools.partial(raw_step, early))

    @pl.loop(1, 8)
    def _(i):
        hooks(before, i)

        @pl.when(i < 3)
        def _():
            x_load(i).start()

        @pl.when(i >= 2)
        def _():
            act_store(i - 2).wait()

        x_load(i).wait()
        first_half(i)
        hooks(middle, i)

        @pl.when((i >= 2) & (i < 7))
        def _():
            x_load(i + 1).start()

        for m in range(count):
            second_half(i - 1, 2 * m)
            between(i, m)
            second_half(i - 1, 2 * m + 1)
        act_store(i).start()
        sent(i - 1)

    for q in range(4):
        second_half(7, q)
    sent(7)
    ahead, behind = sums
    ahead.corner(1)
    ahead.sides(3)
    ahead.centre(2)
    behind.corner(1)
    behind.sides(3)
    ahead.sides(1)
    ahead.centre(3)
    behind.centre(2)
    behind.sides(1)
    ahead.centre(1)
    behind.centre(3)
    for d in range(4):
        for e in range(2):
            if d or e:
                n = number(d, e)
                wait_for(dgp_got.at[n], rsem.at[n], here.xn)
                dgp_all[n] = dgp_got[n]
    dgp_all[here.f] = dgp_t[0]
    across = push(dgp_all, dgp_c, tsem.at[0], usem.at[0], here.cn)
    ahead.total()
    ahead.share_start()
    behind.centre(1)
    wait_for(dgp_c, usem.at[0], here.cn)
    across.wait_send()
    dgp_all[...] = dgp_all[...] + dgp_c[...]
    second = push(dgp_all, dgp_y, tsem.at[1], usem.at[1], here.yn)
    ahead.share_cross()
    behind.total()
    quarter = keep(behind.tmp, out_sum, behind.osem.at[0])
    ahead.share_end(dx_sum)
    quarter.wait()
    wait_for(dgp_y, usem.at[1], here.yn)
    dgp_out[...] = dgp_all[...] + dgp_y[...]
    second.wait_send()
    act_store(6).wait()
    act_store(7).wait()
    for i in range(1, 8):
        dgp_send(i).wait_send()
    rows_x.finish()
    for each in sums:
        each.finish()


def run_experts(expert_in, og, ids, router, gate, up, down):
    count, rows, width = expert_in.shape
    seq = rows * 8
    experts, per, _ = gate.shape
    hidden = experts * per
    tokens = count * rows
    lanes = router.shape[0]
    vm = pltpu.VMEM
    dma = pltpu.SemaphoreType.DMA
    hbm = pl.BlockSpec(memory_space=pl.ANY)
    near = pl.BlockSpec(memory_space=pltpu.VMEM)
    shape = jax.ShapeDtypeStruct
    total = Sum.scratch(count, rows, width, LOW, rows // 2)
    return pl.pallas_call(
        functools.partial(experts_kernel, experts),
        out_shape=(
            shape((count, seq, width), LOW),
            shape((3, count, seq, hidden), LOW),
            shape((count, rows, width), LOW),
            shape((count, rows, width // 4), LOW),
            shape((lanes, tokens), F32),
            shape((8, 8, tokens), F32),
        ),
        in_specs=[hbm, hbm, near, near, hbm, hbm, hbm],
        out_specs=[hbm, hbm, hbm, hbm, near, near],
        scratch_shapes=[
            vm((2, count, rows, width), LOW),
            vm((hidden, width), LOW),
            vm((hidden, width), LOW),
            vm((hidden, width), LOW),
            vm((2, count, rows, width), LOW),
            vm((8, tokens, hidden), LOW),
            vm((2, 3, count, rows, hidden), LOW),
            vm((count, seq, width), LOW),
            vm((count, seq, width), LOW),
            vm((2, hidden // 256 * tokens, 256), F32),
            vm((tokens, hidden), F32),
            vm((8, 8, tokens), F32),
            vm((8, 8, tokens), F32),
            vm((8, 8, tokens), F32),
            vm((8, 8, tokens), F32),
            vm((8, 8, tokens), F32),
            dma((3,)),
            dma((2,)),
            dma((2,)),
            dma((2,)),
            dma((8,)),
            dma((8,)),
            dma((2,)),
            dma((2,)),
        ]
        + Gather.scratch()
        + total
        + total,
        compiler_params=pltpu.CompilerParams(
            collective_id=6, has_side_effects=True, vmem_limit_bytes=VMEM_LIMIT
        ),
        name="experts",
    )(expert_in, og, ids, router, gate.reshape(hidden, width), up.reshape(hidden, width), down.reshape(hidden, width))


def expert_grads_kernel(act, x, og, *refs):
    kept = (len(refs) - 3) // 2
    tokens = act.shape[1] * act.shape[2]
    x_cols = x[...].reshape(tokens, x.shape[2])
    og_cols = og[...].reshape(tokens, og.shape[2])
    for n, right in enumerate((x_cols, x_cols, og_cols)):
        refs[kept + n][...] = dot_tn(act[n].reshape(tokens, act.shape[3]), right)
    for src, dst in zip(refs[:kept], refs[kept + 3 :]):
        dst[...] = src[...]


def expert_grads(act, x, og, *others):
    _, count, seq, hidden = act.shape
    width = x.shape[2]
    block = min(512, width)
    steps = width // block
    cols = pl.BlockSpec((count, seq, block), lambda i: (0, 0, i))
    out = pl.BlockSpec((hidden, block), lambda i: (0, i))

    def pieces(value):
        shape = value.shape[:-2] + (value.shape[-2] // steps, value.shape[-1])
        zeros = (0,) * (len(shape) - 2)
        return pl.BlockSpec(shape, lambda i: zeros + (i, 0))

    grads = jax.ShapeDtypeStruct((hidden, width), F32)
    kept = [pieces(value) for value in others]
    return pl.pallas_call(
        expert_grads_kernel,
        grid=(steps,),
        in_specs=[
            pl.BlockSpec(act.shape, lambda i: (0, 0, 0, 0), pipeline_mode=pl.Buffered(1)),
            cols,
            cols,
        ]
        + kept,
        out_specs=[out, out, out] + kept,
        out_shape=[grads] * 3 + [jax.ShapeDtypeStruct(value.shape, value.dtype) for value in others],
        compiler_params=pltpu.CompilerParams(vmem_limit_bytes=VMEM_LIMIT),
        name="expert_grads",
    )(act, x, og, *others)


PEERS = tuple((d, e) for d in (2, 1, 3, 0) for e in (1, 0) if d or e)


def end_kernel(heads, xn_in, w_in, wo_in, pre_in, qkv_in, prob_in, ctx_in, tokens_in, out_in,
               resid, cot, dx_sum, expert_in, probs, dgp, router, eg_ref, ag_ref, query, key, value,
               cos_ref, sin_ref, qg_ref, kg_ref,
               layer_out, input_out, dq_out, dk_out, dv_out, do_out, aux_out, gains_out,
               tokens, out_full, d_res, low_rows, layer, aux, db, xn, w, wo, pre, qkv, prob, ctx, dctx, dq_s, dk_s, dv_s, dqkv, dwo, dw, dwo_got, dwq_got, kv_x, kv_z,
               aux_got, head_part, head_got, line, line_c, line_y, wide_q, wide_o, wide_kv,
               lsem, psem, rsem, vsem, wsem, kxs, kxr, kzs, kzr, tsem, usem, osem, *rest):
    here = Here()
    here.say()
    sends, outs = [], []
    rows_db = Gather(here, False, low_rows, db, rest[: Gather.slots], BY_X)
    at = Gather.slots
    dn = Sum(here, False, db, rest[at:], BY_X)
    rows = dn.rows
    piece, part = query.shape[0], wo.shape[1]
    seq = xn.shape[1]
    hd = cos_ref.shape[1]
    tile = 256
    scale = 1.0 / math.sqrt(hd)

    def number(d, e):
        return 2 * here.zr(d) + (here.x + e) % 2

    def send(n, d, e, src, got):
        sends.append(push(src, got.at[(4 - d) % 4, e], psem.at[n, d, e], rsem.at[n, (4 - d) % 4, e], here.peer(d, e)))

    def got_from(n, d, e, got):
        wait_for(got.at[d, e], rsem.at[n, d, e], here.xn)
        return got[d, e]

    loads = {}
    for n, (src, dst) in enumerate(((wo_in, wo), (ctx_in, ctx), (qkv_in, qkv), (prob_in, prob), (pre_in, pre),
                                    (xn_in, xn), (w_in, w), (tokens_in, tokens), (out_in, out_full.at[here.t]))):
        loads[n] = keep(src, dst, lsem.at[n])
    count, lanes, width = resid.shape[0], probs.shape[0], resid.shape[2]
    experts = lanes // 8
    step = 32
    steps = rows // step

    def chunk_of(i):
        return i // steps, pl.ds(pl.multiple_of(i % steps * step, step), step)

    def unit_back(up, gain, hat, factor):
        gained = up * gain
        return factor * (gained - hat * jnp.mean(gained * hat, axis=-1, keepdims=True))

    d_probs = jnp.concatenate([dgp[k, :experts, :] for k in range(8)], axis=0)
    mixed = probs[...] * d_probs
    d_logits = (mixed - probs[...] * jnp.sum(mixed, axis=0, keepdims=True)).astype(LOW)
    for n in range(count):
        d_res[n] = dot_tn(d_logits[:, n * rows : (n + 1) * rows], router[...])

    def back(i, gain_part):
        n, r = chunk_of(i)
        hat, factor = unit(resid[n, r, :])
        d_in = d_res[n, r, :] + dx_sum[n, r, :].astype(F32)
        total = cot[n, r, :].astype(F32) + unit_back(d_in, eg_ref[...], hat, factor)
        d_res[n, r, :] = total
        low_rows[n, r, :] = total.astype(LOW)
        return gain_part + jnp.sum(d_in * hat, axis=0, keepdims=True)

    gain_part = lax.fori_loop(0, count * steps, back, jnp.zeros((1, width), F32))
    here.hear()
    rows_db.start()
    router_part = dot_nn(d_logits, expert_in[...].reshape(count * rows, width)).astype(LOW)
    first_row = lax.broadcasted_iota(jnp.int32, (16, piece), 0) == 0
    for k in range(8):
        cols = slice(k * piece, (k + 1) * piece)
        aux[k, pl.ds(0, lanes), :] = router_part[:, cols]
        aux[k, pl.ds(lanes, 16), :] = jnp.where(first_row, gain_part[:, cols], 0.0).astype(LOW)
    for d, e in PEERS:
        send(0, d, e, aux.at[number(d, e)], aux_got)
    rows_db.first_steps()
    loads[8].wait()
    mine = out_full.at[here.t]
    sends.append(push(mine, mine, vsem.at[0], wsem.at[0], here.yn))
    sends.append(push(mine, mine, vsem.at[1], wsem.at[1], here.cn))
    rows_db.last_steps()
    for d in (0,) + ORDER:
        rows_db.arrived(d, 0)
        rows_db.arrived(d, 1)
    across = out_full.at[2 * (1 - here.y) + here.c]
    wait_for(across, wsem.at[0], here.xn)
    sends.append(push(across, across, vsem.at[2], wsem.at[2], here.cn))
    for n in range(8):
        loads[n].wait()

    for i in range(seq // tile):
        r = pl.ds(i * tile, tile)
        dctx[r, :] = dot_nn(db[0, r, :], wo[...]).astype(LOW)
    for d, e in PEERS + ((0, 0),):
        r = span(number(d, e) * piece, piece)
        dwo[r, :] = dot_tn(db[0, :, r], ctx[...]).astype(LOW)
        if d or e:
            send(1, d, e, dwo.at[r, :], dwo_got)
    wait_for(out_full.at[2 * here.y + 1 - here.c], wsem.at[1], here.xn)
    wait_for(out_full.at[2 * (1 - here.y) + 1 - here.c], wsem.at[2], here.xn)

    @pl.loop(0, count * steps)
    def _(i):
        n, r = chunk_of(i)
        routed = jnp.concatenate([out_full[q, n, r, :] for q in range(4)], axis=1).astype(F32)
        layer[n, r, :] = (resid[n, r, :] + routed).astype(LOW)

    outs.append(keep(layer, layer_out, osem.at[4]))
    dk_s[...] = jnp.zeros_like(dk_s)
    dv_s[...] = jnp.zeros_like(dv_s)
    for a in range(heads):
        for i in range(seq // tile):
            r = pl.ds(i * tile, tile)
            n = (i + 1) * tile
            q_tile = qkv[r, pl.ds(a * hd, hd)]
            k_rows = qkv[pl.ds(0, n), pl.ds(heads * hd, hd)]
            v_rows = qkv[pl.ds(0, n), pl.ds((heads + 1) * hd, hd)]
            up = dctx[r, pl.ds(a * hd, hd)]
            low = prob[a, r, pl.ds(0, n)]
            wide = low.astype(F32)
            dprob = dot_nt(up, v_rows)
            delta = jnp.sum(wide * dprob, axis=-1, keepdims=True)
            dscore = (wide * (dprob - delta)).astype(LOW)
            dq_s[r, pl.ds(a * hd, hd)] = dot_nn(dscore, k_rows) * scale
            dk_s[pl.ds(0, n), :] += dot_tn(dscore, q_tile) * scale
            dv_s[pl.ds(0, n), :] += dot_tn(low, up)
    gq = jnp.zeros((1, hd), F32)
    gk = jnp.zeros((1, hd), F32)
    for i in range(seq // tile):
        r = pl.ds(i * tile, tile)
        dqkv[r, pl.ds((heads + 1) * hd, hd)] = dv_s[r, :].astype(LOW)
        for a in range(heads + 1):
            up = dq_s[r, pl.ds(a * hd, hd)] if a < heads else dk_s[r, :]
            one = pre[r, pl.ds(a * hd, hd)]
            factor = lax.rsqrt(jnp.mean(one * one, axis=-1, keepdims=True) + norm_eps)
            hat = one * factor
            turned = up * cos_ref[r, :] + pltpu.roll(up * sin_ref[r, :], hd // 2, 1)
            gain_part = jnp.sum(turned * hat, axis=0, keepdims=True)
            gained = turned * (qg_ref if a < heads else kg_ref)[...]
            back = factor * (gained - hat * jnp.mean(gained * hat, axis=-1, keepdims=True))
            dqkv[r, pl.ds(a * hd, hd)] = back.astype(LOW)
            if a < heads:
                gq = gq + gain_part
            else:
                gk = gk + gain_part
    head_part[...] = jnp.concatenate([gq, gk, jnp.zeros((6, hd), F32)], axis=0)
    for d, e in PEERS:
        send(3, d, e, head_part, head_got)
    rows_db.finish()
    for e in (1, 0):
        for d in FAR_FIRST:
            r = span(here.number(d, e) * rows, rows)
            db[0, r, :] = dot_nt(dqkv[r, :], w[...]).astype(LOW)
            dn.give(d, e)
    for d, e in PEERS + ((0, 0),):
        r = span(number(d, e) * piece, piece)
        dw[r, :] = dot_tn(xn[0, :, r], dqkv[...]).astype(LOW)
        if d in (1, 2):
            send(2, d, e, dw.at[r, pl.ds(0, part)], dwq_got)
        if e:
            sends.append(push(dw.at[r, pl.ds(part, 2 * hd)], kv_x.at[d], kxs.at[d], kxr.at[d], here.xn))
    for d in FAR_FIRST:
        dn.corner(d)
    for d in (2, 1, 3, 0):
        r = span(number(d, 0) * piece, piece)
        wait_for(kv_x.at[d], kxr.at[d], here.xn)
        both = dw[r, pl.ds(part, 2 * hd)].astype(F32) + kv_x[d].astype(F32)
        dw[r, pl.ds(part, 2 * hd)] = both.astype(LOW)
        if d:
            there = (4 - d) % 4
            sends.append(push(dw.at[r, pl.ds(part, 2 * hd)], kv_z.at[there], kzs.at[d], kzr.at[there], here.peer(d, 0)))
    for d in FAR_FIRST:
        dn.sides(d)
    for d in FAR_FIRST:
        dn.centre(d)
    for d, e in PEERS:
        if d in (0, 3):
            send(2, d, e, dw.at[span(number(d, e) * piece, piece), pl.ds(0, part)], dwq_got)

    def merged(n, wide, got, mine):
        for d in (0, 1):
            for e in (0, 1):
                first = mine if (d, e) == (0, 0) else got_from(n, d, e, got)
                both = first.astype(F32) + got_from(n, d + 2, e, got).astype(F32)
                wide[:, span((number(d, e) % 4) * part, part)] = both

    own = span(here.f * piece, piece)
    merged(1, wide_o, dwo_got, dwo[own, :])
    outs.append(keep(wide_o, do_out, osem.at[0]))
    aux_total = aux[here.f].astype(F32)
    for d, e in PEERS:
        aux_total = aux_total + got_from(0, d, e, aux_got).astype(F32)
    aux_out[...] = aux_total
    head_total = head_part[...]
    for d, e in PEERS:
        head_total = head_total + got_from(3, d, e, head_got)
    line[:, pl.ds(piece, hd)] = head_total
    dn.total()
    dn.share_start()
    dn.share_cross()
    dn.share_end(None)

    @pl.loop(0, count * steps)
    def _(i):
        n, r = chunk_of(i)
        hat, factor = unit(tokens[n, r, :].astype(F32))
        up = jnp.concatenate([dn.full[q, n, r, :] for q in range(4)], axis=1).astype(F32)
        low_rows[n, r, :] = (d_res[n, r, :] + unit_back(up, ag_ref[...], hat, factor)).astype(LOW)

    outs.append(keep(low_rows, input_out, osem.at[5]))
    merged(2, wide_q, dwq_got, dw[own, pl.ds(0, part)])
    outs.append(keep(wide_q, dq_out, osem.at[1]))
    kv = dw[own, pl.ds(part, 2 * hd)].astype(F32)
    for d in (1, 2, 3):
        wait_for(kv_z.at[d], kzr.at[d], here.xn)
        kv = kv + kv_z[d].astype(F32)
    wide_kv[...] = kv
    outs.append(keep(wide_kv.at[:, pl.ds(0, hd)], dk_out, osem.at[2]))
    outs.append(keep(wide_kv.at[:, pl.ds(hd, hd)], dv_out, osem.at[3]))

    def row_sums(product):
        high = product.astype(LOW)
        rest_ = (product - high.astype(F32)).astype(LOW)
        ones = jnp.ones((8, product.shape[1]), LOW)
        return dot_nt(ones, high) + dot_nt(ones, rest_)

    line[:, pl.ds(0, piece)] = (
        row_sums(query[...].astype(F32) * wide_q[...])
        + row_sums(key[...].astype(F32) * kv[:, :hd])
        + row_sums(value[...].astype(F32) * kv[:, hd:])
    )
    first = push(line, line_c, tsem.at[0], usem.at[0], here.cn)
    wait_for(line_c, usem.at[0], here.cn)
    first.wait_send()
    line[...] = line[...] + line_c[...]
    second = push(line, line_y, tsem.at[1], usem.at[1], here.yn)
    wait_for(line_y, usem.at[1], here.yn)
    gains_out[...] = line[...] + line_y[...]
    second.wait_send()
    dn.finish()
    for copy in sends:
        copy.wait_send()
    for copy in outs:
        copy.wait()


def end(xn, w, wo, pre, qkv, prob, ctx, tokens, out_sum, resid, cot, dx_sum, expert_in, probs, dgp, router,
        expert_gain, attention_gain, query, key, value, cosine, sine, query_gain, key_gain):
    count, rows, width = tokens.shape
    seq = rows * 8
    lanes = probs.shape[0]
    hd = query_gain.shape[0]
    piece, local = query.shape
    part = local // 4
    heads = part // hd
    vm = pltpu.VMEM
    dma = pltpu.SemaphoreType.DMA
    hbm = pl.BlockSpec(memory_space=pl.ANY)
    near = pl.BlockSpec(memory_space=pltpu.VMEM)
    shape = jax.ShapeDtypeStruct
    return pl.pallas_call(
        functools.partial(end_kernel, heads),
        out_shape=(
            shape((count, rows, width), LOW),
            shape((count, rows, width), LOW),
            shape((piece, local), F32),
            shape((piece, hd), F32),
            shape((piece, hd), F32),
            shape((piece, local), F32),
            shape((lanes + 16, piece), F32),
            shape((8, piece + hd), F32),
        ),
        in_specs=[hbm] * 9 + [near] * 16,
        out_specs=[hbm] * 6 + [near] * 2,
        scratch_shapes=[
            vm((count, rows, width), LOW),
            vm((4, count, rows, width // 4), LOW),
            vm((count, rows, width), F32),
            vm((count, rows, width), LOW),
            vm((count, rows, width), LOW),
            vm((8, lanes + 16, piece), LOW),
            vm((1, seq, width), LOW),
            vm((1, seq, width), LOW),
            vm(w.shape, LOW),
            vm(wo.shape, LOW),
            vm(pre.shape, F32),
            vm(qkv.shape, LOW),
            vm(prob.shape, LOW),
            vm(ctx.shape, LOW),
            vm(ctx.shape, LOW),
            vm((seq, heads * hd), F32),
            vm((seq, hd), F32),
            vm((seq, hd), F32),
            vm((seq, (heads + 2) * hd), LOW),
            vm((width, part), LOW),
            vm((width, part + 2 * hd), LOW),
            vm((4, 2, piece, part), LOW),
            vm((4, 2, piece, part), LOW),
            vm((4, piece, 2 * hd), LOW),
            vm((4, piece, 2 * hd), LOW),
            vm((4, 2, lanes + 16, piece), LOW),
            vm((8, hd), F32),
            vm((4, 2, 8, hd), F32),
            vm((8, piece + hd), F32),
            vm((8, piece + hd), F32),
            vm((8, piece + hd), F32),
            vm((piece, local), F32),
            vm((piece, local), F32),
            vm((piece, 2 * hd), F32),
            dma((9,)),
            dma((4, 4, 2)),
            dma((4, 4, 2)),
            dma((3,)),
            dma((3,)),
            dma((4,)),
            dma((4,)),
            dma((4,)),
            dma((4,)),
            dma((2,)),
            dma((2,)),
            dma((6,)),
        ]
        + Gather.scratch()
        + Sum.scratch(1, rows, width, LOW, BY_X),
        compiler_params=pltpu.CompilerParams(
            collective_id=5, has_side_effects=True, vmem_limit_bytes=VMEM_LIMIT
        ),
        name="end",
    )(xn, w, wo, pre, qkv, prob, ctx, tokens, out_sum, resid, cot, dx_sum, expert_in, probs, dgp, router,
      expert_gain[None], attention_gain[None], query, key, value, cosine, sine, query_gain[None], key_gain[None])


def rotate_half(values):
    middle = values.shape[-1] // 2
    return jnp.concatenate([-values[..., middle:], values[..., :middle]], axis=-1)


def rope_tables(positions, head_width):
    middle = head_width // 2
    frequency = rope_base ** (-jnp.arange(middle, dtype=jnp.float32) * 2.0 / head_width)
    angles = positions.astype(jnp.float32)[:, None] * frequency[None, :]
    angles = jnp.concatenate([angles, angles], axis=1)
    return (jnp.cos(angles), jnp.sin(angles))


def norm_parts(values):
    factor = lax.rsqrt(jnp.mean(values * values, axis=-1, keepdims=True) + norm_eps)
    return (values * factor, factor)


def norm_back(upstream, gain, normal, factor):
    scaled = upstream * gain
    return factor * (scaled - normal * jnp.mean(scaled * normal, axis=-1, keepdims=True))


def head_back(upstream, cosine_heads, sine_heads, gain, normal, factor):
    turned = upstream * cosine_heads - rotate_half(upstream * sine_heads)
    gain_part = jnp.sum(turned * normal, axis=(0, 1))
    return (norm_back(turned, gain, normal, factor), gain_part)


def fetch_weights(query_weight, key_weight, value_weight, output_weight, router_weight):
    return (
        lax.all_gather(query_weight, "fsdp", axis=0, tiled=True),
        lax.all_gather(key_weight, "fsdp", axis=0, tiled=True),
        lax.all_gather(value_weight, "fsdp", axis=0, tiled=True),
        lax.all_gather(output_weight, "fsdp", axis=0, tiled=True),
        lax.all_gather(router_weight, "fsdp", axis=0, tiled=True),
    )


def widen(summed):
    return lax.all_gather(summed, "tp", axis=3, tiled=True)


def carry_back(summed):
    return lax.all_to_all(summed, "fsdp", split_axis=0, concat_axis=0, tiled=True)


def send_home(summed):
    arrived_home = carry_back(widen(summed))
    return arrived_home


def general_device(
    tokens,
    cotangent,
    expert_ids,
    attention_gain,
    query_gain,
    key_gain,
    query_weight,
    key_weight,
    value_weight,
    output_weight,
    expert_gain,
    router_weight,
    gate_weight,
    up_weight,
    down_weight,
):
    micro_count = tokens.shape[0]
    tok_rows = tokens.shape[1]
    width = tokens.shape[2]
    route_count = expert_ids.shape[2]
    head_dim = query_gain.shape[0]
    local_heads = query_weight.shape[1] // head_dim
    local_groups = key_weight.shape[1] // head_dim
    group_size = local_heads // local_groups
    fsdp_count = lax.axis_size("fsdp")
    seq_len = tok_rows * fsdp_count
    experts_here = gate_weight.shape[0]
    expert_count = experts_here * fsdp_count
    capacity = max(2, 5 * tok_rows * route_count // (4 * expert_count))
    key_block = math.gcd(seq_len, 512)
    score_scale = 1.0 / math.sqrt(head_dim)
    query_count = tok_rows * group_size
    routed_total = tok_rows * route_count
    start_row = lax.axis_index("fsdp") * tok_rows
    positions = start_row + jnp.arange(tok_rows, dtype=jnp.int32)
    cosine_table, sine_table = rope_tables(positions, head_dim)
    cosine_heads = cosine_table[:, None, :]
    sine_heads = sine_table[:, None, :]
    query_pos = start_row + jnp.arange(query_count, dtype=jnp.int32) // group_size
    block_total = (start_row + tok_rows + key_block - 1) // key_block
    expert_range = jnp.arange(expert_count, dtype=jnp.int32)
    zero_row = jnp.zeros((1, width), jnp.bfloat16)

    def to_rows(tensor):
        return (
            tensor.reshape(tok_rows, local_groups, group_size, head_dim)
            .transpose(1, 0, 2, 3)
            .reshape(local_groups, query_count, head_dim)
        )

    def from_rows(tensor):
        return (
            tensor.reshape(local_groups, tok_rows, group_size, head_dim)
            .transpose(1, 0, 2, 3)
            .reshape(tok_rows, local_heads, head_dim)
        )

    acc_attention_gain = jnp.zeros((width,), jnp.float32)
    acc_head_gains = jnp.zeros((2, head_dim), jnp.float32)
    acc_query = jnp.zeros((width, local_heads * head_dim), jnp.float32)
    acc_key = jnp.zeros((width, local_groups * head_dim), jnp.float32)
    acc_value = jnp.zeros((width, local_groups * head_dim), jnp.float32)
    acc_output = jnp.zeros((width, local_heads * head_dim), jnp.float32)
    acc_expert_gain = jnp.zeros((width,), jnp.float32)
    acc_router = jnp.zeros((width, expert_count), jnp.float32)
    acc_gate = jnp.zeros(gate_weight.shape, jnp.float32)
    acc_up = jnp.zeros(up_weight.shape, jnp.float32)
    acc_down = jnp.zeros(down_weight.shape, jnp.float32)
    layer_rows = []
    input_rows = []
    for micro_index in range(micro_count):
        inputs = tokens[micro_index].astype(jnp.float32)
        query_full, key_full, value_full, output_full, router_full = fetch_weights(
            query_weight, key_weight, value_weight, output_weight, router_weight
        )
        input_hat, attention_factor = norm_parts(inputs)
        normed = (input_hat * attention_gain).astype(jnp.bfloat16)
        query_pre = jnp.dot(normed, query_full, preferred_element_type=jnp.float32).reshape(
            tok_rows, local_heads, head_dim
        )
        key_pre = jnp.dot(normed, key_full, preferred_element_type=jnp.float32).reshape(
            tok_rows, local_groups, head_dim
        )
        value_low = jnp.dot(normed, value_full, preferred_element_type=jnp.float32).astype(
            jnp.bfloat16
        )
        query_hat, query_factor = norm_parts(query_pre)
        key_hat, key_factor = norm_parts(key_pre)
        query_scaled = query_hat * query_gain
        key_scaled = key_hat * key_gain
        query_low = (query_scaled * cosine_heads + rotate_half(query_scaled) * sine_heads).astype(
            jnp.bfloat16
        )
        key_low = (key_scaled * cosine_heads + rotate_half(key_scaled) * sine_heads).astype(
            jnp.bfloat16
        )
        key_all, value_all = (
            lax.all_gather(
                key_low.reshape(tok_rows, local_groups * head_dim), "fsdp", axis=0, tiled=True
            ),
            lax.all_gather(value_low, "fsdp", axis=0, tiled=True),
        )
        key_heads = key_all.reshape(seq_len, local_groups, head_dim).transpose(1, 0, 2)
        value_heads = value_all.reshape(seq_len, local_groups, head_dim).transpose(1, 0, 2)
        query_rows = to_rows(query_low)

        def scores_at(block_index):
            block_start = block_index * key_block
            key_slice = lax.dynamic_slice_in_dim(key_heads, block_start, key_block, 1)
            raw_scores = (
                jnp.einsum(
                    "gqd,gkd->gqk", query_rows, key_slice, preferred_element_type=jnp.float32
                )
                * score_scale
            )
            allowed = (block_start + jnp.arange(key_block, dtype=jnp.int32))[None, :] <= query_pos[
                :, None
            ]
            return (jnp.where(allowed[None], raw_scores, masked_score), allowed, block_start)

        def stats_step(block_index, carried):
            run_peak, run_total = carried
            scores, allowed, block_start = scores_at(block_index)
            new_peak = jnp.maximum(run_peak, jnp.max(scores, axis=-1))
            terms = jnp.where(allowed[None], jnp.exp(scores - new_peak[..., None]), 0.0)
            return (new_peak, run_total * jnp.exp(run_peak - new_peak) + jnp.sum(terms, axis=-1))

        start_stats = (
            jnp.full((local_groups, query_count), masked_score, jnp.float32),
            jnp.zeros((local_groups, query_count), jnp.float32),
        )
        run_peak, run_total = lax.fori_loop(0, block_total, stats_step, start_stats)
        log_total = run_peak + jnp.log(run_total)

        def value_step(block_index, acc_context):
            scores, allowed, block_start = scores_at(block_index)
            probs_low = jnp.where(
                allowed[None], jnp.exp(scores - log_total[..., None]), 0.0
            ).astype(jnp.bfloat16)
            value_slice = lax.dynamic_slice_in_dim(value_heads, block_start, key_block, 1)
            return acc_context + jnp.einsum(
                "gqk,gkd->gqd", probs_low, value_slice, preferred_element_type=jnp.float32
            )

        context_rows = lax.fori_loop(
            0,
            block_total,
            value_step,
            jnp.zeros((local_groups, query_count, head_dim), jnp.float32),
        )
        context_low = (
            from_rows(context_rows).reshape(tok_rows, local_heads * head_dim).astype(jnp.bfloat16)
        )
        branch_part = jnp.einsum(
            "th,dh->td", context_low, output_full, preferred_element_type=jnp.float32
        )
        resid = inputs + lax.psum(branch_part.astype(jnp.bfloat16), "tp").astype(jnp.float32)
        resid_hat, expert_factor = norm_parts(resid)
        expert_in = (resid_hat * expert_gain).astype(jnp.bfloat16)
        logits = jnp.dot(expert_in, router_full, preferred_element_type=jnp.float32)
        routes_now = expert_ids[micro_index]
        choose = (routes_now[:, :, None] == expert_range[None, None, :]).astype(jnp.float32)
        picked = jnp.sum(choose * logits[:, None, :], axis=-1)
        shifted = jnp.exp(picked - jnp.max(picked, axis=-1, keepdims=True))
        gate_probs = shifted / jnp.sum(shifted, axis=-1, keepdims=True)
        flat_routes = routes_now.reshape(-1)
        onehot = (flat_routes[:, None] == expert_range[None, :]).astype(jnp.int32)
        rank_in = jnp.sum((jnp.cumsum(onehot, axis=0) - onehot) * onehot, axis=1)
        slot_index = flat_routes * capacity + rank_in
        slot_source = (
            jnp.full((expert_count * capacity,), routed_total, jnp.int32)
            .at[slot_index]
            .set(jnp.arange(routed_total, dtype=jnp.int32))
        )
        padded_in = jnp.concatenate([expert_in, zero_row], axis=0)
        outgoing = padded_in[slot_source // route_count].reshape(
            fsdp_count, experts_here, capacity, width
        )
        arrived = lax.all_to_all(outgoing, "fsdp", split_axis=0, concat_axis=0, tiled=True)
        gate_pre = jnp.einsum(
            "secd,efd->secf", arrived, gate_weight, preferred_element_type=jnp.float32
        )
        up_pre = jnp.einsum(
            "secd,efd->secf", arrived, up_weight, preferred_element_type=jnp.float32
        )
        gate_sigmoid = jax.nn.sigmoid(gate_pre)
        inner_low = (gate_pre * gate_sigmoid * up_pre).astype(jnp.bfloat16)
        result_part = jnp.einsum(
            "secf,efd->secd", inner_low, down_weight, preferred_element_type=jnp.float32
        )
        result_low = lax.psum_scatter(
            result_part.astype(jnp.bfloat16), "tp", scatter_dimension=3, tiled=True
        )
        result_home = send_home(result_low)
        routed = (
            result_home.reshape(expert_count * capacity, width)[slot_index]
            .astype(jnp.float32)
            .reshape(tok_rows, route_count, width)
        )
        layer_rows.append(
            (resid + jnp.sum(gate_probs[:, :, None] * routed, axis=1)).astype(jnp.bfloat16)
        )
        query_full, key_full, value_full, output_full, router_full = fetch_weights(
            query_weight, key_weight, value_weight, output_weight, router_weight
        )
        out_grad = cotangent[micro_index].astype(jnp.float32)
        d_route = (
            (gate_probs[:, :, None] * out_grad[:, None, :])
            .astype(jnp.bfloat16)
            .reshape(routed_total, width)
        )
        d_gate_probs = jnp.sum(out_grad[:, None, :] * routed, axis=-1)
        d_pick = gate_probs * (
            d_gate_probs - jnp.sum(gate_probs * d_gate_probs, axis=-1, keepdims=True)
        )
        d_logits = jnp.sum(choose * d_pick[:, :, None], axis=1).astype(jnp.bfloat16)
        grad_outgoing = jnp.concatenate([d_route, zero_row], axis=0)[slot_source].reshape(
            fsdp_count, experts_here, capacity, width
        )
        grad_arrived = lax.all_to_all(
            grad_outgoing, "fsdp", split_axis=0, concat_axis=0, tiled=True
        )
        d_inner = jnp.einsum(
            "secd,efd->secf", grad_arrived, down_weight, preferred_element_type=jnp.float32
        )
        acc_down = acc_down + jnp.einsum(
            "secf,secd->efd", inner_low, grad_arrived, preferred_element_type=jnp.float32
        )
        d_gate_low = (
            d_inner * up_pre * gate_sigmoid * (1.0 + gate_pre * (1.0 - gate_sigmoid))
        ).astype(jnp.bfloat16)
        d_up_low = (d_inner * gate_pre * gate_sigmoid).astype(jnp.bfloat16)
        acc_gate = acc_gate + jnp.einsum(
            "secf,secd->efd", d_gate_low, arrived, preferred_element_type=jnp.float32
        )
        acc_up = acc_up + jnp.einsum(
            "secf,secd->efd", d_up_low, arrived, preferred_element_type=jnp.float32
        )
        d_copy_part = jnp.einsum(
            "secf,efd->secd", d_gate_low, gate_weight, preferred_element_type=jnp.float32
        ) + jnp.einsum("secf,efd->secd", d_up_low, up_weight, preferred_element_type=jnp.float32)
        d_copy_low = lax.psum_scatter(
            d_copy_part.astype(jnp.bfloat16), "tp", scatter_dimension=3, tiled=True
        )
        d_copy_home = send_home(d_copy_low)
        d_copies = (
            d_copy_home.reshape(expert_count * capacity, width)[slot_index]
            .astype(jnp.float32)
            .reshape(tok_rows, route_count, width)
        )
        d_expert_in = jnp.sum(d_copies, axis=1) + jnp.dot(
            d_logits, router_full.T, preferred_element_type=jnp.float32
        )
        acc_router = acc_router + jnp.dot(expert_in.T, d_logits, preferred_element_type=jnp.float32)
        acc_expert_gain = acc_expert_gain + jnp.sum(d_expert_in * resid_hat, axis=0)
        d_resid = out_grad + norm_back(d_expert_in, expert_gain, resid_hat, expert_factor)
        d_branch = d_resid.astype(jnp.bfloat16)
        acc_output = acc_output + jnp.einsum(
            "td,th->dh", d_branch, context_low, preferred_element_type=jnp.float32
        )
        d_context = jnp.dot(d_branch, output_full, preferred_element_type=jnp.float32).astype(
            jnp.bfloat16
        )
        d_context_rows = to_rows(d_context.reshape(tok_rows, local_heads, head_dim))
        delta_rows = jnp.sum(d_context_rows.astype(jnp.float32) * context_rows, axis=-1)

        def grad_step(block_index, carried):
            d_query_rows, key_grads_all = carried
            scores, allowed, block_start = scores_at(block_index)
            probs = jnp.where(allowed[None], jnp.exp(scores - log_total[..., None]), 0.0)
            key_slice = lax.dynamic_slice_in_dim(key_heads, block_start, key_block, 1)
            value_slice = lax.dynamic_slice_in_dim(value_heads, block_start, key_block, 1)
            d_probs = jnp.einsum(
                "gqd,gkd->gqk", d_context_rows, value_slice, preferred_element_type=jnp.float32
            )
            d_scores = (probs * (d_probs - delta_rows[..., None])).astype(jnp.bfloat16)
            d_query_rows = (
                d_query_rows
                + jnp.einsum(
                    "gqk,gkd->gqd", d_scores, key_slice, preferred_element_type=jnp.float32
                )
                * score_scale
            )
            d_key_block = (
                jnp.einsum("gqk,gqd->kgd", d_scores, query_rows, preferred_element_type=jnp.float32)
                * score_scale
            )
            d_value_block = jnp.einsum(
                "gqk,gqd->kgd",
                probs.astype(jnp.bfloat16),
                d_context_rows,
                preferred_element_type=jnp.float32,
            )
            current = lax.dynamic_slice_in_dim(key_grads_all, block_start, key_block, 0)
            updated = current + jnp.concatenate([d_key_block, d_value_block], axis=-1)
            return (
                d_query_rows,
                lax.dynamic_update_slice_in_dim(key_grads_all, updated, block_start, 0),
            )

        start_grads = (
            jnp.zeros((local_groups, query_count, head_dim), jnp.float32),
            jnp.zeros((seq_len, local_groups, 2 * head_dim), jnp.float32),
        )
        d_query_rows, key_grads_all = lax.fori_loop(0, block_total, grad_step, start_grads)
        key_grads = (
            lax.psum_scatter(
                key_grads_all.reshape(seq_len, local_groups * 2 * head_dim).astype(jnp.bfloat16),
                "fsdp",
                scatter_dimension=0,
                tiled=True,
            )
            .astype(jnp.float32)
            .reshape(tok_rows, local_groups, 2 * head_dim)
        )
        d_value_low = (
            key_grads[..., head_dim:]
            .reshape(tok_rows, local_groups * head_dim)
            .astype(jnp.bfloat16)
        )
        d_key_pre, key_gain_part = head_back(
            key_grads[..., :head_dim], cosine_heads, sine_heads, key_gain, key_hat, key_factor
        )
        d_query_pre, query_gain_part = head_back(
            from_rows(d_query_rows), cosine_heads, sine_heads, query_gain, query_hat, query_factor
        )
        d_query_low = d_query_pre.astype(jnp.bfloat16).reshape(tok_rows, local_heads * head_dim)
        d_key_low = d_key_pre.astype(jnp.bfloat16).reshape(tok_rows, local_groups * head_dim)
        d_normed_part = jnp.dot(d_query_low, query_full.T, preferred_element_type=jnp.float32)
        d_normed_part = d_normed_part + jnp.dot(
            d_key_low, key_full.T, preferred_element_type=jnp.float32
        )
        d_normed_part = d_normed_part + jnp.dot(
            d_value_low, value_full.T, preferred_element_type=jnp.float32
        )
        acc_query = acc_query + jnp.dot(normed.T, d_query_low, preferred_element_type=jnp.float32)
        acc_key = acc_key + jnp.dot(normed.T, d_key_low, preferred_element_type=jnp.float32)
        acc_value = acc_value + jnp.dot(normed.T, d_value_low, preferred_element_type=jnp.float32)
        d_normed, head_gain_parts = (
            lax.psum(d_normed_part.astype(jnp.bfloat16), "tp").astype(jnp.float32),
            lax.psum(jnp.stack([query_gain_part, key_gain_part]).astype(jnp.bfloat16), "tp").astype(
                jnp.float32
            ),
        )
        acc_head_gains = acc_head_gains + head_gain_parts
        acc_attention_gain = acc_attention_gain + jnp.sum(d_normed * input_hat, axis=0)
        input_rows.append(
            (d_resid + norm_back(d_normed, attention_gain, input_hat, attention_factor)).astype(
                jnp.bfloat16
            )
        )
    summed = (
        lax.psum_scatter(
            acc_attention_gain.astype(jnp.bfloat16), "fsdp", scatter_dimension=0, tiled=True
        ).astype(jnp.float32),
        lax.psum_scatter(
            acc_head_gains[0].astype(jnp.bfloat16), "fsdp", scatter_dimension=0, tiled=True
        ).astype(jnp.float32),
        lax.psum_scatter(
            acc_head_gains[1].astype(jnp.bfloat16), "fsdp", scatter_dimension=0, tiled=True
        ).astype(jnp.float32),
        lax.psum_scatter(
            acc_query.astype(jnp.bfloat16), "fsdp", scatter_dimension=0, tiled=True
        ).astype(jnp.float32),
        lax.psum_scatter(
            acc_key.astype(jnp.bfloat16), "fsdp", scatter_dimension=0, tiled=True
        ).astype(jnp.float32),
        lax.psum_scatter(
            acc_value.astype(jnp.bfloat16), "fsdp", scatter_dimension=0, tiled=True
        ).astype(jnp.float32),
        lax.psum_scatter(
            acc_output.astype(jnp.bfloat16), "fsdp", scatter_dimension=0, tiled=True
        ).astype(jnp.float32),
        lax.psum_scatter(
            acc_expert_gain.astype(jnp.bfloat16), "fsdp", scatter_dimension=0, tiled=True
        ).astype(jnp.float32),
        lax.psum_scatter(
            acc_router.astype(jnp.bfloat16), "fsdp", scatter_dimension=0, tiled=True
        ).astype(jnp.float32),
    )
    return (
        jnp.stack(layer_rows),
        jnp.stack(input_rows),
        summed[0],
        summed[1],
        summed[2],
        summed[3],
        summed[4],
        summed[5],
        summed[6],
        summed[7],
        summed[8],
        acc_gate,
        acc_up,
        acc_down,
    )


def small_device(
    tokens,
    cotangent,
    expert_ids,
    attention_gain,
    query_gain,
    key_gain,
    query_weight,
    key_weight,
    value_weight,
    output_weight,
    expert_gain,
    router_weight,
    gate_weight,
    up_weight,
    down_weight,
):
    count, rows, width = tokens.shape
    hd = query_gain.shape[0]
    f = lax.axis_index("fsdp")
    n_fsdp = lax.axis_size("fsdp")
    seq = rows * n_fsdp
    experts = gate_weight.shape[0]
    expert_count = experts * n_fsdp
    piece = query_weight.shape[0]

    cosine, sine = signed_tables(seq, hd)
    (normed_all, weights, output_pair, router_all, ids_all, grad_all, pre, qkv, prob, context, resid, expert_in) = begin(
        cotangent,
        query_weight,
        key_weight,
        value_weight,
        output_weight,
        router_weight.T,
        expert_ids.transpose(0, 2, 1),
        tokens,
        attention_gain,
        expert_gain,
        cosine,
        sine,
        query_gain,
        key_gain,
    )
    expert_all, act, dx_sum, out_sum, probs, dgp = run_experts(
        expert_in, grad_all, ids_all, router_all, gate_weight, up_weight, down_weight
    )
    layer_output, input_grad, d_query, d_key, d_value, d_output, aux_sum, line = end(
        normed_all,
        weights,
        output_pair,
        pre,
        qkv,
        prob,
        context,
        tokens,
        out_sum,
        resid,
        cotangent,
        dx_sum,
        expert_in,
        probs,
        dgp,
        router_all,
        expert_gain,
        attention_gain,
        query_weight,
        key_weight,
        value_weight,
        cosine,
        sine,
        query_gain,
        key_gain,
    )
    d_gate, d_up, d_down, layer_output, input_grad, d_query, d_output = expert_grads(
        act, expert_all, grad_all, layer_output, input_grad, d_query, d_output
    )
    own_gain = lax.dynamic_slice_in_dim(attention_gain, f * piece, piece, 0)
    head_piece = hd // n_fsdp
    head_gains = lax.dynamic_slice_in_dim(line[:2, piece:], f * head_piece, head_piece, 1)
    return (
        layer_output,
        input_grad,
        line[0, :piece] / own_gain,
        head_gains[0],
        head_gains[1],
        d_query,
        d_key,
        d_value,
        d_output,
        aux_sum[expert_count],
        aux_sum[:expert_count].T,
        d_gate.reshape(gate_weight.shape),
        d_up.reshape(up_weight.shape),
        d_down.reshape(down_weight.shape),
    )


def solution(mesh):
    body = small_device if (mesh.shape["fsdp"], mesh.shape["tp"]) == (8, 4) else general_device
    return jax.shard_map(
        body,
        mesh=mesh,
        in_specs=(
            P(None, "fsdp", None),
            P(None, "fsdp", None),
            P(None, "fsdp", None),
            P(),
            P(),
            P(),
            P("fsdp", "tp"),
            P("fsdp", "tp"),
            P("fsdp", "tp"),
            P("fsdp", "tp"),
            P(),
            P("fsdp", None),
            P("fsdp", "tp", None),
            P("fsdp", "tp", None),
            P("fsdp", "tp", None),
        ),
        out_specs=(
            P(None, "fsdp", None),
            P(None, "fsdp", None),
            P("fsdp"),
            P("fsdp"),
            P("fsdp"),
            P("fsdp", "tp"),
            P("fsdp", "tp"),
            P("fsdp", "tp"),
            P("fsdp", "tp"),
            P("fsdp"),
            P("fsdp", None),
            P("fsdp", "tp", None),
            P("fsdp", "tp", None),
            P("fsdp", "tp", None),
        ),
        check_vma=False,
    )
```

```python
import functools
import math

import jax
import jax.numpy as jnp
import numpy as np
from jax import lax
from jax.experimental import pallas as pl
from jax.experimental.pallas import tpu as pltpu
from jax.sharding import PartitionSpec as P

norm_eps = 1e-06
rope_base = 1000000.0
masked_score = -1e30
MESH = pl.DeviceIdType.MESH
LOW = jnp.bfloat16
F32 = jnp.float32
VMEM_LIMIT = 62 * 2**20


def coords():
    f = lax.axis_index("fsdp")
    t = lax.axis_index("tp")
    return f // 2, f % 2, t // 2, t % 2


def place(z, x, y, c):
    return (2 * z + x, 2 * y + c)


def span(first, count):
    return pl.ds(pl.multiple_of(first, count), count)


class Here:
    def __init__(self):
        z, x, y, c = coords()
        self.z, self.x, self.y, self.c = z, x, y, c
        self.f, self.t = 2 * z + x, 2 * y + c
        self.xn, self.yn, self.cn = place(z, 1 - x, y, c), place(z, x, 1 - y, c), place(z, x, y, 1 - c)
        self.lanes = ((x, y), (1 - x, y), (x, 1 - y), (1 - x, 1 - y))

    def zr(self, d):
        return (self.z + d) % 4

    def flip(self, k):
        return (self.z // 2 + k // 2) % 2 * 2 + (self.z % 2 + k % 2) % 2

    def zd(self, j):
        inner = (self.z % 3 + 1) // 2
        return self.flip(j + inner * (j // 2) * (1 - 2 * (j % 2)))

    def at_z(self, z):
        return place(z, self.x, self.y, self.c)

    def number(self, j, e):
        return 2 * self.zd(j) + (self.x + e) % 2

    def peer(self, d, e):
        return place(self.zr(d), (self.x + e) % 2, self.y, self.c)

    def greet(self):
        self.say()
        self.hear()

    def say(self):
        peers = [self.peer(d, e) for d in range(4) for e in range(2) if d or e] + [self.yn, self.cn]
        for peer in peers:
            pl.semaphore_signal(pltpu.get_barrier_semaphore(), inc=1, device_id=peer, device_id_type=MESH)

    def hear(self):
        pl.semaphore_wait(pltpu.get_barrier_semaphore(), 9)


def remote(src, dst, send_sem, recv_sem, device):
    return pltpu.make_async_remote_copy(
        src_ref=src, dst_ref=dst, send_sem=send_sem, recv_sem=recv_sem, device_id=device, device_id_type=MESH
    )


def push(src, dst, send_sem, recv_sem, device):
    copy = remote(src, dst, send_sem, recv_sem, device)
    copy.start()
    return copy


def keep(src, dst, sem):
    copy = pltpu.make_async_copy(src, dst, sem)
    copy.start()
    return copy


ORDER = (1, 2, 3)
FAR_FIRST = (3, 2, 1, 0)


class Gather:
    scratch = staticmethod(
        lambda: [pltpu.SemaphoreType.DMA((1,)), pltpu.SemaphoreType.DMA((6,))]
        + [pltpu.SemaphoreType.DMA((4,))] * 9
        + [pltpu.SemaphoreType.DMA((4, 4))] * 2
    )
    slots = 13

    def __init__(self, here, whole, src, dst, sems, by_x, own=None):
        self.here, self.whole, self.src, self.dst, self.own_rows = here, whole, src, dst, own
        (self.loc, self.sz, self.rz, self.sx, self.rx, self.sy, self.ry,
         self.sdx, self.rdx, self.sdy, self.rdy, self.sc, self.rc) = sems
        self.rows, self.cols = src.shape[1], src.shape[2] // 4
        self.half = by_x
        self.sends = []

    def block(self, z, x, y, c, h=None):
        first = (2 * z + x) * self.rows
        rows = span(first, self.rows)
        if h is not None:
            start, count = ((0, self.half), (self.half, self.rows - self.half))[h]
            rows = pl.ds(pl.multiple_of(first + start, 16), count)
        return self.dst.at[:, rows, span((2 * y + c) * self.cols, self.cols)]

    def source(self, z_to, t, first, count):
        seqs = slice(None) if self.whole else pl.ds(z_to // 2, 1)
        return self.src.at[seqs, pl.ds(first, count), span(t * self.cols, self.cols)]

    def push(self, make, when=None):
        if when is None:
            push(*make())
        else:
            pl.when(when)(lambda: push(*make()) and None)
        self.sends.append((make, when))

    def landed(self, ref, sem):
        pltpu.make_async_remote_copy(
            src_ref=ref, dst_ref=ref, send_sem=sem, recv_sem=sem, device_id=self.here.xn, device_id_type=MESH
        ).wait_recv()

    def start(self):
        h = self.here
        self.inner = h.z % 3 > 0
        self.along(0, h.flip(1), True)
        self.along(1, h.flip(3), self.inner)
        if not self.whole:
            self.along(2, h.flip(2), h.z % 3 == 0)
        self.push(lambda: (self.source(h.z, h.t, 0, self.rows), self.block(h.z, h.x, h.y, h.c),
                           self.sx.at[h.z], self.rx.at[h.z], h.xn))
        if self.half:
            self.push(lambda: (self.source(h.z, 2 * (1 - h.y) + h.c, 0, self.half),
                               self.block(h.z, h.x, 1 - h.y, h.c, 0), self.sdx.at[h.z], self.rdx.at[h.z], h.xn))
        own = self.src if self.whole else self.src.at[pl.ds(h.z // 2, 1)]
        if self.own_rows is not None:
            own = self.own_rows
            pltpu.make_async_copy(self.src, own, self.loc.at[0]).start()
            pltpu.make_async_copy(self.src, own, self.loc.at[0]).wait()
        self.own = keep(own, self.dst.at[:, span(h.f * self.rows, self.rows), :], self.loc.at[0])

    def along(self, n, z_to, when):
        h = self.here
        self.push(lambda: (self.source(z_to, h.t, 0, self.rows), self.block(h.z, h.x, h.y, h.c),
                           self.sz.at[n], self.rz.at[h.z], h.at_z(z_to)), None if when is True else when)

    def relay(self, j):
        h, zd = self.here, self.here.zd(j)
        self.landed(self.block(zd, h.x, h.y, h.c), self.rz.at[zd])
        if j > 1 or self.whole:

            def make():
                b = self.block(h.zd(j), h.x, h.y, h.c)
                return b, b, self.sz.at[2 + j], self.rz.at[h.zd(j)], h.at_z(h.flip(3 if j == 1 else 1))

            self.push(make, self.inner)

    def pass_on(self, d, lane, sends, recvs, device, h=None):
        x, y = self.here.lanes[lane]

        def make():
            zd = self.here.zd(d)
            b = self.block(zd, x, y, self.here.c, h)
            return b, b, sends(zd), recvs(zd), device

        self.push(make)

    def spread(self, d):
        h = self.here
        self.pass_on(d, 0, lambda k: self.sx.at[k], lambda k: self.rx.at[k], h.xn)
        self.pass_on(d, 0, lambda k: self.sy.at[k], lambda k: self.ry.at[k], h.yn)
        self.pass_on(d, 0, lambda k: self.sc.at[0, k], lambda k: self.rc.at[0, k], h.cn)

    def cross(self, d):
        h, zd = self.here, self.here.zd(d)
        self.landed(self.block(zd, 1 - h.x, h.y, h.c), self.rx.at[zd])
        self.pass_on(d, 1, lambda k: self.sdy.at[k], lambda k: self.rdy.at[k], h.yn, 1)
        self.pass_on(d, 1, lambda k: self.sc.at[1, k], lambda k: self.rc.at[1, k], h.cn)
        if d != 0:
            self.landed(self.block(zd, h.x, 1 - h.y, h.c), self.ry.at[zd])
            if self.half:
                self.pass_on(d, 2, lambda k: self.sdx.at[k], lambda k: self.rdx.at[k], h.xn, 0)
            self.pass_on(d, 2, lambda k: self.sc.at[2, k], lambda k: self.rc.at[2, k], h.cn)

    def close(self, d):
        h, zd = self.here, self.here.zd(d)
        if self.half:
            self.landed(self.block(zd, 1 - h.x, 1 - h.y, h.c, 0), self.rdx.at[zd])
        self.landed(self.block(zd, 1 - h.x, 1 - h.y, h.c, 1), self.rdy.at[zd])
        self.pass_on(d, 3, lambda k: self.sc.at[3, k], lambda k: self.rc.at[3, k], h.cn)

    def first_steps(self):
        for j in ORDER:
            self.relay(j)
            self.spread(j)
            if j < 3:
                self.cross(j - 1)

    def last_steps(self):
        self.close(0)
        for j in (2, 3):
            self.cross(j)
            self.close(j - 1)
        self.close(3)

    def arrived(self, d, e):
        h, zd = self.here, self.here.zd(d)
        if e == 0:
            if d == 0:
                self.own.wait()
            else:
                self.landed(self.block(zd, h.x, h.y, 1 - h.c), self.rc.at[0, zd])
                self.landed(self.block(zd, h.x, 1 - h.y, 1 - h.c), self.rc.at[2, zd])
        else:
            self.landed(self.block(zd, 1 - h.x, h.y, 1 - h.c), self.rc.at[1, zd])
            self.landed(self.block(zd, 1 - h.x, 1 - h.y, 1 - h.c), self.rc.at[3, zd])

    def finish(self):
        for make, when in self.sends:
            if when is None:
                remote(*make()).wait_send()
            else:
                pl.when(when)(lambda make=make: remote(*make()).wait_send())


def add_into(target, *others):
    count, rows, _ = target.shape
    step = 32
    wide = target.dtype if len(others) == 1 else F32

    @pl.loop(0, count * rows // step)
    def _(i):
        n = i // (rows // step)
        r = pl.ds(pl.multiple_of((i % (rows // step)) * step, step), step)
        total = target[n, r, :].astype(wide)
        for other in others:
            total = total + other[n, r, :].astype(wide)
        target[n, r, :] = total.astype(target.dtype)


class Sum:
    slots = 23

    @staticmethod
    def scratch(count, rows, width, low, by_x):
        dma = pltpu.SemaphoreType.DMA
        cols = width // 4
        vm = pltpu.VMEM
        return [
            vm((4, 4, count, rows, cols), low),
            vm((4, count, max(by_x, 16), cols), low),
            vm((4, count, rows - by_x, cols), low),
            vm((4, count, rows, cols), low),
            vm((4, count, rows, cols), low),
            vm((4, count, rows, cols), low),
            vm((4, 2, rows, cols), low),
            vm((2, rows, cols), low),
            dma((4, 4)), dma((4, 4)),
        ] + [dma((4,))] * 10 + [dma((3,))] * 2 + [dma((5,))]

    def __init__(self, here, whole, part, refs, by_x):
        self.here, self.whole, self.part, self.by_x = here, whole, part, by_x
        (self.fc, self.f1x, self.f1y, self.f2x, self.f2y, self.fz, self.full, self.tmp, self.sc, self.rc,
         self.s1x, self.r1x, self.s1y, self.r1y, self.s2x, self.r2x, self.s2y, self.r2y, self.sz, self.rz,
         self.sg, self.rg, self.osem) = refs
        self.rows, self.cols = part.shape[1] // 8, part.shape[2] // 4
        self.top, self.low = pl.ds(0, by_x), pl.ds(by_x, self.rows - by_x)
        self.sends = []

    def block(self, d, lane, c):
        x, y = self.here.lanes[lane]
        return self.part.at[:, span((2 * self.here.zd(d) + x) * self.rows, self.rows),
                            span((2 * y + c) * self.cols, self.cols)]

    def push(self, make):
        push(*make())
        self.sends.append(make)

    def landed(self, ref, sem):
        pltpu.make_async_remote_copy(
            src_ref=ref, dst_ref=ref, send_sem=sem, recv_sem=sem, device_id=self.here.xn, device_id_type=MESH
        ).wait_recv()

    def giving(self, d, e):
        h = self.here
        for q in (0, 1):
            lane = 2 * q + e
            at = self.part.at[:, span((2 * h.zd(d) + (h.x + e) % 2) * self.rows, self.rows),
                              span((2 * ((h.y + q) % 2) + 1 - h.c) * self.cols, self.cols)]
            yield at, self.fc.at[lane, d], self.sc.at[lane, d], self.rc.at[lane, d], h.cn

    def give(self, d, e):
        for args in self.giving(d, e):
            push(*args)

    def pair(self, lane, d):
        self.landed(self.fc.at[lane, d], self.rc.at[lane, d])
        add_into(self.block(d, lane, self.here.c), self.fc.at[lane, d])

    def mine(self, d, lane, rows=slice(None)):
        return self.block(d, lane, self.here.c).at[:, rows]

    def corner(self, d):
        self.pair(3, d)
        if self.by_x:
            self.push(lambda: (self.mine(d, 3, self.top), self.f1x.at[d], self.s1x.at[d], self.r1x.at[d], self.here.xn))
        self.push(lambda: (self.mine(d, 3, self.low), self.f1y.at[d], self.s1y.at[d], self.r1y.at[d], self.here.yn))

    def sides(self, d):
        self.pair(1, d)
        self.landed(self.f1y.at[d], self.r1y.at[d])
        add_into(self.mine(d, 1, self.low), self.f1y.at[d])
        self.push(lambda: (self.mine(d, 1), self.f2x.at[d], self.s2x.at[d], self.r2x.at[d], self.here.xn))
        self.pair(2, d)
        if self.by_x:
            self.landed(self.f1x.at[d], self.r1x.at[d])
            add_into(self.mine(d, 2, self.top), self.f1x.at[d])
        self.push(lambda: (self.mine(d, 2), self.f2y.at[d], self.s2y.at[d], self.r2y.at[d], self.here.yn))

    def centre(self, d):
        self.pair(0, d)
        self.landed(self.f2x.at[d], self.r2x.at[d])
        self.landed(self.f2y.at[d], self.r2y.at[d])
        add_into(self.mine(d, 0), self.f2x.at[d], self.f2y.at[d])
        if d != 0:
            h = self.here
            self.push(lambda: (self.mine(d, 0), self.fz.at[h.z], self.sz.at[d], self.rz.at[h.z], h.at_z(h.zd(d))))

    def total(self):
        for d in (1, 2, 3):
            self.landed(self.fz.at[self.here.zd(d)], self.rz.at[self.here.zd(d)])
        b = self.block(0, 0, self.here.c)
        step = 32

        @pl.loop(0, 2 * self.rows // step)
        def _(i):
            n = i // (self.rows // step)
            r = pl.ds(pl.multiple_of((i % (self.rows // step)) * step, step), step)
            if self.whole:
                total = b[n, r, :].astype(F32)
                for d in (1, 2, 3):
                    total = total + self.fz[self.here.zd(d), n, r, :].astype(F32)
            else:
                total = jnp.where(self.here.z // 2 == n, b[0, r, :].astype(F32), 0.0)
                for d in (1, 2, 3):
                    total = total + jnp.where(self.here.zd(d) // 2 == n, self.fz[self.here.zd(d), 0, r, :].astype(F32), 0.0)
            self.tmp[n, r, :] = total.astype(self.tmp.dtype)

    def share(self, out):
        self.share_start()
        self.share_cross()
        self.share_end(out)

    def share_start(self):
        h = self.here
        self.keeps = [keep(self.tmp, self.full.at[h.t], self.osem.at[4])]
        self.push(lambda: (self.tmp, self.full.at[h.t], self.sg.at[0], self.rg.at[0], h.yn))
        self.push(lambda: (self.tmp, self.full.at[h.t], self.sg.at[1], self.rg.at[1], h.cn))

    def share_cross(self):
        h = self.here
        ty = 2 * (1 - h.y) + h.c
        self.landed(self.full.at[ty], self.rg.at[0])
        self.push(lambda: (self.full.at[ty], self.full.at[ty], self.sg.at[2], self.rg.at[2], h.cn))

    def share_end(self, out):
        h = self.here
        self.landed(self.full.at[2 * h.y + 1 - h.c], self.rg.at[1])
        self.landed(self.full.at[2 * (1 - h.y) + 1 - h.c], self.rg.at[2])
        self.keeps[0].wait()
        if out is None:
            return
        outs = [keep(self.full.at[q], out.at[:, :, pl.ds(q * self.cols, self.cols)], self.osem.at[q]) for q in range(4)]
        for copy in outs:
            copy.wait()

    def finish(self):
        for make in self.sends:
            remote(*make()).wait_send()
        for d in range(4):
            for e in range(2):
                for args in self.giving(d, e):
                    remote(*args).wait_send()


def wait_for(ref, sem, device):
    pltpu.make_async_remote_copy(
        src_ref=ref, dst_ref=ref, send_sem=sem, recv_sem=sem, device_id=device, device_id_type=MESH
    ).wait_recv()


def signed_tables(length, width):
    middle = width // 2
    frequency = rope_base ** (-np.arange(middle) * 2.0 / width)
    angles = np.arange(length)[:, None] * frequency[None, :]
    cosine, sine = np.cos(angles), np.sin(angles)
    return (
        jnp.asarray(np.concatenate([cosine, cosine], axis=1), F32),
        jnp.asarray(np.concatenate([-sine, sine], axis=1), F32),
    )


def dot_nn(a, b):
    return jnp.dot(a, b, preferred_element_type=F32)


def dot_nt(a, b):
    return lax.dot_general(a, b, (((1,), (1,)), ((), ())), preferred_element_type=F32)


def dot_tn(a, b):
    return lax.dot_general(a, b, (((0,), (0,)), ((), ())), preferred_element_type=F32)


BY_X = 64


class Weights:
    scratch = staticmethod(lambda: [pltpu.SemaphoreType.DMA((8, 4, 2))] * 4 + [pltpu.SemaphoreType.DMA((6,))])
    slots = 5

    def __init__(self, here, query, key, value, output, router, ids, w, wo, router_all, ids_all, sems):
        self.here = here
        self.query, self.output, self.w, self.wo = query, output, w, wo
        piece, part = query.shape[0], wo.shape[1]
        self.piece, self.part = piece, part
        hd = key.shape[1]
        self.shared = (
            (key, lambda f: w.at[span(f * piece, piece), pl.ds(part, hd)]),
            (value, lambda f: w.at[span(f * piece, piece), pl.ds(part + hd, hd)]),
            (router, lambda f: router_all.at[:, span(f * piece, piece)]),
            (ids, lambda f: ids_all.at[:, :, span(f * ids.shape[2], ids.shape[2])]),
        )
        self.qs, self.qr, self.ss, self.sr, self.loc = sems
        self.sends, self.keeps = [], []

    def landed(self, ref, sem):
        pltpu.make_async_remote_copy(
            src_ref=ref, dst_ref=ref, send_sem=sem, recv_sem=sem, device_id=self.here.xn, device_id_type=MESH
        ).wait_recv()

    def start_shared(self):
        h = self.here
        for n, (src, dst) in enumerate(self.shared):
            self.keeps.append(keep(src, dst(h.f), self.loc.at[n]))
            for d, e in ((2, 0), (1, 0), (3, 0), (0, 1)):
                self.sends.append(push(src, dst(h.f), self.ss.at[n, d, e], self.sr.at[n, (4 - d) % 4, e], h.peer(d, e)))

    def pass_shared(self, d):
        h = self.here
        for n, (_, dst) in enumerate(self.shared):
            ref = dst(2 * h.zr(d) + h.x)
            self.landed(ref, self.sr.at[n, d, 0])
            self.sends.append(push(ref, ref, self.ss.at[n, d, 1], self.sr.at[n, d, 1], h.xn))

    def wait_shared(self):
        h = self.here
        for n, (_, dst) in enumerate(self.shared):
            for d in range(4):
                self.landed(dst(2 * h.zr(d) + 1 - h.x), self.sr.at[n, d, 1])

    def start_pairs(self, n):
        h = self.here
        src, dst = ((self.query, self.w), (self.output, self.wo))[n]
        mine = lambda f: dst.at[span(f * self.piece, self.piece), pl.ds(0, self.part)]
        self.keeps.append(keep(src.at[:, span((h.f % 4) * self.part, self.part)], mine(h.f), self.loc.at[4 + n]))
        for d in (2, 1, 3, 0):
            for e in (1, 0):
                if d or e:
                    f = 2 * h.zr(d) + (h.x + e) % 2
                    self.sends.append(push(src.at[:, span((f % 4) * self.part, self.part)], mine(h.f),
                                           self.qs.at[n, d, e], self.qr.at[n, (4 - d) % 4, e], h.peer(d, e)))

    def wait_pairs(self, n, far=range(4)):
        h = self.here
        dst = (self.w, self.wo)[n]
        for d in far:
            for e in (1, 0):
                if d or e:
                    f = 2 * h.zr(d) + (h.x + e) % 2
                    self.landed(dst.at[span(f * self.piece, self.piece), pl.ds(0, self.part)], self.qr.at[n, d, e])

    def finish(self):
        for copy in self.sends:
            copy.wait_send()


def unit(values):
    factor = lax.rsqrt(jnp.mean(values * values, axis=-1, keepdims=True) + norm_eps)
    return values * factor, factor


def begin_kernel(heads, cot, query, key, value, output, router, ids, tokens, ag_ref, eg_ref,
                 cos_ref, sin_ref, qg_ref, kg_ref, xn_out, w_out, wo_out, router_out, ids_out, cot_out, pre_out, qkv_out, prob_out, ctx_out, resid_out, expert_out,
                 normed, resid, xn, w, wo, pre, qkv, prob, ctx, part, own, osem, *sems):
    here = Here()
    here.say()
    count, rows, _ = tokens.shape
    step = 32
    steps = rows // step

    def chunk_of(i):
        return i // steps, pl.ds(pl.multiple_of(i % steps * step, step), step)

    @pl.loop(0, count * steps)
    def _(i):
        n, r = chunk_of(i)
        normed[n, r, :] = (unit(tokens[n, r, :].astype(F32))[0] * ag_ref[...]).astype(LOW)

    here.hear()
    at = 0
    x_rows = Gather(here, False, normed, xn, sems[at : at + Gather.slots], BY_X)
    at += Gather.slots
    c_rows = Gather(here, True, cot, cot_out, sems[at : at + Gather.slots], BY_X + 32, own)
    at += Gather.slots
    moved = Weights(here, query, key, value, output, router, ids, w, wo, router_out, ids_out, sems[at : at + Weights.slots])
    at += Weights.slots
    total = Sum(here, False, part, sems[at:], BY_X)

    x_rows.start()
    moved.start_shared()
    moved.start_pairs(0)
    x_rows.first_steps()
    for d in (1, 3, 2):
        moved.pass_shared(d)
    x_rows.last_steps()
    for d in (0,) + ORDER:
        x_rows.arrived(d, 0)
        x_rows.arrived(d, 1)
    moved.wait_shared()
    moved.wait_pairs(0, (2,))
    moved.start_pairs(1)
    moved.wait_pairs(0, (0, 1, 3))
    for copy in moved.keeps:
        copy.wait()
    outs = [keep(xn, xn_out, osem.at[0]), keep(w, w_out, osem.at[1])]

    seq = xn.shape[1]
    hd = cos_ref.shape[1]
    tile = 256
    scale = 1.0 / math.sqrt(hd)
    for i in range(seq // tile):
        r = pl.ds(i * tile, tile)
        got = dot_nn(xn[0, r, :], w[...])
        pre[r, :] = got[:, : (heads + 1) * hd]
        qkv[r, pl.ds((heads + 1) * hd, hd)] = got[:, (heads + 1) * hd :].astype(LOW)
        for a in range(heads + 1):
            one = got[:, a * hd : (a + 1) * hd]
            factor = lax.rsqrt(jnp.mean(one * one, axis=-1, keepdims=True) + norm_eps)
            gained = one * factor * (qg_ref if a < heads else kg_ref)[...]
            turned = gained * cos_ref[r, :] + pltpu.roll(gained, hd // 2, 1) * sin_ref[r, :]
            qkv[r, pl.ds(a * hd, hd)] = turned.astype(LOW)
    c_rows.start()
    outs += [keep(pre, pre_out, osem.at[2]), keep(qkv, qkv_out, osem.at[3])]
    for a in range(heads):
        for i in range(seq // tile):
            r = pl.ds(i * tile, tile)
            n = (i + 1) * tile
            score = dot_nt(qkv[r, pl.ds(a * hd, hd)], qkv[pl.ds(0, n), pl.ds(heads * hd, hd)]) * scale
            row = lax.broadcasted_iota(jnp.int32, (tile, n), 0) + i * tile
            col = lax.broadcasted_iota(jnp.int32, (tile, n), 1)
            score = jnp.where(col <= row, score, masked_score)
            terms = jnp.exp(score - jnp.max(score, axis=-1, keepdims=True))
            low = (terms * (1.0 / jnp.sum(terms, axis=-1, keepdims=True))).astype(LOW)
            prob[a, r, pl.ds(0, n)] = low
            ctx[r, pl.ds(a * hd, hd)] = dot_nn(low, qkv[pl.ds(0, n), pl.ds((heads + 1) * hd, hd)]).astype(LOW)
        if a == 0:
            c_rows.relay(1)
            c_rows.spread(1)
    outs += [keep(prob, prob_out, osem.at[4]), keep(ctx, ctx_out, osem.at[5])]
    moved.wait_pairs(1)
    outs.append(keep(wo, wo_out, osem.at[6]))
    for e in (1, 0):
        for d in FAR_FIRST:
            at_f = span(here.number(d, e) * rows, rows)
            part[0, at_f, :] = dot_nt(ctx[at_f, :], wo[...]).astype(LOW)
            total.give(d, e)
    for d in FAR_FIRST:
        total.corner(d)
    c_rows.cross(0)
    c_rows.relay(2)
    c_rows.spread(2)
    for d in FAR_FIRST:
        total.sides(d)
    c_rows.cross(1)
    c_rows.relay(3)
    c_rows.spread(3)
    for d in FAR_FIRST:
        total.centre(d)
    c_rows.close(0)
    c_rows.cross(2)
    c_rows.close(1)
    total.total()
    total.share_start()
    c_rows.cross(3)
    c_rows.close(2)
    total.share_cross()
    c_rows.close(3)
    total.share_end(None)
    x_rows.finish()

    @pl.loop(0, count * steps)
    def _(i):
        n, r = chunk_of(i)
        branch = jnp.concatenate([total.full[q, n, r, :] for q in range(4)], axis=1).astype(F32)
        summed = tokens[n, r, :].astype(F32) + branch
        resid[n, r, :] = summed
        normed[n, r, :] = (unit(summed)[0] * eg_ref[...]).astype(LOW)

    outs += [keep(resid, resid_out, osem.at[7]), keep(normed, expert_out, osem.at[8])]
    for d in (0,) + ORDER:
        c_rows.arrived(d, 0)
        c_rows.arrived(d, 1)
    for each in (c_rows, moved, total):
        each.finish()
    for copy in outs:
        copy.wait()


def begin(cot, query, key, value, output, router, ids, tokens, attention_gain, expert_gain,
          cosine, sine, query_gain, key_gain):
    count, rows, width = tokens.shape
    seq = rows * 8
    hd = query_gain.shape[0]
    part = query.shape[1] // 4
    heads = part // hd
    vm = pltpu.VMEM
    hbm = pl.BlockSpec(memory_space=pl.ANY)
    near = pl.BlockSpec(memory_space=pltpu.VMEM)
    shape = jax.ShapeDtypeStruct
    local = [
        ((1, seq, width), LOW),
        ((width, part + 2 * hd), LOW),
        ((width, part), LOW),
        ((seq, (heads + 1) * hd), F32),
        ((seq, (heads + 2) * hd), LOW),
        ((heads, seq, seq), LOW),
        ((seq, heads * hd), LOW),
    ]
    return pl.pallas_call(
        functools.partial(begin_kernel, heads),
        out_shape=(
            shape(*local[0]),
            shape(*local[1]),
            shape(*local[2]),
            shape((router.shape[0], width), LOW),
            shape((count, ids.shape[1], seq), jnp.int32),
            shape((count, seq, width), LOW),
            shape(*local[3]),
            shape(*local[4]),
            shape(*local[5]),
            shape(*local[6]),
            shape((count, rows, width), F32),
            shape((count, rows, width), LOW),
        ),
        in_specs=[hbm] * 7 + [near] * 7,
        out_specs=[hbm] * 12,
        scratch_shapes=[vm((count, rows, width), LOW), vm((count, rows, width), F32)]
        + [vm(*entry) for entry in local]
        + [vm((1, seq, width), LOW), vm((count, rows, width), LOW), pltpu.SemaphoreType.DMA((9,))]
        + Gather.scratch() + Gather.scratch() + Weights.scratch() + Sum.scratch(1, rows, width, LOW, BY_X),
        compiler_params=pltpu.CompilerParams(
            collective_id=4, has_side_effects=True, vmem_limit_bytes=VMEM_LIMIT
        ),
        name="begin",
    )(cot, query, key, value, output, router, ids, tokens, attention_gain[None], expert_gain[None],
      cosine, sine, query_gain[None], key_gain[None])


def experts_kernel(experts, expert_in, og_in, ids, router, g_in, u_in, d_in,
                   x_out, act_out, dx_sum, out_sum, probs_out, dgp_out,
                   x_t, g, u, dn, og_t, raw_s, act_t, dx, out, stage, share_s, dgp_t, dgp_got, dgp_all, dgp_c, dgp_y,
                   wsem, ogsem, xsem, actsem, psem, rsem, tsem, usem, *rest):
    here = Here()
    here.say()
    loads = [keep(src, dst, wsem.at[n]) for n, (src, dst) in enumerate(((d_in, dn), (g_in, g), (u_in, u)))]
    by_x = expert_in.shape[1] // 2
    rows_x = Gather(here, True, expert_in, x_out, rest[: Gather.slots], by_x, x_t.at[0])
    sums = (
        Sum(here, True, dx, rest[Gather.slots : Gather.slots + Sum.slots], by_x),
        Sum(here, True, out, rest[Gather.slots + Sum.slots :], by_x),
    )
    number = here.number
    count, rows, width = expert_in.shape
    hidden = g.shape[0]
    per = hidden // experts
    tokens = count * rows
    lanes = router.shape[0]
    part = stage.shape[2]
    chunk = width // 4
    here.hear()
    rows_x.start()

    def plane(i):
        k = i // 2
        return k + (k + 2) // 3 - 3 * (k // 3)

    def tile(i):
        return span(number(plane(i), i % 2) * rows, rows)

    def og_load(i):
        return pltpu.make_async_copy(og_in.at[:, tile(i), :], og_t.at[i % 2], ogsem.at[i % 2])

    def x_load(i):
        return pltpu.make_async_copy(x_out.at[:, tile(i), :], x_t.at[i % 2], xsem.at[i % 2])

    def act_store(i):
        return pltpu.make_async_copy(act_t.at[i % 2], act_out.at[:, :, tile(i), :], actsem.at[i % 2])

    def dgp_send(i):
        to = place(here.zd(plane(i)), (here.x + i % 2) % 2, here.y, here.c)
        return remote(dgp_t.at[i], dgp_got.at[here.f], psem.at[i], rsem.at[here.f], to)

    def both(step, j):
        for each in sums:
            getattr(each, step)(j)

    first = {2: lambda: (rows_x.relay(1), rows_x.spread(1))}
    early = {
        3: lambda: (rows_x.cross(0),),
        5: lambda: (rows_x.relay(2), rows_x.spread(2)),
        7: lambda: (rows_x.cross(1), rows_x.close(0)),
    }
    before = {
        1: lambda: (rows_x.relay(3), rows_x.spread(3), rows_x.arrived(0, 1)),
        2: lambda: (rows_x.close(2), rows_x.arrived(2, 0), rows_x.arrived(2, 1)),
        3: lambda: (both("corner", 0),),
        5: lambda: (both("corner", 2),),
        7: lambda: (both("corner", 3),),
    }
    middle = {
        1: lambda: (rows_x.cross(2), rows_x.close(1)),
        2: lambda: (rows_x.cross(3),),
        3: lambda: (rows_x.close(3), rows_x.arrived(3, 0), rows_x.arrived(3, 1)),
        4: lambda: (both("sides", 0),),
        5: lambda: (rows_x.arrived(1, 0), rows_x.arrived(1, 1)),
        6: lambda: (both("sides", 2), both("centre", 0)),
    }

    def hooks(table, i):
        for key, run in table.items():
            @pl.when(i == key)
            def _(run=run):
                run()

    row = lax.broadcasted_iota(jnp.int32, (lanes, hidden), 0)
    col = lax.broadcasted_iota(jnp.int32, (lanes, hidden), 1)
    spread = jnp.where(row == here.f * experts + col // per, 1.0, 0.0).astype(LOW)
    row8 = lax.broadcasted_iota(jnp.int32, (8, hidden), 0)
    col8 = lax.broadcasted_iota(jnp.int32, (8, hidden), 1)
    gather8 = jnp.where(row8 == col8 // per, 1.0, 0.0).astype(LOW)

    def first_half(i):
        x_tile = x_t[i % 2].reshape(tokens, width)
        for n, right in enumerate((g, u)):
            for k in range(hidden // part):
                stage[n, pl.ds(k * tokens, tokens), :] = dot_nt(x_tile, right[pl.ds(k * part, part), :])
        logits = dot_nt(router[...], x_tile)
        named_ids = jnp.concatenate([ids[m, :, tile(i)] for m in range(count)], axis=1)
        lane = lax.broadcasted_iota(jnp.int32, logits.shape, 0)
        named = lane == named_ids[0:1, :]
        for k in range(1, named_ids.shape[0]):
            named = named | (lane == named_ids[k : k + 1, :])
        masked = jnp.where(named, logits, masked_score)
        terms = jnp.where(named, jnp.exp(masked - jnp.max(masked, axis=0, keepdims=True)), 0.0)
        probs = terms / jnp.sum(terms, axis=0, keepdims=True)
        share_s[...] = dot_tn(probs.astype(LOW), spread)
        return probs

    def between(i, m):
        r = pl.ds(m * rows, rows)
        gate, up = (
            jnp.concatenate([stage[n, pl.ds(k * tokens + m * rows, rows), :] for k in range(hidden // part)], axis=1)
            for n in range(2)
        )
        raw = raw_s[i, r, :].astype(F32)
        share = share_s[r, :]
        sig = 1.0 / (1.0 + jnp.exp(-gate))
        silu = gate * sig
        inner = silu * up
        dgp_t[i, :, r] = dot_nt(gather8, (inner * raw).astype(LOW))
        d_inner = raw * share
        act_t[i % 2, 0, m] = (d_inner * up * (sig + silu * (1.0 - sig))).astype(LOW)
        act_t[i % 2, 1, m] = (d_inner * silu).astype(LOW)
        act_t[i % 2, 2, m] = (inner * share).astype(LOW)

    def second_half(i, q):
        d_gate, d_up, weighted = (act_t[i % 2, n].reshape(tokens, hidden) for n in range(3))
        cols = pl.ds(q * chunk, chunk)
        got = dot_nn(d_gate, g[:, cols]) + dot_nn(d_up, u[:, cols])
        dx[:, tile(i), cols] = got.astype(LOW).reshape(count, rows, chunk)
        out[:, tile(i), cols] = dot_nn(weighted, dn[:, cols]).astype(LOW).reshape(count, rows, chunk)

    def sent(i):
        for each in sums:
            each.give(plane(i), i % 2)

        @pl.when(i > 0)
        def _():
            dgp_send(i).start()

    og_load(0).start()
    loads[0].wait()

    def raw_step(table, i):
        @pl.when(i + 1 < 8)
        def _():
            og_load(i + 1).start()

        hooks(table, i)
        og_load(i).wait()
        raw_s[i] = dot_nt(og_t[i % 2].reshape(tokens, width), dn[...]).astype(LOW)

    pl.loop(0, 3)(functools.partial(raw_step, first))
    loads[1].wait()
    loads[2].wait()
    rows_x.arrived(0, 0)
    probs_out[...] = first_half(0)
    for m in range(count):
        between(0, m)
    act_store(0).start()
    pl.loop(3, 8)(functools.partial(raw_step, early))

    @pl.loop(1, 8)
    def _(i):
        hooks(before, i)

        @pl.when(i < 3)
        def _():
            x_load(i).start()

        @pl.when(i >= 2)
        def _():
            act_store(i - 2).wait()

        x_load(i).wait()
        first_half(i)
        hooks(middle, i)

        @pl.when((i >= 2) & (i < 7))
        def _():
            x_load(i + 1).start()

        for m in range(count):
            second_half(i - 1, 2 * m)
            between(i, m)
            second_half(i - 1, 2 * m + 1)
        act_store(i).start()
        sent(i - 1)

    for q in range(4):
        second_half(7, q)
    sent(7)
    ahead, behind = sums
    ahead.corner(1)
    ahead.sides(3)
    ahead.centre(2)
    behind.corner(1)
    behind.sides(3)
    ahead.sides(1)
    ahead.centre(3)
    behind.centre(2)
    behind.sides(1)
    ahead.centre(1)
    behind.centre(3)
    for d in range(4):
        for e in range(2):
            if d or e:
                n = number(d, e)
                wait_for(dgp_got.at[n], rsem.at[n], here.xn)
                dgp_all[n] = dgp_got[n]
    dgp_all[here.f] = dgp_t[0]
    across = push(dgp_all, dgp_c, tsem.at[0], usem.at[0], here.cn)
    ahead.total()
    ahead.share_start()
    behind.centre(1)
    wait_for(dgp_c, usem.at[0], here.cn)
    across.wait_send()
    dgp_all[...] = dgp_all[...] + dgp_c[...]
    second = push(dgp_all, dgp_y, tsem.at[1], usem.at[1], here.yn)
    ahead.share_cross()
    behind.total()
    quarter = keep(behind.tmp, out_sum, behind.osem.at[0])
    ahead.share_end(dx_sum)
    quarter.wait()
    wait_for(dgp_y, usem.at[1], here.yn)
    dgp_out[...] = dgp_all[...] + dgp_y[...]
    second.wait_send()
    act_store(6).wait()
    act_store(7).wait()
    for i in range(1, 8):
        dgp_send(i).wait_send()
    rows_x.finish()
    for each in sums:
        each.finish()


def run_experts(expert_in, og, ids, router, gate, up, down):
    count, rows, width = expert_in.shape
    seq = rows * 8
    experts, per, _ = gate.shape
    hidden = experts * per
    tokens = count * rows
    lanes = router.shape[0]
    vm = pltpu.VMEM
    dma = pltpu.SemaphoreType.DMA
    hbm = pl.BlockSpec(memory_space=pl.ANY)
    near = pl.BlockSpec(memory_space=pltpu.VMEM)
    shape = jax.ShapeDtypeStruct
    total = Sum.scratch(count, rows, width, LOW, rows // 2)
    return pl.pallas_call(
        functools.partial(experts_kernel, experts),
        out_shape=(
            shape((count, seq, width), LOW),
            shape((3, count, seq, hidden), LOW),
            shape((count, rows, width), LOW),
            shape((count, rows, width // 4), LOW),
            shape((lanes, tokens), F32),
            shape((8, 8, tokens), F32),
        ),
        in_specs=[hbm, hbm, near, near, hbm, hbm, hbm],
        out_specs=[hbm, hbm, hbm, hbm, near, near],
        scratch_shapes=[
            vm((2, count, rows, width), LOW),
            vm((hidden, width), LOW),
            vm((hidden, width), LOW),
            vm((hidden, width), LOW),
            vm((2, count, rows, width), LOW),
            vm((8, tokens, hidden), LOW),
            vm((2, 3, count, rows, hidden), LOW),
            vm((count, seq, width), LOW),
            vm((count, seq, width), LOW),
            vm((2, hidden // 256 * tokens, 256), F32),
            vm((tokens, hidden), F32),
            vm((8, 8, tokens), F32),
            vm((8, 8, tokens), F32),
            vm((8, 8, tokens), F32),
            vm((8, 8, tokens), F32),
            vm((8, 8, tokens), F32),
            dma((3,)),
            dma((2,)),
            dma((2,)),
            dma((2,)),
            dma((8,)),
            dma((8,)),
            dma((2,)),
            dma((2,)),
        ]
        + Gather.scratch()
        + total
        + total,
        compiler_params=pltpu.CompilerParams(
            collective_id=6, has_side_effects=True, vmem_limit_bytes=VMEM_LIMIT
        ),
        name="experts",
    )(expert_in, og, ids, router, gate.reshape(hidden, width), up.reshape(hidden, width), down.reshape(hidden, width))


def expert_grads_kernel(act, x, og, *refs):
    kept = (len(refs) - 3) // 2
    tokens = act.shape[1] * act.shape[2]
    x_cols = x[...].reshape(tokens, x.shape[2])
    og_cols = og[...].reshape(tokens, og.shape[2])
    for n, right in enumerate((x_cols, x_cols, og_cols)):
        refs[kept + n][...] = dot_tn(act[n].reshape(tokens, act.shape[3]), right)
    for src, dst in zip(refs[:kept], refs[kept + 3 :]):
        dst[...] = src[...]


def expert_grads(act, x, og, *others):
    _, count, seq, hidden = act.shape
    width = x.shape[2]
    block = min(512, width)
    steps = width // block
    cols = pl.BlockSpec((count, seq, block), lambda i: (0, 0, i))
    out = pl.BlockSpec((hidden, block), lambda i: (0, i))

    def pieces(value):
        shape = value.shape[:-2] + (value.shape[-2] // steps, value.shape[-1])
        zeros = (0,) * (len(shape) - 2)
        return pl.BlockSpec(shape, lambda i: zeros + (i, 0))

    grads = jax.ShapeDtypeStruct((hidden, width), F32)
    kept = [pieces(value) for value in others]
    return pl.pallas_call(
        expert_grads_kernel,
        grid=(steps,),
        in_specs=[
            pl.BlockSpec(act.shape, lambda i: (0, 0, 0, 0), pipeline_mode=pl.Buffered(1)),
            cols,
            cols,
        ]
        + kept,
        out_specs=[out, out, out] + kept,
        out_shape=[grads] * 3 + [jax.ShapeDtypeStruct(value.shape, value.dtype) for value in others],
        compiler_params=pltpu.CompilerParams(vmem_limit_bytes=VMEM_LIMIT),
        name="expert_grads",
    )(act, x, og, *others)


PEERS = tuple((d, e) for d in (2, 1, 3, 0) for e in (1, 0) if d or e)


def end_kernel(heads, xn_in, w_in, wo_in, pre_in, qkv_in, prob_in, ctx_in, tokens_in, out_in,
               resid, cot, dx_sum, expert_in, probs, dgp, router, eg_ref, ag_ref, query, key, value,
               cos_ref, sin_ref, qg_ref, kg_ref,
               layer_out, input_out, dq_out, dk_out, dv_out, do_out, aux_out, gains_out,
               tokens, out_full, d_res, low_rows, layer, aux, db, xn, w, wo, pre, qkv, prob, ctx, dctx, dq_s, dk_s, dv_s, dqkv, dwo, dw, dwo_got, dwq_got, kv_x, kv_z,
               aux_got, head_part, head_got, line, line_c, line_y, wide_q, wide_o, wide_kv,
               lsem, psem, rsem, vsem, wsem, kxs, kxr, kzs, kzr, tsem, usem, osem, *rest):
    here = Here()
    here.say()
    sends, outs = [], []
    rows_db = Gather(here, False, low_rows, db, rest[: Gather.slots], BY_X)
    at = Gather.slots
    dn = Sum(here, False, db, rest[at:], BY_X)
    rows = dn.rows
    piece, part = query.shape[0], wo.shape[1]
    seq = xn.shape[1]
    hd = cos_ref.shape[1]
    tile = 256
    scale = 1.0 / math.sqrt(hd)

    def number(d, e):
        return 2 * here.zr(d) + (here.x + e) % 2

    def send(n, d, e, src, got):
        sends.append(push(src, got.at[(4 - d) % 4, e], psem.at[n, d, e], rsem.at[n, (4 - d) % 4, e], here.peer(d, e)))

    def got_from(n, d, e, got):
        wait_for(got.at[d, e], rsem.at[n, d, e], here.xn)
        return got[d, e]

    loads = {}
    for n, (src, dst) in enumerate(((wo_in, wo), (ctx_in, ctx), (qkv_in, qkv), (prob_in, prob), (pre_in, pre),
                                    (xn_in, xn), (w_in, w), (tokens_in, tokens), (out_in, out_full.at[here.t]))):
        loads[n] = keep(src, dst, lsem.at[n])
    count, lanes, width = resid.shape[0], probs.shape[0], resid.shape[2]
    experts = lanes // 8
    step = 32
    steps = rows // step

    def chunk_of(i):
        return i // steps, pl.ds(pl.multiple_of(i % steps * step, step), step)

    def unit_back(up, gain, hat, factor):
        gained = up * gain
        return factor * (gained - hat * jnp.mean(gained * hat, axis=-1, keepdims=True))

    d_probs = jnp.concatenate([dgp[k, :experts, :] for k in range(8)], axis=0)
    mixed = probs[...] * d_probs
    d_logits = (mixed - probs[...] * jnp.sum(mixed, axis=0, keepdims=True)).astype(LOW)
    for n in range(count):
        d_res[n] = dot_tn(d_logits[:, n * rows : (n + 1) * rows], router[...])

    def back(i, gain_part):
        n, r = chunk_of(i)
        hat, factor = unit(resid[n, r, :])
        d_in = d_res[n, r, :] + dx_sum[n, r, :].astype(F32)
        total = cot[n, r, :].astype(F32) + unit_back(d_in, eg_ref[...], hat, factor)
        d_res[n, r, :] = total
        low_rows[n, r, :] = total.astype(LOW)
        return gain_part + jnp.sum(d_in * hat, axis=0, keepdims=True)

    gain_part = lax.fori_loop(0, count * steps, back, jnp.zeros((1, width), F32))
    here.hear()
    rows_db.start()
    router_part = dot_nn(d_logits, expert_in[...].reshape(count * rows, width)).astype(LOW)
    first_row = lax.broadcasted_iota(jnp.int32, (16, piece), 0) == 0
    for k in range(8):
        cols = slice(k * piece, (k + 1) * piece)
        aux[k, pl.ds(0, lanes), :] = router_part[:, cols]
        aux[k, pl.ds(lanes, 16), :] = jnp.where(first_row, gain_part[:, cols], 0.0).astype(LOW)
    for d, e in PEERS:
        send(0, d, e, aux.at[number(d, e)], aux_got)
    rows_db.first_steps()
    loads[8].wait()
    mine = out_full.at[here.t]
    sends.append(push(mine, mine, vsem.at[0], wsem.at[0], here.yn))
    sends.append(push(mine, mine, vsem.at[1], wsem.at[1], here.cn))
    rows_db.last_steps()
    for d in (0,) + ORDER:
        rows_db.arrived(d, 0)
        rows_db.arrived(d, 1)
    across = out_full.at[2 * (1 - here.y) + here.c]
    wait_for(across, wsem.at[0], here.xn)
    sends.append(push(across, across, vsem.at[2], wsem.at[2], here.cn))
    for n in range(8):
        loads[n].wait()

    for i in range(seq // tile):
        r = pl.ds(i * tile, tile)
        dctx[r, :] = dot_nn(db[0, r, :], wo[...]).astype(LOW)
    for d, e in PEERS + ((0, 0),):
        r = span(number(d, e) * piece, piece)
        dwo[r, :] = dot_tn(db[0, :, r], ctx[...]).astype(LOW)
        if d or e:
            send(1, d, e, dwo.at[r, :], dwo_got)
    wait_for(out_full.at[2 * here.y + 1 - here.c], wsem.at[1], here.xn)
    wait_for(out_full.at[2 * (1 - here.y) + 1 - here.c], wsem.at[2], here.xn)

    @pl.loop(0, count * steps)
    def _(i):
        n, r = chunk_of(i)
        routed = jnp.concatenate([out_full[q, n, r, :] for q in range(4)], axis=1).astype(F32)
        layer[n, r, :] = (resid[n, r, :] + routed).astype(LOW)

    outs.append(keep(layer, layer_out, osem.at[4]))
    dk_s[...] = jnp.zeros_like(dk_s)
    dv_s[...] = jnp.zeros_like(dv_s)
    for a in range(heads):
        for i in range(seq // tile):
            r = pl.ds(i * tile, tile)
            n = (i + 1) * tile
            q_tile = qkv[r, pl.ds(a * hd, hd)]
            k_rows = qkv[pl.ds(0, n), pl.ds(heads * hd, hd)]
            v_rows = qkv[pl.ds(0, n), pl.ds((heads + 1) * hd, hd)]
            up = dctx[r, pl.ds(a * hd, hd)]
            low = prob[a, r, pl.ds(0, n)]
            wide = low.astype(F32)
            dprob = dot_nt(up, v_rows)
            delta = jnp.sum(wide * dprob, axis=-1, keepdims=True)
            dscore = (wide * (dprob - delta)).astype(LOW)
            dq_s[r, pl.ds(a * hd, hd)] = dot_nn(dscore, k_rows) * scale
            dk_s[pl.ds(0, n), :] += dot_tn(dscore, q_tile) * scale
            dv_s[pl.ds(0, n), :] += dot_tn(low, up)
    gq = jnp.zeros((1, hd), F32)
    gk = jnp.zeros((1, hd), F32)
    for i in range(seq // tile):
        r = pl.ds(i * tile, tile)
        dqkv[r, pl.ds((heads + 1) * hd, hd)] = dv_s[r, :].astype(LOW)
        for a in range(heads + 1):
            up = dq_s[r, pl.ds(a * hd, hd)] if a < heads else dk_s[r, :]
            one = pre[r, pl.ds(a * hd, hd)]
            factor = lax.rsqrt(jnp.mean(one * one, axis=-1, keepdims=True) + norm_eps)
            hat = one * factor
            turned = up * cos_ref[r, :] + pltpu.roll(up * sin_ref[r, :], hd // 2, 1)
            gain_part = jnp.sum(turned * hat, axis=0, keepdims=True)
            gained = turned * (qg_ref if a < heads else kg_ref)[...]
            back = factor * (gained - hat * jnp.mean(gained * hat, axis=-1, keepdims=True))
            dqkv[r, pl.ds(a * hd, hd)] = back.astype(LOW)
            if a < heads:
                gq = gq + gain_part
            else:
                gk = gk + gain_part
    head_part[...] = jnp.concatenate([gq, gk, jnp.zeros((6, hd), F32)], axis=0)
    for d, e in PEERS:
        send(3, d, e, head_part, head_got)
    rows_db.finish()
    for e in (1, 0):
        for d in FAR_FIRST:
            r = span(here.number(d, e) * rows, rows)
            db[0, r, :] = dot_nt(dqkv[r, :], w[...]).astype(LOW)
            dn.give(d, e)
    for d, e in PEERS + ((0, 0),):
        r = span(number(d, e) * piece, piece)
        dw[r, :] = dot_tn(xn[0, :, r], dqkv[...]).astype(LOW)
        if d in (1, 2):
            send(2, d, e, dw.at[r, pl.ds(0, part)], dwq_got)
        if e:
            sends.append(push(dw.at[r, pl.ds(part, 2 * hd)], kv_x.at[d], kxs.at[d], kxr.at[d], here.xn))
    for d in FAR_FIRST:
        dn.corner(d)
    for d in (2, 1, 3, 0):
        r = span(number(d, 0) * piece, piece)
        wait_for(kv_x.at[d], kxr.at[d], here.xn)
        both = dw[r, pl.ds(part, 2 * hd)].astype(F32) + kv_x[d].astype(F32)
        dw[r, pl.ds(part, 2 * hd)] = both.astype(LOW)
        if d:
            there = (4 - d) % 4
            sends.append(push(dw.at[r, pl.ds(part, 2 * hd)], kv_z.at[there], kzs.at[d], kzr.at[there], here.peer(d, 0)))
    for d in FAR_FIRST:
        dn.sides(d)
    for d in FAR_FIRST:
        dn.centre(d)
    for d, e in PEERS:
        if d in (0, 3):
            send(2, d, e, dw.at[span(number(d, e) * piece, piece), pl.ds(0, part)], dwq_got)

    def merged(n, wide, got, mine):
        for d in (0, 1):
            for e in (0, 1):
                first = mine if (d, e) == (0, 0) else got_from(n, d, e, got)
                both = first.astype(F32) + got_from(n, d + 2, e, got).astype(F32)
                wide[:, span((number(d, e) % 4) * part, part)] = both

    own = span(here.f * piece, piece)
    merged(1, wide_o, dwo_got, dwo[own, :])
    outs.append(keep(wide_o, do_out, osem.at[0]))
    aux_total = aux[here.f].astype(F32)
    for d, e in PEERS:
        aux_total = aux_total + got_from(0, d, e, aux_got).astype(F32)
    aux_out[...] = aux_total
    head_total = head_part[...]
    for d, e in PEERS:
        head_total = head_total + got_from(3, d, e, head_got)
    line[:, pl.ds(piece, hd)] = head_total
    dn.total()
    dn.share_start()
    dn.share_cross()
    dn.share_end(None)

    @pl.loop(0, count * steps)
    def _(i):
        n, r = chunk_of(i)
        hat, factor = unit(tokens[n, r, :].astype(F32))
        up = jnp.concatenate([dn.full[q, n, r, :] for q in range(4)], axis=1).astype(F32)
        low_rows[n, r, :] = (d_res[n, r, :] + unit_back(up, ag_ref[...], hat, factor)).astype(LOW)

    outs.append(keep(low_rows, input_out, osem.at[5]))
    merged(2, wide_q, dwq_got, dw[own, pl.ds(0, part)])
    outs.append(keep(wide_q, dq_out, osem.at[1]))
    kv = dw[own, pl.ds(part, 2 * hd)].astype(F32)
    for d in (1, 2, 3):
        wait_for(kv_z.at[d], kzr.at[d], here.xn)
        kv = kv + kv_z[d].astype(F32)
    wide_kv[...] = kv
    outs.append(keep(wide_kv.at[:, pl.ds(0, hd)], dk_out, osem.at[2]))
    outs.append(keep(wide_kv.at[:, pl.ds(hd, hd)], dv_out, osem.at[3]))

    def row_sums(product):
        high = product.astype(LOW)
        rest_ = (product - high.astype(F32)).astype(LOW)
        ones = jnp.ones((8, product.shape[1]), LOW)
        return dot_nt(ones, high) + dot_nt(ones, rest_)

    line[:, pl.ds(0, piece)] = (
        row_sums(query[...].astype(F32) * wide_q[...])
        + row_sums(key[...].astype(F32) * kv[:, :hd])
        + row_sums(value[...].astype(F32) * kv[:, hd:])
    )
    first = push(line, line_c, tsem.at[0], usem.at[0], here.cn)
    wait_for(line_c, usem.at[0], here.cn)
    first.wait_send()
    line[...] = line[...] + line_c[...]
    second = push(line, line_y, tsem.at[1], usem.at[1], here.yn)
    wait_for(line_y, usem.at[1], here.yn)
    gains_out[...] = line[...] + line_y[...]
    second.wait_send()
    dn.finish()
    for copy in sends:
        copy.wait_send()
    for copy in outs:
        copy.wait()


def end(xn, w, wo, pre, qkv, prob, ctx, tokens, out_sum, resid, cot, dx_sum, expert_in, probs, dgp, router,
        expert_gain, attention_gain, query, key, value, cosine, sine, query_gain, key_gain):
    count, rows, width = tokens.shape
    seq = rows * 8
    lanes = probs.shape[0]
    hd = query_gain.shape[0]
    piece, local = query.shape
    part = local // 4
    heads = part // hd
    vm = pltpu.VMEM
    dma = pltpu.SemaphoreType.DMA
    hbm = pl.BlockSpec(memory_space=pl.ANY)
    near = pl.BlockSpec(memory_space=pltpu.VMEM)
    shape = jax.ShapeDtypeStruct
    return pl.pallas_call(
        functools.partial(end_kernel, heads),
        out_shape=(
            shape((count, rows, width), LOW),
            shape((count, rows, width), LOW),
            shape((piece, local), F32),
            shape((piece, hd), F32),
            shape((piece, hd), F32),
            shape((piece, local), F32),
            shape((lanes + 16, piece), F32),
            shape((8, piece + hd), F32),
        ),
        in_specs=[hbm] * 9 + [near] * 16,
        out_specs=[hbm] * 6 + [near] * 2,
        scratch_shapes=[
            vm((count, rows, width), LOW),
            vm((4, count, rows, width // 4), LOW),
            vm((count, rows, width), F32),
            vm((count, rows, width), LOW),
            vm((count, rows, width), LOW),
            vm((8, lanes + 16, piece), LOW),
            vm((1, seq, width), LOW),
            vm((1, seq, width), LOW),
            vm(w.shape, LOW),
            vm(wo.shape, LOW),
            vm(pre.shape, F32),
            vm(qkv.shape, LOW),
            vm(prob.shape, LOW),
            vm(ctx.shape, LOW),
            vm(ctx.shape, LOW),
            vm((seq, heads * hd), F32),
            vm((seq, hd), F32),
            vm((seq, hd), F32),
            vm((seq, (heads + 2) * hd), LOW),
            vm((width, part), LOW),
            vm((width, part + 2 * hd), LOW),
            vm((4, 2, piece, part), LOW),
            vm((4, 2, piece, part), LOW),
            vm((4, piece, 2 * hd), LOW),
            vm((4, piece, 2 * hd), LOW),
            vm((4, 2, lanes + 16, piece), LOW),
            vm((8, hd), F32),
            vm((4, 2, 8, hd), F32),
            vm((8, piece + hd), F32),
            vm((8, piece + hd), F32),
            vm((8, piece + hd), F32),
            vm((piece, local), F32),
            vm((piece, local), F32),
            vm((piece, 2 * hd), F32),
            dma((9,)),
            dma((4, 4, 2)),
            dma((4, 4, 2)),
            dma((3,)),
            dma((3,)),
            dma((4,)),
            dma((4,)),
            dma((4,)),
            dma((4,)),
            dma((2,)),
            dma((2,)),
            dma((6,)),
        ]
        + Gather.scratch()
        + Sum.scratch(1, rows, width, LOW, BY_X),
        compiler_params=pltpu.CompilerParams(
            collective_id=5, has_side_effects=True, vmem_limit_bytes=VMEM_LIMIT
        ),
        name="end",
    )(xn, w, wo, pre, qkv, prob, ctx, tokens, out_sum, resid, cot, dx_sum, expert_in, probs, dgp, router,
      expert_gain[None], attention_gain[None], query, key, value, cosine, sine, query_gain[None], key_gain[None])


def rotate_half(values):
    middle = values.shape[-1] // 2
    return jnp.concatenate([-values[..., middle:], values[..., :middle]], axis=-1)


def rope_tables(positions, head_width):
    middle = head_width // 2
    frequency = rope_base ** (-jnp.arange(middle, dtype=jnp.float32) * 2.0 / head_width)
    angles = positions.astype(jnp.float32)[:, None] * frequency[None, :]
    angles = jnp.concatenate([angles, angles], axis=1)
    return (jnp.cos(angles), jnp.sin(angles))


def norm_parts(values):
    factor = lax.rsqrt(jnp.mean(values * values, axis=-1, keepdims=True) + norm_eps)
    return (values * factor, factor)


def norm_back(upstream, gain, normal, factor):
    scaled = upstream * gain
    return factor * (scaled - normal * jnp.mean(scaled * normal, axis=-1, keepdims=True))


def head_back(upstream, cosine_heads, sine_heads, gain, normal, factor):
    turned = upstream * cosine_heads - rotate_half(upstream * sine_heads)
    gain_part = jnp.sum(turned * normal, axis=(0, 1))
    return (norm_back(turned, gain, normal, factor), gain_part)


def fetch_weights(query_weight, key_weight, value_weight, output_weight, router_weight):
    return (
        lax.all_gather(query_weight, "fsdp", axis=0, tiled=True),
        lax.all_gather(key_weight, "fsdp", axis=0, tiled=True),
        lax.all_gather(value_weight, "fsdp", axis=0, tiled=True),
        lax.all_gather(output_weight, "fsdp", axis=0, tiled=True),
        lax.all_gather(router_weight, "fsdp", axis=0, tiled=True),
    )


def widen(summed):
    return lax.all_gather(summed, "tp", axis=3, tiled=True)


def carry_back(summed):
    return lax.all_to_all(summed, "fsdp", split_axis=0, concat_axis=0, tiled=True)


def send_home(summed):
    arrived_home = carry_back(widen(summed))
    return arrived_home


def general_device(
    tokens,
    cotangent,
    expert_ids,
    attention_gain,
    query_gain,
    key_gain,
    query_weight,
    key_weight,
    value_weight,
    output_weight,
    expert_gain,
    router_weight,
    gate_weight,
    up_weight,
    down_weight,
):
    micro_count = tokens.shape[0]
    tok_rows = tokens.shape[1]
    width = tokens.shape[2]
    route_count = expert_ids.shape[2]
    head_dim = query_gain.shape[0]
    local_heads = query_weight.shape[1] // head_dim
    local_groups = key_weight.shape[1] // head_dim
    group_size = local_heads // local_groups
    fsdp_count = lax.axis_size("fsdp")
    seq_len = tok_rows * fsdp_count
    experts_here = gate_weight.shape[0]
    expert_count = experts_here * fsdp_count
    capacity = max(2, 5 * tok_rows * route_count // (4 * expert_count))
    key_block = math.gcd(seq_len, 512)
    score_scale = 1.0 / math.sqrt(head_dim)
    query_count = tok_rows * group_size
    routed_total = tok_rows * route_count
    start_row = lax.axis_index("fsdp") * tok_rows
    positions = start_row + jnp.arange(tok_rows, dtype=jnp.int32)
    cosine_table, sine_table = rope_tables(positions, head_dim)
    cosine_heads = cosine_table[:, None, :]
    sine_heads = sine_table[:, None, :]
    query_pos = start_row + jnp.arange(query_count, dtype=jnp.int32) // group_size
    block_total = (start_row + tok_rows + key_block - 1) // key_block
    expert_range = jnp.arange(expert_count, dtype=jnp.int32)
    zero_row = jnp.zeros((1, width), jnp.bfloat16)

    def to_rows(tensor):
        return (
            tensor.reshape(tok_rows, local_groups, group_size, head_dim)
            .transpose(1, 0, 2, 3)
            .reshape(local_groups, query_count, head_dim)
        )

    def from_rows(tensor):
        return (
            tensor.reshape(local_groups, tok_rows, group_size, head_dim)
            .transpose(1, 0, 2, 3)
            .reshape(tok_rows, local_heads, head_dim)
        )

    acc_attention_gain = jnp.zeros((width,), jnp.float32)
    acc_head_gains = jnp.zeros((2, head_dim), jnp.float32)
    acc_query = jnp.zeros((width, local_heads * head_dim), jnp.float32)
    acc_key = jnp.zeros((width, local_groups * head_dim), jnp.float32)
    acc_value = jnp.zeros((width, local_groups * head_dim), jnp.float32)
    acc_output = jnp.zeros((width, local_heads * head_dim), jnp.float32)
    acc_expert_gain = jnp.zeros((width,), jnp.float32)
    acc_router = jnp.zeros((width, expert_count), jnp.float32)
    acc_gate = jnp.zeros(gate_weight.shape, jnp.float32)
    acc_up = jnp.zeros(up_weight.shape, jnp.float32)
    acc_down = jnp.zeros(down_weight.shape, jnp.float32)
    layer_rows = []
    input_rows = []
    for micro_index in range(micro_count):
        inputs = tokens[micro_index].astype(jnp.float32)
        query_full, key_full, value_full, output_full, router_full = fetch_weights(
            query_weight, key_weight, value_weight, output_weight, router_weight
        )
        input_hat, attention_factor = norm_parts(inputs)
        normed = (input_hat * attention_gain).astype(jnp.bfloat16)
        query_pre = jnp.dot(normed, query_full, preferred_element_type=jnp.float32).reshape(
            tok_rows, local_heads, head_dim
        )
        key_pre = jnp.dot(normed, key_full, preferred_element_type=jnp.float32).reshape(
            tok_rows, local_groups, head_dim
        )
        value_low = jnp.dot(normed, value_full, preferred_element_type=jnp.float32).astype(
            jnp.bfloat16
        )
        query_hat, query_factor = norm_parts(query_pre)
        key_hat, key_factor = norm_parts(key_pre)
        query_scaled = query_hat * query_gain
        key_scaled = key_hat * key_gain
        query_low = (query_scaled * cosine_heads + rotate_half(query_scaled) * sine_heads).astype(
            jnp.bfloat16
        )
        key_low = (key_scaled * cosine_heads + rotate_half(key_scaled) * sine_heads).astype(
            jnp.bfloat16
        )
        key_all, value_all = (
            lax.all_gather(
                key_low.reshape(tok_rows, local_groups * head_dim), "fsdp", axis=0, tiled=True
            ),
            lax.all_gather(value_low, "fsdp", axis=0, tiled=True),
        )
        key_heads = key_all.reshape(seq_len, local_groups, head_dim).transpose(1, 0, 2)
        value_heads = value_all.reshape(seq_len, local_groups, head_dim).transpose(1, 0, 2)
        query_rows = to_rows(query_low)

        def scores_at(block_index):
            block_start = block_index * key_block
            key_slice = lax.dynamic_slice_in_dim(key_heads, block_start, key_block, 1)
            raw_scores = (
                jnp.einsum(
                    "gqd,gkd->gqk", query_rows, key_slice, preferred_element_type=jnp.float32
                )
                * score_scale
            )
            allowed = (block_start + jnp.arange(key_block, dtype=jnp.int32))[None, :] <= query_pos[
                :, None
            ]
            return (jnp.where(allowed[None], raw_scores, masked_score), allowed, block_start)

        def stats_step(block_index, carried):
            run_peak, run_total = carried
            scores, allowed, block_start = scores_at(block_index)
            new_peak = jnp.maximum(run_peak, jnp.max(scores, axis=-1))
            terms = jnp.where(allowed[None], jnp.exp(scores - new_peak[..., None]), 0.0)
            return (new_peak, run_total * jnp.exp(run_peak - new_peak) + jnp.sum(terms, axis=-1))

        start_stats = (
            jnp.full((local_groups, query_count), masked_score, jnp.float32),
            jnp.zeros((local_groups, query_count), jnp.float32),
        )
        run_peak, run_total = lax.fori_loop(0, block_total, stats_step, start_stats)
        log_total = run_peak + jnp.log(run_total)

        def value_step(block_index, acc_context):
            scores, allowed, block_start = scores_at(block_index)
            probs_low = jnp.where(
                allowed[None], jnp.exp(scores - log_total[..., None]), 0.0
            ).astype(jnp.bfloat16)
            value_slice = lax.dynamic_slice_in_dim(value_heads, block_start, key_block, 1)
            return acc_context + jnp.einsum(
                "gqk,gkd->gqd", probs_low, value_slice, preferred_element_type=jnp.float32
            )

        context_rows = lax.fori_loop(
            0,
            block_total,
            value_step,
            jnp.zeros((local_groups, query_count, head_dim), jnp.float32),
        )
        context_low = (
            from_rows(context_rows).reshape(tok_rows, local_heads * head_dim).astype(jnp.bfloat16)
        )
        branch_part = jnp.einsum(
            "th,dh->td", context_low, output_full, preferred_element_type=jnp.float32
        )
        resid = inputs + lax.psum(branch_part.astype(jnp.bfloat16), "tp").astype(jnp.float32)
        resid_hat, expert_factor = norm_parts(resid)
        expert_in = (resid_hat * expert_gain).astype(jnp.bfloat16)
        logits = jnp.dot(expert_in, router_full, preferred_element_type=jnp.float32)
        routes_now = expert_ids[micro_index]
        choose = (routes_now[:, :, None] == expert_range[None, None, :]).astype(jnp.float32)
        picked = jnp.sum(choose * logits[:, None, :], axis=-1)
        shifted = jnp.exp(picked - jnp.max(picked, axis=-1, keepdims=True))
        gate_probs = shifted / jnp.sum(shifted, axis=-1, keepdims=True)
        flat_routes = routes_now.reshape(-1)
        onehot = (flat_routes[:, None] == expert_range[None, :]).astype(jnp.int32)
        rank_in = jnp.sum((jnp.cumsum(onehot, axis=0) - onehot) * onehot, axis=1)
        slot_index = flat_routes * capacity + rank_in
        slot_source = (
            jnp.full((expert_count * capacity,), routed_total, jnp.int32)
            .at[slot_index]
            .set(jnp.arange(routed_total, dtype=jnp.int32))
        )
        padded_in = jnp.concatenate([expert_in, zero_row], axis=0)
        outgoing = padded_in[slot_source // route_count].reshape(
            fsdp_count, experts_here, capacity, width
        )
        arrived = lax.all_to_all(outgoing, "fsdp", split_axis=0, concat_axis=0, tiled=True)
        gate_pre = jnp.einsum(
            "secd,efd->secf", arrived, gate_weight, preferred_element_type=jnp.float32
        )
        up_pre = jnp.einsum(
            "secd,efd->secf", arrived, up_weight, preferred_element_type=jnp.float32
        )
        gate_sigmoid = jax.nn.sigmoid(gate_pre)
        inner_low = (gate_pre * gate_sigmoid * up_pre).astype(jnp.bfloat16)
        result_part = jnp.einsum(
            "secf,efd->secd", inner_low, down_weight, preferred_element_type=jnp.float32
        )
        result_low = lax.psum_scatter(
            result_part.astype(jnp.bfloat16), "tp", scatter_dimension=3, tiled=True
        )
        result_home = send_home(result_low)
        routed = (
            result_home.reshape(expert_count * capacity, width)[slot_index]
            .astype(jnp.float32)
            .reshape(tok_rows, route_count, width)
        )
        layer_rows.append(
            (resid + jnp.sum(gate_probs[:, :, None] * routed, axis=1)).astype(jnp.bfloat16)
        )
        query_full, key_full, value_full, output_full, router_full = fetch_weights(
            query_weight, key_weight, value_weight, output_weight, router_weight
        )
        out_grad = cotangent[micro_index].astype(jnp.float32)
        d_route = (
            (gate_probs[:, :, None] * out_grad[:, None, :])
            .astype(jnp.bfloat16)
            .reshape(routed_total, width)
        )
        d_gate_probs = jnp.sum(out_grad[:, None, :] * routed, axis=-1)
        d_pick = gate_probs * (
            d_gate_probs - jnp.sum(gate_probs * d_gate_probs, axis=-1, keepdims=True)
        )
        d_logits = jnp.sum(choose * d_pick[:, :, None], axis=1).astype(jnp.bfloat16)
        grad_outgoing = jnp.concatenate([d_route, zero_row], axis=0)[slot_source].reshape(
            fsdp_count, experts_here, capacity, width
        )
        grad_arrived = lax.all_to_all(
            grad_outgoing, "fsdp", split_axis=0, concat_axis=0, tiled=True
        )
        d_inner = jnp.einsum(
            "secd,efd->secf", grad_arrived, down_weight, preferred_element_type=jnp.float32
        )
        acc_down = acc_down + jnp.einsum(
            "secf,secd->efd", inner_low, grad_arrived, preferred_element_type=jnp.float32
        )
        d_gate_low = (
            d_inner * up_pre * gate_sigmoid * (1.0 + gate_pre * (1.0 - gate_sigmoid))
        ).astype(jnp.bfloat16)
        d_up_low = (d_inner * gate_pre * gate_sigmoid).astype(jnp.bfloat16)
        acc_gate = acc_gate + jnp.einsum(
            "secf,secd->efd", d_gate_low, arrived, preferred_element_type=jnp.float32
        )
        acc_up = acc_up + jnp.einsum(
            "secf,secd->efd", d_up_low, arrived, preferred_element_type=jnp.float32
        )
        d_copy_part = jnp.einsum(
            "secf,efd->secd", d_gate_low, gate_weight, preferred_element_type=jnp.float32
        ) + jnp.einsum("secf,efd->secd", d_up_low, up_weight, preferred_element_type=jnp.float32)
        d_copy_low = lax.psum_scatter(
            d_copy_part.astype(jnp.bfloat16), "tp", scatter_dimension=3, tiled=True
        )
        d_copy_home = send_home(d_copy_low)
        d_copies = (
            d_copy_home.reshape(expert_count * capacity, width)[slot_index]
            .astype(jnp.float32)
            .reshape(tok_rows, route_count, width)
        )
        d_expert_in = jnp.sum(d_copies, axis=1) + jnp.dot(
            d_logits, router_full.T, preferred_element_type=jnp.float32
        )
        acc_router = acc_router + jnp.dot(expert_in.T, d_logits, preferred_element_type=jnp.float32)
        acc_expert_gain = acc_expert_gain + jnp.sum(d_expert_in * resid_hat, axis=0)
        d_resid = out_grad + norm_back(d_expert_in, expert_gain, resid_hat, expert_factor)
        d_branch = d_resid.astype(jnp.bfloat16)
        acc_output = acc_output + jnp.einsum(
            "td,th->dh", d_branch, context_low, preferred_element_type=jnp.float32
        )
        d_context = jnp.dot(d_branch, output_full, preferred_element_type=jnp.float32).astype(
            jnp.bfloat16
        )
        d_context_rows = to_rows(d_context.reshape(tok_rows, local_heads, head_dim))
        delta_rows = jnp.sum(d_context_rows.astype(jnp.float32) * context_rows, axis=-1)

        def grad_step(block_index, carried):
            d_query_rows, key_grads_all = carried
            scores, allowed, block_start = scores_at(block_index)
            probs = jnp.where(allowed[None], jnp.exp(scores - log_total[..., None]), 0.0)
            key_slice = lax.dynamic_slice_in_dim(key_heads, block_start, key_block, 1)
            value_slice = lax.dynamic_slice_in_dim(value_heads, block_start, key_block, 1)
            d_probs = jnp.einsum(
                "gqd,gkd->gqk", d_context_rows, value_slice, preferred_element_type=jnp.float32
            )
            d_scores = (probs * (d_probs - delta_rows[..., None])).astype(jnp.bfloat16)
            d_query_rows = (
                d_query_rows
                + jnp.einsum(
                    "gqk,gkd->gqd", d_scores, key_slice, preferred_element_type=jnp.float32
                )
                * score_scale
            )
            d_key_block = (
                jnp.einsum("gqk,gqd->kgd", d_scores, query_rows, preferred_element_type=jnp.float32)
                * score_scale
            )
            d_value_block = jnp.einsum(
                "gqk,gqd->kgd",
                probs.astype(jnp.bfloat16),
                d_context_rows,
                preferred_element_type=jnp.float32,
            )
            current = lax.dynamic_slice_in_dim(key_grads_all, block_start, key_block, 0)
            updated = current + jnp.concatenate([d_key_block, d_value_block], axis=-1)
            return (
                d_query_rows,
                lax.dynamic_update_slice_in_dim(key_grads_all, updated, block_start, 0),
            )

        start_grads = (
            jnp.zeros((local_groups, query_count, head_dim), jnp.float32),
            jnp.zeros((seq_len, local_groups, 2 * head_dim), jnp.float32),
        )
        d_query_rows, key_grads_all = lax.fori_loop(0, block_total, grad_step, start_grads)
        key_grads = (
            lax.psum_scatter(
                key_grads_all.reshape(seq_len, local_groups * 2 * head_dim).astype(jnp.bfloat16),
                "fsdp",
                scatter_dimension=0,
                tiled=True,
            )
            .astype(jnp.float32)
            .reshape(tok_rows, local_groups, 2 * head_dim)
        )
        d_value_low = (
            key_grads[..., head_dim:]
            .reshape(tok_rows, local_groups * head_dim)
            .astype(jnp.bfloat16)
        )
        d_key_pre, key_gain_part = head_back(
            key_grads[..., :head_dim], cosine_heads, sine_heads, key_gain, key_hat, key_factor
        )
        d_query_pre, query_gain_part = head_back(
            from_rows(d_query_rows), cosine_heads, sine_heads, query_gain, query_hat, query_factor
        )
        d_query_low = d_query_pre.astype(jnp.bfloat16).reshape(tok_rows, local_heads * head_dim)
        d_key_low = d_key_pre.astype(jnp.bfloat16).reshape(tok_rows, local_groups * head_dim)
        d_normed_part = jnp.dot(d_query_low, query_full.T, preferred_element_type=jnp.float32)
        d_normed_part = d_normed_part + jnp.dot(
            d_key_low, key_full.T, preferred_element_type=jnp.float32
        )
        d_normed_part = d_normed_part + jnp.dot(
            d_value_low, value_full.T, preferred_element_type=jnp.float32
        )
        acc_query = acc_query + jnp.dot(normed.T, d_query_low, preferred_element_type=jnp.float32)
        acc_key = acc_key + jnp.dot(normed.T, d_key_low, preferred_element_type=jnp.float32)
        acc_value = acc_value + jnp.dot(normed.T, d_value_low, preferred_element_type=jnp.float32)
        d_normed, head_gain_parts = (
            lax.psum(d_normed_part.astype(jnp.bfloat16), "tp").astype(jnp.float32),
            lax.psum(jnp.stack([query_gain_part, key_gain_part]).astype(jnp.bfloat16), "tp").astype(
                jnp.float32
            ),
        )
        acc_head_gains = acc_head_gains + head_gain_parts
        acc_attention_gain = acc_attention_gain + jnp.sum(d_normed * input_hat, axis=0)
        input_rows.append(
            (d_resid + norm_back(d_normed, attention_gain, input_hat, attention_factor)).astype(
                jnp.bfloat16
            )
        )
    summed = (
        lax.psum_scatter(
            acc_attention_gain.astype(jnp.bfloat16), "fsdp", scatter_dimension=0, tiled=True
        ).astype(jnp.float32),
        lax.psum_scatter(
            acc_head_gains[0].astype(jnp.bfloat16), "fsdp", scatter_dimension=0, tiled=True
        ).astype(jnp.float32),
        lax.psum_scatter(
            acc_head_gains[1].astype(jnp.bfloat16), "fsdp", scatter_dimension=0, tiled=True
        ).astype(jnp.float32),
        lax.psum_scatter(
            acc_query.astype(jnp.bfloat16), "fsdp", scatter_dimension=0, tiled=True
        ).astype(jnp.float32),
        lax.psum_scatter(
            acc_key.astype(jnp.bfloat16), "fsdp", scatter_dimension=0, tiled=True
        ).astype(jnp.float32),
        lax.psum_scatter(
            acc_value.astype(jnp.bfloat16), "fsdp", scatter_dimension=0, tiled=True
        ).astype(jnp.float32),
        lax.psum_scatter(
            acc_output.astype(jnp.bfloat16), "fsdp", scatter_dimension=0, tiled=True
        ).astype(jnp.float32),
        lax.psum_scatter(
            acc_expert_gain.astype(jnp.bfloat16), "fsdp", scatter_dimension=0, tiled=True
        ).astype(jnp.float32),
        lax.psum_scatter(
            acc_router.astype(jnp.bfloat16), "fsdp", scatter_dimension=0, tiled=True
        ).astype(jnp.float32),
    )
    return (
        jnp.stack(layer_rows),
        jnp.stack(input_rows),
        summed[0],
        summed[1],
        summed[2],
        summed[3],
        summed[4],
        summed[5],
        summed[6],
        summed[7],
        summed[8],
        acc_gate,
        acc_up,
        acc_down,
    )


def small_device(
    tokens,
    cotangent,
    expert_ids,
    attention_gain,
    query_gain,
    key_gain,
    query_weight,
    key_weight,
    value_weight,
    output_weight,
    expert_gain,
    router_weight,
    gate_weight,
    up_weight,
    down_weight,
):
    count, rows, width = tokens.shape
    hd = query_gain.shape[0]
    f = lax.axis_index("fsdp")
    n_fsdp = lax.axis_size("fsdp")
    seq = rows * n_fsdp
    experts = gate_weight.shape[0]
    expert_count = experts * n_fsdp
    piece = query_weight.shape[0]

    cosine, sine = signed_tables(seq, hd)
    (normed_all, weights, output_pair, router_all, ids_all, grad_all, pre, qkv, prob, context, resid, expert_in) = begin(
        cotangent,
        query_weight,
        key_weight,
        value_weight,
        output_weight,
        router_weight.T,
        expert_ids.transpose(0, 2, 1),
        tokens,
        attention_gain,
        expert_gain,
        cosine,
        sine,
        query_gain,
        key_gain,
    )
    expert_all, act, dx_sum, out_sum, probs, dgp = run_experts(
        expert_in, grad_all, ids_all, router_all, gate_weight, up_weight, down_weight
    )
    layer_output, input_grad, d_query, d_key, d_value, d_output, aux_sum, line = end(
        normed_all,
        weights,
        output_pair,
        pre,
        qkv,
        prob,
        context,
        tokens,
        out_sum,
        resid,
        cotangent,
        dx_sum,
        expert_in,
        probs,
        dgp,
        router_all,
        expert_gain,
        attention_gain,
        query_weight,
        key_weight,
        value_weight,
        cosine,
        sine,
        query_gain,
        key_gain,
    )
    d_gate, d_up, d_down, layer_output, input_grad, d_query, d_output, d_key, d_value = expert_grads(
        act, expert_all, grad_all, layer_output, input_grad, d_query, d_output, d_key, d_value
    )
    own_gain = lax.dynamic_slice_in_dim(attention_gain, f * piece, piece, 0)
    head_piece = hd // n_fsdp
    head_gains = lax.dynamic_slice_in_dim(line[:2, piece:], f * head_piece, head_piece, 1)
    return (
        layer_output,
        input_grad,
        line[0, :piece] / own_gain,
        head_gains[0],
        head_gains[1],
        d_query,
        d_key,
        d_value,
        d_output,
        aux_sum[expert_count],
        aux_sum[:expert_count].T,
        d_gate.reshape(gate_weight.shape),
        d_up.reshape(up_weight.shape),
        d_down.reshape(down_weight.shape),
    )


def solution(mesh):
    body = small_device if (mesh.shape["fsdp"], mesh.shape["tp"]) == (8, 4) else general_device
    return jax.shard_map(
        body,
        mesh=mesh,
        in_specs=(
            P(None, "fsdp", None),
            P(None, "fsdp", None),
            P(None, "fsdp", None),
            P(),
            P(),
            P(),
            P("fsdp", "tp"),
            P("fsdp", "tp"),
            P("fsdp", "tp"),
            P("fsdp", "tp"),
            P(),
            P("fsdp", None),
            P("fsdp", "tp", None),
            P("fsdp", "tp", None),
            P("fsdp", "tp", None),
        ),
        out_specs=(
            P(None, "fsdp", None),
            P(None, "fsdp", None),
            P("fsdp"),
            P("fsdp"),
            P("fsdp"),
            P("fsdp", "tp"),
            P("fsdp", "tp"),
            P("fsdp", "tp"),
            P("fsdp", "tp"),
            P("fsdp"),
            P("fsdp", None),
            P("fsdp", "tp", None),
            P("fsdp", "tp", None),
            P("fsdp", "tp", None),
        ),
        check_vma=False,
    )
```
